32 devices in a mesh: gx: 4 (over x, core), gy: 4 (over z), gz: 2 (over y).
Axes of the slice: x: 2, y: 2, z: 4, core: 2. Of those that a mesh axis runs over, the one named last changes fastest.
Arguments:
- parts: float32 [52, 52, 14, 128], P('gx', 'gy', 'gz'), may hold values from -6 to 6
- cell_matrix: bfloat16 [343, 343], replicated, may hold values from -0.2 to 2
- cell_potential: float32 [343, 8, 8, 2], P(None, 'gx', 'gy', 'gz'), may hold values from 0 to 1
- projectors: bfloat16 [4, 4, 2, 343, 1536], P('gx', 'gy', 'gz'), may hold values from -0.15625 to 0.15625
- slot_atom: int32 [4, 4, 2, 32], P('gx', 'gy'), may hold values from -1 to 63, as said below
- slot_cells: int32 [4, 4, 2, 32, 4], P('gx', 'gy', 'gz'), may hold values from 0 to 3
- coupling: float32 [1024, 12, 12], P(('gx', 'gy')), may hold values from -1.75 to 1.75
Outputs:
- filtered: float32 [52, 52, 14, 128], P('gx', 'gy', 'gz')
The draws below stay inside these ranges and needn't reach their ends.
Inputs may be any that keep to these rules, and one draw needn't show every extreme that they name: `slot_atom`: entry s of partition (i, j, k) is -1 (an empty slot) or the number, within the column (i, j), of an atom whose projectors reach into that partition. Slots c * 16 to c * 16 + 15 of every partition hold only atoms numbered c * 32 to c * 32 + 31, which are owned by partition c of the column along gz. An atom stands at most once in one partition's list.
All inputs are finite; a program needn't handle non-finite values.
Results may differ from the reference program's by a relative error of at most 0.0058.
Values may be sent and summed in bfloat16 or wider, within the bound.
No kernel may reach another device: no remote copies, remote signals or barrier semaphores. Data moves between devices by JAX's collectives and lax.ppermute only.
A program may use at most 64 MiB of HBM per device.

```python
import jax
import jax.numpy as jnp
from jax import lax

ORB = 128
ORDER = 6
CX = 2
CY = 2
CZ = 1
STEPS = 3
PA = 12
POS = 32
BLK = 4
CELL_NODES = 343
NXD = 13
NYD = 13
NZD = 7
NCX = 8
NCY = 8
NCZ = 2
CELLS = 4
CAP = 16
OWN = 32
COL_ATOMS = 64
ATOMS_ALL = 1024
PROJ_COLS = 1536
N_GX = 4
N_GY = 4
N_GZ = 2


def draw_slot_atom(key, part):
    columns = N_GX * N_GY
    first_key, second_key, third_key = jax.random.split(key, 3)
    busy_owner = jax.random.randint(first_key, (columns,), 0, N_GZ)
    filled = jax.random.randint(second_key, (columns, N_GZ, N_GZ), 0, CAP + 1)
    owners = jnp.arange(N_GZ)[None, None, :]
    sources = jnp.arange(N_GZ)[None, :, None]
    busy_mask = owners == busy_owner[:, None, None]
    filled = jnp.where(busy_mask, CAP, filled)
    filled = jnp.where(sources == 0, jnp.maximum(filled, 1), filled)
    spare_owner = (busy_owner + 1) % N_GZ
    spare_mask = (owners == spare_owner[:, None, None]) & (sources == N_GZ - 1)
    filled = jnp.where(spare_mask, jnp.minimum(filled, CAP - 1), filled)
    local_numbers = jnp.arange(OWN)
    scores = jax.random.randint(third_key, (columns, N_GZ, N_GZ, OWN), 0, 1 << 20) * OWN + local_numbers
    forced = (sources[..., None] == 0) & (local_numbers == OWN - 1)
    scores = jnp.where(forced, -1, scores)
    ranked = jnp.argsort(scores, axis=-1)[..., :CAP]
    atom_number = owners[..., None] * OWN + ranked
    occupied = jnp.arange(CAP)[None, None, None, :] < filled[..., None]
    atom_ids = jnp.where(occupied, atom_number, -1)
    return atom_ids.reshape(N_GX, N_GY, N_GZ, POS).astype(jnp.int32)


def draw_cell_matrix(key, part):
    edge_nodes = ORDER + 1
    cell_nodes = edge_nodes ** 3
    first_key, second_key = jax.random.split(key)
    coupling_part = jnp.clip(jax.random.normal(first_key, (cell_nodes, cell_nodes), jnp.float32), -4.0, 4.0)
    diagonal = jax.random.uniform(second_key, (cell_nodes,), jnp.float32, 1.2, 1.8)
    symmetric = (coupling_part + coupling_part.T) * (0.5 / (2.0 * cell_nodes) ** 0.5)
    edge_index = jnp.arange(edge_nodes)
    line_weight = jnp.where((edge_index == 0) | (edge_index == edge_nodes - 1), 2.0, 1.0)
    multiplicity = (line_weight[:, None, None] * line_weight[None, :, None] * line_weight[None, None, :]).reshape(cell_nodes)
    root_weight = jnp.sqrt(multiplicity)
    identity = jnp.eye(cell_nodes, dtype=jnp.float32)
    off_diagonal = symmetric * (1.0 - identity) / (root_weight[:, None] * root_weight[None, :])
    matrix = off_diagonal + identity * (diagonal / multiplicity)[:, None]
    return matrix.astype(jnp.bfloat16)


def touch_ends(values, rng, low, largest):
    longest = values.shape.index(max(values.shape))
    spots = []
    for shift in (0, 1):
        where = [jax.random.randint(jax.random.fold_in(rng, axis), (), 0, length) for axis, length in enumerate(values.shape)]
        where[longest] = (where[longest] + shift) % values.shape[longest]
        spots.append(tuple(where))
    return values.at[spots[0]].set(low).at[spots[1]].set(largest)


def block_levels(key, shape, shards, least, largest):
    def one(axis_at, blocks):
        steps = jax.random.uniform(jax.random.fold_in(jax.random.fold_in(key, 6), axis_at), (blocks,), jnp.float32, least / len(shards), largest / len(shards))
        return jnp.repeat(jnp.exp(steps), shape[axis_at] // blocks).reshape((-1,) + (1,) * (len(shape) - axis_at - 1))

    loudness = one(*shards[0])
    for cut in shards[1:]:
        loudness = loudness * one(*cut)
    return loudness


def bell_draw(key, extent, scale, limit, cuts=(), kind=jnp.bfloat16):
    entries = jax.random.normal(key, extent, jnp.float32) * scale
    if len(cuts) > 0:
        entries = block_levels(key, extent, cuts, -0.22, 0.18) * entries
    return jnp.clip(entries, min=-limit, max=limit).astype(kind)


def setup_inputs(seed: int = 0) -> dict:
    streams_of = jax.random.split(jax.random.key(seed), 8)
    return {
        "parts": bell_draw(streams_of[0], (N_GX * NXD, N_GY * NYD, N_GZ * NZD, ORB), 1.0, 6.0, ((0, 4), (1, 4), (2, 2)), jnp.float32),
        "cell_matrix": draw_cell_matrix(jax.random.fold_in(streams_of[7], 71), 0),
        "cell_potential": jnp.clip(1.0 * jax.random.uniform(streams_of[2], (CELL_NODES, NCX, NCY, NCZ), jnp.float32) ** block_levels(streams_of[2], (CELL_NODES, NCX, NCY, NCZ), ((1, 4), (2, 4), (3, 2)), -0.2, 0.2), 0.0, 1.0),
        "projectors": bell_draw(streams_of[3], (N_GX, N_GY, N_GZ, CELL_NODES, PROJ_COLS), (BLK * CELL_NODES) ** -0.5, 0.15625, ((0, 4), (1, 4), (2, 2))),
        "slot_atom": draw_slot_atom(jax.random.fold_in(streams_of[7], 71), 0),
        "slot_cells": touch_ends(jax.random.randint(streams_of[5], (N_GX, N_GY, N_GZ, POS, BLK), 0, CELLS), jax.random.fold_in(streams_of[5], 1), 0, CELLS - 1).astype(jnp.int32),
        "coupling": bell_draw(streams_of[6], (ATOMS_ALL, PA, PA), PA ** -0.5, 1.75, ((0, 16),), jnp.float32),
    }


center_value = 2.0
half_width = 3.0


def split_axis(values, which_axis, number, stride):
    rotated = jnp.moveaxis(values, which_axis, 0)
    leading = rotated[:number * stride].reshape((number, stride) + rotated.shape[1:])
    closing = rotated[stride::stride][:, None]
    blocks = jnp.concatenate([leading, closing], axis=1)
    return jnp.moveaxis(blocks, (0, 1), (which_axis, which_axis + 1))


def join_axis(blocks, which_axis, stride):
    rotated = jnp.moveaxis(blocks, (which_axis, which_axis + 1), (0, 1))
    number = rotated.shape[0]
    remaining = rotated.shape[2:]
    leading = rotated[:, :stride].reshape((number * stride,) + remaining)
    final_layer = rotated[:, stride]
    empty_row = jnp.zeros((1,) + remaining, rotated.dtype)
    primary = jnp.concatenate([leading, empty_row], axis=0)
    trailing = jnp.concatenate([jnp.zeros((number, stride - 1) + remaining, rotated.dtype), final_layer[:, None]], axis=1)
    appended = jnp.concatenate([empty_row, trailing.reshape((number * stride,) + remaining)], axis=0)
    return jnp.moveaxis(primary + appended, 0, which_axis)


def cell_values(values, cell_counts):
    blocks = split_axis(values, 0, cell_counts[0], ORDER)
    blocks = split_axis(blocks, 2, cell_counts[1], ORDER)
    blocks = split_axis(blocks, 4, cell_counts[2], ORDER)
    blocks = jnp.transpose(blocks, (1, 3, 5, 0, 2, 4, 6))
    edge_nodes = ORDER + 1
    return blocks.reshape(edge_nodes ** 3, cell_counts[0] * cell_counts[1] * cell_counts[2], blocks.shape[-1])


def assemble(cell_data, cell_counts):
    edge_nodes = ORDER + 1
    blocks = cell_data.reshape((edge_nodes, edge_nodes, edge_nodes, cell_counts[0], cell_counts[1], cell_counts[2], cell_data.shape[-1]))
    blocks = jnp.transpose(blocks, (3, 0, 4, 1, 5, 2, 6))
    blocks = join_axis(blocks, 4, ORDER)
    blocks = join_axis(blocks, 2, ORDER)
    return join_axis(blocks, 0, ORDER)


def device_major(cell_data):
    cell_nodes, total_cells, orbitals = cell_data.shape
    arranged = cell_data.reshape(cell_nodes, N_GX, CX, N_GY, CY, N_GZ, CZ, orbitals)
    arranged = jnp.transpose(arranged, (1, 3, 5, 0, 2, 4, 6, 7))
    return arranged.reshape(N_GX * N_GY * N_GZ, cell_nodes, CX * CY * CZ, orbitals)


def cell_major(blocks):
    devices, cell_nodes, number, orbitals = blocks.shape
    arranged = blocks.reshape(N_GX, N_GY, N_GZ, cell_nodes, CX, CY, CZ, orbitals)
    arranged = jnp.transpose(arranged, (3, 0, 4, 1, 5, 2, 6, 7))
    return arranged.reshape(cell_nodes, N_GX * CX * N_GY * CY * N_GZ * CZ, orbitals)


def reference(parts, cell_matrix, cell_potential, projectors, slot_atom, slot_cells, coupling):
    devices = N_GX * N_GY * N_GZ
    cell_counts = (CX * N_GX, CY * N_GY, CZ * N_GZ)
    cell_nodes = cell_matrix.shape[0]
    orbitals = parts.shape[-1]
    blocks = parts.reshape(N_GX, NXD, N_GY, NYD, N_GZ, NZD, orbitals)
    assembled = join_axis(blocks, 4, ORDER * CZ)
    assembled = join_axis(assembled, 2, ORDER * CY)
    assembled = join_axis(assembled, 0, ORDER * CX)
    projector_cols = projectors.reshape(devices, cell_nodes, POS * BLK, PA)
    cell_index = slot_cells.reshape(devices, POS * BLK)
    column = jnp.arange(devices, dtype=jnp.int32) // N_GZ
    atom_ids = slot_atom.reshape(devices, POS)
    atom_count = coupling.shape[0]
    global_ids = jnp.where(atom_ids >= 0, column[:, None] * COL_ATOMS + atom_ids, atom_count).astype(jnp.int32)
    potential = device_major(cell_potential.reshape(cell_nodes, -1, 1))[..., 0]

    def apply_hamiltonian(values):
        cell_data = device_major(cell_values(values, cell_counts))

        def project_slots(inputs):
            cells_dev, proj_dev, index_dev = inputs
            picked = jnp.take(cells_dev.astype(jnp.bfloat16), index_dev, axis=1).astype(jnp.float32)
            products = jnp.einsum('nqa,nqo->qao', proj_dev.astype(jnp.float32), picked)
            return products.reshape(POS, BLK, PA, orbitals).sum(axis=1)

        partials = lax.map(project_slots, (cell_data, projector_cols, cell_index))
        totals = jax.ops.segment_sum(partials.reshape(devices * POS, PA, orbitals), global_ids.reshape(-1), num_segments=atom_count + 1)[:atom_count]
        coupled = jnp.einsum('tab,tbo->tao', coupling, totals, precision=lax.Precision.HIGHEST)
        coefficient = jnp.concatenate([coupled.astype(jnp.bfloat16), jnp.zeros((1, PA, orbitals), jnp.bfloat16)], axis=0)
        slot_coef = coefficient[global_ids]

        def cell_work(inputs):
            cells_dev, potential_dev, proj_dev, index_dev, coef_dev = inputs
            cell_bf = cells_dev.astype(jnp.bfloat16)
            stiffness = jnp.dot(cell_matrix, cell_bf.reshape(cell_nodes, -1), preferred_element_type=jnp.float32).reshape(cells_dev.shape)
            stiffness = stiffness + potential_dev[:, :, None] * cells_dev
            spread = jnp.broadcast_to(coef_dev[:, None], (POS, BLK, PA, orbitals)).reshape(POS * BLK, PA, orbitals)
            contribution = jnp.einsum('nqa,qao->nqo', proj_dev.astype(jnp.float32), spread.astype(jnp.float32))
            return stiffness.at[:, index_dev].add(contribution)

        result = lax.map(cell_work, (cell_data, potential, projector_cols, cell_index, slot_coef))
        return assemble(cell_major(result), cell_counts)

    previous = assembled
    current = (apply_hamiltonian(assembled) - center_value * assembled) / half_width
    for degree in range(1, STEPS):
        following = 2.0 * (apply_hamiltonian(current) - center_value * current) / half_width - previous
        previous, current = current, following
    output = split_axis(current, 0, N_GX, ORDER * CX)
    output = split_axis(output, 2, N_GY, ORDER * CY)
    output = split_axis(output, 4, N_GZ, ORDER * CZ)
    return output.reshape(N_GX * NXD, N_GY * NYD, N_GZ * NZD, orbitals)
```

```python
import functools

import jax
import jax.numpy as jnp
import numpy as np
from jax import lax
from jax.experimental import pallas as pl
from jax.experimental.pallas import tpu as pltpu
from jax.sharding import PartitionSpec as P

ORDER = 6
STEPS = 3
PA = 12
POS = 32
BLK = 4

center_value = 2.0
half_width = 3.0

EDGE = ORDER + 1
PAD = 8
SLOTS = POS * PA
F32 = jnp.float32
BF16 = jnp.bfloat16
HALO = jnp.bfloat16


def up(value, multiple):
    return -(-value // multiple) * multiple


class Sizes:
    def __init__(self, nx, ny, nz, orbitals, links):
        assert nz == EDGE
        self.nx, self.ny, self.orb = nx, ny, orbitals
        self.cells = [(p, q) for p in range((nx - 1) // ORDER) for q in range((ny - 1) // ORDER)]
        self.rows = nx * ny * PAD
        self.line_x = ny * PAD
        self.xface = up(ny * PAD, 16)
        self.yface = up(nx * PAD, 16)
        self.face_b = up(ny, PAD)
        self.zface = up(nx * self.face_b, 16)
        self.cell_rows = EDGE * EDGE * PAD
        self.cell_pad = up(self.cell_rows, 16)
        self.all_pad = up(self.cell_pad * len(self.cells), 128)
        self.fcell = EDGE * PAD
        self.fall = up(self.fcell * len(self.cells), 256)
        self.links = links
        self.spill = 2 * PAD * PAD


VMEM = pl.BlockSpec(memory_space=pltpu.VMEM)
SMEM = pl.BlockSpec(memory_space=pltpu.SMEM)


def kernel_call(body, outs, scalars, arrays, scratch=(), flops=0, limit=24 << 20):
    nbytes = sum(int(np.prod(a.shape)) * a.dtype.itemsize for a in list(arrays) + list(outs))
    return pl.pallas_call(
        body,
        out_shape=outs,
        in_specs=[SMEM] * len(scalars) + [VMEM] * len(arrays),
        out_specs=[VMEM] * len(outs),
        scratch_shapes=list(scratch),
        compiler_params=pltpu.CompilerParams(vmem_limit_bytes=limit),
        cost_estimate=pl.CostEstimate(flops=flops, bytes_accessed=nbytes, transcendentals=0),
    )(*scalars, *arrays)


def shape(rows, cols, dtype):
    return jax.ShapeDtypeStruct((rows, cols), dtype)


def dot(a, b):
    return jnp.dot(a, b, preferred_element_type=F32)


def matrices_body(sz, proj, row_key, face_key, col_key, qt, *qt_faces):
    nodes = proj.shape[0]
    keys = jnp.concatenate([row_key[...]] + [f[...] for f in face_key], axis=0)
    expand = (keys == lax.broadcasted_iota(jnp.int32, (keys.shape[0], nodes), 1)).astype(BF16)
    spread = dot(expand, proj[...]).astype(BF16)
    cols = proj.shape[1]
    key = col_key[...]
    for g in range(len(sz.cells)):
        pick = (key == lax.broadcasted_iota(jnp.int32, (cols, SLOTS), 1) + g * SLOTS).astype(BF16)
        block = dot(spread, pick).astype(BF16)
        qt[g * sz.cell_pad : (g + 1) * sz.cell_pad, :] = block[: sz.cell_pad]
        for j, qf in enumerate(qt_faces):
            at = sz.cell_pad + j * PAD * PAD
            qf[g * PAD * PAD : (g + 1) * PAD * PAD, :] = block[at : at + PAD * PAD]
    rest = sz.all_pad - sz.cell_pad * len(sz.cells)
    if rest:
        qt[sz.cell_pad * len(sz.cells) :, :] = jnp.zeros((rest, SLOTS), BF16)


def make_matrices(sz, proj, row_key, face_keys, col_key):
    count = len(face_keys)

    def body(*refs):
        proj_r, row_r = refs[0], refs[1]
        faces = refs[2 : 2 + count]
        matrices_body(sz, proj_r, row_r, faces, refs[2 + count], *refs[3 + count :])

    outs = [shape(sz.all_pad, SLOTS, BF16)]
    outs += [shape(len(sz.cells) * PAD * PAD, SLOTS, BF16)] * count
    return kernel_call(
        body, outs, [], [proj, row_key, *face_keys, col_key], flops=3 * 10**9, limit=32 << 20
    )


def turn_body(sz, qt, kin, pot, row_key, lane_key, q, kout, vout):
    q[...] = qt[...].T
    nodes = kin.shape[0]
    expand = row_key[...] == lax.broadcasted_iota(jnp.int32, (sz.cell_pad, nodes), 1)
    gather = lane_key[...] == lax.broadcasted_iota(jnp.int32, (nodes, sz.cell_pad), 0)
    tall = dot(expand.astype(BF16), kin[...]).astype(BF16)
    kout[...] = dot(tall, gather.astype(BF16)).astype(BF16)
    values = jnp.dot(
        expand.astype(F32), pot[...], precision=lax.Precision.HIGHEST, preferred_element_type=F32
    )
    for g in range(len(sz.cells)):
        vout[g * sz.cell_pad : (g + 1) * sz.cell_pad, :] = jnp.broadcast_to(
            values[:, g : g + 1], (sz.cell_pad, sz.orb)
        )


def turn_matrices(sz, qt, kin, pot, row_key, lane_key):
    outs = [
        shape(SLOTS, sz.all_pad, BF16),
        shape(sz.cell_pad, sz.cell_pad, BF16),
        shape(len(sz.cells) * sz.cell_pad, sz.orb, F32),
    ]
    return kernel_call(
        functools.partial(turn_body, sz), outs, [], [qt, kin, pot, row_key, lane_key], flops=10**9
    )


def cell_block(sz, z, cell):
    p, q = cell
    layers = []
    for a in range(EDGE):
        start = (ORDER * p + a) * sz.line_x + ORDER * q * PAD
        layers.append(z[start : start + EDGE * PAD, :])
    layers.append(jnp.zeros((sz.cell_pad - sz.cell_rows, sz.orb), F32))
    return jnp.concatenate(layers, axis=0)


def write_faces(sz, r, sx_lo, sx_hi, sy_lo, sy_hi):
    pad_x = jnp.zeros((sz.xface - sz.line_x, sz.orb), F32)
    pad_y = jnp.zeros((sz.yface - sz.nx * PAD, sz.orb), F32)
    last = (sz.nx - 1) * sz.line_x
    sx_lo[...] = jnp.concatenate([r[0 : sz.line_x, :], pad_x], axis=0).astype(HALO)
    sx_hi[...] = jnp.concatenate([r[last : last + sz.line_x, :], pad_x], axis=0).astype(HALO)
    for out, b in ((sy_lo, 0), (sy_hi, sz.ny - 1)):
        rows = [r[a * sz.line_x + b * PAD : a * sz.line_x + (b + 1) * PAD, :] for a in range(sz.nx)]
        out[...] = jnp.concatenate(rows + [pad_y], axis=0)


def face_outs(sz):
    return [shape(sz.xface, sz.orb, HALO)] * 2 + [shape(sz.yface, sz.orb, F32)] * 2


def start_body(sz, parts, r4, sx_lo, sx_hi, sy_lo, sy_hi):
    nz = parts.shape[2]
    r4[...] = jnp.zeros(r4.shape, F32)
    r4[:, :, :nz, :] = parts[...]
    r = r4.reshape(sz.rows, sz.orb)
    write_faces(sz, r, sx_lo, sx_hi, sy_lo, sy_hi)


def start_faces(sz, parts):
    outs = [jax.ShapeDtypeStruct((sz.nx, sz.ny, PAD, sz.orb), F32)] + face_outs(sz)
    r4, *faces = kernel_call(functools.partial(start_body, sz), outs, [], [parts])
    return r4.reshape(sz.rows, sz.orb), faces


def cross_body(sz, xr_lo, xr_hi, ry_lo, ry_hi, sy_lo, sy_hi):
    last = (sz.nx - 1) * PAD
    lo, hi = xr_lo[...].astype(F32), xr_hi[...].astype(F32)
    for raw, out, b in ((ry_lo, sy_lo, 0), (ry_hi, sy_hi, sz.ny - 1)):
        value = raw[...]
        value = jnp.concatenate(
            [
                value[:PAD] + lo[b * PAD : (b + 1) * PAD],
                value[PAD:last],
                value[last : last + PAD] + hi[b * PAD : (b + 1) * PAD],
                value[last + PAD :],
            ],
            axis=0,
        )
        out[...] = value.astype(HALO)


def cross_faces(sz, xr_lo, xr_hi, ry_lo, ry_hi):
    outs = [shape(sz.yface, sz.orb, HALO)] * 2
    return kernel_call(functools.partial(cross_body, sz), outs, [], [xr_lo, xr_hi, ry_lo, ry_hi])


def add_xy(sz, ra, r, xr_lo, xr_hi, yr_lo, yr_hi):
    ra[0 : sz.rows, :] = r[...]
    last = (sz.nx - 1) * sz.line_x
    ra[0 : sz.line_x, :] += xr_lo[...].astype(F32)[: sz.line_x]
    ra[last : last + sz.line_x, :] += xr_hi[...].astype(F32)[: sz.line_x]
    for recv, b in ((yr_lo, 0), (yr_hi, sz.ny - 1)):
        value = recv[...].astype(F32)
        for a in range(sz.nx):
            at = a * sz.line_x + b * PAD
            ra[at : at + PAD, :] += value[a * PAD : (a + 1) * PAD]


def pack_z(sz, ra, c, valid):
    rows = []
    for a in range(sz.nx):
        for b in range(0, sz.face_b, PAD):
            rows.append(ra[pl.ds(a * sz.line_x + b * PAD + c, PAD, stride=PAD), :])
    rest = sz.zface - sz.nx * sz.face_b
    if rest:
        rows.append(jnp.zeros((rest, sz.orb), F32))
    return (jnp.concatenate(rows, axis=0) * valid).astype(HALO)


def add_z(sz, y, c, face):
    for a in range(sz.nx):
        for b in range(0, sz.ny, PAD):
            n = min(PAD, sz.ny - b)
            at = pl.ds(a * sz.line_x + b * PAD + c, n, stride=PAD)
            y[at, :] = y[at, :] + face[a * sz.face_b + b : a * sz.face_b + b + n]


def face_cells(sz, ra, c):
    rows = []
    for p, q in sz.cells:
        for a in range(EDGE):
            at = (ORDER * p + a) * sz.line_x + ORDER * q * PAD
            rows.append(ra[pl.ds(at + c, PAD, stride=PAD), :])
        rows.append(jnp.zeros((PAD, sz.orb), F32))
    return jnp.concatenate(rows, axis=0).astype(BF16)


def project_body(sz, shifts, has_local, refs):
    take = iter(refs)
    info = next(take)
    r = next(take)
    loc = next(take) if has_local else None
    halos = [next(take) for _ in range(4)]
    q = next(take)
    qfaces = [next(take) for _ in range(sz.links)]
    maps = next(take)
    y, own = next(take), next(take)
    messages = [next(take) for _ in range(shifts)]
    ra = next(take)
    ra[sz.rows :, :] = jnp.zeros((sz.spill, sz.orb), F32)
    add_xy(sz, ra, r, *halos)
    y[...] = ra[0 : sz.rows, :] + loc[...] if has_local else ra[0 : sz.rows, :]
    blocks = [cell_block(sz, y, cell).astype(BF16) for cell in sz.cells]
    rest = sz.all_pad - sz.cell_pad * len(sz.cells)
    if rest:
        blocks.append(jnp.zeros((rest, sz.orb), BF16))
    sums = [dot(q[...], jnp.concatenate(blocks, axis=0)).astype(BF16)]
    for j in range(sz.links):
        sums.append(dot(qfaces[j][...], face_cells(sz, ra, info[0, j])).astype(BF16))
    known = jnp.concatenate(sums, axis=0)
    mapped = dot(maps[...], known)
    own[...] = mapped[:SLOTS]
    link_of = link_shifts(sz, shifts)
    for s, message in enumerate(messages):
        message[0:SLOTS, :] = mapped[(s + 1) * SLOTS : (s + 2) * SLOTS].astype(HALO)
        for j, shift in enumerate(link_of):
            if shift == s + 1:
                face = pack_z(sz, ra, info[0, j], info[1, j].astype(F32))
                message[SLOTS : SLOTS + sz.zface, :] = face


def link_shifts(sz, shifts):
    return [1, shifts][: sz.links]


def project(sz, shifts, info, r, loc, halos, q, qfaces, maps):
    outs = [shape(sz.rows, sz.orb, F32), shape(SLOTS, sz.orb, F32)]
    for s in range(1, shifts + 1):
        rows = SLOTS + (sz.zface if s in link_shifts(sz, shifts) else 0)
        outs.append(shape(rows, sz.orb, HALO))
    arrays = [r] + ([loc] if loc is not None else []) + list(halos) + [q, *qfaces, maps]

    def body(*refs):
        project_body(sz, shifts, loc is not None, refs)

    limit = (32 << 20) if maps.size < 10**7 else (56 << 20)
    y, own, *messages = kernel_call(
        body,
        outs,
        [info],
        arrays,
        scratch=[pltpu.VMEM((sz.rows + sz.spill, sz.orb), F32)],
        flops=4 * 10**8,
        limit=limit,
    )
    return y, own, messages


def apply_body(sz, shifts, has_previous, scale, keep, refs):
    take = iter(refs)
    info = next(take)
    yin = next(take)
    previous = next(take) if has_previous else None
    own = next(take)
    messages = [next(take) for _ in range(shifts)]
    cblk, qt, kin, pot = next(take), next(take), next(take), next(take)
    r, loc, y = next(take), next(take), next(take)
    faces = [next(take) for _ in range(4)]
    totals = own[...]
    for message in messages:
        totals = totals + message[0:SLOTS, :].astype(F32)
    coef = dot(cblk[...], totals.astype(BF16)).astype(BF16)
    y[...] = yin[...]
    for j, shift in enumerate(link_shifts(sz, shifts)):
        add_z(sz, y, info[2, j], messages[shift - 1][SLOTS : SLOTS + sz.zface, :].astype(F32))
    blocks = [cell_block(sz, y, cell) for cell in sz.cells]
    stiff = dot(kin[...], jnp.concatenate([b.astype(BF16) for b in blocks], axis=1))
    r[...] = jnp.zeros(r.shape, F32)
    for g, (p, q) in enumerate(sz.cells):
        rows = slice(g * sz.cell_pad, (g + 1) * sz.cell_pad)
        value = stiff[:, g * sz.orb : (g + 1) * sz.orb] + pot[rows, :] * blocks[g]
        value = (value + dot(qt[rows, :], coef)) * scale
        for a in range(EDGE):
            start = (ORDER * p + a) * sz.line_x + ORDER * q * PAD
            r[start : start + EDGE * PAD, :] += value[a * EDGE * PAD : (a + 1) * EDGE * PAD]
    local = (-center_value * scale) * y[...]
    loc[...] = local - previous[...] if has_previous else local
    write_faces(sz, r, *faces)


def apply(sz, shifts, info, y, previous, own, messages, cblk, qt, kin, pot, scale):
    outs = [shape(sz.rows, sz.orb, F32)] * 3 + face_outs(sz)
    arrays = [y] + ([previous] if previous is not None else [])
    arrays += [own, *messages, cblk, qt, kin, pot]

    def body(*refs):
        apply_body(sz, shifts, previous is not None, scale, True, refs)

    r, loc, y, *faces = kernel_call(body, outs, [info], arrays, flops=6 * 10**8, limit=32 << 20)
    return r, loc, y, faces


def last_faces_body(sz, refs):
    take = iter(refs)
    info, r = next(take), next(take)
    halos = [next(take) for _ in range(4)]
    outs = [next(take) for _ in range(sz.links)]
    ra = next(take)
    ra[sz.rows :, :] = jnp.zeros((sz.spill, sz.orb), F32)
    add_xy(sz, ra, r, *halos)
    for j, out in enumerate(outs):
        out[...] = pack_z(sz, ra, info[0, j], info[1, j].astype(F32))


def last_faces(sz, info, r, halos):
    def body(*refs):
        last_faces_body(sz, refs)

    outs = [shape(sz.zface, sz.orb, HALO)] * sz.links
    scratch = [pltpu.VMEM((sz.rows + sz.spill, sz.orb), F32)]
    return kernel_call(body, outs, [info], [r, *halos], scratch=scratch)


def finish_body(sz, refs):
    take = iter(refs)
    info, r, loc = next(take), next(take), next(take)
    halos = [next(take) for _ in range(4)]
    zr = [next(take) for _ in range(sz.links)]
    out, ra = next(take), next(take)
    add_xy(sz, ra, r, *halos)
    for j, face in enumerate(zr):
        add_z(sz, ra, info[2, j], face[...].astype(F32))
    value = ra[0 : sz.rows, :] + loc[...]
    out[...] = value.reshape(sz.nx, sz.ny, PAD, sz.orb)[:, :, : out.shape[2], :]


def finish(sz, info, r, loc, halos, zr, nz):
    def body(*refs):
        finish_body(sz, refs)

    outs = [jax.ShapeDtypeStruct((sz.nx, sz.ny, nz, sz.orb), F32)]
    scratch = [pltpu.VMEM((sz.rows + sz.spill, sz.orb), F32)]
    return kernel_call(body, outs, [info], [r, loc, *halos, *zr], scratch=scratch)[0]


def swap_faces(axis, lo, hi):
    count = lax.axis_size(axis)
    forward = [(i, i + 1) for i in range(count - 1)]
    backward = [(target, source) for source, target in forward]
    return lax.ppermute(hi, axis, forward), lax.ppermute(lo, axis, backward)


def local(parts, cell_matrix, cell_potential, projectors, slot_atom, slot_cells, coupling):
    nx, ny, nz, orbitals = parts.shape
    nodes = cell_matrix.shape[0]
    devices = lax.axis_size("gz")
    shifts = devices - 1
    me = lax.axis_index("gz")
    links = min(2, shifts)
    sz = Sizes(nx, ny, nz, orbitals, links)
    cells = len(sz.cells)

    if devices == 2:
        layer = jnp.where(me == 0, ORDER, 0)
        info = jnp.stack([layer, jnp.ones_like(layer), layer])[:, None]
    else:
        send = jnp.array([ORDER, 0], jnp.int32)
        valid = jnp.stack([me < devices - 1, me > 0]).astype(jnp.int32)
        info = jnp.stack([send, valid, ORDER - send])
    info = info.astype(jnp.int32)
    ring = [[(i, (i + s) % devices) for i in range(devices)] for s in range(devices)]

    i = np.arange(sz.cell_pad)
    real = (i < sz.cell_rows) & (i % PAD < EDGE)
    node = np.where(real, i // PAD * EDGE + i % PAD, -1).astype(np.int32)
    row_key, lane_key = jnp.asarray(node[:, None]), jnp.asarray(node[None, :])
    i = np.arange(PAD * PAD)
    real = (i < sz.fcell) & (i % PAD < EDGE)
    base = np.where(real, (i // PAD * EDGE + i % PAD) * EDGE, -EDGE * PAD).astype(np.int32)
    face_keys = [jnp.asarray(base[:, None]) + info[2, j] for j in range(links)]
    i = np.arange(POS * BLK * PA)
    slot_row = (i // (BLK * PA) * PA + i % PA).astype(np.int32)
    cell_index = jnp.repeat(slot_cells.reshape(POS * BLK), PA)
    col_key = (cell_index * SLOTS + slot_row)[:, None]

    table = slot_atom.reshape(devices, POS)
    rotated = [table[(me + s) % devices] for s in range(devices)]

    def atom_keys(atoms, empty):
        offset = np.arange(PA, dtype=np.int32)
        keys = jnp.where(atoms[:, None] >= 0, atoms[:, None] * PA + offset, empty)
        return keys.reshape(SLOTS)

    known = [atom_keys(rotated[0], -2)]
    for j, shift in enumerate(link_shifts(sz, shifts)):
        known.append(jnp.where(info[1, j] > 0, atom_keys(rotated[shift], -2), -2))
    known = jnp.concatenate(known)
    wanted = jnp.concatenate([atom_keys(atoms, -1) for atoms in rotated])
    maps = (wanted[:, None] == known[None, :]).astype(BF16)
    picked = jnp.take(coupling, jnp.clip(rotated[0], 0, coupling.shape[0] - 1), axis=0)
    picked = jnp.where(rotated[0][:, None, None] >= 0, picked, 0.0).astype(BF16)
    eye = jnp.eye(POS, dtype=BF16)
    cblk = (picked[:, :, None, :] * eye[:, None, :, None]).reshape(SLOTS, SLOTS)

    r, (sx_lo, sx_hi, sy_lo, sy_hi) = start_faces(sz, parts)

    def exchange_xy(sx_lo, sx_hi, sy_lo, sy_hi):
        xr = swap_faces("gx", sx_lo, sx_hi)
        cross = cross_faces(sz, *xr, sy_lo, sy_hi)
        yr = swap_faces("gy", *cross)
        return (*xr, *yr)

    halos = exchange_xy(sx_lo, sx_hi, sy_lo, sy_hi)
    qt, *qt_faces = make_matrices(
        sz, projectors.reshape(nodes, POS * BLK * PA), row_key, face_keys, col_key
    )
    qfaces = []
    for j, shift in enumerate(link_shifts(sz, shifts)):
        back = [(target, source) for source, target in ring[shift]]
        qfaces.append(lax.ppermute(qt_faces[j], "gz", back).T)
    q, kin, pot = turn_matrices(
        sz, qt, cell_matrix, cell_potential.reshape(nodes, cells), row_key, lane_key
    )

    loc = previous = None
    scale = 1.0 / half_width
    for step in range(STEPS):
        y, own, messages = project(sz, shifts, info, r, loc, halos, q, qfaces, maps)
        received = [lax.ppermute(m, "gz", ring[s + 1]) for s, m in enumerate(messages)]
        r, loc, y, faces = apply(
            sz, shifts, info, y, previous, own, received, cblk, qt, kin, pot, scale
        )
        previous, scale = y, 2.0 / half_width
        halos = exchange_xy(*faces)
    sent = last_faces(sz, info, r, halos)
    zr = [lax.ppermute(f, "gz", ring[s]) for f, s in zip(sent, link_shifts(sz, shifts))]
    return finish(sz, info, r, loc, halos, zr, nz)


def solution(mesh):
    in_specs = (
        P("gx", "gy", "gz", None),
        P(),
        P(None, "gx", "gy", "gz"),
        P("gx", "gy", "gz", None, None),
        P("gx", "gy", None, None),
        P("gx", "gy", "gz", None, None),
        P(("gx", "gy"), None, None),
    )
    out_specs = P("gx", "gy", "gz", None)
    return jax.shard_map(local, mesh=mesh, in_specs=in_specs, out_specs=out_specs, check_vma=False)
```

```python
import functools

import jax
import jax.numpy as jnp
import numpy as np
from jax import lax
from jax.experimental import pallas as pl
from jax.experimental.pallas import tpu as pltpu
from jax.sharding import PartitionSpec as P

ORDER = 6
STEPS = 3
PA = 12
POS = 32
BLK = 4

center_value = 2.0
half_width = 3.0

EDGE = ORDER + 1
PAD = 8
SLOTS = POS * PA
F32 = jnp.float32
BF16 = jnp.bfloat16
HALO = jnp.bfloat16


def up(value, multiple):
    return -(-value // multiple) * multiple


class Sizes:
    def __init__(self, nx, ny, nz, orbitals, shifts):
        assert nz == EDGE
        self.nx, self.ny, self.orb = nx, ny, orbitals
        self.cells = [(p, q) for p in range((nx - 1) // ORDER) for q in range((ny - 1) // ORDER)]
        self.rows = nx * ny * PAD
        self.line_x = ny * PAD
        self.xface = up(ny * PAD, 16)
        self.yface = up(nx * PAD, 16)
        self.face_b = up(ny, PAD)
        self.zface = up(nx * self.face_b, 16)
        self.cell_rows = EDGE * EDGE * PAD
        self.cell_pad = up(self.cell_rows, 16)
        self.all_pad = up(self.cell_pad * len(self.cells), 128)
        self.fcell = EDGE * PAD
        self.fall = up(self.fcell * len(self.cells), 256)
        self.shifts, self.links = shifts, min(2, shifts)
        self.spill = 2 * PAD * PAD


VMEM = pl.BlockSpec(memory_space=pltpu.VMEM)


def kernel_call(body, outs, arrays, scratch=(), flops=0, limit=24 << 20):
    nbytes = sum(int(np.prod(a.shape)) * a.dtype.itemsize for a in list(arrays) + list(outs))
    return pl.pallas_call(
        body,
        out_shape=outs,
        in_specs=[VMEM] * len(arrays),
        out_specs=[VMEM] * len(outs),
        scratch_shapes=list(scratch),
        compiler_params=pltpu.CompilerParams(vmem_limit_bytes=limit),
        cost_estimate=pl.CostEstimate(flops=flops, bytes_accessed=nbytes, transcendentals=0),
    )(*arrays)


def shape(rows, cols, dtype):
    return jax.ShapeDtypeStruct((rows, cols), dtype)


def dot(a, b):
    return jnp.dot(a, b, preferred_element_type=F32)


def is_odd(axis):
    return lax.rem(lax.axis_index(axis), 2) == 1


def by_parity(axis, even, odd):
    return jnp.where(is_odd(axis), odd, even)


def link_shifts(sz):
    return [1, sz.shifts][: sz.links]


def layer_sent(sz, j):
    if sz.links == 1:
        return jnp.where(lax.axis_index("gz") == 0, ORDER, 0)
    return [ORDER, 0][j]


def layer_received(sz, j):
    return layer_sent(sz, 0) if sz.links == 1 else [0, ORDER][j]


def link_valid(sz, j):
    if sz.links == 1:
        return None
    me = lax.axis_index("gz")
    return jnp.where(me < sz.shifts, 1, 0) if j == 0 else jnp.where(me > 0, 1, 0)


def iota(rows, cols, dim):
    return lax.broadcasted_iota(jnp.int32, (rows, cols), dim)


def twelfth(value):
    return (value * (2**19 // PA + 1)) >> 19


def node_key(i):
    low = i & (PAD - 1)
    return jnp.where((low < EDGE) & (i < EDGE * EDGE * PAD), (i >> 3) * EDGE + low, -1)


def dot_last(a, b, precision=None):
    dims = (((1,), (1,)), ((), ()))
    return lax.dot_general(a, b, dims, precision=precision, preferred_element_type=F32)


def sum_body(sz, proj, cells, qt, *qt_faces):
    nodes, cols = proj.shape
    i = iota(cols, POS, 0)
    first = iota(cols, POS, 1) * (BLK * PA)
    in_slot = ((i >= first) & (i < first + BLK * PA)).astype(BF16)
    of_block = dot(in_slot, cells[...].astype(F32).astype(BF16))
    i = iota(cols, BLK, 0)
    block = twelfth(i)
    cell = jnp.sum(
        jnp.where((block & (BLK - 1)) == iota(cols, BLK, 1), of_block, 0.0), axis=1, keepdims=True
    )
    i, block = i[:, :1], block[:, :1]
    row = (block >> (BLK.bit_length() - 1)) * PA + (i - block * PA)
    key = cell.astype(jnp.int32) * SLOTS + row
    targets = len(sz.cells) * SLOTS
    pick = (key == iota(cols, targets, 1)).astype(BF16)
    summed = dot(proj[...], pick).astype(BF16)
    keys = [node_key(iota(sz.cell_pad, nodes, 0))]
    for j in range(sz.links):
        keys.append(
            jnp.where(
                iota(PAD * PAD, nodes, 0) < sz.fcell,
                node_key(iota(PAD * PAD, nodes, 0)) * EDGE + layer_received(sz, j),
                -1,
            )
        )
        low = iota(PAD * PAD, nodes, 0) & (PAD - 1)
        keys[-1] = jnp.where(low < EDGE, keys[-1], -1)
    expand = (jnp.concatenate(keys, axis=0) == iota(sz.cell_pad + sz.links * PAD * PAD, nodes, 1))
    full = dot(expand.astype(BF16), summed)
    for g in range(len(sz.cells)):
        value = full[:, g * SLOTS : (g + 1) * SLOTS]
        qt[g * sz.cell_pad : (g + 1) * sz.cell_pad, :] = value[: sz.cell_pad].astype(BF16)
    rest = sz.all_pad - sz.cell_pad * len(sz.cells)
    if rest:
        qt[sz.cell_pad * len(sz.cells) :, :] = jnp.zeros((rest, SLOTS), BF16)
    for j, qf in enumerate(qt_faces):
        at = sz.cell_pad + j * PAD * PAD
        rows = [full[at : at + PAD * PAD, g * SLOTS : (g + 1) * SLOTS] for g in range(len(sz.cells))]
        qf[...] = jnp.concatenate(rows, axis=0).T.astype(BF16)


def sum_matrices(sz, proj, cells):
    outs = [shape(sz.all_pad, SLOTS, BF16)]
    outs += [shape(SLOTS, len(sz.cells) * PAD * PAD, BF16)] * sz.links
    body = functools.partial(sum_body, sz)
    return kernel_call(body, outs, [proj, cells], flops=3 * 10**9, limit=32 << 20)


def slot_keys(sz, table, dim):
    exact = lax.Precision.HIGHEST
    shape2 = (SLOTS, POS) if dim == 0 else (POS, SLOTS)
    i, s = iota(*shape2, dim), iota(*shape2, 1 - dim)
    spread = ((i >= s * PA) & (i < s * PA + PA)).astype(F32)
    if dim == 0:
        atoms = dot_last(spread, table, exact)
    else:
        atoms = jnp.dot(table, spread, precision=exact, preferred_element_type=F32)
    devices = sz.shifts + 1
    at = iota(*atoms.shape, 1 - dim)
    me = lax.axis_index("gz")
    keys = []
    for shift in range(devices):
        chosen = jnp.where(at == lax.rem(me + shift, devices), atoms, 0.0)
        atom = jnp.sum(chosen, axis=1 - dim, keepdims=True).astype(jnp.int32)
        i = iota(*atom.shape, dim)
        keys.append((atom, jnp.where(atom >= 0, atom * PA + i - twelfth(i) * PA, -1)))
    return keys


def turn_body(sz, qt, kin, pot, atoms, coupling, *refs):
    q, kout, vout, maps = refs[:4]
    back = refs[4] if sz.links else None
    c_hi, c_lo, wide = refs[-3:]
    q[...] = qt[...].T
    nodes = kin.shape[0]
    expand = (node_key(iota(sz.cell_pad, nodes, 0)) == iota(sz.cell_pad, nodes, 1)).astype(BF16)
    gather = (node_key(iota(nodes, sz.cell_pad, 1)) == iota(nodes, sz.cell_pad, 0)).astype(BF16)
    tall = dot(expand, kin[...]).astype(BF16)
    kout[...] = dot(tall, gather).astype(BF16)
    value, values = pot[...], 0.0
    for _ in range(3):
        part = value.astype(BF16)
        values = values + dot_last(expand, part)
        value = value - part.astype(F32)
    for g in range(len(sz.cells)):
        vout[g * sz.cell_pad : (g + 1) * sz.cell_pad, :] = jnp.broadcast_to(
            values[:, g : g + 1], (sz.cell_pad, sz.orb)
        )
    table = atoms[...].astype(F32)
    rows, cols = slot_keys(sz, table, 0), slot_keys(sz, table, 1)
    known = [jnp.where(cols[0][1] >= 0, cols[0][1], -2)]
    for j, shift in enumerate(link_shifts(sz)):
        key = jnp.where(cols[shift][1] >= 0, cols[shift][1], -2)
        valid = link_valid(sz, j)
        known.append(key if valid is None else jnp.where(valid == 1, key, -2))
    for s in range(sz.shifts):
        for j, key in enumerate(known):
            maps[s * SLOTS : (s + 1) * SLOTS, j * SLOTS : (j + 1) * SLOTS] = (
                rows[s + 1][1] == key
            ).astype(BF16)
    for j, key in enumerate(known[1:]):
        back[:, j * SLOTS : (j + 1) * SLOTS] = (rows[0][1] == key).astype(BF16)
    pa, pb, atom_count = coupling.shape
    wide[...] = jnp.zeros(wide.shape, F32)
    wide[:, :pb, :] = coupling[...]
    table2 = wide[...].reshape(pa * 16, atom_count)
    hot = (rows[0][0] == iota(SLOTS, atom_count, 1)).astype(BF16)
    i, lane = iota(SLOTS, pa * 16, 0), iota(SLOTS, pa * 16, 1)
    own_row = (lane >> 4) == i - twelfth(i) * PA
    lane, j = iota(pa * 16, SLOTS, 0), iota(pa * 16, SLOTS, 1)
    fold = ((lane & 15) == j - twelfth(j) * PA).astype(BF16)
    same = twelfth(iota(SLOTS, SLOTS, 0)) == twelfth(iota(SLOTS, SLOTS, 1))
    for out in (c_hi, c_lo):
        part = table2.astype(BF16)
        table2 = table2 - part.astype(F32)
        picked = jnp.where(own_row, dot_last(hot, part), 0.0).astype(BF16)
        out[...] = jnp.where(same, dot(picked, fold), 0.0).astype(BF16)


def turn_matrices(sz, qt, kin, pot, atoms, coupling):
    known = (1 + sz.links) * SLOTS
    outs = [
        shape(SLOTS, sz.all_pad, BF16),
        shape(sz.cell_pad, sz.cell_pad, BF16),
        shape(len(sz.cells) * sz.cell_pad, sz.orb, F32),
        shape(sz.shifts * SLOTS, known, BF16),
        shape(SLOTS, sz.links * SLOTS, BF16),
        shape(SLOTS, SLOTS, BF16),
        shape(SLOTS, SLOTS, BF16),
    ]
    limit = (32 << 20) if sz.shifts < 8 else (56 << 20)
    return kernel_call(
        functools.partial(turn_body, sz),
        outs,
        [qt, kin, pot, atoms, coupling],
        scratch=[pltpu.VMEM((coupling.shape[0], 16, coupling.shape[2]), F32)],
        flops=10**9,
        limit=limit,
    )


def cell_block(sz, z, cell):
    p, q = cell
    layers = []
    for a in range(EDGE):
        start = (ORDER * p + a) * sz.line_x + ORDER * q * PAD
        layers.append(z[start : start + EDGE * PAD, :])
    layers.append(jnp.zeros((sz.cell_pad - sz.cell_rows, sz.orb), F32))
    return jnp.concatenate(layers, axis=0)


def write_pair(axis, low, high, first, second):
    first[...] = by_parity(axis, low, high).astype(first.dtype)
    second[...] = by_parity(axis, high, low).astype(second.dtype)


def read_pair(axis, first, second):
    one, two = first[...].astype(F32), second[...].astype(F32)
    return by_parity(axis, one, two), by_parity(axis, two, one)


def write_faces(sz, r, sx_one, sx_two, sy_lo, sy_hi):
    pad_x = jnp.zeros((sz.xface - sz.line_x, sz.orb), F32)
    pad_y = jnp.zeros((sz.yface - sz.nx * PAD, sz.orb), F32)
    last = (sz.nx - 1) * sz.line_x
    low = jnp.concatenate([r[0 : sz.line_x, :], pad_x], axis=0)
    high = jnp.concatenate([r[last : last + sz.line_x, :], pad_x], axis=0)
    write_pair("gx", low, high, sx_one, sx_two)
    for out, b in ((sy_lo, 0), (sy_hi, sz.ny - 1)):
        rows = [r[a * sz.line_x + b * PAD : a * sz.line_x + (b + 1) * PAD, :] for a in range(sz.nx)]
        out[...] = jnp.concatenate(rows + [pad_y], axis=0)


def face_outs(sz):
    return [shape(sz.xface, sz.orb, HALO)] * 2 + [shape(sz.yface, sz.orb, F32)] * 2


def start_body(sz, parts, r4, *faces):
    nz = parts.shape[2]
    r4[...] = jnp.zeros(r4.shape, F32)
    r4[:, :, :nz, :] = parts[...]
    write_faces(sz, r4.reshape(sz.rows, sz.orb), *faces)


def start_faces(sz, parts):
    outs = [jax.ShapeDtypeStruct((sz.nx, sz.ny, PAD, sz.orb), F32)] + face_outs(sz)
    r4, *faces = kernel_call(functools.partial(start_body, sz), outs, [parts])
    return r4.reshape(sz.rows, sz.orb), faces


def cross_body(sz, xr_one, xr_two, ry_lo, ry_hi, sy_one, sy_two):
    last = (sz.nx - 1) * PAD
    lo, hi = read_pair("gx", xr_one, xr_two)
    faces = []
    for raw, b in ((ry_lo, 0), (ry_hi, sz.ny - 1)):
        value = raw[...]
        parts = [
            value[:PAD] + lo[b * PAD : (b + 1) * PAD],
            value[PAD:last],
            value[last : last + PAD] + hi[b * PAD : (b + 1) * PAD],
            value[last + PAD :],
        ]
        faces.append(jnp.concatenate(parts, axis=0))
    write_pair("gy", *faces, sy_one, sy_two)


def cross_faces(sz, *faces):
    outs = [shape(sz.yface, sz.orb, HALO)] * 2
    return kernel_call(functools.partial(cross_body, sz), outs, list(faces))


def add_xy(sz, ra, r, xr_one, xr_two, yr_one, yr_two):
    ra[0 : sz.rows, :] = r[...]
    last = (sz.nx - 1) * sz.line_x
    low, high = read_pair("gx", xr_one, xr_two)
    ra[0 : sz.line_x, :] += low[: sz.line_x]
    ra[last : last + sz.line_x, :] += high[: sz.line_x]
    for value, b in zip(read_pair("gy", yr_one, yr_two), (0, sz.ny - 1)):
        for a in range(sz.nx):
            at = a * sz.line_x + b * PAD
            ra[at : at + PAD, :] += value[a * PAD : (a + 1) * PAD]


def pack_z(sz, ra, j):
    rows, c = [], layer_sent(sz, j)
    for a in range(sz.nx):
        for b in range(0, sz.face_b, PAD):
            rows.append(ra[pl.ds(a * sz.line_x + b * PAD + c, PAD, stride=PAD), :])
    rest = sz.zface - sz.nx * sz.face_b
    if rest:
        rows.append(jnp.zeros((rest, sz.orb), F32))
    value, valid = jnp.concatenate(rows, axis=0), link_valid(sz, j)
    return (value if valid is None else value * valid.astype(F32)).astype(HALO)


def add_z(sz, y, j, face):
    c = layer_received(sz, j)
    for a in range(sz.nx):
        for b in range(0, sz.ny, PAD):
            n = min(PAD, sz.ny - b)
            at = pl.ds(a * sz.line_x + b * PAD + c, n, stride=PAD)
            y[at, :] = y[at, :] + face[a * sz.face_b + b : a * sz.face_b + b + n]


def face_cells(sz, ra, j):
    rows, c = [], layer_sent(sz, j)
    for p, q in sz.cells:
        for a in range(EDGE):
            at = (ORDER * p + a) * sz.line_x + ORDER * q * PAD
            rows.append(ra[pl.ds(at + c, PAD, stride=PAD), :])
        rows.append(jnp.zeros((PAD, sz.orb), F32))
    return jnp.concatenate(rows, axis=0).astype(BF16)


def project_body(sz, has_local, refs):
    take = iter(refs)
    r = next(take)
    loc = next(take) if has_local else None
    halos = [next(take) for _ in range(4)]
    q = next(take)
    qfaces = [next(take) for _ in range(sz.links)]
    maps, back = next(take), next(take)
    y, own = next(take), next(take)
    messages = [next(take) for _ in range(sz.shifts)]
    ra = next(take)
    ra[sz.rows :, :] = jnp.zeros((sz.spill, sz.orb), F32)
    add_xy(sz, ra, r, *halos)
    y[...] = ra[0 : sz.rows, :] + loc[...] if has_local else ra[0 : sz.rows, :]
    blocks = [cell_block(sz, y, cell).astype(BF16) for cell in sz.cells]
    rest = sz.all_pad - sz.cell_pad * len(sz.cells)
    if rest:
        blocks.append(jnp.zeros((rest, sz.orb), BF16))
    beside = [dot(f[...], face_cells(sz, ra, j)).astype(BF16) for j, f in enumerate(qfaces)]
    sums = dot(q[...], jnp.concatenate(blocks, axis=0))
    mapped = dot(maps[...], jnp.concatenate([sums.astype(BF16)] + beside, axis=0))
    for s, message in enumerate(messages):
        message[0:SLOTS, :] = mapped[s * SLOTS : (s + 1) * SLOTS].astype(HALO)
        for j, shift in enumerate(link_shifts(sz)):
            if shift == s + 1:
                message[SLOTS : SLOTS + sz.zface, :] = pack_z(sz, ra, j)
    own[...] = sums + dot(back[...], jnp.concatenate(beside, axis=0))


def project(sz, r, loc, halos, q, qfaces, maps, back):
    outs = [shape(sz.rows, sz.orb, F32), shape(SLOTS, sz.orb, F32)]
    for s in range(1, sz.shifts + 1):
        outs.append(shape(SLOTS + (sz.zface if s in link_shifts(sz) else 0), sz.orb, HALO))
    arrays = [r] + ([loc] if loc is not None else []) + list(halos) + [q, *qfaces, maps, back]

    def body(*refs):
        project_body(sz, loc is not None, refs)

    y, own, *messages = kernel_call(
        body,
        outs,
        arrays,
        scratch=[pltpu.VMEM((sz.rows + sz.spill, sz.orb), F32)],
        flops=4 * 10**8,
        limit=(32 << 20) if sz.shifts < 8 else (56 << 20),
    )
    return y, own, messages


def apply_body(sz, has_previous, scale, refs):
    take = iter(refs)
    yin = next(take)
    previous = next(take) if has_previous else None
    own = next(take)
    messages = [next(take) for _ in range(sz.shifts)]
    c_hi, c_lo, qt, kin, pot = [next(take) for _ in range(5)]
    r, loc, y = next(take), next(take), next(take)
    faces = [next(take) for _ in range(4)]
    totals = own[...]
    for message in messages:
        totals = totals + message[0:SLOTS, :].astype(F32)
    high = totals.astype(BF16)
    low = (totals - high.astype(F32)).astype(BF16)
    coef = (dot(c_hi[...], high) + (dot(c_hi[...], low) + dot(c_lo[...], high))).astype(BF16)
    y[...] = yin[...]
    for j, shift in enumerate(link_shifts(sz)):
        add_z(sz, y, j, messages[shift - 1][SLOTS : SLOTS + sz.zface, :].astype(F32))
    blocks = [cell_block(sz, y, cell) for cell in sz.cells]
    stiff = dot(kin[...], jnp.concatenate([b.astype(BF16) for b in blocks], axis=1))
    r[...] = jnp.zeros(r.shape, F32)
    for g, (p, q) in enumerate(sz.cells):
        rows = slice(g * sz.cell_pad, (g + 1) * sz.cell_pad)
        value = stiff[:, g * sz.orb : (g + 1) * sz.orb] + pot[rows, :] * blocks[g]
        value = (value + dot(qt[rows, :], coef)) * scale
        for a in range(EDGE):
            start = (ORDER * p + a) * sz.line_x + ORDER * q * PAD
            r[start : start + EDGE * PAD, :] += value[a * EDGE * PAD : (a + 1) * EDGE * PAD]
    local = (-center_value * scale) * y[...]
    loc[...] = local - previous[...] if has_previous else local
    write_faces(sz, r, *faces)


def apply(sz, y, previous, own, messages, c_hi, c_lo, qt, kin, pot, scale):
    outs = [shape(sz.rows, sz.orb, F32)] * 3 + face_outs(sz)
    arrays = [y] + ([previous] if previous is not None else [])
    arrays += [own, *messages, c_hi, c_lo, qt, kin, pot]

    def body(*refs):
        apply_body(sz, previous is not None, scale, refs)

    r, loc, y, *faces = kernel_call(body, outs, arrays, flops=6 * 10**8, limit=32 << 20)
    return r, loc, y, faces


def last_faces_body(sz, refs):
    take = iter(refs)
    r = next(take)
    halos = [next(take) for _ in range(4)]
    outs = [next(take) for _ in range(sz.links)]
    ra = next(take)
    ra[sz.rows :, :] = jnp.zeros((sz.spill, sz.orb), F32)
    add_xy(sz, ra, r, *halos)
    for j, out in enumerate(outs):
        out[...] = pack_z(sz, ra, j)


def last_faces(sz, r, halos):
    def body(*refs):
        last_faces_body(sz, refs)

    outs = [shape(sz.zface, sz.orb, HALO)] * sz.links
    scratch = [pltpu.VMEM((sz.rows + sz.spill, sz.orb), F32)]
    return kernel_call(body, outs, [r, *halos], scratch=scratch)


def finish_body(sz, refs):
    take = iter(refs)
    r, loc = next(take), next(take)
    halos = [next(take) for _ in range(4)]
    zr = [next(take) for _ in range(sz.links)]
    out, ra = next(take), next(take)
    add_xy(sz, ra, r, *halos)
    for j, face in enumerate(zr):
        add_z(sz, ra, j, face[...].astype(F32))
    value = ra[0 : sz.rows, :] + loc[...]
    out[...] = value.reshape(sz.nx, sz.ny, PAD, sz.orb)[:, :, : out.shape[2], :]


def finish(sz, r, loc, halos, zr, nz):
    def body(*refs):
        finish_body(sz, refs)

    outs = [jax.ShapeDtypeStruct((sz.nx, sz.ny, nz, sz.orb), F32)]
    scratch = [pltpu.VMEM((sz.rows + sz.spill, sz.orb), F32)]
    return kernel_call(body, outs, [r, loc, *halos, *zr], scratch=scratch)[0]


def swap_faces(axis, one, two):
    count = lax.axis_size(axis)
    pairs = []
    for low in (1, 0):
        lows = range(low, count - 1, 2)
        pairs.append([(i, i + 1) for i in lows] + [(i + 1, i) for i in lows])
    return lax.ppermute(one, axis, pairs[0]), lax.ppermute(two, axis, pairs[1])


def local(parts, cell_matrix, cell_potential, projectors, slot_atom, slot_cells, coupling):
    nx, ny, nz, orbitals = parts.shape
    nodes = cell_matrix.shape[0]
    devices = lax.axis_size("gz")
    sz = Sizes(nx, ny, nz, orbitals, devices - 1)
    ring = [[(i, (i + s) % devices) for i in range(devices)] for s in range(devices)]

    r, faces = start_faces(sz, parts)

    def exchange_xy(sx_one, sx_two, sy_lo, sy_hi):
        xr = swap_faces("gx", sx_one, sx_two)
        cross = cross_faces(sz, *xr, sy_lo, sy_hi)
        yr = swap_faces("gy", *cross)
        return (*xr, *yr)

    halos = exchange_xy(*faces)
    proj = projectors.reshape(nodes, POS * BLK * PA)
    qt, *face_rows = sum_matrices(sz, proj, slot_cells.reshape(POS, BLK))
    qfaces = []
    for j, shift in enumerate(link_shifts(sz)):
        back = [(target, source) for source, target in ring[shift]]
        qfaces.append(lax.ppermute(face_rows[j], "gz", back))
    pot = jnp.transpose(cell_potential, (1, 2, 3, 0)).reshape(len(sz.cells), nodes)
    q, kin, pot, maps, back, c_hi, c_lo = turn_matrices(
        sz,
        qt,
        cell_matrix,
        pot,
        slot_atom.reshape(devices, POS),
        jnp.transpose(coupling, (1, 2, 0)),
    )

    loc = previous = None
    scale = 1.0 / half_width
    for step in range(STEPS):
        y, own, messages = project(sz, r, loc, halos, q, qfaces, maps, back)
        received = [lax.ppermute(m, "gz", ring[s + 1]) for s, m in enumerate(messages)]
        r, loc, y, faces = apply(sz, y, previous, own, received, c_hi, c_lo, qt, kin, pot, scale)
        previous, scale = y, 2.0 / half_width
        halos = exchange_xy(*faces)
    sent = last_faces(sz, r, halos)
    zr = [lax.ppermute(f, "gz", ring[s]) for f, s in zip(sent, link_shifts(sz))]
    return finish(sz, r, loc, halos, zr, nz)


def solution(mesh):
    in_specs = (
        P("gx", "gy", "gz", None),
        P(),
        P(None, "gx", "gy", "gz"),
        P("gx", "gy", "gz", None, None),
        P("gx", "gy", None, None),
        P("gx", "gy", "gz", None, None),
        P(("gx", "gy"), None, None),
    )
    out_specs = P("gx", "gy", "gz", None)
    return jax.shard_map(local, mesh=mesh, in_specs=in_specs, out_specs=out_specs, check_vma=False)
```

```python
import functools

import jax
import jax.numpy as jnp
import numpy as np
from jax import lax
from jax.experimental import pallas as pl
from jax.experimental.pallas import tpu as pltpu
from jax.sharding import PartitionSpec as P

ORDER = 6
STEPS = 3
PA = 12
POS = 32
BLK = 4

center_value = 2.0
half_width = 3.0

EDGE = ORDER + 1
PAD = 8
SLOTS = POS * PA
F32 = jnp.float32
BF16 = jnp.bfloat16
HALO = jnp.bfloat16


def up(value, multiple):
    return -(-value // multiple) * multiple


class Sizes:
    def __init__(self, nx, ny, nz, orbitals, shifts):
        assert nz == EDGE
        self.nx, self.ny, self.orb = nx, ny, orbitals
        self.cells = [(p, q) for p in range((nx - 1) // ORDER) for q in range((ny - 1) // ORDER)]
        self.rows = nx * ny * PAD
        self.line_x = ny * PAD
        self.xface = up(ny * PAD, 16)
        self.yface = up(nx * PAD, 16)
        self.face_b = up(ny, PAD)
        self.zface = up(nx * self.face_b, 16)
        self.cell_rows = EDGE * EDGE * PAD
        self.cell_pad = up(self.cell_rows, 16)
        self.all_pad = up(self.cell_pad * len(self.cells), 128)
        self.fcell = EDGE * PAD
        self.fall = up(self.fcell * len(self.cells), 256)
        self.shifts, self.links = shifts, min(2, shifts)
        self.spill = 2 * PAD * PAD


VMEM = pl.BlockSpec(memory_space=pltpu.VMEM)


def kernel_call(body, outs, arrays, scratch=(), flops=0, limit=24 << 20):
    nbytes = sum(int(np.prod(a.shape)) * a.dtype.itemsize for a in list(arrays) + list(outs))
    return pl.pallas_call(
        body,
        out_shape=outs,
        in_specs=[VMEM] * len(arrays),
        out_specs=[VMEM] * len(outs),
        scratch_shapes=list(scratch),
        compiler_params=pltpu.CompilerParams(vmem_limit_bytes=limit),
        cost_estimate=pl.CostEstimate(flops=flops, bytes_accessed=nbytes, transcendentals=0),
    )(*arrays)


def shape(rows, cols, dtype):
    return jax.ShapeDtypeStruct((rows, cols), dtype)


def dot(a, b):
    return jnp.dot(a, b, preferred_element_type=F32)


def is_odd(axis):
    return lax.rem(lax.axis_index(axis), 2) == 1


def by_parity(axis, even, odd):
    return jnp.where(is_odd(axis), odd, even)


def link_shifts(sz):
    return [1, sz.shifts][: sz.links]


def layer_sent(sz, j):
    if sz.links == 1:
        return jnp.where(lax.axis_index("gz") == 0, ORDER, 0)
    return [ORDER, 0][j]


def layer_received(sz, j):
    return layer_sent(sz, 0) if sz.links == 1 else [0, ORDER][j]


def link_valid(sz, j):
    if sz.links == 1:
        return None
    me = lax.axis_index("gz")
    return jnp.where(me < sz.shifts, 1, 0) if j == 0 else jnp.where(me > 0, 1, 0)


def iota(rows, cols, dim):
    return lax.broadcasted_iota(jnp.int32, (rows, cols), dim)


def twelfth(value):
    return (value * (2**19 // PA + 1)) >> 19


def node_key(i):
    low = i & (PAD - 1)
    return jnp.where((low < EDGE) & (i < EDGE * EDGE * PAD), (i >> 3) * EDGE + low, -1)


def dot_last(a, b, precision=None):
    dims = (((1,), (1,)), ((), ()))
    return lax.dot_general(a, b, dims, precision=precision, preferred_element_type=F32)


def sum_body(sz, proj, cells, qt, *qt_faces):
    nodes, cols = proj.shape
    i = iota(cols, POS, 0)
    first = iota(cols, POS, 1) * (BLK * PA)
    in_slot = ((i >= first) & (i < first + BLK * PA)).astype(BF16)
    of_block = dot_last(in_slot, cells[...].astype(F32).astype(BF16))
    i = iota(cols, BLK, 0)
    block = twelfth(i)
    cell = jnp.sum(
        jnp.where((block & (BLK - 1)) == iota(cols, BLK, 1), of_block, 0.0), axis=1, keepdims=True
    )
    i, block = i[:, :1], block[:, :1]
    row = (block >> (BLK.bit_length() - 1)) * PA + (i - block * PA)
    key = cell.astype(jnp.int32) * SLOTS + row
    targets = len(sz.cells) * SLOTS
    pick = (key == iota(cols, targets, 1)).astype(BF16)
    keys = [node_key(iota(sz.cell_pad, nodes, 0))]
    for j in range(sz.links):
        keys.append(
            jnp.where(
                iota(PAD * PAD, nodes, 0) < sz.fcell,
                node_key(iota(PAD * PAD, nodes, 0)) * EDGE + layer_received(sz, j),
                -1,
            )
        )
        low = iota(PAD * PAD, nodes, 0) & (PAD - 1)
        keys[-1] = jnp.where(low < EDGE, keys[-1], -1)
    expand = (jnp.concatenate(keys, axis=0) == iota(sz.cell_pad + sz.links * PAD * PAD, nodes, 1))
    summed = dot(proj[...], pick).astype(BF16)
    full = dot(expand.astype(BF16), summed)
    for g in range(len(sz.cells)):
        value = full[:, g * SLOTS : (g + 1) * SLOTS]
        qt[g * sz.cell_pad : (g + 1) * sz.cell_pad, :] = value[: sz.cell_pad].astype(BF16)
    rest = sz.all_pad - sz.cell_pad * len(sz.cells)
    if rest:
        qt[sz.cell_pad * len(sz.cells) :, :] = jnp.zeros((rest, SLOTS), BF16)
    for j, qf in enumerate(qt_faces):
        at = sz.cell_pad + j * PAD * PAD
        rows = [full[at : at + PAD * PAD, g * SLOTS : (g + 1) * SLOTS] for g in range(len(sz.cells))]
        qf[...] = jnp.concatenate(rows, axis=0).T.astype(BF16)


def sum_matrices(sz, proj, cells):
    outs = [shape(sz.all_pad, SLOTS, BF16)]
    outs += [shape(SLOTS, len(sz.cells) * PAD * PAD, BF16)] * sz.links
    body = functools.partial(sum_body, sz)
    return kernel_call(body, outs, [proj, cells], flops=3 * 10**9, limit=32 << 20)


def slot_keys(sz, table, dim):
    exact = lax.Precision.HIGHEST
    shape2 = (SLOTS, POS) if dim == 0 else (POS, SLOTS)
    i, s = iota(*shape2, dim), iota(*shape2, 1 - dim)
    spread = ((i >= s * PA) & (i < s * PA + PA)).astype(F32)
    if dim == 0:
        atoms = dot_last(spread, table, exact)
    else:
        atoms = jnp.dot(table, spread, precision=exact, preferred_element_type=F32)
    devices = sz.shifts + 1
    at = iota(*atoms.shape, 1 - dim)
    me = lax.axis_index("gz")
    keys = []
    for shift in range(devices):
        chosen = jnp.where(at == lax.rem(me + shift, devices), atoms, 0.0)
        atom = jnp.sum(chosen, axis=1 - dim, keepdims=True).astype(jnp.int32)
        i = iota(*atom.shape, dim)
        keys.append((atom, jnp.where(atom >= 0, atom * PA + i - twelfth(i) * PA, -1)))
    return keys


def turn_body(sz, qt, kin, pot, atoms, coupling, *refs):
    q, kout, vout, maps = refs[:4]
    back = refs[4] if sz.links else None
    c_hi, c_lo, wide = refs[-3:]
    q[...] = qt[...].T
    nodes = kin.shape[0]
    expand = (node_key(iota(sz.cell_pad, nodes, 0)) == iota(sz.cell_pad, nodes, 1)).astype(BF16)
    gather = (node_key(iota(nodes, sz.cell_pad, 1)) == iota(nodes, sz.cell_pad, 0)).astype(BF16)
    tall = dot(expand, kin[...]).astype(BF16)
    kout[...] = dot(tall, gather).astype(BF16)
    value, values = pot[...], 0.0
    for _ in range(3):
        part = value.astype(BF16)
        values = values + dot_last(expand, part)
        value = value - part.astype(F32)
    for g in range(len(sz.cells)):
        vout[g * sz.cell_pad : (g + 1) * sz.cell_pad, :] = jnp.broadcast_to(
            values[:, g : g + 1], (sz.cell_pad, sz.orb)
        )
    table = atoms[...].astype(F32)
    rows, cols = slot_keys(sz, table, 0), slot_keys(sz, table, 1)
    known = [jnp.where(cols[0][1] >= 0, cols[0][1], -2)]
    for j, shift in enumerate(link_shifts(sz)):
        key = jnp.where(cols[shift][1] >= 0, cols[shift][1], -2)
        valid = link_valid(sz, j)
        known.append(key if valid is None else jnp.where(valid == 1, key, -2))
    for s in range(sz.shifts):
        for j, key in enumerate(known):
            maps[s * SLOTS : (s + 1) * SLOTS, j * SLOTS : (j + 1) * SLOTS] = (
                rows[s + 1][1] == key
            ).astype(BF16)
    for j, key in enumerate(known[1:]):
        back[:, j * SLOTS : (j + 1) * SLOTS] = (rows[0][1] == key).astype(BF16)
    pa, pb, atom_count = coupling.shape
    wide[...] = jnp.zeros(wide.shape, F32)
    wide[:, :pb, :] = coupling[...]
    table2 = wide[...].reshape(pa * 16, atom_count)
    hot = (rows[0][0] == iota(SLOTS, atom_count, 1)).astype(BF16)
    i, lane = iota(SLOTS, pa * 16, 0), iota(SLOTS, pa * 16, 1)
    own_row = (lane >> 4) == i - twelfth(i) * PA
    lane, j = iota(pa * 16, SLOTS, 0), iota(pa * 16, SLOTS, 1)
    fold = ((lane & 15) == j - twelfth(j) * PA).astype(BF16)
    same = twelfth(iota(SLOTS, SLOTS, 0)) == twelfth(iota(SLOTS, SLOTS, 1))
    for out in (c_hi, c_lo):
        part = table2.astype(BF16)
        table2 = table2 - part.astype(F32)
        picked = jnp.where(own_row, dot_last(hot, part), 0.0).astype(BF16)
        out[...] = jnp.where(same, dot(picked, fold), 0.0).astype(BF16)


def turn_matrices(sz, qt, kin, pot, atoms, coupling):
    known = (1 + sz.links) * SLOTS
    outs = [
        shape(SLOTS, sz.all_pad, BF16),
        shape(sz.cell_pad, sz.cell_pad, BF16),
        shape(len(sz.cells) * sz.cell_pad, sz.orb, F32),
        shape(sz.shifts * SLOTS, known, BF16),
        shape(SLOTS, sz.links * SLOTS, BF16),
        shape(SLOTS, SLOTS, BF16),
        shape(SLOTS, SLOTS, BF16),
    ]
    limit = (32 << 20) if sz.shifts < 8 else (56 << 20)
    return kernel_call(
        functools.partial(turn_body, sz),
        outs,
        [qt, kin, pot, atoms, coupling],
        scratch=[pltpu.VMEM((coupling.shape[0], 16, coupling.shape[2]), F32)],
        flops=10**9,
        limit=limit,
    )


def cell_block(sz, z, cell):
    p, q = cell
    layers = []
    for a in range(EDGE):
        start = (ORDER * p + a) * sz.line_x + ORDER * q * PAD
        layers.append(z[start : start + EDGE * PAD, :])
    layers.append(jnp.zeros((sz.cell_pad - sz.cell_rows, sz.orb), F32))
    return jnp.concatenate(layers, axis=0)


def write_pair(axis, low, high, first, second):
    first[...] = by_parity(axis, low, high).astype(first.dtype)
    second[...] = by_parity(axis, high, low).astype(second.dtype)


def read_pair(axis, first, second):
    one, two = first[...].astype(F32), second[...].astype(F32)
    low, high = by_parity(axis, one, two), by_parity(axis, two, one)
    at, last = lax.axis_index(axis), lax.axis_size(axis) - 1
    return jnp.where(at > 0, low, 0.0), jnp.where(at < last, high, 0.0)


def write_faces(sz, r, sx_one, sx_two, sy_lo, sy_hi):
    pad_x = jnp.zeros((sz.xface - sz.line_x, sz.orb), F32)
    pad_y = jnp.zeros((sz.yface - sz.nx * PAD, sz.orb), F32)
    last = (sz.nx - 1) * sz.line_x
    low = jnp.concatenate([r[0 : sz.line_x, :], pad_x], axis=0)
    high = jnp.concatenate([r[last : last + sz.line_x, :], pad_x], axis=0)
    write_pair("gx", low, high, sx_one, sx_two)
    for out, b in ((sy_lo, 0), (sy_hi, sz.ny - 1)):
        rows = [r[a * sz.line_x + b * PAD : a * sz.line_x + (b + 1) * PAD, :] for a in range(sz.nx)]
        out[...] = jnp.concatenate(rows + [pad_y], axis=0)


def face_outs(sz):
    return [shape(sz.xface, sz.orb, HALO)] * 2 + [shape(sz.yface, sz.orb, F32)] * 2


def start_body(sz, parts, r4, *faces):
    nz = parts.shape[2]
    r4[...] = jnp.zeros(r4.shape, F32)
    r4[:, :, :nz, :] = parts[...]
    write_faces(sz, r4.reshape(sz.rows, sz.orb), *faces)


def start_faces(sz, parts):
    outs = [jax.ShapeDtypeStruct((sz.nx, sz.ny, PAD, sz.orb), F32)] + face_outs(sz)
    r4, *faces = kernel_call(functools.partial(start_body, sz), outs, [parts])
    return r4.reshape(sz.rows, sz.orb), faces


def cross_body(sz, xr_one, xr_two, ry_lo, ry_hi, sy_one, sy_two):
    last = (sz.nx - 1) * PAD
    lo, hi = read_pair("gx", xr_one, xr_two)
    faces = []
    for raw, b in ((ry_lo, 0), (ry_hi, sz.ny - 1)):
        value = raw[...]
        parts = [
            value[:PAD] + lo[b * PAD : (b + 1) * PAD],
            value[PAD:last],
            value[last : last + PAD] + hi[b * PAD : (b + 1) * PAD],
            value[last + PAD :],
        ]
        faces.append(jnp.concatenate(parts, axis=0))
    write_pair("gy", *faces, sy_one, sy_two)


def cross_faces(sz, *faces):
    outs = [shape(sz.yface, sz.orb, HALO)] * 2
    return kernel_call(functools.partial(cross_body, sz), outs, list(faces))


def add_xy(sz, ra, r, xr_one, xr_two, yr_one, yr_two):
    ra[0 : sz.rows, :] = r[...]
    last = (sz.nx - 1) * sz.line_x
    low, high = read_pair("gx", xr_one, xr_two)
    ra[0 : sz.line_x, :] += low[: sz.line_x]
    ra[last : last + sz.line_x, :] += high[: sz.line_x]
    for value, b in zip(read_pair("gy", yr_one, yr_two), (0, sz.ny - 1)):
        for a in range(sz.nx):
            at = a * sz.line_x + b * PAD
            ra[at : at + PAD, :] += value[a * PAD : (a + 1) * PAD]


def pack_z(sz, ra, j):
    rows, c = [], layer_sent(sz, j)
    for a in range(sz.nx):
        for b in range(0, sz.face_b, PAD):
            rows.append(ra[pl.ds(a * sz.line_x + b * PAD + c, PAD, stride=PAD), :])
    rest = sz.zface - sz.nx * sz.face_b
    if rest:
        rows.append(jnp.zeros((rest, sz.orb), F32))
    value, valid = jnp.concatenate(rows, axis=0), link_valid(sz, j)
    return (value if valid is None else value * valid.astype(F32)).astype(HALO)


def add_z(sz, y, j, face):
    c = layer_received(sz, j)
    for a in range(sz.nx):
        for b in range(0, sz.ny, PAD):
            n = min(PAD, sz.ny - b)
            at = pl.ds(a * sz.line_x + b * PAD + c, n, stride=PAD)
            y[at, :] = y[at, :] + face[a * sz.face_b + b : a * sz.face_b + b + n]


def face_cells(sz, ra, j):
    rows, c = [], layer_sent(sz, j)
    for p, q in sz.cells:
        for a in range(EDGE):
            at = (ORDER * p + a) * sz.line_x + ORDER * q * PAD
            rows.append(ra[pl.ds(at + c, PAD, stride=PAD), :])
        rows.append(jnp.zeros((PAD, sz.orb), F32))
    return jnp.concatenate(rows, axis=0).astype(BF16)


def project_body(sz, has_local, refs):
    take = iter(refs)
    r = next(take)
    loc = next(take) if has_local else None
    halos = [next(take) for _ in range(4)]
    q = next(take)
    qfaces = [next(take) for _ in range(sz.links)]
    maps, back = next(take), next(take)
    y, own = next(take), next(take)
    messages = [next(take) for _ in range(sz.shifts)]
    ra = next(take)
    ra[sz.rows :, :] = jnp.zeros((sz.spill, sz.orb), F32)
    add_xy(sz, ra, r, *halos)
    y[...] = ra[0 : sz.rows, :] + loc[...] if has_local else ra[0 : sz.rows, :]
    blocks = [cell_block(sz, y, cell).astype(BF16) for cell in sz.cells]
    rest = sz.all_pad - sz.cell_pad * len(sz.cells)
    if rest:
        blocks.append(jnp.zeros((rest, sz.orb), BF16))
    beside = [dot(f[...], face_cells(sz, ra, j)).astype(BF16) for j, f in enumerate(qfaces)]
    sums = dot(q[...], jnp.concatenate(blocks, axis=0))
    mapped = dot(maps[...], jnp.concatenate([sums.astype(BF16)] + beside, axis=0))
    for s, message in enumerate(messages):
        message[0:SLOTS, :] = mapped[s * SLOTS : (s + 1) * SLOTS].astype(HALO)
        for j, shift in enumerate(link_shifts(sz)):
            if shift == s + 1:
                message[SLOTS : SLOTS + sz.zface, :] = pack_z(sz, ra, j)
    own[...] = sums + dot(back[...], jnp.concatenate(beside, axis=0))


def project(sz, r, loc, halos, q, qfaces, maps, back):
    outs = [shape(sz.rows, sz.orb, F32), shape(SLOTS, sz.orb, F32)]
    for s in range(1, sz.shifts + 1):
        outs.append(shape(SLOTS + (sz.zface if s in link_shifts(sz) else 0), sz.orb, HALO))
    arrays = [r] + ([loc] if loc is not None else []) + list(halos) + [q, *qfaces, maps, back]

    def body(*refs):
        project_body(sz, loc is not None, refs)

    y, own, *messages = kernel_call(
        body,
        outs,
        arrays,
        scratch=[pltpu.VMEM((sz.rows + sz.spill, sz.orb), F32)],
        flops=4 * 10**8,
        limit=(32 << 20) if sz.shifts < 8 else (56 << 20),
    )
    return y, own, messages


def apply_body(sz, has_previous, scale, refs):
    take = iter(refs)
    yin = next(take)
    previous = next(take) if has_previous else None
    own = next(take)
    messages = [next(take) for _ in range(sz.shifts)]
    c_hi, c_lo, qt, kin, pot = [next(take) for _ in range(5)]
    r, loc, y = next(take), next(take), next(take)
    faces = [next(take) for _ in range(4)]
    totals = own[...]
    for message in messages:
        totals = totals + message[0:SLOTS, :].astype(F32)
    high = totals.astype(BF16)
    low = (totals - high.astype(F32)).astype(BF16)
    coef = (dot(c_hi[...], high) + (dot(c_hi[...], low) + dot(c_lo[...], high))).astype(BF16)
    y[...] = yin[...]
    for j, shift in enumerate(link_shifts(sz)):
        add_z(sz, y, j, messages[shift - 1][SLOTS : SLOTS + sz.zface, :].astype(F32))
    blocks = [cell_block(sz, y, cell) for cell in sz.cells]
    stiff = dot(kin[...], jnp.concatenate([b.astype(BF16) for b in blocks], axis=1))
    r[...] = jnp.zeros(r.shape, F32)
    for g, (p, q) in enumerate(sz.cells):
        rows = slice(g * sz.cell_pad, (g + 1) * sz.cell_pad)
        value = stiff[:, g * sz.orb : (g + 1) * sz.orb] + pot[rows, :] * blocks[g]
        value = (value + dot(qt[rows, :], coef)) * scale
        for a in range(EDGE):
            start = (ORDER * p + a) * sz.line_x + ORDER * q * PAD
            r[start : start + EDGE * PAD, :] += value[a * EDGE * PAD : (a + 1) * EDGE * PAD]
    local = (-center_value * scale) * y[...]
    loc[...] = local - previous[...] if has_previous else local
    write_faces(sz, r, *faces)


def apply(sz, y, previous, own, messages, c_hi, c_lo, qt, kin, pot, scale):
    outs = [shape(sz.rows, sz.orb, F32)] * 3 + face_outs(sz)
    arrays = [y] + ([previous] if previous is not None else [])
    arrays += [own, *messages, c_hi, c_lo, qt, kin, pot]

    def body(*refs):
        apply_body(sz, previous is not None, scale, refs)

    r, loc, y, *faces = kernel_call(body, outs, arrays, flops=6 * 10**8, limit=32 << 20)
    return r, loc, y, faces


def last_faces_body(sz, refs):
    take = iter(refs)
    r = next(take)
    halos = [next(take) for _ in range(4)]
    outs = [next(take) for _ in range(sz.links)]
    ra = next(take)
    ra[sz.rows :, :] = jnp.zeros((sz.spill, sz.orb), F32)
    add_xy(sz, ra, r, *halos)
    for j, out in enumerate(outs):
        out[...] = pack_z(sz, ra, j)


def last_faces(sz, r, halos):
    def body(*refs):
        last_faces_body(sz, refs)

    outs = [shape(sz.zface, sz.orb, HALO)] * sz.links
    scratch = [pltpu.VMEM((sz.rows + sz.spill, sz.orb), F32)]
    return kernel_call(body, outs, [r, *halos], scratch=scratch)


def finish_body(sz, refs):
    take = iter(refs)
    r, loc = next(take), next(take)
    halos = [next(take) for _ in range(4)]
    zr = [next(take) for _ in range(sz.links)]
    out, ra = next(take), next(take)
    add_xy(sz, ra, r, *halos)
    for j, face in enumerate(zr):
        add_z(sz, ra, j, face[...].astype(F32))
    value = ra[0 : sz.rows, :] + loc[...]
    out[...] = value.reshape(sz.nx, sz.ny, PAD, sz.orb)[:, :, : out.shape[2], :]


def finish(sz, r, loc, halos, zr, nz):
    def body(*refs):
        finish_body(sz, refs)

    outs = [jax.ShapeDtypeStruct((sz.nx, sz.ny, nz, sz.orb), F32)]
    scratch = [pltpu.VMEM((sz.rows + sz.spill, sz.orb), F32)]
    return kernel_call(body, outs, [r, loc, *halos, *zr], scratch=scratch)[0]


def swap_faces(axis, one, two):
    count = lax.axis_size(axis)
    pairs = []
    for low in (1, 0):
        lows = range(low, count - 1, 2)
        pair = [(i, i + 1) for i in lows] + [(i + 1, i) for i in lows]
        alone = set(range(count)) - {source for source, _ in pair}
        pairs.append(pair + [(i, i) for i in sorted(alone)])
    return lax.ppermute(one, axis, pairs[0]), lax.ppermute(two, axis, pairs[1])


def local(parts, cell_matrix, cell_potential, projectors, slot_atom, slot_cells, coupling):
    nx, ny, nz, orbitals = parts.shape
    nodes = cell_matrix.shape[0]
    devices = lax.axis_size("gz")
    sz = Sizes(nx, ny, nz, orbitals, devices - 1)
    ring = [[(i, (i + s) % devices) for i in range(devices)] for s in range(devices)]

    proj = projectors.reshape(nodes, POS * BLK * PA)
    cells = jnp.transpose(slot_cells.reshape(POS, BLK))
    r, faces = start_faces(sz, parts)

    def exchange_xy(sx_one, sx_two, sy_lo, sy_hi):
        xr = swap_faces("gx", sx_one, sx_two)
        cross = cross_faces(sz, *xr, sy_lo, sy_hi)
        yr = swap_faces("gy", *cross)
        return (*xr, *yr)

    halos = exchange_xy(*faces)
    qt, *face_rows = sum_matrices(sz, proj, cells)
    qfaces = []
    for j, shift in enumerate(link_shifts(sz)):
        back = [(target, source) for source, target in ring[shift]]
        qfaces.append(lax.ppermute(face_rows[j], "gz", back))
    pot = jnp.transpose(cell_potential, (1, 2, 3, 0)).reshape(len(sz.cells), nodes)
    q, kin, pot, maps, back, c_hi, c_lo = turn_matrices(
        sz,
        qt,
        cell_matrix,
        pot,
        slot_atom.reshape(devices, POS),
        jnp.transpose(coupling, (1, 2, 0)),
    )

    loc = previous = None
    scale = 1.0 / half_width
    for step in range(STEPS):
        y, own, messages = project(sz, r, loc, halos, q, qfaces, maps, back)
        received = [lax.ppermute(m, "gz", ring[s + 1]) for s, m in enumerate(messages)]
        r, loc, y, faces = apply(sz, y, previous, own, received, c_hi, c_lo, qt, kin, pot, scale)
        previous, scale = y, 2.0 / half_width
        halos = exchange_xy(*faces)
    sent = last_faces(sz, r, halos)
    zr = [lax.ppermute(f, "gz", ring[s]) for f, s in zip(sent, link_shifts(sz))]
    return finish(sz, r, loc, halos, zr, nz)


def solution(mesh):
    in_specs = (
        P("gx", "gy", "gz", None),
        P(),
        P(None, "gx", "gy", "gz"),
        P("gx", "gy", "gz", None, None),
        P("gx", "gy", None, None),
        P("gx", "gy", "gz", None, None),
        P(("gx", "gy"), None, None),
    )
    out_specs = P("gx", "gy", "gz", None)
    return jax.shard_map(local, mesh=mesh, in_specs=in_specs, out_specs=out_specs, check_vma=False)
```

```python
import functools

import jax
import jax.numpy as jnp
import numpy as np
from jax import lax
from jax.experimental import pallas as pl
from jax.experimental.pallas import tpu as pltpu
from jax.sharding import PartitionSpec as P

ORDER = 6
STEPS = 3
PA = 12
POS = 32
BLK = 4

center_value = 2.0
half_width = 3.0

EDGE = ORDER + 1
PAD = 8
SLOTS = POS * PA
F32 = jnp.float32
BF16 = jnp.bfloat16
HALO = jnp.bfloat16


def up(value, multiple):
    return -(-value // multiple) * multiple


class Sizes:
    def __init__(self, nx, ny, nz, orbitals, shifts):
        assert nz == EDGE
        self.nx, self.ny, self.orb = nx, ny, orbitals
        self.cells = [(p, q) for p in range((nx - 1) // ORDER) for q in range((ny - 1) // ORDER)]
        self.rows = nx * ny * PAD
        self.line_x = ny * PAD
        self.xface = up(ny * PAD, 16)
        self.yface = up(nx * PAD, 16)
        self.face_b = up(ny, PAD)
        self.zface = up(nx * self.face_b, 16)
        self.cell_rows = EDGE * EDGE * PAD
        self.cell_pad = up(self.cell_rows, 16)
        self.all_pad = up(self.cell_pad * len(self.cells), 128)
        self.fcell = EDGE * PAD
        self.fall = up(self.fcell * len(self.cells), 256)
        self.shifts, self.links = shifts, min(2, shifts)
        self.spill = 2 * PAD * PAD


VMEM = pl.BlockSpec(memory_space=pltpu.VMEM)


def kernel_call(body, outs, arrays, scratch=(), flops=0, limit=24 << 20):
    nbytes = sum(int(np.prod(a.shape)) * a.dtype.itemsize for a in list(arrays) + list(outs))
    return pl.pallas_call(
        body,
        out_shape=outs,
        in_specs=[VMEM] * len(arrays),
        out_specs=[VMEM] * len(outs),
        scratch_shapes=list(scratch),
        compiler_params=pltpu.CompilerParams(vmem_limit_bytes=limit),
        cost_estimate=pl.CostEstimate(flops=flops, bytes_accessed=nbytes, transcendentals=0),
    )(*arrays)


def shape(rows, cols, dtype):
    return jax.ShapeDtypeStruct((rows, cols), dtype)


def dot(a, b):
    return jnp.dot(a, b, preferred_element_type=F32)


def is_odd(axis):
    return lax.rem(lax.axis_index(axis), 2) == 1


def by_parity(axis, even, odd):
    return jnp.where(is_odd(axis), odd, even)


def link_shifts(sz):
    return [1, sz.shifts][: sz.links]


def layer_sent(sz, j):
    if sz.links == 1:
        return jnp.where(lax.axis_index("gz") == 0, ORDER, 0)
    return [ORDER, 0][j]


def layer_received(sz, j):
    return layer_sent(sz, 0) if sz.links == 1 else [0, ORDER][j]


def link_valid(sz, j):
    if sz.links == 1:
        return None
    me = lax.axis_index("gz")
    return jnp.where(me < sz.shifts, 1, 0) if j == 0 else jnp.where(me > 0, 1, 0)


def iota(rows, cols, dim):
    return lax.broadcasted_iota(jnp.int32, (rows, cols), dim)


def twelfth(value):
    return (value * (2**19 // PA + 1)) >> 19


def node_key(i):
    low = i & (PAD - 1)
    return jnp.where((low < EDGE) & (i < EDGE * EDGE * PAD), (i >> 3) * EDGE + low, -1)


def dot_last(a, b, precision=None):
    dims = (((1,), (1,)), ((), ()))
    return lax.dot_general(a, b, dims, precision=precision, preferred_element_type=F32)


def sum_body(sz, proj, cells, qt, *qt_faces):
    nodes, cols = proj.shape
    i = iota(cols, POS, 0)
    first = iota(cols, POS, 1) * (BLK * PA)
    in_slot = ((i >= first) & (i < first + BLK * PA)).astype(BF16)
    of_block = dot_last(in_slot, cells[...].astype(F32).astype(BF16))
    i = iota(cols, BLK, 0)
    block = twelfth(i)
    cell = jnp.sum(
        jnp.where((block & (BLK - 1)) == iota(cols, BLK, 1), of_block, 0.0), axis=1, keepdims=True
    )
    i, block = i[:, :1], block[:, :1]
    row = (block >> (BLK.bit_length() - 1)) * PA + (i - block * PA)
    key = cell.astype(jnp.int32) * SLOTS + row
    targets = len(sz.cells) * SLOTS
    pick = (key == iota(cols, targets, 1)).astype(BF16)
    keys = [node_key(iota(sz.cell_pad, nodes, 0))]
    for j in range(sz.links):
        keys.append(
            jnp.where(
                iota(PAD * PAD, nodes, 0) < sz.fcell,
                node_key(iota(PAD * PAD, nodes, 0)) * EDGE + layer_received(sz, j),
                -1,
            )
        )
        low = iota(PAD * PAD, nodes, 0) & (PAD - 1)
        keys[-1] = jnp.where(low < EDGE, keys[-1], -1)
    expand = (jnp.concatenate(keys, axis=0) == iota(sz.cell_pad + sz.links * PAD * PAD, nodes, 1))
    summed = dot(proj[...], pick).astype(BF16)
    full = dot(expand.astype(BF16), summed)
    for g in range(len(sz.cells)):
        value = full[:, g * SLOTS : (g + 1) * SLOTS]
        qt[g * sz.cell_pad : (g + 1) * sz.cell_pad, :] = value[: sz.cell_pad].astype(BF16)
    rest = sz.all_pad - sz.cell_pad * len(sz.cells)
    if rest:
        qt[sz.cell_pad * len(sz.cells) :, :] = jnp.zeros((rest, SLOTS), BF16)
    for j, qf in enumerate(qt_faces):
        at = sz.cell_pad + j * PAD * PAD
        rows = [full[at : at + PAD * PAD, g * SLOTS : (g + 1) * SLOTS] for g in range(len(sz.cells))]
        qf[...] = jnp.concatenate(rows, axis=0).T.astype(BF16)


def sum_matrices(sz, proj, cells):
    outs = [shape(sz.all_pad, SLOTS, BF16)]
    outs += [shape(SLOTS, len(sz.cells) * PAD * PAD, BF16)] * sz.links
    body = functools.partial(sum_body, sz)
    return kernel_call(body, outs, [proj, cells], flops=3 * 10**9, limit=32 << 20)


def slot_keys(sz, table, dim):
    exact = lax.Precision.HIGHEST
    shape2 = (SLOTS, POS) if dim == 0 else (POS, SLOTS)
    i, s = iota(*shape2, dim), iota(*shape2, 1 - dim)
    spread = ((i >= s * PA) & (i < s * PA + PA)).astype(F32)
    if dim == 0:
        atoms = dot_last(spread, table, exact)
    else:
        atoms = jnp.dot(table, spread, precision=exact, preferred_element_type=F32)
    devices = sz.shifts + 1
    at = iota(*atoms.shape, 1 - dim)
    me = lax.axis_index("gz")
    keys = []
    for shift in range(devices):
        chosen = jnp.where(at == lax.rem(me + shift, devices), atoms, 0.0)
        atom = jnp.sum(chosen, axis=1 - dim, keepdims=True).astype(jnp.int32)
        i = iota(*atom.shape, dim)
        keys.append((atom, jnp.where(atom >= 0, atom * PA + i - twelfth(i) * PA, -1)))
    return keys


def turn_body(sz, qt, kin, pot, atoms, coupling, *refs):
    q, kout, vout, maps = refs[:4]
    back = refs[4] if sz.links else None
    c_hi, c_lo, wide = refs[-3:]
    q[...] = qt[...].T
    nodes = kin.shape[0]
    expand = (node_key(iota(sz.cell_pad, nodes, 0)) == iota(sz.cell_pad, nodes, 1)).astype(BF16)
    gather = (node_key(iota(nodes, sz.cell_pad, 1)) == iota(nodes, sz.cell_pad, 0)).astype(BF16)
    tall = dot(expand, kin[...]).astype(BF16)
    kout[...] = dot(tall, gather).astype(BF16)
    value, values = pot[...], 0.0
    for _ in range(3):
        part = value.astype(BF16)
        values = values + dot_last(expand, part)
        value = value - part.astype(F32)
    for g in range(len(sz.cells)):
        vout[g * sz.cell_pad : (g + 1) * sz.cell_pad, :] = jnp.broadcast_to(
            values[:, g : g + 1], (sz.cell_pad, sz.orb)
        )
    table = atoms[...].astype(F32)
    rows, cols = slot_keys(sz, table, 0), slot_keys(sz, table, 1)
    known = [jnp.where(cols[0][1] >= 0, cols[0][1], -2)]
    for j, shift in enumerate(link_shifts(sz)):
        key = jnp.where(cols[shift][1] >= 0, cols[shift][1], -2)
        valid = link_valid(sz, j)
        known.append(key if valid is None else jnp.where(valid == 1, key, -2))
    for s in range(sz.shifts):
        for j, key in enumerate(known):
            maps[s * SLOTS : (s + 1) * SLOTS, j * SLOTS : (j + 1) * SLOTS] = (
                rows[s + 1][1] == key
            ).astype(BF16)
    for j, key in enumerate(known[1:]):
        back[:, j * SLOTS : (j + 1) * SLOTS] = (rows[0][1] == key).astype(BF16)
    pa, pb, atom_count = coupling.shape
    wide[...] = jnp.zeros(wide.shape, F32)
    wide[:, :pb, :] = coupling[...]
    table2 = wide[...].reshape(pa * 16, atom_count)
    hot = (rows[0][0] == iota(SLOTS, atom_count, 1)).astype(BF16)
    i, lane = iota(SLOTS, pa * 16, 0), iota(SLOTS, pa * 16, 1)
    own_row = (lane >> 4) == i - twelfth(i) * PA
    lane, j = iota(pa * 16, SLOTS, 0), iota(pa * 16, SLOTS, 1)
    fold = ((lane & 15) == j - twelfth(j) * PA).astype(BF16)
    same = twelfth(iota(SLOTS, SLOTS, 0)) == twelfth(iota(SLOTS, SLOTS, 1))
    for out in (c_hi, c_lo):
        part = table2.astype(BF16)
        table2 = table2 - part.astype(F32)
        picked = jnp.where(own_row, dot_last(hot, part), 0.0).astype(BF16)
        out[...] = jnp.where(same, dot(picked, fold), 0.0).astype(BF16)


def turn_matrices(sz, qt, kin, pot, atoms, coupling):
    known = (1 + sz.links) * SLOTS
    outs = [
        shape(SLOTS, sz.all_pad, BF16),
        shape(sz.cell_pad, sz.cell_pad, BF16),
        shape(len(sz.cells) * sz.cell_pad, sz.orb, F32),
        shape(sz.shifts * SLOTS, known, BF16),
        shape(SLOTS, sz.links * SLOTS, BF16),
        shape(SLOTS, SLOTS, BF16),
        shape(SLOTS, SLOTS, BF16),
    ]
    limit = (32 << 20) if sz.shifts < 8 else (56 << 20)
    return kernel_call(
        functools.partial(turn_body, sz),
        outs,
        [qt, kin, pot, atoms, coupling],
        scratch=[pltpu.VMEM((coupling.shape[0], 16, coupling.shape[2]), F32)],
        flops=10**9,
        limit=limit,
    )


def cell_block(sz, z, cell):
    p, q = cell
    layers = []
    for a in range(EDGE):
        start = (ORDER * p + a) * sz.line_x + ORDER * q * PAD
        layers.append(z[start : start + EDGE * PAD, :])
    layers.append(jnp.zeros((sz.cell_pad - sz.cell_rows, sz.orb), F32))
    return jnp.concatenate(layers, axis=0)


def write_pair(axis, low, high, first, second):
    first[...] = by_parity(axis, low, high).astype(first.dtype)
    second[...] = by_parity(axis, high, low).astype(second.dtype)


def read_pair(axis, first, second):
    one, two = first[...].astype(F32), second[...].astype(F32)
    low, high = by_parity(axis, one, two), by_parity(axis, two, one)
    at, last = lax.axis_index(axis), lax.axis_size(axis) - 1
    return jnp.where(at > 0, low, 0.0), jnp.where(at < last, high, 0.0)


def write_faces(sz, r, sx_one, sx_two, sy_lo, sy_hi):
    pad_x = jnp.zeros((sz.xface - sz.line_x, sz.orb), F32)
    pad_y = jnp.zeros((sz.yface - sz.nx * PAD, sz.orb), F32)
    last = (sz.nx - 1) * sz.line_x
    low = jnp.concatenate([r[0 : sz.line_x, :], pad_x], axis=0)
    high = jnp.concatenate([r[last : last + sz.line_x, :], pad_x], axis=0)
    write_pair("gx", low, high, sx_one, sx_two)
    for out, b in ((sy_lo, 0), (sy_hi, sz.ny - 1)):
        rows = [r[a * sz.line_x + b * PAD : a * sz.line_x + (b + 1) * PAD, :] for a in range(sz.nx)]
        out[...] = jnp.concatenate(rows + [pad_y], axis=0)


def face_outs(sz):
    return [shape(sz.xface, sz.orb, HALO)] * 2 + [shape(sz.yface, sz.orb, F32)] * 2


def start_body(sz, parts, r4, *faces):
    nz = parts.shape[2]
    r4[...] = jnp.zeros(r4.shape, F32)
    r4[:, :, :nz, :] = parts[...]
    write_faces(sz, r4.reshape(sz.rows, sz.orb), *faces)


def start_faces(sz, parts):
    outs = [jax.ShapeDtypeStruct((sz.nx, sz.ny, PAD, sz.orb), F32)] + face_outs(sz)
    r4, *faces = kernel_call(functools.partial(start_body, sz), outs, [parts])
    return r4.reshape(sz.rows, sz.orb), faces


def cross_body(sz, xr_one, xr_two, ry_lo, ry_hi, sy_one, sy_two):
    last = (sz.nx - 1) * PAD
    lo, hi = read_pair("gx", xr_one, xr_two)
    faces = []
    for raw, b in ((ry_lo, 0), (ry_hi, sz.ny - 1)):
        value = raw[...]
        parts = [
            value[:PAD] + lo[b * PAD : (b + 1) * PAD],
            value[PAD:last],
            value[last : last + PAD] + hi[b * PAD : (b + 1) * PAD],
            value[last + PAD :],
        ]
        faces.append(jnp.concatenate(parts, axis=0))
    write_pair("gy", *faces, sy_one, sy_two)


def cross_faces(sz, *faces):
    outs = [shape(sz.yface, sz.orb, HALO)] * 2
    return kernel_call(functools.partial(cross_body, sz), outs, list(faces))


def add_xy(sz, ra, r, xr_one, xr_two, yr_one, yr_two):
    ra[0 : sz.rows, :] = r[...]
    last = (sz.nx - 1) * sz.line_x
    low, high = read_pair("gx", xr_one, xr_two)
    ra[0 : sz.line_x, :] += low[: sz.line_x]
    ra[last : last + sz.line_x, :] += high[: sz.line_x]
    for value, b in zip(read_pair("gy", yr_one, yr_two), (0, sz.ny - 1)):
        for a in range(sz.nx):
            at = a * sz.line_x + b * PAD
            ra[at : at + PAD, :] += value[a * PAD : (a + 1) * PAD]


def pack_z(sz, ra, j):
    rows, c = [], layer_sent(sz, j)
    for a in range(sz.nx):
        for b in range(0, sz.face_b, PAD):
            rows.append(ra[pl.ds(a * sz.line_x + b * PAD + c, PAD, stride=PAD), :])
    rest = sz.zface - sz.nx * sz.face_b
    if rest:
        rows.append(jnp.zeros((rest, sz.orb), F32))
    value, valid = jnp.concatenate(rows, axis=0), link_valid(sz, j)
    return (value if valid is None else value * valid.astype(F32)).astype(HALO)


def add_z(sz, y, j, face):
    c = layer_received(sz, j)
    for a in range(sz.nx):
        for b in range(0, sz.ny, PAD):
            n = min(PAD, sz.ny - b)
            at = pl.ds(a * sz.line_x + b * PAD + c, n, stride=PAD)
            y[at, :] = y[at, :] + face[a * sz.face_b + b : a * sz.face_b + b + n]


def face_cells(sz, ra, j):
    rows, c = [], layer_sent(sz, j)
    for p, q in sz.cells:
        for a in range(EDGE):
            at = (ORDER * p + a) * sz.line_x + ORDER * q * PAD
            rows.append(ra[pl.ds(at + c, PAD, stride=PAD), :])
        rows.append(jnp.zeros((PAD, sz.orb), F32))
    return jnp.concatenate(rows, axis=0).astype(BF16)


def project_body(sz, has_local, refs):
    take = iter(refs)
    r = next(take)
    loc = next(take) if has_local else None
    halos = [next(take) for _ in range(4)]
    q = next(take)
    qfaces = [next(take) for _ in range(sz.links)]
    maps, back = next(take), next(take)
    y, own = next(take), next(take)
    messages = [next(take) for _ in range(sz.shifts)]
    ra = next(take)
    ra[sz.rows :, :] = jnp.zeros((sz.spill, sz.orb), F32)
    add_xy(sz, ra, r, *halos)
    y[...] = ra[0 : sz.rows, :] + loc[...] if has_local else ra[0 : sz.rows, :]
    blocks = [cell_block(sz, y, cell).astype(BF16) for cell in sz.cells]
    rest = sz.all_pad - sz.cell_pad * len(sz.cells)
    if rest:
        blocks.append(jnp.zeros((rest, sz.orb), BF16))
    beside = [dot(f[...], face_cells(sz, ra, j)).astype(BF16) for j, f in enumerate(qfaces)]
    sums = dot(q[...], jnp.concatenate(blocks, axis=0))
    mapped = dot(maps[...], jnp.concatenate([sums.astype(BF16)] + beside, axis=0))
    for s, message in enumerate(messages):
        message[0:SLOTS, :] = mapped[s * SLOTS : (s + 1) * SLOTS].astype(HALO)
        for j, shift in enumerate(link_shifts(sz)):
            if shift == s + 1:
                message[SLOTS : SLOTS + sz.zface, :] = pack_z(sz, ra, j)
    own[...] = sums + dot(back[...], jnp.concatenate(beside, axis=0))


def project(sz, r, loc, halos, q, qfaces, maps, back):
    outs = [shape(sz.rows, sz.orb, F32), shape(SLOTS, sz.orb, F32)]
    for s in range(1, sz.shifts + 1):
        outs.append(shape(SLOTS + (sz.zface if s in link_shifts(sz) else 0), sz.orb, HALO))
    arrays = [r] + ([loc] if loc is not None else []) + list(halos) + [q, *qfaces, maps, back]

    def body(*refs):
        project_body(sz, loc is not None, refs)

    y, own, *messages = kernel_call(
        body,
        outs,
        arrays,
        scratch=[pltpu.VMEM((sz.rows + sz.spill, sz.orb), F32)],
        flops=4 * 10**8,
        limit=(32 << 20) if sz.shifts < 8 else (56 << 20),
    )
    return y, own, messages


def apply_body(sz, has_previous, scale, refs):
    take = iter(refs)
    yin = next(take)
    previous = next(take) if has_previous else None
    own = next(take)
    messages = [next(take) for _ in range(sz.shifts)]
    c_hi, c_lo, qt, kin, pot = [next(take) for _ in range(5)]
    r, loc, y = next(take), next(take), next(take)
    faces = [next(take) for _ in range(4)]
    totals = own[...]
    for message in messages:
        totals = totals + message[0:SLOTS, :].astype(F32)
    high = totals.astype(BF16)
    low = (totals - high.astype(F32)).astype(BF16)
    coef = (dot(c_hi[...], high) + (dot(c_hi[...], low) + dot(c_lo[...], high))).astype(BF16)
    y[...] = yin[...]
    for j, shift in enumerate(link_shifts(sz)):
        add_z(sz, y, j, messages[shift - 1][SLOTS : SLOTS + sz.zface, :].astype(F32))
    blocks = [cell_block(sz, y, cell) for cell in sz.cells]
    stiff = dot(kin[...], jnp.concatenate([b.astype(BF16) for b in blocks], axis=1))
    r[...] = jnp.zeros(r.shape, F32)
    for g, (p, q) in enumerate(sz.cells):
        rows = slice(g * sz.cell_pad, (g + 1) * sz.cell_pad)
        value = stiff[:, g * sz.orb : (g + 1) * sz.orb] + pot[rows, :] * blocks[g]
        value = (value + dot(qt[rows, :], coef)) * scale
        for a in range(EDGE):
            start = (ORDER * p + a) * sz.line_x + ORDER * q * PAD
            r[start : start + EDGE * PAD, :] += value[a * EDGE * PAD : (a + 1) * EDGE * PAD]
    local = (-center_value * scale) * y[...]
    loc[...] = local - previous[...] if has_previous else local
    write_faces(sz, r, *faces)


def apply(sz, y, previous, own, messages, c_hi, c_lo, qt, kin, pot, scale):
    outs = [shape(sz.rows, sz.orb, F32)] * 3 + face_outs(sz)
    arrays = [y] + ([previous] if previous is not None else [])
    arrays += [own, *messages, c_hi, c_lo, qt, kin, pot]

    def body(*refs):
        apply_body(sz, previous is not None, scale, refs)

    r, loc, y, *faces = kernel_call(body, outs, arrays, flops=6 * 10**8, limit=32 << 20)
    return r, loc, y, faces


def last_faces_body(sz, refs):
    take = iter(refs)
    r = next(take)
    halos = [next(take) for _ in range(4)]
    outs = [next(take) for _ in range(sz.links)]
    ra = next(take)
    ra[sz.rows :, :] = jnp.zeros((sz.spill, sz.orb), F32)
    add_xy(sz, ra, r, *halos)
    for j, out in enumerate(outs):
        out[...] = pack_z(sz, ra, j)


def last_faces(sz, r, halos):
    def body(*refs):
        last_faces_body(sz, refs)

    outs = [shape(sz.zface, sz.orb, HALO)] * sz.links
    scratch = [pltpu.VMEM((sz.rows + sz.spill, sz.orb), F32)]
    return kernel_call(body, outs, [r, *halos], scratch=scratch)


def finish_body(sz, refs):
    take = iter(refs)
    r, loc = next(take), next(take)
    halos = [next(take) for _ in range(4)]
    zr = [next(take) for _ in range(sz.links)]
    out, ra = next(take), next(take)
    add_xy(sz, ra, r, *halos)
    for j, face in enumerate(zr):
        add_z(sz, ra, j, face[...].astype(F32))
    value = ra[0 : sz.rows, :] + loc[...]
    out[...] = value.reshape(sz.nx, sz.ny, PAD, sz.orb)[:, :, : out.shape[2], :]


def finish(sz, r, loc, halos, zr, nz):
    def body(*refs):
        finish_body(sz, refs)

    outs = [jax.ShapeDtypeStruct((sz.nx, sz.ny, nz, sz.orb), F32)]
    scratch = [pltpu.VMEM((sz.rows + sz.spill, sz.orb), F32)]
    return kernel_call(body, outs, [r, loc, *halos, *zr], scratch=scratch)[0]


def swap_faces(axis, one, two):
    count = lax.axis_size(axis)
    pairs = []
    for low in (1, 0):
        lows = range(low, count - 1, 2)
        pair = [(i, i + 1) for i in lows] + [(i + 1, i) for i in lows]
        alone = sorted(set(range(count)) - {source for source, _ in pair})
        pairs.append(pair + list(zip(alone, alone[::-1])))
    return lax.ppermute(one, axis, pairs[0]), lax.ppermute(two, axis, pairs[1])


def local(parts, cell_matrix, cell_potential, projectors, slot_atom, slot_cells, coupling):
    nx, ny, nz, orbitals = parts.shape
    nodes = cell_matrix.shape[0]
    devices = lax.axis_size("gz")
    sz = Sizes(nx, ny, nz, orbitals, devices - 1)
    ring = [[(i, (i + s) % devices) for i in range(devices)] for s in range(devices)]

    proj = projectors.reshape(nodes, POS * BLK * PA)
    cells = jnp.transpose(slot_cells.reshape(POS, BLK))
    r, faces = start_faces(sz, parts)

    def exchange_xy(sx_one, sx_two, sy_lo, sy_hi):
        xr = swap_faces("gx", sx_one, sx_two)
        cross = cross_faces(sz, *xr, sy_lo, sy_hi)
        yr = swap_faces("gy", *cross)
        return (*xr, *yr)

    halos = exchange_xy(*faces)
    qt, *face_rows = sum_matrices(sz, proj, cells)
    qfaces = []
    for j, shift in enumerate(link_shifts(sz)):
        back = [(target, source) for source, target in ring[shift]]
        qfaces.append(lax.ppermute(face_rows[j], "gz", back))
    pot = jnp.transpose(cell_potential, (1, 2, 3, 0)).reshape(len(sz.cells), nodes)
    q, kin, pot, maps, back, c_hi, c_lo = turn_matrices(
        sz,
        qt,
        cell_matrix,
        pot,
        slot_atom.reshape(devices, POS),
        jnp.transpose(coupling, (1, 2, 0)),
    )

    loc = previous = None
    scale = 1.0 / half_width
    for step in range(STEPS):
        y, own, messages = project(sz, r, loc, halos, q, qfaces, maps, back)
        received = [lax.ppermute(m, "gz", ring[s + 1]) for s, m in enumerate(messages)]
        r, loc, y, faces = apply(sz, y, previous, own, received, c_hi, c_lo, qt, kin, pot, scale)
        previous, scale = y, 2.0 / half_width
        halos = exchange_xy(*faces)
    sent = last_faces(sz, r, halos)
    zr = [lax.ppermute(f, "gz", ring[s]) for f, s in zip(sent, link_shifts(sz))]
    return finish(sz, r, loc, halos, zr, nz)


def solution(mesh):
    in_specs = (
        P("gx", "gy", "gz", None),
        P(),
        P(None, "gx", "gy", "gz"),
        P("gx", "gy", "gz", None, None),
        P("gx", "gy", None, None),
        P("gx", "gy", "gz", None, None),
        P(("gx", "gy"), None, None),
    )
    out_specs = P("gx", "gy", "gz", None)
    return jax.shard_map(local, mesh=mesh, in_specs=in_specs, out_specs=out_specs, check_vma=False)
```

```python
import functools

import jax
import jax.numpy as jnp
import numpy as np
from jax import lax
from jax.experimental import pallas as pl
from jax.experimental.pallas import tpu as pltpu
from jax.sharding import PartitionSpec as P

ORDER = 6
STEPS = 3
PA = 12
POS = 32
BLK = 4

center_value = 2.0
half_width = 3.0

EDGE = ORDER + 1
PAD = 8
SLOTS = POS * PA
F32 = jnp.float32
BF16 = jnp.bfloat16
HALO = jnp.bfloat16


def up(value, multiple):
    return -(-value // multiple) * multiple


class Sizes:
    def __init__(self, nx, ny, nz, orbitals, shifts):
        assert nz == EDGE
        self.nx, self.ny, self.orb = nx, ny, orbitals
        self.cells = [(p, q) for p in range((nx - 1) // ORDER) for q in range((ny - 1) // ORDER)]
        self.rows = nx * ny * PAD
        self.line_x = ny * PAD
        self.xface = up(ny * PAD, 16)
        self.yface = up(nx * PAD, 16)
        self.face_b = up(ny, PAD)
        self.zface = up(nx * self.face_b, 16)
        self.cell_rows = EDGE * EDGE * PAD
        self.cell_pad = up(self.cell_rows, 16)
        self.all_pad = up(self.cell_pad * len(self.cells), 128)
        self.fcell = EDGE * PAD
        self.fall = up(self.fcell * len(self.cells), 256)
        self.shifts, self.links = shifts, min(2, shifts)
        self.spill = 2 * PAD * PAD


VMEM = pl.BlockSpec(memory_space=pltpu.VMEM)


def kernel_call(body, outs, arrays, scratch=(), flops=0, limit=24 << 20):
    nbytes = sum(int(np.prod(a.shape)) * a.dtype.itemsize for a in list(arrays) + list(outs))
    return pl.pallas_call(
        body,
        out_shape=outs,
        in_specs=[VMEM] * len(arrays),
        out_specs=[VMEM] * len(outs),
        scratch_shapes=list(scratch),
        compiler_params=pltpu.CompilerParams(vmem_limit_bytes=limit),
        cost_estimate=pl.CostEstimate(flops=flops, bytes_accessed=nbytes, transcendentals=0),
    )(*arrays)


def shape(rows, cols, dtype):
    return jax.ShapeDtypeStruct((rows, cols), dtype)


def dot(a, b):
    return jnp.dot(a, b, preferred_element_type=F32)


def is_odd(axis):
    return lax.rem(lax.axis_index(axis), 2) == 1


def by_parity(axis, even, odd):
    return jnp.where(is_odd(axis), odd, even)


def link_shifts(sz):
    return [1, sz.shifts][: sz.links]


def layer_sent(sz, j):
    if sz.links == 1:
        return jnp.where(lax.axis_index("gz") == 0, ORDER, 0)
    return [ORDER, 0][j]


def layer_received(sz, j):
    return layer_sent(sz, 0) if sz.links == 1 else [0, ORDER][j]


def link_valid(sz, j):
    if sz.links == 1:
        return None
    me = lax.axis_index("gz")
    return jnp.where(me < sz.shifts, 1, 0) if j == 0 else jnp.where(me > 0, 1, 0)


def iota(rows, cols, dim):
    return lax.broadcasted_iota(jnp.int32, (rows, cols), dim)


def twelfth(value):
    return (value * (2**19 // PA + 1)) >> 19


def node_key(i):
    low = i & (PAD - 1)
    return jnp.where((low < EDGE) & (i < EDGE * EDGE * PAD), (i >> 3) * EDGE + low, -1)


def dot_last(a, b, precision=None):
    dims = (((1,), (1,)), ((), ()))
    return lax.dot_general(a, b, dims, precision=precision, preferred_element_type=F32)


def sum_body(sz, proj, cells, qt, *qt_faces):
    nodes, cols = proj.shape
    i = iota(cols, POS, 0)
    first = iota(cols, POS, 1) * (BLK * PA)
    in_slot = ((i >= first) & (i < first + BLK * PA)).astype(BF16)
    of_block = dot_last(in_slot, cells[...].astype(F32).astype(BF16))
    i = iota(cols, BLK, 0)
    block = twelfth(i)
    cell = jnp.sum(
        jnp.where((block & (BLK - 1)) == iota(cols, BLK, 1), of_block, 0.0), axis=1, keepdims=True
    )
    i, block = i[:, :1], block[:, :1]
    row = (block >> (BLK.bit_length() - 1)) * PA + (i - block * PA)
    key = cell.astype(jnp.int32) * SLOTS + row
    targets = len(sz.cells) * SLOTS
    pick = (key == iota(cols, targets, 1)).astype(BF16)
    keys = [node_key(iota(sz.cell_pad, nodes, 0))]
    for j in range(sz.links):
        keys.append(
            jnp.where(
                iota(PAD * PAD, nodes, 0) < sz.fcell,
                node_key(iota(PAD * PAD, nodes, 0)) * EDGE + layer_received(sz, j),
                -1,
            )
        )
        low = iota(PAD * PAD, nodes, 0) & (PAD - 1)
        keys[-1] = jnp.where(low < EDGE, keys[-1], -1)
    expand = (jnp.concatenate(keys, axis=0) == iota(sz.cell_pad + sz.links * PAD * PAD, nodes, 1))
    summed = dot(proj[...], pick).astype(BF16)
    full = dot(expand.astype(BF16), summed)
    for g in range(len(sz.cells)):
        value = full[:, g * SLOTS : (g + 1) * SLOTS]
        qt[g * sz.cell_pad : (g + 1) * sz.cell_pad, :] = value[: sz.cell_pad].astype(BF16)
    rest = sz.all_pad - sz.cell_pad * len(sz.cells)
    if rest:
        qt[sz.cell_pad * len(sz.cells) :, :] = jnp.zeros((rest, SLOTS), BF16)
    for j, qf in enumerate(qt_faces):
        at = sz.cell_pad + j * PAD * PAD
        rows = [full[at : at + PAD * PAD, g * SLOTS : (g + 1) * SLOTS] for g in range(len(sz.cells))]
        qf[...] = jnp.concatenate(rows, axis=0).T.astype(BF16)


def sum_matrices(sz, proj, cells):
    outs = [shape(sz.all_pad, SLOTS, BF16)]
    outs += [shape(SLOTS, len(sz.cells) * PAD * PAD, BF16)] * sz.links
    body = functools.partial(sum_body, sz)
    return kernel_call(body, outs, [proj, cells], flops=3 * 10**9, limit=32 << 20)


def slot_keys(sz, table, dim):
    exact = lax.Precision.HIGHEST
    shape2 = (SLOTS, POS) if dim == 0 else (POS, SLOTS)
    i, s = iota(*shape2, dim), iota(*shape2, 1 - dim)
    spread = ((i >= s * PA) & (i < s * PA + PA)).astype(F32)
    if dim == 0:
        atoms = dot_last(spread, table, exact)
    else:
        atoms = jnp.dot(table, spread, precision=exact, preferred_element_type=F32)
    devices = sz.shifts + 1
    at = iota(*atoms.shape, 1 - dim)
    me = lax.axis_index("gz")
    keys = []
    for shift in range(devices):
        chosen = jnp.where(at == lax.rem(me + shift, devices), atoms, 0.0)
        atom = jnp.sum(chosen, axis=1 - dim, keepdims=True).astype(jnp.int32)
        i = iota(*atom.shape, dim)
        keys.append((atom, jnp.where(atom >= 0, atom * PA + i - twelfth(i) * PA, -1)))
    return keys


def turn_body(sz, qt, kin, pot, atoms, coupling, *refs):
    q, kout, vout, maps = refs[:4]
    back = refs[4] if sz.links else None
    c_hi, c_lo, wide = refs[-3:]
    q[...] = qt[...].T
    nodes = kin.shape[0]
    expand = (node_key(iota(sz.cell_pad, nodes, 0)) == iota(sz.cell_pad, nodes, 1)).astype(BF16)
    gather = (node_key(iota(nodes, sz.cell_pad, 1)) == iota(nodes, sz.cell_pad, 0)).astype(BF16)
    tall = dot(expand, kin[...]).astype(BF16)
    kout[...] = dot(tall, gather).astype(BF16)
    value, values = pot[...], 0.0
    for _ in range(3):
        part = value.astype(BF16)
        values = values + dot_last(expand, part)
        value = value - part.astype(F32)
    for g in range(len(sz.cells)):
        vout[g * sz.cell_pad : (g + 1) * sz.cell_pad, :] = jnp.broadcast_to(
            values[:, g : g + 1], (sz.cell_pad, sz.orb)
        )
    table = atoms[...].astype(F32)
    rows, cols = slot_keys(sz, table, 0), slot_keys(sz, table, 1)
    known = [jnp.where(cols[0][1] >= 0, cols[0][1], -2)]
    for j, shift in enumerate(link_shifts(sz)):
        key = jnp.where(cols[shift][1] >= 0, cols[shift][1], -2)
        valid = link_valid(sz, j)
        known.append(key if valid is None else jnp.where(valid == 1, key, -2))
    for s in range(sz.shifts):
        for j, key in enumerate(known):
            maps[s * SLOTS : (s + 1) * SLOTS, j * SLOTS : (j + 1) * SLOTS] = (
                rows[s + 1][1] == key
            ).astype(BF16)
    for j, key in enumerate(known[1:]):
        back[:, j * SLOTS : (j + 1) * SLOTS] = (rows[0][1] == key).astype(BF16)
    pa, pb, atom_count = coupling.shape
    wide[...] = jnp.zeros(wide.shape, F32)
    wide[:, :pb, :] = coupling[...]
    table2 = wide[...].reshape(pa * 16, atom_count)
    hot = (rows[0][0] == iota(SLOTS, atom_count, 1)).astype(BF16)
    i, lane = iota(SLOTS, pa * 16, 0), iota(SLOTS, pa * 16, 1)
    own_row = (lane >> 4) == i - twelfth(i) * PA
    lane, j = iota(pa * 16, SLOTS, 0), iota(pa * 16, SLOTS, 1)
    fold = ((lane & 15) == j - twelfth(j) * PA).astype(BF16)
    same = twelfth(iota(SLOTS, SLOTS, 0)) == twelfth(iota(SLOTS, SLOTS, 1))
    for out in (c_hi, c_lo):
        part = table2.astype(BF16)
        table2 = table2 - part.astype(F32)
        picked = jnp.where(own_row, dot_last(hot, part), 0.0).astype(BF16)
        out[...] = jnp.where(same, dot(picked, fold), 0.0).astype(BF16)


def turn_matrices(sz, qt, kin, pot, atoms, coupling):
    known = (1 + sz.links) * SLOTS
    outs = [
        shape(SLOTS, sz.all_pad, BF16),
        shape(sz.cell_pad, sz.cell_pad, BF16),
        shape(len(sz.cells) * sz.cell_pad, sz.orb, F32),
        shape(sz.shifts * SLOTS, known, BF16),
        shape(SLOTS, sz.links * SLOTS, BF16),
        shape(SLOTS, SLOTS, BF16),
        shape(SLOTS, SLOTS, BF16),
    ]
    limit = (32 << 20) if sz.shifts < 8 else (56 << 20)
    return kernel_call(
        functools.partial(turn_body, sz),
        outs,
        [qt, kin, pot, atoms, coupling],
        scratch=[pltpu.VMEM((coupling.shape[0], 16, coupling.shape[2]), F32)],
        flops=10**9,
        limit=limit,
    )


def cell_block(sz, z, cell):
    p, q = cell
    layers = []
    for a in range(EDGE):
        start = (ORDER * p + a) * sz.line_x + ORDER * q * PAD
        layers.append(z[start : start + EDGE * PAD, :])
    layers.append(jnp.zeros((sz.cell_pad - sz.cell_rows, sz.orb), F32))
    return jnp.concatenate(layers, axis=0)


def write_pair(axis, low, high, first, second):
    first[...] = by_parity(axis, low, high).astype(first.dtype)
    second[...] = by_parity(axis, high, low).astype(second.dtype)


def read_pair(axis, first, second):
    one, two = first[...].astype(F32), second[...].astype(F32)
    low, high = by_parity(axis, one, two), by_parity(axis, two, one)
    at, last = lax.axis_index(axis), lax.axis_size(axis) - 1
    return jnp.where(at > 0, low, 0.0), jnp.where(at < last, high, 0.0)


def write_faces(sz, r, sx_one, sx_two, sy_lo, sy_hi):
    pad_x = jnp.zeros((sz.xface - sz.line_x, sz.orb), F32)
    pad_y = jnp.zeros((sz.yface - sz.nx * PAD, sz.orb), F32)
    last = (sz.nx - 1) * sz.line_x
    low = jnp.concatenate([r[0 : sz.line_x, :], pad_x], axis=0)
    high = jnp.concatenate([r[last : last + sz.line_x, :], pad_x], axis=0)
    write_pair("gx", low, high, sx_one, sx_two)
    for out, b in ((sy_lo, 0), (sy_hi, sz.ny - 1)):
        rows = [r[a * sz.line_x + b * PAD : a * sz.line_x + (b + 1) * PAD, :] for a in range(sz.nx)]
        out[...] = jnp.concatenate(rows + [pad_y], axis=0)


def face_outs(sz):
    return [shape(sz.xface, sz.orb, HALO)] * 2 + [shape(sz.yface, sz.orb, F32)] * 2


def start_body(sz, parts, r4, *faces):
    nz = parts.shape[2]
    r4[...] = jnp.zeros(r4.shape, F32)
    r4[:, :, :nz, :] = parts[...]
    write_faces(sz, r4.reshape(sz.rows, sz.orb), *faces)


def start_faces(sz, parts):
    outs = [jax.ShapeDtypeStruct((sz.nx, sz.ny, PAD, sz.orb), F32)] + face_outs(sz)
    r4, *faces = kernel_call(functools.partial(start_body, sz), outs, [parts])
    return r4.reshape(sz.rows, sz.orb), faces


def cross_body(sz, xr_one, xr_two, ry_lo, ry_hi, sy_one, sy_two):
    last = (sz.nx - 1) * PAD
    lo, hi = read_pair("gx", xr_one, xr_two)
    faces = []
    for raw, b in ((ry_lo, 0), (ry_hi, sz.ny - 1)):
        value = raw[...]
        parts = [
            value[:PAD] + lo[b * PAD : (b + 1) * PAD],
            value[PAD:last],
            value[last : last + PAD] + hi[b * PAD : (b + 1) * PAD],
            value[last + PAD :],
        ]
        faces.append(jnp.concatenate(parts, axis=0))
    write_pair("gy", *faces, sy_one, sy_two)


def cross_faces(sz, *faces):
    outs = [shape(sz.yface, sz.orb, HALO)] * 2
    return kernel_call(functools.partial(cross_body, sz), outs, list(faces))


def add_xy(sz, ra, r, xr_one, xr_two, yr_one, yr_two):
    ra[0 : sz.rows, :] = r[...]
    last = (sz.nx - 1) * sz.line_x
    low, high = read_pair("gx", xr_one, xr_two)
    ra[0 : sz.line_x, :] += low[: sz.line_x]
    ra[last : last + sz.line_x, :] += high[: sz.line_x]
    for value, b in zip(read_pair("gy", yr_one, yr_two), (0, sz.ny - 1)):
        for a in range(sz.nx):
            at = a * sz.line_x + b * PAD
            ra[at : at + PAD, :] += value[a * PAD : (a + 1) * PAD]


def pack_z(sz, ra, j):
    rows, c = [], layer_sent(sz, j)
    for a in range(sz.nx):
        for b in range(0, sz.face_b, PAD):
            rows.append(ra[pl.ds(a * sz.line_x + b * PAD + c, PAD, stride=PAD), :])
    rest = sz.zface - sz.nx * sz.face_b
    if rest:
        rows.append(jnp.zeros((rest, sz.orb), F32))
    value, valid = jnp.concatenate(rows, axis=0), link_valid(sz, j)
    return (value if valid is None else value * valid.astype(F32)).astype(HALO)


def add_z(sz, y, j, face):
    c = layer_received(sz, j)
    for a in range(sz.nx):
        for b in range(0, sz.ny, PAD):
            n = min(PAD, sz.ny - b)
            at = pl.ds(a * sz.line_x + b * PAD + c, n, stride=PAD)
            y[at, :] = y[at, :] + face[a * sz.face_b + b : a * sz.face_b + b + n]


def face_cells(sz, ra, j):
    rows, c = [], layer_sent(sz, j)
    for p, q in sz.cells:
        for a in range(EDGE):
            at = (ORDER * p + a) * sz.line_x + ORDER * q * PAD
            rows.append(ra[pl.ds(at + c, PAD, stride=PAD), :])
        rows.append(jnp.zeros((PAD, sz.orb), F32))
    return jnp.concatenate(rows, axis=0).astype(BF16)


def project_body(sz, has_local, refs):
    take = iter(refs)
    r = next(take)
    loc = next(take) if has_local else None
    halos = [next(take) for _ in range(4)]
    q = next(take)
    qfaces = [next(take) for _ in range(sz.links)]
    maps, back = next(take), next(take)
    y, own = next(take), next(take)
    messages = [next(take) for _ in range(sz.shifts)]
    ra = next(take)
    ra[sz.rows :, :] = jnp.zeros((sz.spill, sz.orb), F32)
    add_xy(sz, ra, r, *halos)
    y[...] = ra[0 : sz.rows, :] + loc[...] if has_local else ra[0 : sz.rows, :]
    blocks = [cell_block(sz, y, cell).astype(BF16) for cell in sz.cells]
    rest = sz.all_pad - sz.cell_pad * len(sz.cells)
    if rest:
        blocks.append(jnp.zeros((rest, sz.orb), BF16))
    beside = [dot(f[...], face_cells(sz, ra, j)).astype(BF16) for j, f in enumerate(qfaces)]
    sums = dot(q[...], jnp.concatenate(blocks, axis=0))
    mapped = dot(maps[...], jnp.concatenate([sums.astype(BF16)] + beside, axis=0))
    for s, message in enumerate(messages):
        message[0:SLOTS, :] = mapped[s * SLOTS : (s + 1) * SLOTS].astype(HALO)
        for j, shift in enumerate(link_shifts(sz)):
            if shift == s + 1:
                message[SLOTS : SLOTS + sz.zface, :] = pack_z(sz, ra, j)
    own[...] = sums + dot(back[...], jnp.concatenate(beside, axis=0))


def project(sz, r, loc, halos, q, qfaces, maps, back):
    outs = [shape(sz.rows, sz.orb, F32), shape(SLOTS, sz.orb, F32)]
    for s in range(1, sz.shifts + 1):
        outs.append(shape(SLOTS + (sz.zface if s in link_shifts(sz) else 0), sz.orb, HALO))
    arrays = [r] + ([loc] if loc is not None else []) + list(halos) + [q, *qfaces, maps, back]

    def body(*refs):
        project_body(sz, loc is not None, refs)

    y, own, *messages = kernel_call(
        body,
        outs,
        arrays,
        scratch=[pltpu.VMEM((sz.rows + sz.spill, sz.orb), F32)],
        flops=4 * 10**8,
        limit=(32 << 20) if sz.shifts < 8 else (56 << 20),
    )
    return y, own, messages


def apply_body(sz, has_previous, scale, refs):
    take = iter(refs)
    yin = next(take)
    previous = next(take) if has_previous else None
    own = next(take)
    messages = [next(take) for _ in range(sz.shifts)]
    c_hi, c_lo, qt, kin, pot = [next(take) for _ in range(5)]
    r, loc, y = next(take), next(take), next(take)
    faces = [next(take) for _ in range(4)]
    totals = own[...]
    for message in messages:
        totals = totals + message[0:SLOTS, :].astype(F32)
    high = totals.astype(BF16)
    low = (totals - high.astype(F32)).astype(BF16)
    coef = (dot(c_hi[...], high) + (dot(c_hi[...], low) + dot(c_lo[...], high))).astype(BF16)
    y[...] = yin[...]
    for j, shift in enumerate(link_shifts(sz)):
        add_z(sz, y, j, messages[shift - 1][SLOTS : SLOTS + sz.zface, :].astype(F32))
    blocks = [cell_block(sz, y, cell) for cell in sz.cells]
    stiff = dot(kin[...], jnp.concatenate([b.astype(BF16) for b in blocks], axis=1))
    r[...] = jnp.zeros(r.shape, F32)
    for g, (p, q) in enumerate(sz.cells):
        rows = slice(g * sz.cell_pad, (g + 1) * sz.cell_pad)
        value = stiff[:, g * sz.orb : (g + 1) * sz.orb] + pot[rows, :] * blocks[g]
        value = (value + dot(qt[rows, :], coef)) * scale
        for a in range(EDGE):
            start = (ORDER * p + a) * sz.line_x + ORDER * q * PAD
            r[start : start + EDGE * PAD, :] += value[a * EDGE * PAD : (a + 1) * EDGE * PAD]
    local = (-center_value * scale) * y[...]
    loc[...] = local - previous[...] if has_previous else local
    write_faces(sz, r, *faces)


def apply(sz, y, previous, own, messages, c_hi, c_lo, qt, kin, pot, scale):
    outs = [shape(sz.rows, sz.orb, F32)] * 3 + face_outs(sz)
    arrays = [y] + ([previous] if previous is not None else [])
    arrays += [own, *messages, c_hi, c_lo, qt, kin, pot]

    def body(*refs):
        apply_body(sz, previous is not None, scale, refs)

    r, loc, y, *faces = kernel_call(body, outs, arrays, flops=6 * 10**8, limit=32 << 20)
    return r, loc, y, faces


def last_faces_body(sz, refs):
    take = iter(refs)
    r = next(take)
    halos = [next(take) for _ in range(4)]
    outs = [next(take) for _ in range(sz.links)]
    ra = next(take)
    ra[sz.rows :, :] = jnp.zeros((sz.spill, sz.orb), F32)
    add_xy(sz, ra, r, *halos)
    for j, out in enumerate(outs):
        out[...] = pack_z(sz, ra, j)


def last_faces(sz, r, halos):
    def body(*refs):
        last_faces_body(sz, refs)

    outs = [shape(sz.zface, sz.orb, HALO)] * sz.links
    scratch = [pltpu.VMEM((sz.rows + sz.spill, sz.orb), F32)]
    return kernel_call(body, outs, [r, *halos], scratch=scratch)


def finish_body(sz, refs):
    take = iter(refs)
    r, loc = next(take), next(take)
    halos = [next(take) for _ in range(4)]
    zr = [next(take) for _ in range(sz.links)]
    out, ra = next(take), next(take)
    add_xy(sz, ra, r, *halos)
    for j, face in enumerate(zr):
        add_z(sz, ra, j, face[...].astype(F32))
    value = ra[0 : sz.rows, :] + loc[...]
    out[...] = value.reshape(sz.nx, sz.ny, PAD, sz.orb)[:, :, : out.shape[2], :]


def finish(sz, r, loc, halos, zr, nz):
    def body(*refs):
        finish_body(sz, refs)

    outs = [jax.ShapeDtypeStruct((sz.nx, sz.ny, nz, sz.orb), F32)]
    scratch = [pltpu.VMEM((sz.rows + sz.spill, sz.orb), F32)]
    return kernel_call(body, outs, [r, loc, *halos, *zr], scratch=scratch)[0]


def swap_faces(axis, one, two):
    axes = ("gx", "gy")
    wide, deep = lax.axis_size("gx"), lax.axis_size("gy")
    count = wide if axis == "gx" else deep

    def partner(i, j, low):
        at = i if axis == "gx" else j
        to = at + 1 if at % 2 == low else at - 1
        if 0 <= to < count:
            return (to, j) if axis == "gx" else (i, to)
        if axis == "gy" and wide % 2 == 0:
            return (i ^ 1, j)
        ends = sorted({k for k in range(count) if not 0 <= k + (1 if k % 2 == low else -1) < count})
        to = ends[::-1][ends.index(at)]
        return (to, j) if axis == "gx" else (i, to)

    out = []
    for face, low in ((one, 1), (two, 0)):
        pairs = []
        for i in range(wide):
            for j in range(deep):
                to = partner(i, j, low)
                pairs.append((i * deep + j, to[0] * deep + to[1]))
        out.append(lax.ppermute(face, axes, pairs))
    return out


def local(parts, cell_matrix, cell_potential, projectors, slot_atom, slot_cells, coupling):
    nx, ny, nz, orbitals = parts.shape
    nodes = cell_matrix.shape[0]
    devices = lax.axis_size("gz")
    sz = Sizes(nx, ny, nz, orbitals, devices - 1)
    ring = [[(i, (i + s) % devices) for i in range(devices)] for s in range(devices)]

    proj = projectors.reshape(nodes, POS * BLK * PA)
    cells = jnp.transpose(slot_cells.reshape(POS, BLK))
    r, faces = start_faces(sz, parts)

    def exchange_xy(sx_one, sx_two, sy_lo, sy_hi):
        xr = swap_faces("gx", sx_one, sx_two)
        cross = cross_faces(sz, *xr, sy_lo, sy_hi)
        yr = swap_faces("gy", *cross)
        return (*xr, *yr)

    halos = exchange_xy(*faces)
    qt, *face_rows = sum_matrices(sz, proj, cells)
    qfaces = []
    for j, shift in enumerate(link_shifts(sz)):
        back = [(target, source) for source, target in ring[shift]]
        qfaces.append(lax.ppermute(face_rows[j], "gz", back))
    pot = jnp.transpose(cell_potential, (1, 2, 3, 0)).reshape(len(sz.cells), nodes)
    q, kin, pot, maps, back, c_hi, c_lo = turn_matrices(
        sz,
        qt,
        cell_matrix,
        pot,
        slot_atom.reshape(devices, POS),
        jnp.transpose(coupling, (1, 2, 0)),
    )

    loc = previous = None
    scale = 1.0 / half_width
    for step in range(STEPS):
        y, own, messages = project(sz, r, loc, halos, q, qfaces, maps, back)
        received = [lax.ppermute(m, "gz", ring[s + 1]) for s, m in enumerate(messages)]
        r, loc, y, faces = apply(sz, y, previous, own, received, c_hi, c_lo, qt, kin, pot, scale)
        previous, scale = y, 2.0 / half_width
        halos = exchange_xy(*faces)
    sent = last_faces(sz, r, halos)
    zr = [lax.ppermute(f, "gz", ring[s]) for f, s in zip(sent, link_shifts(sz))]
    return finish(sz, r, loc, halos, zr, nz)


def solution(mesh):
    in_specs = (
        P("gx", "gy", "gz", None),
        P(),
        P(None, "gx", "gy", "gz"),
        P("gx", "gy", "gz", None, None),
        P("gx", "gy", None, None),
        P("gx", "gy", "gz", None, None),
        P(("gx", "gy"), None, None),
    )
    out_specs = P("gx", "gy", "gz", None)
    return jax.shard_map(local, mesh=mesh, in_specs=in_specs, out_specs=out_specs, check_vma=False)
```

```python
import functools

import jax
import jax.numpy as jnp
import numpy as np
from jax import lax
from jax.experimental import pallas as pl
from jax.experimental.pallas import tpu as pltpu
from jax.sharding import PartitionSpec as P

ORDER = 6
STEPS = 3
PA = 12
POS = 32
BLK = 4

center_value = 2.0
half_width = 3.0

EDGE = ORDER + 1
PAD = 8
SLOTS = POS * PA
F32 = jnp.float32
BF16 = jnp.bfloat16
HALO = jnp.bfloat16


def up(value, multiple):
    return -(-value // multiple) * multiple


class Sizes:
    def __init__(self, nx, ny, nz, orbitals, shifts):
        assert nz == EDGE
        self.nx, self.ny, self.orb = nx, ny, orbitals
        self.cells = [(p, q) for p in range((nx - 1) // ORDER) for q in range((ny - 1) // ORDER)]
        self.rows = nx * ny * PAD
        self.line_x = ny * PAD
        self.xface = up(ny * PAD, 16)
        self.yface = up(nx * PAD, 16)
        self.face_b = up(ny, PAD)
        self.zface = up(nx * self.face_b, 16)
        self.cell_rows = EDGE * EDGE * PAD
        self.cell_pad = up(self.cell_rows, 16)
        self.all_pad = up(self.cell_pad * len(self.cells), 128)
        self.fcell = EDGE * PAD
        self.fall = up(self.fcell * len(self.cells), 256)
        self.shifts, self.links = shifts, min(2, shifts)
        self.rows_all = self.rows + (self.face_b - ny + 1) * PAD


VMEM = pl.BlockSpec(memory_space=pltpu.VMEM)


def kernel_call(body, outs, arrays, scratch=(), flops=0, limit=24 << 20):
    nbytes = sum(int(np.prod(a.shape)) * a.dtype.itemsize for a in list(arrays) + list(outs))
    return pl.pallas_call(
        body,
        out_shape=outs,
        in_specs=[VMEM] * len(arrays),
        out_specs=[VMEM] * len(outs),
        scratch_shapes=list(scratch),
        compiler_params=pltpu.CompilerParams(vmem_limit_bytes=limit),
        cost_estimate=pl.CostEstimate(flops=flops, bytes_accessed=nbytes, transcendentals=0),
    )(*arrays)


def shape(rows, cols, dtype):
    return jax.ShapeDtypeStruct((rows, cols), dtype)


def dot(a, b):
    return jnp.dot(a, b, preferred_element_type=F32)


def is_odd(axis):
    return lax.rem(lax.axis_index(axis), 2) == 1


def by_parity(axis, even, odd):
    return jnp.where(is_odd(axis), odd, even)


def link_shifts(sz):
    return [1, sz.shifts][: sz.links]


def layer_sent(sz, j):
    if sz.links == 1:
        return jnp.where(lax.axis_index("gz") == 0, ORDER, 0)
    return [ORDER, 0][j]


def layer_received(sz, j):
    return layer_sent(sz, 0) if sz.links == 1 else [0, ORDER][j]


def link_valid(sz, j):
    if sz.links == 1:
        return None
    me = lax.axis_index("gz")
    return jnp.where(me < sz.shifts, 1, 0) if j == 0 else jnp.where(me > 0, 1, 0)


def iota(rows, cols, dim):
    return lax.broadcasted_iota(jnp.int32, (rows, cols), dim)


def twelfth(value):
    return (value * (2**19 // PA + 1)) >> 19


def node_key(i):
    low = i & (PAD - 1)
    return jnp.where((low < EDGE) & (i < EDGE * EDGE * PAD), (i >> 3) * EDGE + low, -1)


def dot_last(a, b, precision=None):
    dims = (((1,), (1,)), ((), ()))
    return lax.dot_general(a, b, dims, precision=precision, preferred_element_type=F32)


def sum_body(sz, proj, cells, qt, *qt_faces):
    nodes, cols = proj.shape
    i = iota(cols, POS, 0)
    first = iota(cols, POS, 1) * (BLK * PA)
    in_slot = ((i >= first) & (i < first + BLK * PA)).astype(BF16)
    of_block = dot_last(in_slot, cells[...].astype(BF16))
    i = iota(cols, BLK, 0)
    block = twelfth(i)
    cell = jnp.sum(
        jnp.where((block & (BLK - 1)) == iota(cols, BLK, 1), of_block, 0.0), axis=1, keepdims=True
    )
    i, block = i[:, :1], block[:, :1]
    row = (block >> (BLK.bit_length() - 1)) * PA + (i - block * PA)
    key = cell.astype(jnp.int32) * SLOTS + row
    targets = len(sz.cells) * SLOTS
    pick = (key == iota(cols, targets, 1)).astype(BF16)
    keys = [node_key(iota(sz.cell_pad, nodes, 0))]
    for j in range(sz.links):
        keys.append(
            jnp.where(
                iota(PAD * PAD, nodes, 0) < sz.fcell,
                node_key(iota(PAD * PAD, nodes, 0)) * EDGE + layer_received(sz, j),
                -1,
            )
        )
        low = iota(PAD * PAD, nodes, 0) & (PAD - 1)
        keys[-1] = jnp.where(low < EDGE, keys[-1], -1)
    expand = (jnp.concatenate(keys, axis=0) == iota(sz.cell_pad + sz.links * PAD * PAD, nodes, 1))
    summed = dot(proj[...], pick).astype(BF16)
    full = dot(expand.astype(BF16), summed)
    for g in range(len(sz.cells)):
        value = full[:, g * SLOTS : (g + 1) * SLOTS]
        qt[g * sz.cell_pad : (g + 1) * sz.cell_pad, :] = value[: sz.cell_pad].astype(BF16)
    rest = sz.all_pad - sz.cell_pad * len(sz.cells)
    if rest:
        qt[sz.cell_pad * len(sz.cells) :, :] = jnp.zeros((rest, SLOTS), BF16)
    for j, qf in enumerate(qt_faces):
        at = sz.cell_pad + j * PAD * PAD
        rows = [full[at : at + PAD * PAD, g * SLOTS : (g + 1) * SLOTS] for g in range(len(sz.cells))]
        qf[...] = jnp.concatenate(rows, axis=0).T.astype(BF16)


def sum_matrices(sz, proj, cells):
    outs = [shape(sz.all_pad, SLOTS, BF16)]
    outs += [shape(SLOTS, len(sz.cells) * PAD * PAD, BF16)] * sz.links
    body = functools.partial(sum_body, sz)
    return kernel_call(body, outs, [proj, cells], flops=3 * 10**9, limit=32 << 20)


def slot_keys(sz, table, dim):
    exact = lax.Precision.HIGHEST
    shape2 = (SLOTS, POS) if dim == 0 else (POS, SLOTS)
    i, s = iota(*shape2, dim), iota(*shape2, 1 - dim)
    spread = ((i >= s * PA) & (i < s * PA + PA)).astype(F32)
    if dim == 0:
        atoms = dot_last(spread, table, exact)
    else:
        atoms = jnp.dot(table, spread, precision=exact, preferred_element_type=F32)
    devices = sz.shifts + 1
    at = iota(*atoms.shape, 1 - dim)
    me = lax.axis_index("gz")
    keys = []
    for shift in range(devices):
        chosen = jnp.where(at == lax.rem(me + shift, devices), atoms, 0.0)
        atom = jnp.sum(chosen, axis=1 - dim, keepdims=True).astype(jnp.int32)
        i = iota(*atom.shape, dim)
        keys.append((atom, jnp.where(atom >= 0, atom * PA + i - twelfth(i) * PA, -1)))
    return keys


def turn_body(sz, qt, kin, pot, atoms, coupling, *refs):
    q, kout, vout, maps = refs[:4]
    back = refs[4] if sz.links else None
    c_hi, c_lo, wide = refs[-3:]
    q[...] = qt[...].T
    nodes = kin.shape[0]
    expand = (node_key(iota(sz.cell_pad, nodes, 0)) == iota(sz.cell_pad, nodes, 1)).astype(BF16)
    gather = (node_key(iota(nodes, sz.cell_pad, 1)) == iota(nodes, sz.cell_pad, 0)).astype(BF16)
    tall = dot(expand, kin[...]).astype(BF16)
    kout[...] = dot(tall, gather).astype(BF16)
    value, values = pot[...], 0.0
    for _ in range(3):
        part = value.astype(BF16)
        values = values + dot_last(expand, part)
        value = value - part.astype(F32)
    for g in range(len(sz.cells)):
        vout[g * sz.cell_pad : (g + 1) * sz.cell_pad, :] = jnp.broadcast_to(
            values[:, g : g + 1], (sz.cell_pad, sz.orb)
        )
    table = atoms[...].astype(F32)
    rows, cols = slot_keys(sz, table, 0), slot_keys(sz, table, 1)
    known = [jnp.where(cols[0][1] >= 0, cols[0][1], -2)]
    for j, shift in enumerate(link_shifts(sz)):
        key = jnp.where(cols[shift][1] >= 0, cols[shift][1], -2)
        valid = link_valid(sz, j)
        known.append(key if valid is None else jnp.where(valid == 1, key, -2))
    for s in range(sz.shifts):
        for j, key in enumerate(known):
            maps[s * SLOTS : (s + 1) * SLOTS, j * SLOTS : (j + 1) * SLOTS] = (
                rows[s + 1][1] == key
            ).astype(BF16)
    for j, key in enumerate(known[1:]):
        back[:, j * SLOTS : (j + 1) * SLOTS] = (rows[0][1] == key).astype(BF16)
    pa, pb, atom_count = coupling.shape
    wide[...] = jnp.zeros(wide.shape, F32)
    wide[:, :pb, :] = coupling[...]
    table2 = wide[...].reshape(pa * 16, atom_count)
    hot = (rows[0][0] == iota(SLOTS, atom_count, 1)).astype(BF16)
    i, lane = iota(SLOTS, pa * 16, 0), iota(SLOTS, pa * 16, 1)
    own_row = (lane >> 4) == i - twelfth(i) * PA
    lane, j = iota(pa * 16, SLOTS, 0), iota(pa * 16, SLOTS, 1)
    fold = ((lane & 15) == j - twelfth(j) * PA).astype(BF16)
    same = twelfth(iota(SLOTS, SLOTS, 0)) == twelfth(iota(SLOTS, SLOTS, 1))
    for out in (c_hi, c_lo):
        part = table2.astype(BF16)
        table2 = table2 - part.astype(F32)
        picked = jnp.where(own_row, dot_last(hot, part), 0.0).astype(BF16)
        out[...] = jnp.where(same, dot(picked, fold), 0.0).astype(BF16)


def turn_matrices(sz, qt, kin, pot, atoms, coupling):
    known = (1 + sz.links) * SLOTS
    outs = [
        shape(SLOTS, sz.all_pad, BF16),
        shape(sz.cell_pad, sz.cell_pad, BF16),
        shape(len(sz.cells) * sz.cell_pad, sz.orb, F32),
        shape(sz.shifts * SLOTS, known, BF16),
        shape(SLOTS, sz.links * SLOTS, BF16),
        shape(SLOTS, SLOTS, BF16),
        shape(SLOTS, SLOTS, BF16),
    ]
    limit = (32 << 20) if sz.shifts < 8 else (56 << 20)
    return kernel_call(
        functools.partial(turn_body, sz),
        outs,
        [qt, kin, pot, atoms, coupling],
        scratch=[pltpu.VMEM((coupling.shape[0], 16, coupling.shape[2]), F32)],
        flops=10**9,
        limit=limit,
    )


def cell_block(sz, z, cell):
    p, q = cell
    layers = []
    for a in range(EDGE):
        start = (ORDER * p + a) * sz.line_x + ORDER * q * PAD
        layers.append(z[start : start + EDGE * PAD, :])
    layers.append(jnp.zeros((sz.cell_pad - sz.cell_rows, sz.orb), F32))
    return jnp.concatenate(layers, axis=0)


def write_pair(axis, low, high, first, second):
    first[...] = by_parity(axis, low, high).astype(first.dtype)
    second[...] = by_parity(axis, high, low).astype(second.dtype)


def read_pair(axis, first, second):
    one, two = first[...].astype(F32), second[...].astype(F32)
    low, high = by_parity(axis, one, two), by_parity(axis, two, one)
    at, last = lax.axis_index(axis), lax.axis_size(axis) - 1
    return jnp.where(at > 0, low, 0.0), jnp.where(at < last, high, 0.0)


def write_faces(sz, r, sx_one, sx_two, sy_lo, sy_hi):
    pad_x = jnp.zeros((sz.xface - sz.line_x, sz.orb), F32)
    pad_y = jnp.zeros((sz.yface - sz.nx * PAD, sz.orb), F32)
    last = (sz.nx - 1) * sz.line_x
    low = jnp.concatenate([r[0 : sz.line_x, :], pad_x], axis=0)
    high = jnp.concatenate([r[last : last + sz.line_x, :], pad_x], axis=0)
    write_pair("gx", low, high, sx_one, sx_two)
    for out, b in ((sy_lo, 0), (sy_hi, sz.ny - 1)):
        rows = [r[a * sz.line_x + b * PAD : a * sz.line_x + (b + 1) * PAD, :] for a in range(sz.nx)]
        out[...] = jnp.concatenate(rows + [pad_y], axis=0)


def face_outs(sz):
    return [shape(sz.xface, sz.orb, HALO)] * 2 + [shape(sz.yface, sz.orb, F32)] * 2


def start_body(sz, parts, r, *faces):
    nz = parts.shape[2]
    r[...] = jnp.zeros(r.shape, F32)
    for a in range(sz.nx):
        for b in range(sz.ny):
            at = a * sz.line_x + b * PAD
            r[at : at + nz, :] = parts[a, b]
    write_faces(sz, r, *faces)


def start_faces(sz, parts):
    outs = [shape(sz.rows_all, sz.orb, F32)] + face_outs(sz)
    r, *faces = kernel_call(functools.partial(start_body, sz), outs, [parts])
    return r, faces


def cross_body(sz, xr_one, xr_two, ry_lo, ry_hi, sy_one, sy_two):
    last = (sz.nx - 1) * PAD
    lo, hi = read_pair("gx", xr_one, xr_two)
    faces = []
    for raw, b in ((ry_lo, 0), (ry_hi, sz.ny - 1)):
        value = raw[...]
        parts = [
            value[:PAD] + lo[b * PAD : (b + 1) * PAD],
            value[PAD:last],
            value[last : last + PAD] + hi[b * PAD : (b + 1) * PAD],
            value[last + PAD :],
        ]
        faces.append(jnp.concatenate(parts, axis=0))
    write_pair("gy", *faces, sy_one, sy_two)


def cross_faces(sz, *faces):
    outs = [shape(sz.yface, sz.orb, HALO)] * 2
    return kernel_call(functools.partial(cross_body, sz), outs, list(faces))


def add_xy(sz, ra, xr_one, xr_two, yr_one, yr_two):
    last = (sz.nx - 1) * sz.line_x
    low, high = read_pair("gx", xr_one, xr_two)
    ra[0 : sz.line_x, :] += low[: sz.line_x]
    ra[last : last + sz.line_x, :] += high[: sz.line_x]
    for value, b in zip(read_pair("gy", yr_one, yr_two), (0, sz.ny - 1)):
        for a in range(sz.nx):
            at = a * sz.line_x + b * PAD
            ra[at : at + PAD, :] += value[a * PAD : (a + 1) * PAD]


def local_term(weight, fields, at):
    value = weight * fields[0][at, :]
    return value - fields[1][at, :] if len(fields) > 1 else value


def layer_rows(y, weight, fields, at):
    rows = pl.ds(at, PAD, stride=PAD)
    return y[rows, :] - local_term(weight, fields, rows) if fields else y[rows, :]


def pack_z(sz, y, weight, fields, j):
    rows, c = [], layer_sent(sz, j)
    for a in range(sz.nx):
        for b in range(0, sz.face_b, PAD):
            rows.append(layer_rows(y, weight, fields, a * sz.line_x + b * PAD + c))
    rest = sz.zface - sz.nx * sz.face_b
    if rest:
        rows.append(jnp.zeros((rest, sz.orb), F32))
    value, valid = jnp.concatenate(rows, axis=0), link_valid(sz, j)
    return (value if valid is None else value * valid.astype(F32)).astype(HALO)


def add_z(sz, y, j, face):
    c = layer_received(sz, j)
    for a in range(sz.nx):
        for b in range(0, sz.ny, PAD):
            n = min(PAD, sz.ny - b)
            at = pl.ds(a * sz.line_x + b * PAD + c, n, stride=PAD)
            y[at, :] = y[at, :] + face[a * sz.face_b + b : a * sz.face_b + b + n]


def face_cells(sz, y, weight, fields, j):
    rows, c = [], layer_sent(sz, j)
    for p, q in sz.cells:
        for a in range(EDGE):
            at = (ORDER * p + a) * sz.line_x + ORDER * q * PAD
            rows.append(layer_rows(y, weight, fields, at + c))
        rows.append(jnp.zeros((PAD, sz.orb), F32))
    return jnp.concatenate(rows, axis=0).astype(BF16)


def project_body(sz, weight, past, refs):
    take = iter(refs)
    r = next(take)
    fields = [next(take) for _ in range(past)]
    halos = [next(take) for _ in range(4)]
    q = next(take)
    qfaces = [next(take) for _ in range(sz.links)]
    maps, back = next(take), next(take)
    y, own = next(take), next(take)
    messages = [next(take) for _ in range(sz.shifts)]
    everything = slice(0, sz.rows_all)
    y[...] = r[...] + local_term(weight, fields, everything) if past else r[...]
    add_xy(sz, y, *halos)
    blocks = [cell_block(sz, y, cell).astype(BF16) for cell in sz.cells]
    rest = sz.all_pad - sz.cell_pad * len(sz.cells)
    if rest:
        blocks.append(jnp.zeros((rest, sz.orb), BF16))
    beside = []
    for j, matrix in enumerate(qfaces):
        beside.append(dot(matrix[...], face_cells(sz, y, weight, fields, j)).astype(BF16))
    sums = dot(q[...], jnp.concatenate(blocks, axis=0))
    mapped = dot(maps[...], jnp.concatenate([sums.astype(BF16)] + beside, axis=0))
    for s, message in enumerate(messages):
        message[0:SLOTS, :] = mapped[s * SLOTS : (s + 1) * SLOTS].astype(HALO)
        for j, shift in enumerate(link_shifts(sz)):
            if shift == s + 1:
                message[SLOTS : SLOTS + sz.zface, :] = pack_z(sz, y, weight, fields, j)
    own[...] = sums + dot(back[...], jnp.concatenate(beside, axis=0))


def project(sz, r, weight, fields, halos, q, qfaces, maps, back):
    outs = [shape(sz.rows_all, sz.orb, F32), shape(SLOTS, sz.orb, F32)]
    for s in range(1, sz.shifts + 1):
        outs.append(shape(SLOTS + (sz.zface if s in link_shifts(sz) else 0), sz.orb, HALO))

    def body(*refs):
        project_body(sz, weight, len(fields), refs)

    y, own, *messages = kernel_call(
        body,
        outs,
        [r, *fields, *halos, q, *qfaces, maps, back],
        flops=4 * 10**8,
        limit=(32 << 20) if sz.shifts < 8 else (56 << 20),
    )
    return y, own, messages


def apply_body(sz, scale, refs):
    take = iter(refs)
    yin, own = next(take), next(take)
    messages = [next(take) for _ in range(sz.shifts)]
    c_hi, c_lo, qt, kin, pot = [next(take) for _ in range(5)]
    r, y = next(take), next(take)
    faces = [next(take) for _ in range(4)]
    totals = own[...]
    for message in messages:
        totals = totals + message[0:SLOTS, :].astype(F32)
    high = totals.astype(BF16)
    low = (totals - high.astype(F32)).astype(BF16)
    coef = (dot(c_hi[...], high) + (dot(c_hi[...], low) + dot(c_lo[...], high))).astype(BF16)
    y[...] = yin[...]
    for j, shift in enumerate(link_shifts(sz)):
        add_z(sz, y, j, messages[shift - 1][SLOTS : SLOTS + sz.zface, :].astype(F32))
    blocks = [cell_block(sz, y, cell) for cell in sz.cells]
    stiff = dot(kin[...], jnp.concatenate([b.astype(BF16) for b in blocks], axis=1))
    for g, (p, q) in enumerate(sz.cells):
        rows = slice(g * sz.cell_pad, (g + 1) * sz.cell_pad)
        value = stiff[:, g * sz.orb : (g + 1) * sz.orb] + pot[rows, :] * blocks[g]
        value = (value + dot(qt[rows, :], coef)) * scale
        for a in range(EDGE):
            start = (ORDER * p + a) * sz.line_x + ORDER * q * PAD
            line = value[a * EDGE * PAD : (a + 1) * EDGE * PAD]
            shared = EDGE * PAD if p and a == 0 else PAD if q else 0
            if shared:
                r[start : start + shared, :] += line[:shared]
            if shared < EDGE * PAD:
                r[start + shared : start + EDGE * PAD, :] = line[shared:]
    r[sz.rows :, :] = jnp.zeros((sz.rows_all - sz.rows, sz.orb), F32)
    write_faces(sz, r, *faces)


def apply(sz, y, own, messages, c_hi, c_lo, qt, kin, pot, scale):
    outs = [shape(sz.rows_all, sz.orb, F32)] * 2 + face_outs(sz)
    arrays = [y, own, *messages, c_hi, c_lo, qt, kin, pot]

    def body(*refs):
        apply_body(sz, scale, refs)

    r, y, *faces = kernel_call(body, outs, arrays, flops=6 * 10**8, limit=32 << 20)
    return r, y, faces


def last_faces_body(sz, refs):
    take = iter(refs)
    r = next(take)
    halos = [next(take) for _ in range(4)]
    ra = next(take)
    outs = [next(take) for _ in range(sz.links)]
    ra[...] = r[...]
    add_xy(sz, ra, *halos)
    for j, out in enumerate(outs):
        out[...] = pack_z(sz, ra, None, [], j)


def last_faces(sz, r, halos):
    def body(*refs):
        last_faces_body(sz, refs)

    outs = [shape(sz.rows_all, sz.orb, F32)] + [shape(sz.zface, sz.orb, HALO)] * sz.links
    ra, *sent = kernel_call(body, outs, [r, *halos])
    return ra, sent


def finish_body(sz, weight, past, refs):
    take = iter(refs)
    r = next(take)
    fields = [next(take) for _ in range(past)]
    zr = [next(take) for _ in range(sz.links)]
    out, ra = next(take), next(take)
    ra[...] = r[...] + local_term(weight, fields, slice(0, sz.rows_all))
    for j, face in enumerate(zr):
        add_z(sz, ra, j, face[...].astype(F32))
    value = ra[0 : sz.rows, :]
    out[...] = value.reshape(sz.nx, sz.ny, PAD, sz.orb)[:, :, : out.shape[2], :]


def finish(sz, r, weight, fields, zr, nz):
    def body(*refs):
        finish_body(sz, weight, len(fields), refs)

    outs = [jax.ShapeDtypeStruct((sz.nx, sz.ny, nz, sz.orb), F32)]
    scratch = [pltpu.VMEM((sz.rows_all, sz.orb), F32)]
    return kernel_call(body, outs, [r, *fields, *zr], scratch=scratch)[0]


def swap_faces(axis, one, two):
    axes = ("gx", "gy")
    wide, deep = lax.axis_size("gx"), lax.axis_size("gy")
    count = wide if axis == "gx" else deep

    def partner(i, j, low):
        at = i if axis == "gx" else j
        to = at + 1 if at % 2 == low else at - 1
        if 0 <= to < count:
            return (to, j) if axis == "gx" else (i, to)
        if axis == "gy" and wide % 2 == 0:
            return (i ^ 1, j)
        ends = sorted({k for k in range(count) if not 0 <= k + (1 if k % 2 == low else -1) < count})
        to = ends[::-1][ends.index(at)]
        return (to, j) if axis == "gx" else (i, to)

    out = []
    for face, low in ((one, 1), (two, 0)):
        pairs = []
        for i in range(wide):
            for j in range(deep):
                to = partner(i, j, low)
                pairs.append((i * deep + j, to[0] * deep + to[1]))
        out.append(lax.ppermute(face, axes, pairs))
    return out


def local(parts, cell_matrix, cell_potential, projectors, slot_atom, slot_cells, coupling):
    nx, ny, nz, orbitals = parts.shape
    nodes = cell_matrix.shape[0]
    devices = lax.axis_size("gz")
    sz = Sizes(nx, ny, nz, orbitals, devices - 1)
    ring = [[(i, (i + s) % devices) for i in range(devices)] for s in range(devices)]

    proj = projectors.reshape(nodes, POS * BLK * PA)
    proj = jnp.pad(proj, ((0, up(nodes, 16) - nodes), (0, 0)))
    cells = jnp.transpose(slot_cells.reshape(POS, BLK)).astype(F32)
    r, faces = start_faces(sz, parts)

    def exchange_xy(sx_one, sx_two, sy_lo, sy_hi):
        xr = swap_faces("gx", sx_one, sx_two)
        cross = cross_faces(sz, *xr, sy_lo, sy_hi)
        yr = swap_faces("gy", *cross)
        return (*xr, *yr)

    halos = exchange_xy(*faces)
    qt, *face_rows = sum_matrices(sz, proj, cells)
    qfaces = []
    for j, shift in enumerate(link_shifts(sz)):
        back = [(target, source) for source, target in ring[shift]]
        qfaces.append(lax.ppermute(face_rows[j], "gz", back))
    pot = jnp.transpose(cell_potential, (1, 2, 3, 0)).reshape(len(sz.cells), nodes)
    q, kin, pot, maps, back, c_hi, c_lo = turn_matrices(
        sz,
        qt,
        cell_matrix,
        pot,
        slot_atom.reshape(devices, POS),
        jnp.transpose(coupling, (1, 2, 0)),
    )

    fields, scale = [], 1.0 / half_width
    weight = 0.0
    for step in range(STEPS):
        y, own, messages = project(sz, r, weight, fields, halos, q, qfaces, maps, back)
        received = [lax.ppermute(m, "gz", ring[s + 1]) for s, m in enumerate(messages)]
        r, y, faces = apply(sz, y, own, received, c_hi, c_lo, qt, kin, pot, scale)
        fields, weight = [y] + fields[:1], -center_value * scale
        scale = 2.0 / half_width
        halos = exchange_xy(*faces)
    r, sent = last_faces(sz, r, halos)
    zr = [lax.ppermute(f, "gz", ring[s]) for f, s in zip(sent, link_shifts(sz))]
    return finish(sz, r, weight, fields, zr, nz)


def solution(mesh):
    in_specs = (
        P("gx", "gy", "gz", None),
        P(),
        P(None, "gx", "gy", "gz"),
        P("gx", "gy", "gz", None, None),
        P("gx", "gy", None, None),
        P("gx", "gy", "gz", None, None),
        P(("gx", "gy"), None, None),
    )
    out_specs = P("gx", "gy", "gz", None)
    return jax.shard_map(local, mesh=mesh, in_specs=in_specs, out_specs=out_specs, check_vma=False)
```

```python
import functools

import jax
import jax.numpy as jnp
import numpy as np
from jax import lax
from jax.experimental import pallas as pl
from jax.experimental.pallas import tpu as pltpu
from jax.sharding import PartitionSpec as P

ORDER = 6
STEPS = 3
PA = 12
POS = 32
BLK = 4

center_value = 2.0
half_width = 3.0

EDGE = ORDER + 1
PAD = 8
SLOTS = POS * PA
F32 = jnp.float32
BF16 = jnp.bfloat16
HALO = jnp.bfloat16


def up(value, multiple):
    return -(-value // multiple) * multiple


class Sizes:
    def __init__(self, nx, ny, nz, orbitals, shifts):
        assert nz == EDGE
        self.nx, self.ny, self.orb = nx, ny, orbitals
        self.cells = [(p, q) for p in range((nx - 1) // ORDER) for q in range((ny - 1) // ORDER)]
        self.rows = nx * ny * PAD
        self.line_x = ny * PAD
        self.xface = up(ny * PAD, 16)
        self.yface = up(nx * PAD, 16)
        self.face_b = up(ny, PAD)
        self.zface = up(nx * self.face_b, 16)
        self.cell_rows = EDGE * EDGE * PAD
        self.cell_pad = up(self.cell_rows, 16)
        self.all_pad = up(self.cell_pad * len(self.cells), 128)
        self.fcell = EDGE * PAD
        self.fall = up(self.fcell * len(self.cells), 256)
        self.shifts, self.links = shifts, min(2, shifts)
        self.rows_all = self.rows + (self.face_b - ny + 1) * PAD


VMEM = pl.BlockSpec(memory_space=pltpu.VMEM)


def kernel_call(body, outs, arrays, scratch=(), flops=0, limit=24 << 20, after=()):
    used = len(arrays)

    def with_waits(*refs):
        body(*refs[:used], *refs[used + len(after) :])

    nbytes = sum(int(np.prod(a.shape)) * a.dtype.itemsize for a in list(arrays) + list(outs))
    return pl.pallas_call(
        with_waits,
        out_shape=outs,
        in_specs=[VMEM] * used + [pl.BlockSpec(memory_space=pl.ANY)] * len(after),
        out_specs=[VMEM] * len(outs),
        scratch_shapes=list(scratch),
        compiler_params=pltpu.CompilerParams(vmem_limit_bytes=limit),
        cost_estimate=pl.CostEstimate(flops=flops, bytes_accessed=nbytes, transcendentals=0),
    )(*arrays, *after)


def shape(rows, cols, dtype):
    return jax.ShapeDtypeStruct((rows, cols), dtype)


def dot(a, b):
    return jnp.dot(a, b, preferred_element_type=F32)


def is_odd(axis):
    return lax.rem(lax.axis_index(axis), 2) == 1


def by_parity(axis, even, odd):
    return jnp.where(is_odd(axis), odd, even)


def link_shifts(sz):
    return [1, sz.shifts][: sz.links]


def layer_sent(sz, j):
    if sz.links == 1:
        return jnp.where(lax.axis_index("gz") == 0, ORDER, 0)
    return [ORDER, 0][j]


def layer_received(sz, j):
    return layer_sent(sz, 0) if sz.links == 1 else [0, ORDER][j]


def link_valid(sz, j):
    if sz.links == 1:
        return None
    me = lax.axis_index("gz")
    return jnp.where(me < sz.shifts, 1, 0) if j == 0 else jnp.where(me > 0, 1, 0)


def iota(rows, cols, dim):
    return lax.broadcasted_iota(jnp.int32, (rows, cols), dim)


def twelfth(value):
    return (value * (2**19 // PA + 1)) >> 19


def node_key(i):
    low = i & (PAD - 1)
    return jnp.where((low < EDGE) & (i < EDGE * EDGE * PAD), (i >> 3) * EDGE + low, -1)


def dot_last(a, b, precision=None):
    dims = (((1,), (1,)), ((), ()))
    return lax.dot_general(a, b, dims, precision=precision, preferred_element_type=F32)


def sum_body(sz, proj, cells, qt, *qt_faces):
    nodes, cols = proj.shape
    i = iota(cols, POS, 0)
    first = iota(cols, POS, 1) * (BLK * PA)
    in_slot = ((i >= first) & (i < first + BLK * PA)).astype(BF16)
    of_block = dot_last(in_slot, cells[...].astype(BF16))
    i = iota(cols, BLK, 0)
    block = twelfth(i)
    cell = jnp.sum(
        jnp.where((block & (BLK - 1)) == iota(cols, BLK, 1), of_block, 0.0), axis=1, keepdims=True
    )
    i, block = i[:, :1], block[:, :1]
    row = (block >> (BLK.bit_length() - 1)) * PA + (i - block * PA)
    key = cell.astype(jnp.int32) * SLOTS + row
    targets = len(sz.cells) * SLOTS
    pick = (key == iota(cols, targets, 1)).astype(BF16)
    keys = [node_key(iota(sz.cell_pad, nodes, 0))]
    for j in range(sz.links):
        keys.append(
            jnp.where(
                iota(PAD * PAD, nodes, 0) < sz.fcell,
                node_key(iota(PAD * PAD, nodes, 0)) * EDGE + layer_received(sz, j),
                -1,
            )
        )
        low = iota(PAD * PAD, nodes, 0) & (PAD - 1)
        keys[-1] = jnp.where(low < EDGE, keys[-1], -1)
    expand = (jnp.concatenate(keys, axis=0) == iota(sz.cell_pad + sz.links * PAD * PAD, nodes, 1))
    summed = dot(proj[...], pick).astype(BF16)
    full = dot(expand.astype(BF16), summed)
    for g in range(len(sz.cells)):
        value = full[:, g * SLOTS : (g + 1) * SLOTS]
        qt[g * sz.cell_pad : (g + 1) * sz.cell_pad, :] = value[: sz.cell_pad].astype(BF16)
    rest = sz.all_pad - sz.cell_pad * len(sz.cells)
    if rest:
        qt[sz.cell_pad * len(sz.cells) :, :] = jnp.zeros((rest, SLOTS), BF16)
    for j, qf in enumerate(qt_faces):
        at = sz.cell_pad + j * PAD * PAD
        rows = [full[at : at + PAD * PAD, g * SLOTS : (g + 1) * SLOTS] for g in range(len(sz.cells))]
        qf[...] = jnp.concatenate(rows, axis=0).T.astype(BF16)


def sum_matrices(sz, proj, cells, after):
    outs = [shape(sz.all_pad, SLOTS, BF16)]
    outs += [shape(SLOTS, len(sz.cells) * PAD * PAD, BF16)] * sz.links
    body = functools.partial(sum_body, sz)
    return kernel_call(
        body, outs, [proj, cells], flops=3 * 10**9, limit=32 << 20, after=after
    )


def slot_keys(sz, table, dim):
    exact = lax.Precision.HIGHEST
    shape2 = (SLOTS, POS) if dim == 0 else (POS, SLOTS)
    i, s = iota(*shape2, dim), iota(*shape2, 1 - dim)
    spread = ((i >= s * PA) & (i < s * PA + PA)).astype(F32)
    if dim == 0:
        atoms = dot_last(spread, table, exact)
    else:
        atoms = jnp.dot(table, spread, precision=exact, preferred_element_type=F32)
    devices = sz.shifts + 1
    at = iota(*atoms.shape, 1 - dim)
    me = lax.axis_index("gz")
    keys = []
    for shift in range(devices):
        chosen = jnp.where(at == lax.rem(me + shift, devices), atoms, 0.0)
        atom = jnp.sum(chosen, axis=1 - dim, keepdims=True).astype(jnp.int32)
        i = iota(*atom.shape, dim)
        keys.append((atom, jnp.where(atom >= 0, atom * PA + i - twelfth(i) * PA, -1)))
    return keys


def turn_body(qt, q):
    q[...] = qt[...].T


def turn_matrix(sz, qt):
    return kernel_call(turn_body, [shape(SLOTS, sz.all_pad, BF16)], [qt], flops=10**8)[0]


def other_body(sz, kin, pot, atoms, coupling, kout, vout, maps, back, c_hi, c_lo, wide):
    nodes = kin.shape[0]
    expand = (node_key(iota(sz.cell_pad, nodes, 0)) == iota(sz.cell_pad, nodes, 1)).astype(BF16)
    gather = (node_key(iota(nodes, sz.cell_pad, 1)) == iota(nodes, sz.cell_pad, 0)).astype(BF16)
    tall = dot(expand, kin[...]).astype(BF16)
    kout[...] = dot(tall, gather).astype(BF16)
    value, values = pot[...], 0.0
    for _ in range(3):
        part = value.astype(BF16)
        values = values + dot_last(expand, part)
        value = value - part.astype(F32)
    for g in range(len(sz.cells)):
        vout[g * sz.cell_pad : (g + 1) * sz.cell_pad, :] = jnp.broadcast_to(
            values[:, g : g + 1], (sz.cell_pad, sz.orb)
        )
    table = atoms[...].astype(F32)
    rows, cols = slot_keys(sz, table, 0), slot_keys(sz, table, 1)
    known = [jnp.where(cols[0][1] >= 0, cols[0][1], -2)]
    for j, shift in enumerate(link_shifts(sz)):
        key = jnp.where(cols[shift][1] >= 0, cols[shift][1], -2)
        valid = link_valid(sz, j)
        known.append(key if valid is None else jnp.where(valid == 1, key, -2))
    for s in range(sz.shifts):
        for j, key in enumerate(known):
            maps[s * SLOTS : (s + 1) * SLOTS, j * SLOTS : (j + 1) * SLOTS] = (
                rows[s + 1][1] == key
            ).astype(BF16)
    for j, key in enumerate(known[1:]):
        back[:, j * SLOTS : (j + 1) * SLOTS] = (rows[0][1] == key).astype(BF16)
    pa, pb, atom_count = coupling.shape
    wide[...] = jnp.zeros(wide.shape, F32)
    wide[:, :pb, :] = coupling[...]
    table2 = wide[...].reshape(pa * 16, atom_count)
    hot = (rows[0][0] == iota(SLOTS, atom_count, 1)).astype(BF16)
    i, lane = iota(SLOTS, pa * 16, 0), iota(SLOTS, pa * 16, 1)
    own_row = (lane >> 4) == i - twelfth(i) * PA
    lane, j = iota(pa * 16, SLOTS, 0), iota(pa * 16, SLOTS, 1)
    fold = ((lane & 15) == j - twelfth(j) * PA).astype(BF16)
    same = twelfth(iota(SLOTS, SLOTS, 0)) == twelfth(iota(SLOTS, SLOTS, 1))
    for out in (c_hi, c_lo):
        part = table2.astype(BF16)
        table2 = table2 - part.astype(F32)
        picked = jnp.where(own_row, dot_last(hot, part), 0.0).astype(BF16)
        out[...] = jnp.where(same, dot(picked, fold), 0.0).astype(BF16)


def other_matrices(sz, kin, pot, atoms, coupling):
    known = (1 + sz.links) * SLOTS
    outs = [
        shape(sz.cell_pad, sz.cell_pad, BF16),
        shape(len(sz.cells) * sz.cell_pad, sz.orb, F32),
        shape(sz.shifts * SLOTS, known, BF16),
        shape(SLOTS, sz.links * SLOTS, BF16),
        shape(SLOTS, SLOTS, BF16),
        shape(SLOTS, SLOTS, BF16),
    ]
    limit = (32 << 20) if sz.shifts < 8 else (56 << 20)
    return kernel_call(
        functools.partial(other_body, sz),
        outs,
        [kin, pot, atoms, coupling],
        scratch=[pltpu.VMEM((coupling.shape[0], 16, coupling.shape[2]), F32)],
        flops=10**9,
        limit=limit,
    )


def cell_block(sz, z, cell):
    p, q = cell
    layers = []
    for a in range(EDGE):
        start = (ORDER * p + a) * sz.line_x + ORDER * q * PAD
        layers.append(z[start : start + EDGE * PAD, :])
    layers.append(jnp.zeros((sz.cell_pad - sz.cell_rows, sz.orb), F32))
    return jnp.concatenate(layers, axis=0)


def write_pair(axis, low, high, first, second):
    first[...] = by_parity(axis, low, high).astype(first.dtype)
    second[...] = by_parity(axis, high, low).astype(second.dtype)


def read_pair(axis, first, second):
    one, two = first[...].astype(F32), second[...].astype(F32)
    low, high = by_parity(axis, one, two), by_parity(axis, two, one)
    at, last = lax.axis_index(axis), lax.axis_size(axis) - 1
    return jnp.where(at > 0, low, 0.0), jnp.where(at < last, high, 0.0)


def write_faces(sz, r, sx_one, sx_two, sy_lo, sy_hi):
    pad_x = jnp.zeros((sz.xface - sz.line_x, sz.orb), F32)
    pad_y = jnp.zeros((sz.yface - sz.nx * PAD, sz.orb), F32)
    last = (sz.nx - 1) * sz.line_x
    low = jnp.concatenate([r[0 : sz.line_x, :], pad_x], axis=0)
    high = jnp.concatenate([r[last : last + sz.line_x, :], pad_x], axis=0)
    write_pair("gx", low, high, sx_one, sx_two)
    for out, b in ((sy_lo, 0), (sy_hi, sz.ny - 1)):
        rows = [r[a * sz.line_x + b * PAD : a * sz.line_x + (b + 1) * PAD, :] for a in range(sz.nx)]
        out[...] = jnp.concatenate(rows + [pad_y], axis=0)


def face_outs(sz):
    return [shape(sz.xface, sz.orb, HALO)] * 2 + [shape(sz.yface, sz.orb, F32)] * 2


def start_body(sz, parts, r, *sends):
    nz = parts.shape[2]
    r[...] = jnp.zeros(r.shape, F32)
    for a in range(sz.nx):
        for b in range(sz.ny):
            at = a * sz.line_x + b * PAD
            r[at : at + nz, :] = parts[a, b]
    for j, out in enumerate(sends):
        out[...] = pack_z(sz, r, None, [], j)


def start_field(sz, parts):
    outs = [shape(sz.rows_all, sz.orb, F32)] + [shape(sz.zface, sz.orb, HALO)] * sz.links
    r, *sends = kernel_call(functools.partial(start_body, sz), outs, [parts])
    return r, sends


def start_faces_body(sz, rin, *refs):
    zr, r, faces = refs[: sz.links], refs[sz.links], refs[sz.links + 1 :]
    r[...] = rin[...]
    for j, face in enumerate(zr):
        add_z(sz, r, j, face[...].astype(F32))
    write_faces(sz, r, *faces)


def start_faces(sz, r, zr, after):
    outs = [shape(sz.rows_all, sz.orb, F32)] + face_outs(sz)
    body = functools.partial(start_faces_body, sz)
    r, *faces = kernel_call(body, outs, [r, *zr], after=after)
    return r, faces


def cross_body(sz, xr_one, xr_two, ry_lo, ry_hi, sy_one, sy_two):
    last = (sz.nx - 1) * PAD
    lo, hi = read_pair("gx", xr_one, xr_two)
    faces = []
    for raw, b in ((ry_lo, 0), (ry_hi, sz.ny - 1)):
        value = raw[...]
        parts = [
            value[:PAD] + lo[b * PAD : (b + 1) * PAD],
            value[PAD:last],
            value[last : last + PAD] + hi[b * PAD : (b + 1) * PAD],
            value[last + PAD :],
        ]
        faces.append(jnp.concatenate(parts, axis=0))
    write_pair("gy", *faces, sy_one, sy_two)


def cross_faces(sz, faces, after=()):
    outs = [shape(sz.yface, sz.orb, HALO)] * 2
    return kernel_call(functools.partial(cross_body, sz), outs, faces, after=after)


def add_xy(sz, ra, xr_one, xr_two, yr_one, yr_two):
    last = (sz.nx - 1) * sz.line_x
    low, high = read_pair("gx", xr_one, xr_two)
    ra[0 : sz.line_x, :] += low[: sz.line_x]
    ra[last : last + sz.line_x, :] += high[: sz.line_x]
    for value, b in zip(read_pair("gy", yr_one, yr_two), (0, sz.ny - 1)):
        for a in range(sz.nx):
            at = a * sz.line_x + b * PAD
            ra[at : at + PAD, :] += value[a * PAD : (a + 1) * PAD]


def local_term(weight, fields, at):
    value = weight * fields[0][at, :]
    return value - fields[1][at, :] if len(fields) > 1 else value


def layer_rows(y, weight, fields, at):
    rows = pl.ds(at, PAD, stride=PAD)
    return y[rows, :] - local_term(weight, fields, rows) if fields else y[rows, :]


def pack_z(sz, y, weight, fields, j):
    rows, c = [], layer_sent(sz, j)
    for a in range(sz.nx):
        for b in range(0, sz.face_b, PAD):
            rows.append(layer_rows(y, weight, fields, a * sz.line_x + b * PAD + c))
    rest = sz.zface - sz.nx * sz.face_b
    if rest:
        rows.append(jnp.zeros((rest, sz.orb), F32))
    value, valid = jnp.concatenate(rows, axis=0), link_valid(sz, j)
    return (value if valid is None else value * valid.astype(F32)).astype(HALO)


def add_z(sz, y, j, face):
    c = layer_received(sz, j)
    for a in range(sz.nx):
        for b in range(0, sz.ny, PAD):
            n = min(PAD, sz.ny - b)
            at = pl.ds(a * sz.line_x + b * PAD + c, n, stride=PAD)
            y[at, :] = y[at, :] + face[a * sz.face_b + b : a * sz.face_b + b + n]


def face_cells(sz, y, weight, fields, j):
    rows, c = [], layer_sent(sz, j)
    for p, q in sz.cells:
        for a in range(EDGE):
            at = (ORDER * p + a) * sz.line_x + ORDER * q * PAD
            rows.append(layer_rows(y, weight, fields, at + c))
        rows.append(jnp.zeros((PAD, sz.orb), F32))
    return jnp.concatenate(rows, axis=0).astype(BF16)


def project_body(sz, weight, past, with_face, refs):
    take = iter(refs)
    r = next(take)
    fields = [next(take) for _ in range(past)]
    halos = [next(take) for _ in range(4)]
    q = next(take)
    maps = next(take)
    if with_face:
        back, *qfaces = [next(take) for _ in range(1 + sz.links)]
    y, own = next(take), next(take)
    messages = [next(take) for _ in range(sz.shifts)]
    everything = slice(0, sz.rows_all)
    y[...] = r[...] + local_term(weight, fields, everything) if past else r[...]
    add_xy(sz, y, *halos)
    blocks = [cell_block(sz, y, cell).astype(BF16) for cell in sz.cells]
    rest = sz.all_pad - sz.cell_pad * len(sz.cells)
    if rest:
        blocks.append(jnp.zeros((rest, sz.orb), BF16))
    beside = []
    if with_face:
        for j, matrix in enumerate(qfaces):
            beside.append(dot(matrix[...], face_cells(sz, y, weight, fields, j)).astype(BF16))
    sums = dot(q[...], jnp.concatenate(blocks, axis=0))
    known = jnp.concatenate([sums.astype(BF16)] + beside, axis=0)
    mapped = dot(maps[:, : known.shape[0]], known)
    for s, message in enumerate(messages):
        message[0:SLOTS, :] = mapped[s * SLOTS : (s + 1) * SLOTS].astype(HALO)
        for j, shift in enumerate(link_shifts(sz)):
            if with_face and shift == s + 1:
                message[SLOTS : SLOTS + sz.zface, :] = pack_z(sz, y, weight, fields, j)
    if beside:
        sums = sums + dot(back[...], jnp.concatenate(beside, axis=0))
    own[...] = sums


def project(sz, r, weight, fields, halos, q, maps, back_and_faces):
    with_face = bool(back_and_faces)
    outs = [shape(sz.rows_all, sz.orb, F32), shape(SLOTS, sz.orb, F32)]
    for s in range(1, sz.shifts + 1):
        face = sz.zface if with_face and s in link_shifts(sz) else 0
        outs.append(shape(SLOTS + face, sz.orb, HALO))

    def body(*refs):
        project_body(sz, weight, len(fields), with_face, refs)

    y, own, *messages = kernel_call(
        body,
        outs,
        [r, *fields, *halos, q, maps, *back_and_faces],
        flops=4 * 10**8,
        limit=(32 << 20) if sz.shifts < 8 else (56 << 20),
    )
    return y, own, messages


def apply_body(sz, scale, refs):
    take = iter(refs)
    yin, own = next(take), next(take)
    messages = [next(take) for _ in range(sz.shifts)]
    c_hi, c_lo, qt, kin, pot = [next(take) for _ in range(5)]
    r, y = next(take), next(take)
    faces = [next(take) for _ in range(4)]
    totals = own[...]
    for message in messages:
        totals = totals + message[0:SLOTS, :].astype(F32)
    high = totals.astype(BF16)
    low = (totals - high.astype(F32)).astype(BF16)
    coef = (dot(c_hi[...], high) + (dot(c_hi[...], low) + dot(c_lo[...], high))).astype(BF16)
    y[...] = yin[...]
    for j, shift in enumerate(link_shifts(sz)):
        if messages[shift - 1].shape[0] == SLOTS:
            continue
        add_z(sz, y, j, messages[shift - 1][SLOTS : SLOTS + sz.zface, :].astype(F32))
    blocks = [cell_block(sz, y, cell) for cell in sz.cells]
    stiff = dot(kin[...], jnp.concatenate([b.astype(BF16) for b in blocks], axis=1))
    for g, (p, q) in enumerate(sz.cells):
        rows = slice(g * sz.cell_pad, (g + 1) * sz.cell_pad)
        value = stiff[:, g * sz.orb : (g + 1) * sz.orb] + pot[rows, :] * blocks[g]
        value = (value + dot(qt[rows, :], coef)) * scale
        for a in range(EDGE):
            start = (ORDER * p + a) * sz.line_x + ORDER * q * PAD
            line = value[a * EDGE * PAD : (a + 1) * EDGE * PAD]
            shared = EDGE * PAD if p and a == 0 else PAD if q else 0
            if shared:
                r[start : start + shared, :] += line[:shared]
            if shared < EDGE * PAD:
                r[start + shared : start + EDGE * PAD, :] = line[shared:]
    r[sz.rows :, :] = jnp.zeros((sz.rows_all - sz.rows, sz.orb), F32)
    write_faces(sz, r, *faces)


def apply(sz, y, own, messages, c_hi, c_lo, qt, kin, pot, scale):
    outs = [shape(sz.rows_all, sz.orb, F32)] * 2 + face_outs(sz)
    arrays = [y, own, *messages, c_hi, c_lo, qt, kin, pot]

    def body(*refs):
        apply_body(sz, scale, refs)

    r, y, *faces = kernel_call(body, outs, arrays, flops=6 * 10**8, limit=32 << 20)
    return r, y, faces


def last_faces_body(sz, refs):
    take = iter(refs)
    r = next(take)
    halos = [next(take) for _ in range(4)]
    ra = next(take)
    outs = [next(take) for _ in range(sz.links)]
    ra[...] = r[...]
    add_xy(sz, ra, *halos)
    for j, out in enumerate(outs):
        out[...] = pack_z(sz, ra, None, [], j)


def last_faces(sz, r, halos):
    def body(*refs):
        last_faces_body(sz, refs)

    outs = [shape(sz.rows_all, sz.orb, F32)] + [shape(sz.zface, sz.orb, HALO)] * sz.links
    ra, *sent = kernel_call(body, outs, [r, *halos])
    return ra, sent


def finish_body(sz, weight, past, refs):
    take = iter(refs)
    r = next(take)
    fields = [next(take) for _ in range(past)]
    zr = [next(take) for _ in range(sz.links)]
    out, ra = next(take), next(take)
    ra[...] = r[...] + local_term(weight, fields, slice(0, sz.rows_all))
    for j, face in enumerate(zr):
        add_z(sz, ra, j, face[...].astype(F32))
    value = ra[0 : sz.rows, :]
    out[...] = value.reshape(sz.nx, sz.ny, PAD, sz.orb)[:, :, : out.shape[2], :]


def finish(sz, r, weight, fields, zr, nz):
    def body(*refs):
        finish_body(sz, weight, len(fields), refs)

    outs = [jax.ShapeDtypeStruct((sz.nx, sz.ny, nz, sz.orb), F32)]
    scratch = [pltpu.VMEM((sz.rows_all, sz.orb), F32)]
    return kernel_call(body, outs, [r, *fields, *zr], scratch=scratch)[0]


def swap_faces(axis, one, two):
    axes = ("gx", "gy")
    wide, deep = lax.axis_size("gx"), lax.axis_size("gy")
    count = wide if axis == "gx" else deep

    def partner(i, j, low):
        at = i if axis == "gx" else j
        to = at + 1 if at % 2 == low else at - 1
        if 0 <= to < count:
            return (to, j) if axis == "gx" else (i, to)
        if axis == "gy" and wide % 2 == 0:
            return (i ^ 1, j)
        ends = sorted({k for k in range(count) if not 0 <= k + (1 if k % 2 == low else -1) < count})
        to = ends[::-1][ends.index(at)]
        return (to, j) if axis == "gx" else (i, to)

    out = []
    for face, low in ((one, 1), (two, 0)):
        pairs = []
        for i in range(wide):
            for j in range(deep):
                to = partner(i, j, low)
                pairs.append((i * deep + j, to[0] * deep + to[1]))
        out.append(lax.ppermute(face, axes, pairs))
    return out


def local(parts, cell_matrix, cell_potential, projectors, slot_atom, slot_cells, coupling):
    nx, ny, nz, orbitals = parts.shape
    nodes = cell_matrix.shape[0]
    devices = lax.axis_size("gz")
    sz = Sizes(nx, ny, nz, orbitals, devices - 1)
    ring = [[(i, (i + s) % devices) for i in range(devices)] for s in range(devices)]

    def exchange_z(faces):
        return [lax.ppermute(f, "gz", ring[s]) for f, s in zip(faces, link_shifts(sz))]

    def exchange_xy(sx_one, sx_two, sy_lo, sy_hi, after=()):
        xr = swap_faces("gx", sx_one, sx_two)
        cross = cross_faces(sz, [*xr, sy_lo, sy_hi], after)
        yr = swap_faces("gy", *cross)
        return (*xr, *yr), cross

    r, sends = start_field(sz, parts)
    zr = exchange_z(sends)
    pot = jnp.transpose(cell_potential, (1, 2, 3, 0)).reshape(len(sz.cells), nodes)
    kin, pot, maps, back, c_hi, c_lo = other_matrices(
        sz, cell_matrix, pot, slot_atom.reshape(devices, POS), jnp.transpose(coupling, (1, 2, 0))
    )
    proj = projectors.reshape(nodes, POS * BLK * PA)
    proj = jnp.pad(proj, ((0, up(nodes, 16) - nodes), (0, 0)))
    cells = jnp.transpose(slot_cells.reshape(POS, BLK)).astype(F32)
    r, faces = start_faces(sz, r, zr, [c_lo, proj, cells])
    qt, *face_rows = sum_matrices(sz, proj, cells, [faces[0]])
    halos, cross = exchange_xy(*faces, after=[qt])
    q = turn_matrix(sz, qt)
    face_rows, _ = lax.optimization_barrier((face_rows, cross[0]))
    qfaces = []
    for j, shift in enumerate(link_shifts(sz)):
        home = [(target, source) for source, target in ring[shift]]
        qfaces.append(lax.ppermute(face_rows[j], "gz", home))

    fields, scale = [], 1.0 / half_width
    weight = 0.0
    for step in range(STEPS):
        y, own, messages = project(
            sz, r, weight, fields, halos, q, maps, [back, *qfaces] if step else []
        )
        received = [lax.ppermute(m, "gz", ring[s + 1]) for s, m in enumerate(messages)]
        r, y, faces = apply(sz, y, own, received, c_hi, c_lo, qt, kin, pot, scale)
        fields, weight = [y] + fields[:1], -center_value * scale
        scale = 2.0 / half_width
        halos, _ = exchange_xy(*faces)
    r, sent = last_faces(sz, r, halos)
    return finish(sz, r, weight, fields, exchange_z(sent), nz)


def solution(mesh):
    in_specs = (
        P("gx", "gy", "gz", None),
        P(),
        P(None, "gx", "gy", "gz"),
        P("gx", "gy", "gz", None, None),
        P("gx", "gy", None, None),
        P("gx", "gy", "gz", None, None),
        P(("gx", "gy"), None, None),
    )
    out_specs = P("gx", "gy", "gz", None)
    return jax.shard_map(local, mesh=mesh, in_specs=in_specs, out_specs=out_specs, check_vma=False)
```

```python
import functools

import jax
import jax.numpy as jnp
import numpy as np
from jax import lax
from jax.experimental import pallas as pl
from jax.experimental.pallas import tpu as pltpu
from jax.sharding import PartitionSpec as P

ORDER = 6
STEPS = 3
PA = 12
POS = 32
BLK = 4

center_value = 2.0
half_width = 3.0

EDGE = ORDER + 1
PAD = 8
SLOTS = POS * PA
F32 = jnp.float32
BF16 = jnp.bfloat16
HALO = jnp.bfloat16


def up(value, multiple):
    return -(-value // multiple) * multiple


class Sizes:
    def __init__(self, nx, ny, nz, orbitals, shifts):
        assert nz == EDGE
        self.nx, self.ny, self.orb = nx, ny, orbitals
        self.cells = [(p, q) for p in range((nx - 1) // ORDER) for q in range((ny - 1) // ORDER)]
        self.rows = nx * ny * PAD
        self.line_x = ny * PAD
        self.xface = up(ny * PAD, 16)
        self.yface = up(nx * PAD, 16)
        self.face_b = up(ny, PAD)
        self.zface = up(nx * self.face_b, 16)
        self.cell_rows = EDGE * EDGE * PAD
        self.cell_pad = up(self.cell_rows, 16)
        self.all_pad = up(self.cell_pad * len(self.cells), 128)
        self.fcell = EDGE * PAD
        self.fall = up(self.fcell * len(self.cells), 256)
        self.shifts, self.links = shifts, min(2, shifts)
        self.rows_all = self.rows + (self.face_b - ny + 1) * PAD


VMEM = pl.BlockSpec(memory_space=pltpu.VMEM)


def kernel_call(body, outs, arrays, scratch=(), flops=0, limit=24 << 20, after=(), out_specs=None):
    used = len(arrays)

    def with_waits(*refs):
        body(*refs[:used], *refs[used + len(after) :])

    nbytes = sum(int(np.prod(a.shape)) * a.dtype.itemsize for a in list(arrays) + list(outs))
    return pl.pallas_call(
        with_waits,
        out_shape=outs,
        in_specs=[VMEM] * used + [pl.BlockSpec(memory_space=pl.ANY)] * len(after),
        out_specs=out_specs or [VMEM] * len(outs),
        scratch_shapes=list(scratch),
        compiler_params=pltpu.CompilerParams(vmem_limit_bytes=limit),
        cost_estimate=pl.CostEstimate(flops=flops, bytes_accessed=nbytes, transcendentals=0),
    )(*arrays, *after)


def shape(rows, cols, dtype):
    return jax.ShapeDtypeStruct((rows, cols), dtype)


def dot(a, b):
    return jnp.dot(a, b, preferred_element_type=F32)


def is_odd(axis):
    return lax.rem(lax.axis_index(axis), 2) == 1


def by_parity(axis, even, odd):
    return jnp.where(is_odd(axis), odd, even)


def link_shifts(sz):
    return [1, sz.shifts][: sz.links]


def layer_sent(sz, j):
    if sz.links == 1:
        return jnp.where(lax.axis_index("gz") == 0, ORDER, 0)
    return [ORDER, 0][j]


def layer_received(sz, j):
    return layer_sent(sz, 0) if sz.links == 1 else [0, ORDER][j]


def link_valid(sz, j):
    if sz.links == 1:
        return None
    me = lax.axis_index("gz")
    return jnp.where(me < sz.shifts, 1, 0) if j == 0 else jnp.where(me > 0, 1, 0)


def iota(rows, cols, dim):
    return lax.broadcasted_iota(jnp.int32, (rows, cols), dim)


def twelfth(value):
    return (value * (2**19 // PA + 1)) >> 19


def node_key(i):
    low = i & (PAD - 1)
    return jnp.where((low < EDGE) & (i < EDGE * EDGE * PAD), (i >> 3) * EDGE + low, -1)


def dot_last(a, b, precision=None):
    dims = (((1,), (1,)), ((), ()))
    return lax.dot_general(a, b, dims, precision=precision, preferred_element_type=F32)


def sum_body(sz, proj, cells, qt, *qt_faces):
    nodes, cols = proj.shape
    i = iota(cols, POS, 0)
    first = iota(cols, POS, 1) * (BLK * PA)
    in_slot = ((i >= first) & (i < first + BLK * PA)).astype(BF16)
    of_block = dot_last(in_slot, cells[...].astype(BF16))
    i = iota(cols, BLK, 0)
    block = twelfth(i)
    cell = jnp.sum(
        jnp.where((block & (BLK - 1)) == iota(cols, BLK, 1), of_block, 0.0), axis=1, keepdims=True
    )
    i, block = i[:, :1], block[:, :1]
    row = (block >> (BLK.bit_length() - 1)) * PA + (i - block * PA)
    key = cell.astype(jnp.int32) * SLOTS + row
    targets = len(sz.cells) * SLOTS
    pick = (key == iota(cols, targets, 1)).astype(BF16)
    keys = [node_key(iota(sz.cell_pad, nodes, 0))]
    for j in range(sz.links):
        keys.append(
            jnp.where(
                iota(PAD * PAD, nodes, 0) < sz.fcell,
                node_key(iota(PAD * PAD, nodes, 0)) * EDGE + layer_received(sz, j),
                -1,
            )
        )
        low = iota(PAD * PAD, nodes, 0) & (PAD - 1)
        keys[-1] = jnp.where(low < EDGE, keys[-1], -1)
    expand = (jnp.concatenate(keys, axis=0) == iota(sz.cell_pad + sz.links * PAD * PAD, nodes, 1))
    summed = dot(proj[...], pick).astype(BF16)
    full = dot(expand.astype(BF16), summed)
    for g in range(len(sz.cells)):
        value = full[:, g * SLOTS : (g + 1) * SLOTS]
        qt[g * sz.cell_pad : (g + 1) * sz.cell_pad, :] = value[: sz.cell_pad].astype(BF16)
    rest = sz.all_pad - sz.cell_pad * len(sz.cells)
    if rest:
        qt[sz.cell_pad * len(sz.cells) :, :] = jnp.zeros((rest, SLOTS), BF16)
    for j, qf in enumerate(qt_faces):
        at = sz.cell_pad + j * PAD * PAD
        rows = [full[at : at + PAD * PAD, g * SLOTS : (g + 1) * SLOTS] for g in range(len(sz.cells))]
        qf[...] = jnp.concatenate(rows, axis=0).T.astype(BF16)


def sum_matrices(sz, proj, cells):
    outs = [shape(sz.all_pad, SLOTS, BF16)]
    outs += [shape(SLOTS, len(sz.cells) * PAD * PAD, BF16)] * sz.links
    body = functools.partial(sum_body, sz)
    return kernel_call(body, outs, [proj, cells], flops=3 * 10**9, limit=32 << 20)


def slot_keys(sz, table, dim):
    exact = lax.Precision.HIGHEST
    shape2 = (SLOTS, POS) if dim == 0 else (POS, SLOTS)
    i, s = iota(*shape2, dim), iota(*shape2, 1 - dim)
    spread = ((i >= s * PA) & (i < s * PA + PA)).astype(F32)
    if dim == 0:
        atoms = dot_last(spread, table, exact)
    else:
        atoms = jnp.dot(table, spread, precision=exact, preferred_element_type=F32)
    devices = sz.shifts + 1
    at = iota(*atoms.shape, 1 - dim)
    me = lax.axis_index("gz")
    keys = []
    for shift in range(devices):
        chosen = jnp.where(at == lax.rem(me + shift, devices), atoms, 0.0)
        atom = jnp.sum(chosen, axis=1 - dim, keepdims=True).astype(jnp.int32)
        i = iota(*atom.shape, dim)
        keys.append((atom, jnp.where(atom >= 0, atom * PA + i - twelfth(i) * PA, -1)))
    return keys


def turn_body(sz, qt, kin, pot, atoms, coupling, *refs):
    q, kout, vout, maps = refs[:4]
    back = refs[4] if sz.links else None
    c_hi, c_lo, wide = refs[-3:]
    q[...] = qt[...].T
    nodes = kin.shape[0]
    expand = (node_key(iota(sz.cell_pad, nodes, 0)) == iota(sz.cell_pad, nodes, 1)).astype(BF16)
    gather = (node_key(iota(nodes, sz.cell_pad, 1)) == iota(nodes, sz.cell_pad, 0)).astype(BF16)
    tall = dot(expand, kin[...]).astype(BF16)
    kout[...] = dot(tall, gather).astype(BF16)
    value, values = pot[...], 0.0
    for _ in range(3):
        part = value.astype(BF16)
        values = values + dot_last(expand, part)
        value = value - part.astype(F32)
    for g in range(len(sz.cells)):
        vout[g * sz.cell_pad : (g + 1) * sz.cell_pad, :] = jnp.broadcast_to(
            values[:, g : g + 1], (sz.cell_pad, sz.orb)
        )
    table = atoms[...].astype(F32)
    rows, cols = slot_keys(sz, table, 0), slot_keys(sz, table, 1)
    known = [jnp.where(cols[0][1] >= 0, cols[0][1], -2)]
    for j, shift in enumerate(link_shifts(sz)):
        key = jnp.where(cols[shift][1] >= 0, cols[shift][1], -2)
        valid = link_valid(sz, j)
        known.append(key if valid is None else jnp.where(valid == 1, key, -2))
    for s in range(sz.shifts):
        for j, key in enumerate(known):
            maps[s * SLOTS : (s + 1) * SLOTS, j * SLOTS : (j + 1) * SLOTS] = (
                rows[s + 1][1] == key
            ).astype(BF16)
    for j, key in enumerate(known[1:]):
        back[:, j * SLOTS : (j + 1) * SLOTS] = (rows[0][1] == key).astype(BF16)
    pa, pb, atom_count = coupling.shape
    wide[...] = jnp.zeros(wide.shape, F32)
    wide[:, :pb, :] = coupling[...]
    table2 = wide[...].reshape(pa * 16, atom_count)
    hot = (rows[0][0] == iota(SLOTS, atom_count, 1)).astype(BF16)
    i, lane = iota(SLOTS, pa * 16, 0), iota(SLOTS, pa * 16, 1)
    own_row = (lane >> 4) == i - twelfth(i) * PA
    lane, j = iota(pa * 16, SLOTS, 0), iota(pa * 16, SLOTS, 1)
    fold = ((lane & 15) == j - twelfth(j) * PA).astype(BF16)
    same = twelfth(iota(SLOTS, SLOTS, 0)) == twelfth(iota(SLOTS, SLOTS, 1))
    for out in (c_hi, c_lo):
        part = table2.astype(BF16)
        table2 = table2 - part.astype(F32)
        picked = jnp.where(own_row, dot_last(hot, part), 0.0).astype(BF16)
        out[...] = jnp.where(same, dot(picked, fold), 0.0).astype(BF16)


def turn_matrices(sz, qt, kin, pot, atoms, coupling):
    known = (1 + sz.links) * SLOTS
    outs = [
        shape(SLOTS, sz.all_pad, BF16),
        shape(sz.cell_pad, sz.cell_pad, BF16),
        shape(len(sz.cells) * sz.cell_pad, sz.orb, F32),
        shape(sz.shifts * SLOTS, known, BF16),
        shape(SLOTS, sz.links * SLOTS, BF16),
        shape(SLOTS, SLOTS, BF16),
        shape(SLOTS, SLOTS, BF16),
    ]
    limit = (32 << 20) if sz.shifts < 8 else (56 << 20)
    return kernel_call(
        functools.partial(turn_body, sz),
        outs,
        [qt, kin, pot, atoms, coupling],
        scratch=[pltpu.VMEM((coupling.shape[0], 16, coupling.shape[2]), F32)],
        flops=10**9,
        limit=limit,
    )


def cell_block(sz, z, cell):
    p, q = cell
    layers = []
    for a in range(EDGE):
        start = (ORDER * p + a) * sz.line_x + ORDER * q * PAD
        layers.append(z[start : start + EDGE * PAD, :])
    layers.append(jnp.zeros((sz.cell_pad - sz.cell_rows, sz.orb), F32))
    return jnp.concatenate(layers, axis=0)


def write_pair(axis, low, high, first, second):
    first[...] = by_parity(axis, low, high).astype(first.dtype)
    second[...] = by_parity(axis, high, low).astype(second.dtype)


def read_pair(axis, first, second):
    one, two = first[...].astype(F32), second[...].astype(F32)
    low, high = by_parity(axis, one, two), by_parity(axis, two, one)
    at, last = lax.axis_index(axis), lax.axis_size(axis) - 1
    return jnp.where(at > 0, low, 0.0), jnp.where(at < last, high, 0.0)


def write_faces(sz, r, sx_one, sx_two, sy_lo, sy_hi):
    pad_x = jnp.zeros((sz.xface - sz.line_x, sz.orb), F32)
    pad_y = jnp.zeros((sz.yface - sz.nx * PAD, sz.orb), F32)
    last = (sz.nx - 1) * sz.line_x
    low = jnp.concatenate([r[0 : sz.line_x, :], pad_x], axis=0)
    high = jnp.concatenate([r[last : last + sz.line_x, :], pad_x], axis=0)
    write_pair("gx", low, high, sx_one, sx_two)
    for out, b in ((sy_lo, 0), (sy_hi, sz.ny - 1)):
        rows = [r[a * sz.line_x + b * PAD : a * sz.line_x + (b + 1) * PAD, :] for a in range(sz.nx)]
        out[...] = jnp.concatenate(rows + [pad_y], axis=0)


def face_outs(sz):
    return [shape(sz.xface, sz.orb, HALO)] * 2 + [shape(sz.yface, sz.orb, F32)] * 2


def start_body(sz, parts, r, *faces):
    nz = parts.shape[2]
    r[...] = jnp.zeros(r.shape, F32)
    for a in range(sz.nx):
        for b in range(sz.ny):
            at = a * sz.line_x + b * PAD
            r[at : at + nz, :] = parts[a, b]
    write_faces(sz, r, *faces)


def start_faces(sz, parts, after):
    outs = [shape(sz.rows_all, sz.orb, F32)] + face_outs(sz)
    r, *faces = kernel_call(functools.partial(start_body, sz), outs, [parts], after=after)
    return r, faces


def cross_body(sz, xr_one, xr_two, ry_lo, ry_hi, sy_one, sy_two):
    last = (sz.nx - 1) * PAD
    lo, hi = read_pair("gx", xr_one, xr_two)
    faces = []
    for raw, b in ((ry_lo, 0), (ry_hi, sz.ny - 1)):
        value = raw[...]
        parts = [
            value[:PAD] + lo[b * PAD : (b + 1) * PAD],
            value[PAD:last],
            value[last : last + PAD] + hi[b * PAD : (b + 1) * PAD],
            value[last + PAD :],
        ]
        faces.append(jnp.concatenate(parts, axis=0))
    write_pair("gy", *faces, sy_one, sy_two)


def cross_faces(sz, *faces):
    outs = [shape(sz.yface, sz.orb, HALO)] * 2
    return kernel_call(functools.partial(cross_body, sz), outs, list(faces))


def add_xy(sz, ra, xr_one, xr_two, yr_one, yr_two):
    last = (sz.nx - 1) * sz.line_x
    low, high = read_pair("gx", xr_one, xr_two)
    ra[0 : sz.line_x, :] += low[: sz.line_x]
    ra[last : last + sz.line_x, :] += high[: sz.line_x]
    for value, b in zip(read_pair("gy", yr_one, yr_two), (0, sz.ny - 1)):
        for a in range(sz.nx):
            at = a * sz.line_x + b * PAD
            ra[at : at + PAD, :] += value[a * PAD : (a + 1) * PAD]


def local_term(weight, fields, at):
    value = weight * fields[0][at, :]
    return value - fields[1][at, :] if len(fields) > 1 else value


def layer_rows(y, weight, fields, at):
    rows = pl.ds(at, PAD, stride=PAD)
    return y[rows, :] - local_term(weight, fields, rows) if fields else y[rows, :]


def pack_z(sz, y, weight, fields, j):
    rows, c = [], layer_sent(sz, j)
    for a in range(sz.nx):
        for b in range(0, sz.face_b, PAD):
            rows.append(layer_rows(y, weight, fields, a * sz.line_x + b * PAD + c))
    rest = sz.zface - sz.nx * sz.face_b
    if rest:
        rows.append(jnp.zeros((rest, sz.orb), F32))
    value, valid = jnp.concatenate(rows, axis=0), link_valid(sz, j)
    return (value if valid is None else value * valid.astype(F32)).astype(HALO)


def add_z(sz, y, j, face):
    c = layer_received(sz, j)
    for a in range(sz.nx):
        for b in range(0, sz.ny, PAD):
            n = min(PAD, sz.ny - b)
            at = pl.ds(a * sz.line_x + b * PAD + c, n, stride=PAD)
            y[at, :] = y[at, :] + face[a * sz.face_b + b : a * sz.face_b + b + n]


def face_cells(sz, y, weight, fields, j):
    rows, c = [], layer_sent(sz, j)
    for p, q in sz.cells:
        for a in range(EDGE):
            at = (ORDER * p + a) * sz.line_x + ORDER * q * PAD
            rows.append(layer_rows(y, weight, fields, at + c))
        rows.append(jnp.zeros((PAD, sz.orb), F32))
    return jnp.concatenate(rows, axis=0).astype(BF16)


def project_body(sz, weight, past, refs):
    take = iter(refs)
    r = next(take)
    fields = [next(take) for _ in range(past)]
    halos = [next(take) for _ in range(4)]
    q = next(take)
    qfaces = [next(take) for _ in range(sz.links)]
    maps = next(take)
    y, own = next(take), next(take)
    beside = [next(take) for _ in range(sz.links)]
    messages = [next(take) for _ in range(sz.shifts)]
    everything = slice(0, sz.rows_all)
    y[...] = r[...] + local_term(weight, fields, everything) if past else r[...]
    add_xy(sz, y, *halos)
    blocks = [cell_block(sz, y, cell).astype(BF16) for cell in sz.cells]
    rest = sz.all_pad - sz.cell_pad * len(sz.cells)
    if rest:
        blocks.append(jnp.zeros((rest, sz.orb), BF16))
    sums = dot(q[...], jnp.concatenate(blocks, axis=0))
    own[...] = sums
    known = [sums.astype(BF16)]
    for j, matrix in enumerate(qfaces):
        value, valid = dot(matrix[...], face_cells(sz, y, weight, fields, j)), link_valid(sz, j)
        beside[j][...] = (value if valid is None else value * valid.astype(F32)).astype(BF16)
        known.append(beside[j][...])
    shift_of = link_shifts(sz)
    for s, message in enumerate(messages):
        rows = slice(s * SLOTS, (s + 1) * SLOTS)
        mapped = [0] + [j + 1 for j, shift in enumerate(shift_of) if shift != s + 1]
        direct = [j for j, shift in enumerate(shift_of) if shift == s + 1]
        total = sum(dot(maps[rows, k * SLOTS : (k + 1) * SLOTS], known[k]) for k in mapped)
        for j in direct:
            total = total + known[j + 1].astype(F32)
            message[SLOTS : SLOTS + sz.zface, :] = pack_z(sz, y, weight, fields, j)
        message[0:SLOTS, :] = total.astype(HALO)


def project(sz, r, weight, fields, halos, q, qfaces, maps):
    outs = [shape(sz.rows_all, sz.orb, F32), shape(SLOTS, sz.orb, F32)]
    outs += [shape(SLOTS, sz.orb, BF16)] * sz.links
    for s in range(1, sz.shifts + 1):
        outs.append(shape(SLOTS + (sz.zface if s in link_shifts(sz) else 0), sz.orb, HALO))

    def body(*refs):
        project_body(sz, weight, len(fields), refs)

    y, own, *rest = kernel_call(
        body,
        outs,
        [r, *fields, *halos, q, *qfaces, maps],
        flops=4 * 10**8,
        limit=(32 << 20) if sz.shifts < 8 else (56 << 20),
    )
    return y, [own, *rest[: sz.links]], rest[sz.links :]


def couple(c_hi, c_lo, totals):
    high = totals.astype(BF16)
    low = (totals - high.astype(F32)).astype(BF16)
    return dot(c_hi[...], high) + (dot(c_hi[...], low) + dot(c_lo[...], high))


def couple_body(sz, own, *refs):
    beside = refs[: sz.links]
    back, c_hi, c_lo, coupled = refs[sz.links :]
    totals = own[...]
    for j, part in enumerate(beside):
        totals = totals + dot(back[:, j * SLOTS : (j + 1) * SLOTS], part[...])
    coupled[...] = couple(c_hi, c_lo, totals)


def couple_own(sz, own, back, c_hi, c_lo):
    outs = [shape(SLOTS, sz.orb, F32)]
    body = functools.partial(couple_body, sz)
    return kernel_call(body, outs, [*own, back, c_hi, c_lo], flops=2 * 10**8)[0]


def apply_body(sz, scale, refs):
    take = iter(refs)
    yin, own = next(take), next(take)
    messages = [next(take) for _ in range(sz.shifts)]
    c_hi, c_lo, qt, kin, pot = [next(take) for _ in range(5)]
    r, y = next(take), next(take)
    faces = [next(take) for _ in range(4)]
    if len(messages) == 1:
        high = messages[0][0:SLOTS, :].astype(BF16)
        coef = own[...] + (dot(c_hi[...], high) + dot(c_lo[...], high))
    else:
        totals = sum(message[0:SLOTS, :].astype(F32) for message in messages)
        coef = own[...] + couple(c_hi, c_lo, totals)
    coef = coef.astype(BF16)
    y[...] = yin[...]
    for j, shift in enumerate(link_shifts(sz)):
        add_z(sz, y, j, messages[shift - 1][SLOTS : SLOTS + sz.zface, :].astype(F32))
    blocks = [cell_block(sz, y, cell) for cell in sz.cells]
    stiff = dot(kin[...], jnp.concatenate([b.astype(BF16) for b in blocks], axis=1))
    for g, (p, q) in enumerate(sz.cells):
        rows = slice(g * sz.cell_pad, (g + 1) * sz.cell_pad)
        value = stiff[:, g * sz.orb : (g + 1) * sz.orb] + pot[rows, :] * blocks[g]
        value = (value + dot(qt[rows, :], coef)) * scale
        for a in range(EDGE):
            start = (ORDER * p + a) * sz.line_x + ORDER * q * PAD
            line = value[a * EDGE * PAD : (a + 1) * EDGE * PAD]
            shared = EDGE * PAD if p and a == 0 else PAD if q else 0
            if shared:
                r[start : start + shared, :] += line[:shared]
            if shared < EDGE * PAD:
                r[start + shared : start + EDGE * PAD, :] = line[shared:]
    r[sz.rows :, :] = jnp.zeros((sz.rows_all - sz.rows, sz.orb), F32)
    write_faces(sz, r, *faces)


def apply(sz, y, own, messages, c_hi, c_lo, qt, kin, pot, scale):
    outs = [shape(sz.rows_all, sz.orb, F32)] * 2 + face_outs(sz)
    arrays = [y, own, *messages, c_hi, c_lo, qt, kin, pot]

    def body(*refs):
        apply_body(sz, scale, refs)

    r, y, *faces = kernel_call(body, outs, arrays, flops=6 * 10**8, limit=32 << 20)
    return r, y, faces


def last_faces_body(sz, refs):
    take = iter(refs)
    r = next(take)
    halos = [next(take) for _ in range(4)]
    ra = next(take)
    outs = [next(take) for _ in range(sz.links)]
    ra[...] = r[...]
    add_xy(sz, ra, *halos)
    for j, out in enumerate(outs):
        out[...] = pack_z(sz, ra, None, [], j)


def last_faces(sz, r, halos):
    def body(*refs):
        last_faces_body(sz, refs)

    outs = [shape(sz.rows_all, sz.orb, F32)] + [shape(sz.zface, sz.orb, HALO)] * sz.links
    ra, *sent = kernel_call(body, outs, [r, *halos])
    return ra, sent


def add_local_body(weight, past, r, *refs):
    fields, out = refs[:past], refs[past]
    out[...] = r[...] + local_term(weight, fields, slice(0, out.shape[0]))


def add_local(sz, r, weight, fields):
    body = functools.partial(add_local_body, weight, len(fields))
    return kernel_call(body, [shape(sz.rows_all, sz.orb, F32)], [r, *fields])[0]


def finish_body(sz, r, *refs):
    zr = refs[: sz.links]
    out, ra, block, sent = refs[sz.links :]
    ra[...] = r[...]
    for j, face in enumerate(zr):
        add_z(sz, ra, j, face[...].astype(F32))
    nz = block.shape[2]
    pieces, copies = 3, []
    for k in range(pieces):
        first, last = k * sz.nx // pieces, (k + 1) * sz.nx // pieces
        value = ra[first * sz.line_x : last * sz.line_x, :]
        value = value.reshape(last - first, sz.ny, PAD, sz.orb)[:, :, :nz, :]
        block[first:last] = value
        copy = pltpu.make_async_copy(block.at[first:last], out.at[first:last], sent.at[k])
        copy.start()
        copies.append(copy)
    for copy in copies:
        copy.wait()


def finish(sz, r, zr, nz):
    outs = [jax.ShapeDtypeStruct((sz.nx, sz.ny, nz, sz.orb), F32)]
    scratch = [
        pltpu.VMEM((sz.rows_all, sz.orb), F32),
        pltpu.VMEM((sz.nx, sz.ny, nz, sz.orb), F32),
        pltpu.SemaphoreType.DMA((3,)),
    ]
    body = functools.partial(finish_body, sz)
    anywhere = [pl.BlockSpec(memory_space=pl.ANY)]
    return kernel_call(body, outs, [r, *zr], scratch=scratch, out_specs=anywhere)[0]


def swap_faces(axis, one, two):
    axes = ("gx", "gy")
    wide, deep = lax.axis_size("gx"), lax.axis_size("gy")
    count = wide if axis == "gx" else deep

    def partner(i, j, low):
        at = i if axis == "gx" else j
        to = at + 1 if at % 2 == low else at - 1
        if 0 <= to < count:
            return (to, j) if axis == "gx" else (i, to)
        if axis == "gy" and wide % 2 == 0:
            return (i ^ 1, j)
        ends = sorted({k for k in range(count) if not 0 <= k + (1 if k % 2 == low else -1) < count})
        to = ends[::-1][ends.index(at)]
        return (to, j) if axis == "gx" else (i, to)

    out = []
    for face, low in ((one, 1), (two, 0)):
        pairs = []
        for i in range(wide):
            for j in range(deep):
                to = partner(i, j, low)
                pairs.append((i * deep + j, to[0] * deep + to[1]))
        out.append(lax.ppermute(face, axes, pairs))
    return out


def local(parts, cell_matrix, cell_potential, projectors, slot_atom, slot_cells, coupling):
    nx, ny, nz, orbitals = parts.shape
    nodes = cell_matrix.shape[0]
    devices = lax.axis_size("gz")
    sz = Sizes(nx, ny, nz, orbitals, devices - 1)
    ring = [[(i, (i + s) % devices) for i in range(devices)] for s in range(devices)]

    proj = projectors.reshape(nodes, POS * BLK * PA)
    proj = jnp.pad(proj, ((0, up(nodes, 16) - nodes), (0, 0)))
    cells = jnp.transpose(slot_cells.reshape(POS, BLK)).astype(F32)
    r, faces = start_faces(sz, parts, [cells, proj])

    def exchange_xy(sx_one, sx_two, sy_lo, sy_hi):
        xr = swap_faces("gx", sx_one, sx_two)
        cross = cross_faces(sz, *xr, sy_lo, sy_hi)
        yr = swap_faces("gy", *cross)
        return (*xr, *yr)

    halos = exchange_xy(*faces)
    qt, *face_rows = sum_matrices(sz, proj, cells)
    qfaces = []
    for j, shift in enumerate(link_shifts(sz)):
        back = [(target, source) for source, target in ring[shift]]
        qfaces.append(lax.ppermute(face_rows[j], "gz", back))
    pot = jnp.transpose(cell_potential, (1, 2, 3, 0)).reshape(len(sz.cells), nodes)
    q, kin, pot, maps, back, c_hi, c_lo = turn_matrices(
        sz,
        qt,
        cell_matrix,
        pot,
        slot_atom.reshape(devices, POS),
        jnp.transpose(coupling, (1, 2, 0)),
    )

    fields, scale = [], 1.0 / half_width
    weight = 0.0
    for step in range(STEPS):
        y, own, messages = project(sz, r, weight, fields, halos, q, qfaces, maps)
        received = [lax.ppermute(m, "gz", ring[s + 1]) for s, m in enumerate(messages)]
        own = couple_own(sz, own, back, c_hi, c_lo)
        r, y, faces = apply(sz, y, own, received, c_hi, c_lo, qt, kin, pot, scale)
        fields, weight = [y] + fields[:1], -center_value * scale
        scale = 2.0 / half_width
        halos = exchange_xy(*faces)
    r, sent = last_faces(sz, r, halos)
    zr = [lax.ppermute(f, "gz", ring[s]) for f, s in zip(sent, link_shifts(sz))]
    return finish(sz, add_local(sz, r, weight, fields), zr, nz)


def solution(mesh):
    in_specs = (
        P("gx", "gy", "gz", None),
        P(),
        P(None, "gx", "gy", "gz"),
        P("gx", "gy", "gz", None, None),
        P("gx", "gy", None, None),
        P("gx", "gy", "gz", None, None),
        P(("gx", "gy"), None, None),
    )
    out_specs = P("gx", "gy", "gz", None)
    return jax.shard_map(local, mesh=mesh, in_specs=in_specs, out_specs=out_specs, check_vma=False)
```

```python
import functools

import jax
import jax.numpy as jnp
import numpy as np
from jax import lax
from jax.experimental import pallas as pl
from jax.experimental.pallas import tpu as pltpu
from jax.sharding import PartitionSpec as P

ORDER = 6
STEPS = 3
PA = 12
POS = 32
BLK = 4

center_value = 2.0
half_width = 3.0

EDGE = ORDER + 1
PAD = 8
SLOTS = POS * PA
F32 = jnp.float32
BF16 = jnp.bfloat16
HALO = jnp.bfloat16


def up(value, multiple):
    return -(-value // multiple) * multiple


class Sizes:
    def __init__(self, nx, ny, nz, orbitals, shifts):
        assert nz == EDGE
        self.nx, self.ny, self.orb = nx, ny, orbitals
        self.cells = [(p, q) for p in range((nx - 1) // ORDER) for q in range((ny - 1) // ORDER)]
        self.rows = nx * ny * PAD
        self.line_x = ny * PAD
        self.xface = up(ny * PAD, 16)
        self.yface = up(nx * PAD, 16)
        self.face_b = up(ny, PAD)
        self.zface = up(nx * self.face_b, 16)
        self.cell_rows = EDGE * EDGE * PAD
        self.cell_pad = up(self.cell_rows, 16)
        self.all_pad = up(self.cell_pad * len(self.cells), 128)
        self.fcell = EDGE * PAD
        self.fall = up(self.fcell * len(self.cells), 256)
        self.shifts, self.links = shifts, min(2, shifts)
        self.rows_all = self.rows + (self.face_b - ny + 1) * PAD


VMEM = pl.BlockSpec(memory_space=pltpu.VMEM)


def kernel_call(body, outs, arrays, scratch=(), flops=0, limit=24 << 20, after=(), out_specs=None):
    used = len(arrays)

    def with_waits(*refs):
        body(*refs[:used], *refs[used + len(after) :])

    nbytes = sum(int(np.prod(a.shape)) * a.dtype.itemsize for a in list(arrays) + list(outs))
    return pl.pallas_call(
        with_waits,
        out_shape=outs,
        in_specs=[VMEM] * used + [pl.BlockSpec(memory_space=pl.ANY)] * len(after),
        out_specs=out_specs or [VMEM] * len(outs),
        scratch_shapes=list(scratch),
        compiler_params=pltpu.CompilerParams(vmem_limit_bytes=limit),
        cost_estimate=pl.CostEstimate(flops=flops, bytes_accessed=nbytes, transcendentals=0),
    )(*arrays, *after)


def shape(rows, cols, dtype):
    return jax.ShapeDtypeStruct((rows, cols), dtype)


def dot(a, b):
    return jnp.dot(a, b, preferred_element_type=F32)


def is_odd(axis):
    return lax.rem(lax.axis_index(axis), 2) == 1


def by_parity(axis, even, odd):
    return jnp.where(is_odd(axis), odd, even)


def link_shifts(sz):
    return [1, sz.shifts][: sz.links]


def layer_sent(sz, j):
    if sz.links == 1:
        return jnp.where(lax.axis_index("gz") == 0, ORDER, 0)
    return [ORDER, 0][j]


def layer_received(sz, j):
    return layer_sent(sz, 0) if sz.links == 1 else [0, ORDER][j]


def link_valid(sz, j):
    if sz.links == 1:
        return None
    me = lax.axis_index("gz")
    return jnp.where(me < sz.shifts, 1, 0) if j == 0 else jnp.where(me > 0, 1, 0)


def iota(rows, cols, dim):
    return lax.broadcasted_iota(jnp.int32, (rows, cols), dim)


def twelfth(value):
    return (value * (2**19 // PA + 1)) >> 19


def node_key(i):
    low = i & (PAD - 1)
    return jnp.where((low < EDGE) & (i < EDGE * EDGE * PAD), (i >> 3) * EDGE + low, -1)


def dot_last(a, b, precision=None):
    dims = (((1,), (1,)), ((), ()))
    return lax.dot_general(a, b, dims, precision=precision, preferred_element_type=F32)


def sum_body(sz, proj, cells, qt, *qt_faces):
    nodes, cols = proj.shape
    i = iota(cols, POS, 0)
    first = iota(cols, POS, 1) * (BLK * PA)
    in_slot = ((i >= first) & (i < first + BLK * PA)).astype(BF16)
    of_block = dot_last(in_slot, cells[...].astype(BF16))
    i = iota(cols, BLK, 0)
    block = twelfth(i)
    cell = jnp.sum(
        jnp.where((block & (BLK - 1)) == iota(cols, BLK, 1), of_block, 0.0), axis=1, keepdims=True
    )
    i, block = i[:, :1], block[:, :1]
    row = (block >> (BLK.bit_length() - 1)) * PA + (i - block * PA)
    halves, group, width = [], cols // 2, SLOTS // 2
    targets = len(sz.cells) * width
    for h in range(2):
        mine = slice(h * group, (h + 1) * group)
        key = cell[mine].astype(jnp.int32) * width + (row[mine] - h * width)
        pick = (key == iota(group, targets, 1)).astype(BF16)
        halves.append(dot(proj[:, mine], pick))
    parts = []
    for g in range(len(sz.cells)):
        parts += [half[:, g * width : (g + 1) * width] for half in halves]
    summed = jnp.concatenate(parts, axis=1).astype(BF16)
    keys = [node_key(iota(sz.cell_pad, nodes, 0))]
    for j in range(sz.links):
        keys.append(
            jnp.where(
                iota(PAD * PAD, nodes, 0) < sz.fcell,
                node_key(iota(PAD * PAD, nodes, 0)) * EDGE + layer_received(sz, j),
                -1,
            )
        )
        low = iota(PAD * PAD, nodes, 0) & (PAD - 1)
        keys[-1] = jnp.where(low < EDGE, keys[-1], -1)
    expand = (jnp.concatenate(keys, axis=0) == iota(sz.cell_pad + sz.links * PAD * PAD, nodes, 1))
    full = dot(expand.astype(BF16), summed)
    for g in range(len(sz.cells)):
        value = full[:, g * SLOTS : (g + 1) * SLOTS]
        qt[g * sz.cell_pad : (g + 1) * sz.cell_pad, :] = value[: sz.cell_pad].astype(BF16)
    rest = sz.all_pad - sz.cell_pad * len(sz.cells)
    if rest:
        qt[sz.cell_pad * len(sz.cells) :, :] = jnp.zeros((rest, SLOTS), BF16)
    for j, qf in enumerate(qt_faces):
        at = sz.cell_pad + j * PAD * PAD
        rows = [full[at : at + PAD * PAD, g * SLOTS : (g + 1) * SLOTS] for g in range(len(sz.cells))]
        qf[...] = jnp.concatenate(rows, axis=0).T.astype(BF16)


def sum_matrices(sz, proj, cells):
    outs = [shape(sz.all_pad, SLOTS, BF16)]
    outs += [shape(SLOTS, len(sz.cells) * PAD * PAD, BF16)] * sz.links
    body = functools.partial(sum_body, sz)
    return kernel_call(body, outs, [proj, cells], flops=3 * 10**9, limit=32 << 20)


def slot_keys(sz, table, dim):
    exact = lax.Precision.HIGHEST
    shape2 = (SLOTS, POS) if dim == 0 else (POS, SLOTS)
    i, s = iota(*shape2, dim), iota(*shape2, 1 - dim)
    spread = ((i >= s * PA) & (i < s * PA + PA)).astype(F32)
    if dim == 0:
        atoms = dot_last(spread, table, exact)
    else:
        atoms = jnp.dot(table, spread, precision=exact, preferred_element_type=F32)
    devices = sz.shifts + 1
    at = iota(*atoms.shape, 1 - dim)
    me = lax.axis_index("gz")
    keys = []
    for shift in range(devices):
        chosen = jnp.where(at == lax.rem(me + shift, devices), atoms, 0.0)
        atom = jnp.sum(chosen, axis=1 - dim, keepdims=True).astype(jnp.int32)
        i = iota(*atom.shape, dim)
        keys.append((atom, jnp.where(atom >= 0, atom * PA + i - twelfth(i) * PA, -1)))
    return keys


def turn_body(sz, qt, kin, pot, atoms, coupling, *refs):
    q, kout, vout, maps = refs[:4]
    back = refs[4] if sz.links else None
    c_hi, c_lo, wide = refs[-3:]
    q[...] = qt[...].T
    nodes = kin.shape[0]
    expand = (node_key(iota(sz.cell_pad, nodes, 0)) == iota(sz.cell_pad, nodes, 1)).astype(BF16)
    gather = (node_key(iota(nodes, sz.cell_pad, 1)) == iota(nodes, sz.cell_pad, 0)).astype(BF16)
    tall = dot(expand, kin[...]).astype(BF16)
    kout[...] = dot(tall, gather).astype(BF16)
    value, values = pot[...], 0.0
    for _ in range(3):
        part = value.astype(BF16)
        values = values + dot_last(expand, part)
        value = value - part.astype(F32)
    for g in range(len(sz.cells)):
        vout[g * sz.cell_pad : (g + 1) * sz.cell_pad, :] = jnp.broadcast_to(
            values[:, g : g + 1], (sz.cell_pad, sz.orb)
        )
    table = atoms[...].astype(F32)
    rows, cols = slot_keys(sz, table, 0), slot_keys(sz, table, 1)
    known = [jnp.where(cols[0][1] >= 0, cols[0][1], -2)]
    for j, shift in enumerate(link_shifts(sz)):
        key = jnp.where(cols[shift][1] >= 0, cols[shift][1], -2)
        valid = link_valid(sz, j)
        known.append(key if valid is None else jnp.where(valid == 1, key, -2))
    for s in range(sz.shifts):
        for j, key in enumerate(known):
            maps[s * SLOTS : (s + 1) * SLOTS, j * SLOTS : (j + 1) * SLOTS] = (
                rows[s + 1][1] == key
            ).astype(BF16)
    for j, key in enumerate(known[1:]):
        back[:, j * SLOTS : (j + 1) * SLOTS] = (rows[0][1] == key).astype(BF16)
    pa, pb, atom_count = coupling.shape
    wide[...] = jnp.zeros(wide.shape, F32)
    wide[:, :pb, :] = coupling[...]
    table2 = wide[...].reshape(pa * 16, atom_count)
    hot = (rows[0][0] == iota(SLOTS, atom_count, 1)).astype(BF16)
    i, lane = iota(SLOTS, pa * 16, 0), iota(SLOTS, pa * 16, 1)
    own_row = (lane >> 4) == i - twelfth(i) * PA
    lane, j = iota(pa * 16, SLOTS, 0), iota(pa * 16, SLOTS, 1)
    fold = ((lane & 15) == j - twelfth(j) * PA).astype(BF16)
    same = twelfth(iota(SLOTS, SLOTS, 0)) == twelfth(iota(SLOTS, SLOTS, 1))
    for out in (c_hi, c_lo):
        part = table2.astype(BF16)
        table2 = table2 - part.astype(F32)
        picked = jnp.where(own_row, dot_last(hot, part), 0.0).astype(BF16)
        out[...] = jnp.where(same, dot(picked, fold), 0.0).astype(BF16)


def turn_matrices(sz, qt, kin, pot, atoms, coupling):
    known = (1 + sz.links) * SLOTS
    outs = [
        shape(SLOTS, sz.all_pad, BF16),
        shape(sz.cell_pad, sz.cell_pad, BF16),
        shape(len(sz.cells) * sz.cell_pad, sz.orb, F32),
        shape(sz.shifts * SLOTS, known, BF16),
        shape(SLOTS, sz.links * SLOTS, BF16),
        shape(SLOTS, SLOTS, BF16),
        shape(SLOTS, SLOTS, BF16),
    ]
    limit = (32 << 20) if sz.shifts < 8 else (56 << 20)
    return kernel_call(
        functools.partial(turn_body, sz),
        outs,
        [qt, kin, pot, atoms, coupling],
        scratch=[pltpu.VMEM((coupling.shape[0], 16, coupling.shape[2]), F32)],
        flops=10**9,
        limit=limit,
    )


def cell_block(sz, z, cell):
    p, q = cell
    layers = []
    for a in range(EDGE):
        start = (ORDER * p + a) * sz.line_x + ORDER * q * PAD
        layers.append(z[start : start + EDGE * PAD, :])
    layers.append(jnp.zeros((sz.cell_pad - sz.cell_rows, sz.orb), F32))
    return jnp.concatenate(layers, axis=0)


def write_pair(axis, low, high, first, second):
    first[...] = by_parity(axis, low, high).astype(first.dtype)
    second[...] = by_parity(axis, high, low).astype(second.dtype)


def read_pair(axis, first, second):
    one, two = first[...].astype(F32), second[...].astype(F32)
    low, high = by_parity(axis, one, two), by_parity(axis, two, one)
    at, last = lax.axis_index(axis), lax.axis_size(axis) - 1
    return jnp.where(at > 0, low, 0.0), jnp.where(at < last, high, 0.0)


def write_faces(sz, r, sx_one, sx_two, sy_lo, sy_hi):
    pad_x = jnp.zeros((sz.xface - sz.line_x, sz.orb), F32)
    pad_y = jnp.zeros((sz.yface - sz.nx * PAD, sz.orb), F32)
    last = (sz.nx - 1) * sz.line_x
    low = jnp.concatenate([r[0 : sz.line_x, :], pad_x], axis=0)
    high = jnp.concatenate([r[last : last + sz.line_x, :], pad_x], axis=0)
    write_pair("gx", low, high, sx_one, sx_two)
    for out, b in ((sy_lo, 0), (sy_hi, sz.ny - 1)):
        rows = [r[a * sz.line_x + b * PAD : a * sz.line_x + (b + 1) * PAD, :] for a in range(sz.nx)]
        out[...] = jnp.concatenate(rows + [pad_y], axis=0)


def face_outs(sz):
    return [shape(sz.xface, sz.orb, HALO)] * 2 + [shape(sz.yface, sz.orb, F32)] * 2


def start_body(sz, parts, r, *faces):
    nz = parts.shape[2]
    r[...] = jnp.zeros(r.shape, F32)
    for a in range(sz.nx):
        for b in range(sz.ny):
            at = a * sz.line_x + b * PAD
            r[at : at + nz, :] = parts[a, b]
    write_faces(sz, r, *faces)


def start_faces(sz, parts, after):
    outs = [shape(sz.rows_all, sz.orb, F32)] + face_outs(sz)
    r, *faces = kernel_call(functools.partial(start_body, sz), outs, [parts], after=after)
    return r, faces


def cross_body(sz, xr_one, xr_two, ry_lo, ry_hi, sy_one, sy_two):
    last = (sz.nx - 1) * PAD
    lo, hi = read_pair("gx", xr_one, xr_two)
    faces = []
    for raw, b in ((ry_lo, 0), (ry_hi, sz.ny - 1)):
        value = raw[...]
        parts = [
            value[:PAD] + lo[b * PAD : (b + 1) * PAD],
            value[PAD:last],
            value[last : last + PAD] + hi[b * PAD : (b + 1) * PAD],
            value[last + PAD :],
        ]
        faces.append(jnp.concatenate(parts, axis=0))
    write_pair("gy", *faces, sy_one, sy_two)


def cross_faces(sz, *faces):
    outs = [shape(sz.yface, sz.orb, HALO)] * 2
    return kernel_call(functools.partial(cross_body, sz), outs, list(faces))


def add_xy(sz, ra, xr_one, xr_two, yr_one, yr_two):
    last = (sz.nx - 1) * sz.line_x
    low, high = read_pair("gx", xr_one, xr_two)
    ra[0 : sz.line_x, :] += low[: sz.line_x]
    ra[last : last + sz.line_x, :] += high[: sz.line_x]
    for value, b in zip(read_pair("gy", yr_one, yr_two), (0, sz.ny - 1)):
        for a in range(sz.nx):
            at = a * sz.line_x + b * PAD
            ra[at : at + PAD, :] += value[a * PAD : (a + 1) * PAD]


def local_term(weight, fields, at):
    value = weight * fields[0][at, :]
    return value - fields[1][at, :] if len(fields) > 1 else value


def layer_rows(y, weight, fields, at):
    rows = pl.ds(at, PAD, stride=PAD)
    return y[rows, :] - local_term(weight, fields, rows) if fields else y[rows, :]


def pack_z(sz, y, weight, fields, j):
    rows, c = [], layer_sent(sz, j)
    for a in range(sz.nx):
        for b in range(0, sz.face_b, PAD):
            rows.append(layer_rows(y, weight, fields, a * sz.line_x + b * PAD + c))
    rest = sz.zface - sz.nx * sz.face_b
    if rest:
        rows.append(jnp.zeros((rest, sz.orb), F32))
    value, valid = jnp.concatenate(rows, axis=0), link_valid(sz, j)
    return (value if valid is None else value * valid.astype(F32)).astype(HALO)


def add_z(sz, y, j, face):
    c = layer_received(sz, j)
    for a in range(sz.nx):
        for b in range(0, sz.ny, PAD):
            n = min(PAD, sz.ny - b)
            at = pl.ds(a * sz.line_x + b * PAD + c, n, stride=PAD)
            y[at, :] = y[at, :] + face[a * sz.face_b + b : a * sz.face_b + b + n]


def face_cells(sz, y, weight, fields, j):
    rows, c = [], layer_sent(sz, j)
    for p, q in sz.cells:
        for a in range(EDGE):
            at = (ORDER * p + a) * sz.line_x + ORDER * q * PAD
            rows.append(layer_rows(y, weight, fields, at + c))
        rows.append(jnp.zeros((PAD, sz.orb), F32))
    return jnp.concatenate(rows, axis=0).astype(BF16)


def project_body(sz, weight, past, refs):
    take = iter(refs)
    r = next(take)
    fields = [next(take) for _ in range(past)]
    halos = [next(take) for _ in range(4)]
    q = next(take)
    qfaces = [next(take) for _ in range(sz.links)]
    maps = next(take)
    y, own = next(take), next(take)
    beside = [next(take) for _ in range(sz.links)]
    messages = [next(take) for _ in range(sz.shifts)]
    everything = slice(0, sz.rows_all)
    y[...] = r[...] + local_term(weight, fields, everything) if past else r[...]
    add_xy(sz, y, *halos)
    blocks = [cell_block(sz, y, cell).astype(BF16) for cell in sz.cells]
    rest = sz.all_pad - sz.cell_pad * len(sz.cells)
    if rest:
        blocks.append(jnp.zeros((rest, sz.orb), BF16))
    sums = dot(q[...], jnp.concatenate(blocks, axis=0))
    own[...] = sums
    known = [sums.astype(BF16)]
    for j, matrix in enumerate(qfaces):
        value, valid = dot(matrix[...], face_cells(sz, y, weight, fields, j)), link_valid(sz, j)
        beside[j][...] = (value if valid is None else value * valid.astype(F32)).astype(BF16)
        known.append(beside[j][...])
    shift_of = link_shifts(sz)
    for s, message in enumerate(messages):
        rows = slice(s * SLOTS, (s + 1) * SLOTS)
        mapped = [0] + [j + 1 for j, shift in enumerate(shift_of) if shift != s + 1]
        direct = [j for j, shift in enumerate(shift_of) if shift == s + 1]
        total = sum(dot(maps[rows, k * SLOTS : (k + 1) * SLOTS], known[k]) for k in mapped)
        for j in direct:
            total = total + known[j + 1].astype(F32)
            message[SLOTS : SLOTS + sz.zface, :] = pack_z(sz, y, weight, fields, j)
        message[0:SLOTS, :] = total.astype(HALO)


def project(sz, r, weight, fields, halos, q, qfaces, maps):
    outs = [shape(sz.rows_all, sz.orb, F32), shape(SLOTS, sz.orb, F32)]
    outs += [shape(SLOTS, sz.orb, BF16)] * sz.links
    for s in range(1, sz.shifts + 1):
        outs.append(shape(SLOTS + (sz.zface if s in link_shifts(sz) else 0), sz.orb, HALO))

    def body(*refs):
        project_body(sz, weight, len(fields), refs)

    y, own, *rest = kernel_call(
        body,
        outs,
        [r, *fields, *halos, q, *qfaces, maps],
        flops=4 * 10**8,
        limit=(32 << 20) if sz.shifts < 8 else (56 << 20),
    )
    return y, [own, *rest[: sz.links]], rest[sz.links :]


def couple(c_hi, c_lo, totals):
    high = totals.astype(BF16)
    low = (totals - high.astype(F32)).astype(BF16)
    return dot(c_hi[...], high) + (dot(c_hi[...], low) + dot(c_lo[...], high))


def couple_body(sz, own, *refs):
    beside = refs[: sz.links]
    back, c_hi, c_lo, coupled = refs[sz.links :]
    totals = own[...]
    for j, part in enumerate(beside):
        totals = totals + dot(back[:, j * SLOTS : (j + 1) * SLOTS], part[...])
    coupled[...] = couple(c_hi, c_lo, totals)


def couple_own(sz, own, back, c_hi, c_lo):
    outs = [shape(SLOTS, sz.orb, F32)]
    body = functools.partial(couple_body, sz)
    return kernel_call(body, outs, [*own, back, c_hi, c_lo], flops=2 * 10**8)[0]


def apply_body(sz, scale, refs):
    take = iter(refs)
    yin, own = next(take), next(take)
    messages = [next(take) for _ in range(sz.shifts)]
    c_hi, c_lo, qt, kin, pot = [next(take) for _ in range(5)]
    r, y = next(take), next(take)
    faces = [next(take) for _ in range(4)]
    if len(messages) == 1:
        high = messages[0][0:SLOTS, :].astype(BF16)
        coef = own[...] + (dot(c_hi[...], high) + dot(c_lo[...], high))
    else:
        totals = sum(message[0:SLOTS, :].astype(F32) for message in messages)
        coef = own[...] + couple(c_hi, c_lo, totals)
    coef = coef.astype(BF16)
    y[...] = yin[...]
    for j, shift in enumerate(link_shifts(sz)):
        add_z(sz, y, j, messages[shift - 1][SLOTS : SLOTS + sz.zface, :].astype(F32))
    blocks = [cell_block(sz, y, cell) for cell in sz.cells]
    stiff = dot(kin[...], jnp.concatenate([b.astype(BF16) for b in blocks], axis=1))
    for g, (p, q) in enumerate(sz.cells):
        rows = slice(g * sz.cell_pad, (g + 1) * sz.cell_pad)
        value = stiff[:, g * sz.orb : (g + 1) * sz.orb] + pot[rows, :] * blocks[g]
        value = (value + dot(qt[rows, :], coef)) * scale
        for a in range(EDGE):
            start = (ORDER * p + a) * sz.line_x + ORDER * q * PAD
            line = value[a * EDGE * PAD : (a + 1) * EDGE * PAD]
            shared = EDGE * PAD if p and a == 0 else PAD if q else 0
            if shared:
                r[start : start + shared, :] += line[:shared]
            if shared < EDGE * PAD:
                r[start + shared : start + EDGE * PAD, :] = line[shared:]
    r[sz.rows :, :] = jnp.zeros((sz.rows_all - sz.rows, sz.orb), F32)
    write_faces(sz, r, *faces)


def apply(sz, y, own, messages, c_hi, c_lo, qt, kin, pot, scale):
    outs = [shape(sz.rows_all, sz.orb, F32)] * 2 + face_outs(sz)
    arrays = [y, own, *messages, c_hi, c_lo, qt, kin, pot]

    def body(*refs):
        apply_body(sz, scale, refs)

    r, y, *faces = kernel_call(body, outs, arrays, flops=6 * 10**8, limit=32 << 20)
    return r, y, faces


def last_faces_body(sz, refs):
    take = iter(refs)
    r = next(take)
    halos = [next(take) for _ in range(4)]
    ra = next(take)
    outs = [next(take) for _ in range(sz.links)]
    ra[...] = r[...]
    add_xy(sz, ra, *halos)
    for j, out in enumerate(outs):
        out[...] = pack_z(sz, ra, None, [], j)


def last_faces(sz, r, halos):
    def body(*refs):
        last_faces_body(sz, refs)

    outs = [shape(sz.rows_all, sz.orb, F32)] + [shape(sz.zface, sz.orb, HALO)] * sz.links
    ra, *sent = kernel_call(body, outs, [r, *halos])
    return ra, sent


def add_local_body(weight, past, r, *refs):
    fields, out = refs[:past], refs[past]
    out[...] = r[...] + local_term(weight, fields, slice(0, out.shape[0]))


def add_local(sz, r, weight, fields):
    body = functools.partial(add_local_body, weight, len(fields))
    return kernel_call(body, [shape(sz.rows_all, sz.orb, F32)], [r, *fields])[0]


def finish_body(sz, r, *refs):
    zr = refs[: sz.links]
    out, ra, block, sent = refs[sz.links :]
    ra[...] = r[...]
    for j, face in enumerate(zr):
        add_z(sz, ra, j, face[...].astype(F32))
    nz = block.shape[2]
    pieces, copies = 3, []
    for k in range(pieces):
        first, last = k * sz.nx // pieces, (k + 1) * sz.nx // pieces
        value = ra[first * sz.line_x : last * sz.line_x, :]
        value = value.reshape(last - first, sz.ny, PAD, sz.orb)[:, :, :nz, :]
        block[first:last] = value
        copy = pltpu.make_async_copy(block.at[first:last], out.at[first:last], sent.at[k])
        copy.start()
        copies.append(copy)
    for copy in copies:
        copy.wait()


def finish(sz, r, zr, nz):
    outs = [jax.ShapeDtypeStruct((sz.nx, sz.ny, nz, sz.orb), F32)]
    scratch = [
        pltpu.VMEM((sz.rows_all, sz.orb), F32),
        pltpu.VMEM((sz.nx, sz.ny, nz, sz.orb), F32),
        pltpu.SemaphoreType.DMA((3,)),
    ]
    body = functools.partial(finish_body, sz)
    anywhere = [pl.BlockSpec(memory_space=pl.ANY)]
    return kernel_call(body, outs, [r, *zr], scratch=scratch, out_specs=anywhere)[0]


def swap_faces(axis, one, two):
    axes = ("gx", "gy")
    wide, deep = lax.axis_size("gx"), lax.axis_size("gy")
    count = wide if axis == "gx" else deep

    def partner(i, j, low):
        at = i if axis == "gx" else j
        to = at + 1 if at % 2 == low else at - 1
        if 0 <= to < count:
            return (to, j) if axis == "gx" else (i, to)
        if axis == "gy" and wide % 2 == 0:
            return (i ^ 1, j)
        ends = sorted({k for k in range(count) if not 0 <= k + (1 if k % 2 == low else -1) < count})
        to = ends[::-1][ends.index(at)]
        return (to, j) if axis == "gx" else (i, to)

    out = []
    for face, low in ((one, 1), (two, 0)):
        pairs = []
        for i in range(wide):
            for j in range(deep):
                to = partner(i, j, low)
                pairs.append((i * deep + j, to[0] * deep + to[1]))
        out.append(lax.ppermute(face, axes, pairs))
    return out


def local(parts, cell_matrix, cell_potential, projectors, slot_atom, slot_cells, coupling):
    nx, ny, nz, orbitals = parts.shape
    nodes = cell_matrix.shape[0]
    devices = lax.axis_size("gz")
    sz = Sizes(nx, ny, nz, orbitals, devices - 1)
    ring = [[(i, (i + s) % devices) for i in range(devices)] for s in range(devices)]

    proj = projectors.reshape(nodes, POS * BLK * PA)
    proj = jnp.pad(proj, ((0, up(nodes, 16) - nodes), (0, 0)))
    cells = jnp.transpose(slot_cells.reshape(POS, BLK)).astype(F32)
    r, faces = start_faces(sz, parts, [cells, proj])

    def exchange_xy(sx_one, sx_two, sy_lo, sy_hi):
        xr = swap_faces("gx", sx_one, sx_two)
        cross = cross_faces(sz, *xr, sy_lo, sy_hi)
        yr = swap_faces("gy", *cross)
        return (*xr, *yr)

    halos = exchange_xy(*faces)
    qt, *face_rows = sum_matrices(sz, proj, cells)
    qfaces = []
    for j, shift in enumerate(link_shifts(sz)):
        back = [(target, source) for source, target in ring[shift]]
        qfaces.append(lax.ppermute(face_rows[j], "gz", back))
    pot = jnp.transpose(cell_potential, (1, 2, 3, 0)).reshape(len(sz.cells), nodes)
    q, kin, pot, maps, back, c_hi, c_lo = turn_matrices(
        sz,
        qt,
        cell_matrix,
        pot,
        slot_atom.reshape(devices, POS),
        jnp.transpose(coupling, (1, 2, 0)),
    )

    fields, scale = [], 1.0 / half_width
    weight = 0.0
    for step in range(STEPS):
        y, own, messages = project(sz, r, weight, fields, halos, q, qfaces, maps)
        received = [lax.ppermute(m, "gz", ring[s + 1]) for s, m in enumerate(messages)]
        own = couple_own(sz, own, back, c_hi, c_lo)
        r, y, faces = apply(sz, y, own, received, c_hi, c_lo, qt, kin, pot, scale)
        fields, weight = [y] + fields[:1], -center_value * scale
        scale = 2.0 / half_width
        halos = exchange_xy(*faces)
    r, sent = last_faces(sz, r, halos)
    zr = [lax.ppermute(f, "gz", ring[s]) for f, s in zip(sent, link_shifts(sz))]
    return finish(sz, add_local(sz, r, weight, fields), zr, nz)


def solution(mesh):
    in_specs = (
        P("gx", "gy", "gz", None),
        P(),
        P(None, "gx", "gy", "gz"),
        P("gx", "gy", "gz", None, None),
        P("gx", "gy", None, None),
        P("gx", "gy", "gz", None, None),
        P(("gx", "gy"), None, None),
    )
    out_specs = P("gx", "gy", "gz", None)
    return jax.shard_map(local, mesh=mesh, in_specs=in_specs, out_specs=out_specs, check_vma=False)
```

```python
import functools

import jax
import jax.numpy as jnp
import numpy as np
from jax import lax
from jax.experimental import pallas as pl
from jax.experimental.pallas import tpu as pltpu
from jax.sharding import PartitionSpec as P

ORDER = 6
STEPS = 3
PA = 12
POS = 32
BLK = 4

center_value = 2.0
half_width = 3.0

EDGE = ORDER + 1
PAD = 8
SLOTS = POS * PA
F32 = jnp.float32
BF16 = jnp.bfloat16
HALO = jnp.bfloat16


def up(value, multiple):
    return -(-value // multiple) * multiple


class Sizes:
    def __init__(self, nx, ny, nz, orbitals, shifts):
        assert nz == EDGE
        self.nx, self.ny, self.orb = nx, ny, orbitals
        self.cells = [(p, q) for p in range((nx - 1) // ORDER) for q in range((ny - 1) // ORDER)]
        self.rows = nx * ny * PAD
        self.line_x = ny * PAD
        self.xface = up(ny * PAD, 16)
        self.yface = up(nx * PAD, 16)
        self.face_b = up(ny, PAD)
        self.zface = up(nx * self.face_b, 16)
        self.cell_rows = EDGE * EDGE * PAD
        self.cell_pad = up(self.cell_rows, 16)
        self.all_pad = up(self.cell_pad * len(self.cells), 128)
        self.fcell = EDGE * PAD
        self.fall = up(self.fcell * len(self.cells), 256)
        self.shifts, self.links = shifts, min(2, shifts)
        self.rows_all = self.rows + (self.face_b - ny + 1) * PAD


VMEM = pl.BlockSpec(memory_space=pltpu.VMEM)


def kernel_call(body, outs, arrays, scratch=(), flops=0, limit=24 << 20, after=(), out_specs=None):
    used = len(arrays)

    def with_waits(*refs):
        body(*refs[:used], *refs[used + len(after) :])

    nbytes = sum(int(np.prod(a.shape)) * a.dtype.itemsize for a in list(arrays) + list(outs))
    return pl.pallas_call(
        with_waits,
        out_shape=outs,
        in_specs=[VMEM] * used + [pl.BlockSpec(memory_space=pl.ANY)] * len(after),
        out_specs=out_specs or [VMEM] * len(outs),
        scratch_shapes=list(scratch),
        compiler_params=pltpu.CompilerParams(vmem_limit_bytes=limit),
        cost_estimate=pl.CostEstimate(flops=flops, bytes_accessed=nbytes, transcendentals=0),
    )(*arrays, *after)


def shape(rows, cols, dtype):
    return jax.ShapeDtypeStruct((rows, cols), dtype)


def dot(a, b):
    return jnp.dot(a, b, preferred_element_type=F32)


FIRST = {"gx": 1, "gy": 0}


def if_first(axis, value, otherwise):
    return jnp.where(lax.rem(lax.axis_index(axis), 2) == FIRST[axis], value, otherwise)


def link_shifts(sz):
    return [1, sz.shifts][: sz.links]


def layer_sent(sz, j):
    if sz.links == 1:
        return jnp.where(lax.axis_index("gz") == 0, ORDER, 0)
    return [ORDER, 0][j]


def layer_received(sz, j):
    return layer_sent(sz, 0) if sz.links == 1 else [0, ORDER][j]


def link_valid(sz, j):
    if sz.links == 1:
        return None
    me = lax.axis_index("gz")
    return jnp.where(me < sz.shifts, 1, 0) if j == 0 else jnp.where(me > 0, 1, 0)


def iota(rows, cols, dim):
    return lax.broadcasted_iota(jnp.int32, (rows, cols), dim)


def twelfth(value):
    return (value * (2**19 // PA + 1)) >> 19


def node_key(i):
    low = i & (PAD - 1)
    return jnp.where((low < EDGE) & (i < EDGE * EDGE * PAD), (i >> 3) * EDGE + low, -1)


def dot_last(a, b, precision=None):
    dims = (((1,), (1,)), ((), ()))
    return lax.dot_general(a, b, dims, precision=precision, preferred_element_type=F32)


def sum_body(sz, proj, cells, qt, *qt_faces):
    nodes, cols = proj.shape
    i = iota(cols, POS, 0)
    first = iota(cols, POS, 1) * (BLK * PA)
    in_slot = ((i >= first) & (i < first + BLK * PA)).astype(BF16)
    of_block = dot_last(in_slot, cells[...].astype(BF16))
    i = iota(cols, BLK, 0)
    block = twelfth(i)
    cell = jnp.sum(
        jnp.where((block & (BLK - 1)) == iota(cols, BLK, 1), of_block, 0.0), axis=1, keepdims=True
    )
    i, block = i[:, :1], block[:, :1]
    row = (block >> (BLK.bit_length() - 1)) * PA + (i - block * PA)
    halves, group, width = [], cols // 2, SLOTS // 2
    targets = len(sz.cells) * width
    for h in range(2):
        mine = slice(h * group, (h + 1) * group)
        key = cell[mine].astype(jnp.int32) * width + (row[mine] - h * width)
        pick = (key == iota(group, targets, 1)).astype(BF16)
        halves.append(dot(proj[:, mine], pick))
    parts = []
    for g in range(len(sz.cells)):
        parts += [half[:, g * width : (g + 1) * width] for half in halves]
    summed = jnp.concatenate(parts, axis=1).astype(BF16)
    keys = [node_key(iota(sz.cell_pad, nodes, 0))]
    for j in range(sz.links):
        keys.append(
            jnp.where(
                iota(PAD * PAD, nodes, 0) < sz.fcell,
                node_key(iota(PAD * PAD, nodes, 0)) * EDGE + layer_received(sz, j),
                -1,
            )
        )
        low = iota(PAD * PAD, nodes, 0) & (PAD - 1)
        keys[-1] = jnp.where(low < EDGE, keys[-1], -1)
    expand = (jnp.concatenate(keys, axis=0) == iota(sz.cell_pad + sz.links * PAD * PAD, nodes, 1))
    full = dot(expand.astype(BF16), summed)
    for g in range(len(sz.cells)):
        value = full[:, g * SLOTS : (g + 1) * SLOTS]
        qt[g * sz.cell_pad : (g + 1) * sz.cell_pad, :] = value[: sz.cell_pad].astype(BF16)
    rest = sz.all_pad - sz.cell_pad * len(sz.cells)
    if rest:
        qt[sz.cell_pad * len(sz.cells) :, :] = jnp.zeros((rest, SLOTS), BF16)
    for j, qf in enumerate(qt_faces):
        at = sz.cell_pad + j * PAD * PAD
        rows = [full[at : at + PAD * PAD, g * SLOTS : (g + 1) * SLOTS] for g in range(len(sz.cells))]
        qf[...] = jnp.concatenate(rows, axis=0).T.astype(BF16)


def sum_matrices(sz, proj, cells):
    outs = [shape(sz.all_pad, SLOTS, BF16)]
    outs += [shape(SLOTS, len(sz.cells) * PAD * PAD, BF16)] * sz.links
    body = functools.partial(sum_body, sz)
    return kernel_call(body, outs, [proj, cells], flops=3 * 10**9, limit=32 << 20)


def slot_keys(sz, table, dim):
    exact = lax.Precision.HIGHEST
    shape2 = (SLOTS, POS) if dim == 0 else (POS, SLOTS)
    i, s = iota(*shape2, dim), iota(*shape2, 1 - dim)
    spread = ((i >= s * PA) & (i < s * PA + PA)).astype(F32)
    if dim == 0:
        atoms = dot_last(spread, table, exact)
    else:
        atoms = jnp.dot(table, spread, precision=exact, preferred_element_type=F32)
    devices = sz.shifts + 1
    at = iota(*atoms.shape, 1 - dim)
    me = lax.axis_index("gz")
    keys = []
    for shift in range(devices):
        chosen = jnp.where(at == lax.rem(me + shift, devices), atoms, 0.0)
        atom = jnp.sum(chosen, axis=1 - dim, keepdims=True).astype(jnp.int32)
        i = iota(*atom.shape, dim)
        keys.append((atom, jnp.where(atom >= 0, atom * PA + i - twelfth(i) * PA, -1)))
    return keys


def turn_body(sz, qt, kin, pot, atoms, coupling, *refs):
    q, kout, vout, maps = refs[:4]
    back = refs[4] if sz.links else None
    c_hi, c_lo, wide = refs[-3:]
    q[...] = qt[...].T
    nodes = kin.shape[0]
    expand = (node_key(iota(sz.cell_pad, nodes, 0)) == iota(sz.cell_pad, nodes, 1)).astype(BF16)
    gather = (node_key(iota(nodes, sz.cell_pad, 1)) == iota(nodes, sz.cell_pad, 0)).astype(BF16)
    tall = dot(expand, kin[...]).astype(BF16)
    kout[...] = dot(tall, gather).astype(BF16)
    value, values = pot[...], 0.0
    for _ in range(3):
        part = value.astype(BF16)
        values = values + dot_last(expand, part)
        value = value - part.astype(F32)
    for g in range(len(sz.cells)):
        vout[g * sz.cell_pad : (g + 1) * sz.cell_pad, :] = jnp.broadcast_to(
            values[:, g : g + 1], (sz.cell_pad, sz.orb)
        )
    table = atoms[...].astype(F32)
    rows, cols = slot_keys(sz, table, 0), slot_keys(sz, table, 1)
    known = [jnp.where(cols[0][1] >= 0, cols[0][1], -2)]
    for j, shift in enumerate(link_shifts(sz)):
        key = jnp.where(cols[shift][1] >= 0, cols[shift][1], -2)
        valid = link_valid(sz, j)
        known.append(key if valid is None else jnp.where(valid == 1, key, -2))
    for s in range(sz.shifts):
        for j, key in enumerate(known):
            maps[s * SLOTS : (s + 1) * SLOTS, j * SLOTS : (j + 1) * SLOTS] = (
                rows[s + 1][1] == key
            ).astype(BF16)
    for j, key in enumerate(known[1:]):
        back[:, j * SLOTS : (j + 1) * SLOTS] = (rows[0][1] == key).astype(BF16)
    pa, pb, atom_count = coupling.shape
    wide[...] = jnp.zeros(wide.shape, F32)
    wide[:, :pb, :] = coupling[...]
    table2 = wide[...].reshape(pa * 16, atom_count)
    hot = (rows[0][0] == iota(SLOTS, atom_count, 1)).astype(BF16)
    i, lane = iota(SLOTS, pa * 16, 0), iota(SLOTS, pa * 16, 1)
    own_row = (lane >> 4) == i - twelfth(i) * PA
    lane, j = iota(pa * 16, SLOTS, 0), iota(pa * 16, SLOTS, 1)
    fold = ((lane & 15) == j - twelfth(j) * PA).astype(BF16)
    same = twelfth(iota(SLOTS, SLOTS, 0)) == twelfth(iota(SLOTS, SLOTS, 1))
    for out in (c_hi, c_lo):
        part = table2.astype(BF16)
        table2 = table2 - part.astype(F32)
        picked = jnp.where(own_row, dot_last(hot, part), 0.0).astype(BF16)
        out[...] = jnp.where(same, dot(picked, fold), 0.0).astype(BF16)


def turn_matrices(sz, qt, kin, pot, atoms, coupling):
    known = (1 + sz.links) * SLOTS
    outs = [
        shape(SLOTS, sz.all_pad, BF16),
        shape(sz.cell_pad, sz.cell_pad, BF16),
        shape(len(sz.cells) * sz.cell_pad, sz.orb, F32),
        shape(sz.shifts * SLOTS, known, BF16),
        shape(SLOTS, sz.links * SLOTS, BF16),
        shape(SLOTS, SLOTS, BF16),
        shape(SLOTS, SLOTS, BF16),
    ]
    limit = (32 << 20) if sz.shifts < 8 else (56 << 20)
    return kernel_call(
        functools.partial(turn_body, sz),
        outs,
        [qt, kin, pot, atoms, coupling],
        scratch=[pltpu.VMEM((coupling.shape[0], 16, coupling.shape[2]), F32)],
        flops=10**9,
        limit=limit,
    )


def cell_block(sz, z, cell):
    p, q = cell
    layers = []
    for a in range(EDGE):
        start = (ORDER * p + a) * sz.line_x + ORDER * q * PAD
        layers.append(z[start : start + EDGE * PAD, :])
    layers.append(jnp.zeros((sz.cell_pad - sz.cell_rows, sz.orb), F32))
    return jnp.concatenate(layers, axis=0)


def write_pair(axis, low, high, first, second):
    first[...] = if_first(axis, high, low).astype(first.dtype)
    second[...] = if_first(axis, low, high).astype(second.dtype)


def read_pair(axis, first, second):
    one, two = first[...].astype(F32), second[...].astype(F32)
    low, high = if_first(axis, two, one), if_first(axis, one, two)
    at, last = lax.axis_index(axis), lax.axis_size(axis) - 1
    return jnp.where(at > 0, low, 0.0), jnp.where(at < last, high, 0.0)


def write_faces(sz, r, sx_one, sx_two, sy_lo, sy_hi):
    pad_x = jnp.zeros((sz.xface - sz.line_x, sz.orb), F32)
    pad_y = jnp.zeros((sz.yface - sz.nx * PAD, sz.orb), F32)
    last = (sz.nx - 1) * sz.line_x
    low = jnp.concatenate([r[0 : sz.line_x, :], pad_x], axis=0)
    high = jnp.concatenate([r[last : last + sz.line_x, :], pad_x], axis=0)
    write_pair("gx", low, high, sx_one, sx_two)
    for out, b in ((sy_lo, 0), (sy_hi, sz.ny - 1)):
        rows = [r[a * sz.line_x + b * PAD : a * sz.line_x + (b + 1) * PAD, :] for a in range(sz.nx)]
        out[...] = jnp.concatenate(rows + [pad_y], axis=0)


def face_outs(sz):
    return [shape(sz.xface, sz.orb, HALO)] * 2 + [shape(sz.yface, sz.orb, F32)] * 2


def start_body(sz, parts, r, *faces):
    nz = parts.shape[2]
    r[...] = jnp.zeros(r.shape, F32)
    for a in range(sz.nx):
        for b in range(sz.ny):
            at = a * sz.line_x + b * PAD
            r[at : at + nz, :] = parts[a, b]
    write_faces(sz, r, *faces)


def start_faces(sz, parts, after):
    outs = [shape(sz.rows_all, sz.orb, F32)] + face_outs(sz)
    r, *faces = kernel_call(functools.partial(start_body, sz), outs, [parts], after=after)
    return r, faces


def cross_body(sz, xr_one, xr_two, ry_lo, ry_hi, sy_one, sy_two):
    last = (sz.nx - 1) * PAD
    lo, hi = read_pair("gx", xr_one, xr_two)
    faces = []
    for raw, b in ((ry_lo, 0), (ry_hi, sz.ny - 1)):
        value = raw[...]
        parts = [
            value[:PAD] + lo[b * PAD : (b + 1) * PAD],
            value[PAD:last],
            value[last : last + PAD] + hi[b * PAD : (b + 1) * PAD],
            value[last + PAD :],
        ]
        faces.append(jnp.concatenate(parts, axis=0))
    write_pair("gy", *faces, sy_one, sy_two)


def cross_faces(sz, *faces):
    outs = [shape(sz.yface, sz.orb, HALO)] * 2
    return kernel_call(functools.partial(cross_body, sz), outs, list(faces))


def add_xy(sz, ra, xr_one, xr_two, yr_one, yr_two):
    last = (sz.nx - 1) * sz.line_x
    low, high = read_pair("gx", xr_one, xr_two)
    ra[0 : sz.line_x, :] += low[: sz.line_x]
    ra[last : last + sz.line_x, :] += high[: sz.line_x]
    for value, b in zip(read_pair("gy", yr_one, yr_two), (0, sz.ny - 1)):
        for a in range(sz.nx):
            at = a * sz.line_x + b * PAD
            ra[at : at + PAD, :] += value[a * PAD : (a + 1) * PAD]


def local_term(weight, fields, at):
    value = weight * fields[0][at, :]
    return value - fields[1][at, :] if len(fields) > 1 else value


def layer_rows(y, weight, fields, at):
    rows = pl.ds(at, PAD, stride=PAD)
    return y[rows, :] - local_term(weight, fields, rows) if fields else y[rows, :]


def pack_z(sz, y, weight, fields, j):
    rows, c = [], layer_sent(sz, j)
    for a in range(sz.nx):
        for b in range(0, sz.face_b, PAD):
            rows.append(layer_rows(y, weight, fields, a * sz.line_x + b * PAD + c))
    rest = sz.zface - sz.nx * sz.face_b
    if rest:
        rows.append(jnp.zeros((rest, sz.orb), F32))
    value, valid = jnp.concatenate(rows, axis=0), link_valid(sz, j)
    return (value if valid is None else value * valid.astype(F32)).astype(HALO)


def add_z(sz, y, j, face):
    c = layer_received(sz, j)
    for a in range(sz.nx):
        for b in range(0, sz.ny, PAD):
            n = min(PAD, sz.ny - b)
            at = pl.ds(a * sz.line_x + b * PAD + c, n, stride=PAD)
            y[at, :] = y[at, :] + face[a * sz.face_b + b : a * sz.face_b + b + n]


def face_cells(sz, y, weight, fields, j):
    rows, c = [], layer_sent(sz, j)
    for p, q in sz.cells:
        for a in range(EDGE):
            at = (ORDER * p + a) * sz.line_x + ORDER * q * PAD
            rows.append(layer_rows(y, weight, fields, at + c))
        rows.append(jnp.zeros((PAD, sz.orb), F32))
    return jnp.concatenate(rows, axis=0).astype(BF16)


def project_body(sz, weight, past, refs):
    take = iter(refs)
    r = next(take)
    fields = [next(take) for _ in range(past)]
    halos = [next(take) for _ in range(4)]
    q = next(take)
    qfaces = [next(take) for _ in range(sz.links)]
    maps = next(take)
    y, own = next(take), next(take)
    beside = [next(take) for _ in range(sz.links)]
    messages = [next(take) for _ in range(sz.shifts)]
    everything = slice(0, sz.rows_all)
    y[...] = r[...] + local_term(weight, fields, everything) if past else r[...]
    add_xy(sz, y, *halos)
    blocks = [cell_block(sz, y, cell).astype(BF16) for cell in sz.cells]
    rest = sz.all_pad - sz.cell_pad * len(sz.cells)
    if rest:
        blocks.append(jnp.zeros((rest, sz.orb), BF16))
    sums = dot(q[...], jnp.concatenate(blocks, axis=0))
    own[...] = sums
    known = [sums.astype(BF16)]
    for j, matrix in enumerate(qfaces):
        value, valid = dot(matrix[...], face_cells(sz, y, weight, fields, j)), link_valid(sz, j)
        beside[j][...] = (value if valid is None else value * valid.astype(F32)).astype(BF16)
        known.append(beside[j][...])
    shift_of = link_shifts(sz)
    for s, message in enumerate(messages):
        rows = slice(s * SLOTS, (s + 1) * SLOTS)
        mapped = [0] + [j + 1 for j, shift in enumerate(shift_of) if shift != s + 1]
        direct = [j for j, shift in enumerate(shift_of) if shift == s + 1]
        total = sum(dot(maps[rows, k * SLOTS : (k + 1) * SLOTS], known[k]) for k in mapped)
        for j in direct:
            total = total + known[j + 1].astype(F32)
            message[SLOTS : SLOTS + sz.zface, :] = pack_z(sz, y, weight, fields, j)
        message[0:SLOTS, :] = total.astype(HALO)


def project(sz, r, weight, fields, halos, q, qfaces, maps):
    outs = [shape(sz.rows_all, sz.orb, F32), shape(SLOTS, sz.orb, F32)]
    outs += [shape(SLOTS, sz.orb, BF16)] * sz.links
    for s in range(1, sz.shifts + 1):
        outs.append(shape(SLOTS + (sz.zface if s in link_shifts(sz) else 0), sz.orb, HALO))

    def body(*refs):
        project_body(sz, weight, len(fields), refs)

    y, own, *rest = kernel_call(
        body,
        outs,
        [r, *fields, *halos, q, *qfaces, maps],
        flops=4 * 10**8,
        limit=(32 << 20) if sz.shifts < 8 else (56 << 20),
    )
    return y, [own, *rest[: sz.links]], rest[sz.links :]


def couple(c_hi, c_lo, totals):
    high = totals.astype(BF16)
    low = (totals - high.astype(F32)).astype(BF16)
    return dot(c_hi[...], high) + (dot(c_hi[...], low) + dot(c_lo[...], high))


def couple_body(sz, own, *refs):
    beside = refs[: sz.links]
    back, c_hi, c_lo, coupled = refs[sz.links :]
    totals = own[...]
    for j, part in enumerate(beside):
        totals = totals + dot(back[:, j * SLOTS : (j + 1) * SLOTS], part[...])
    coupled[...] = couple(c_hi, c_lo, totals)


def couple_own(sz, own, back, c_hi, c_lo):
    outs = [shape(SLOTS, sz.orb, F32)]
    body = functools.partial(couple_body, sz)
    return kernel_call(body, outs, [*own, back, c_hi, c_lo], flops=2 * 10**8)[0]


def apply_body(sz, scale, refs):
    take = iter(refs)
    yin, own = next(take), next(take)
    messages = [next(take) for _ in range(sz.shifts)]
    c_hi, c_lo, qt, kin, pot = [next(take) for _ in range(5)]
    r, y = next(take), next(take)
    faces = [next(take) for _ in range(4)]
    if len(messages) == 1:
        high = messages[0][0:SLOTS, :].astype(BF16)
        coef = own[...] + (dot(c_hi[...], high) + dot(c_lo[...], high))
    else:
        totals = sum(message[0:SLOTS, :].astype(F32) for message in messages)
        coef = own[...] + couple(c_hi, c_lo, totals)
    coef = coef.astype(BF16)
    y[...] = yin[...]
    for j, shift in enumerate(link_shifts(sz)):
        add_z(sz, y, j, messages[shift - 1][SLOTS : SLOTS + sz.zface, :].astype(F32))
    blocks = [cell_block(sz, y, cell) for cell in sz.cells]
    stiff = dot(kin[...], jnp.concatenate([b.astype(BF16) for b in blocks], axis=1))
    for g, (p, q) in enumerate(sz.cells):
        rows = slice(g * sz.cell_pad, (g + 1) * sz.cell_pad)
        value = stiff[:, g * sz.orb : (g + 1) * sz.orb] + pot[rows, :] * blocks[g]
        value = (value + dot(qt[rows, :], coef)) * scale
        for a in range(EDGE):
            start = (ORDER * p + a) * sz.line_x + ORDER * q * PAD
            line = value[a * EDGE * PAD : (a + 1) * EDGE * PAD]
            shared = EDGE * PAD if p and a == 0 else PAD if q else 0
            if shared:
                r[start : start + shared, :] += line[:shared]
            if shared < EDGE * PAD:
                r[start + shared : start + EDGE * PAD, :] = line[shared:]
    r[sz.rows :, :] = jnp.zeros((sz.rows_all - sz.rows, sz.orb), F32)
    write_faces(sz, r, *faces)


def apply(sz, y, own, messages, c_hi, c_lo, qt, kin, pot, scale):
    outs = [shape(sz.rows_all, sz.orb, F32)] * 2 + face_outs(sz)
    arrays = [y, own, *messages, c_hi, c_lo, qt, kin, pot]

    def body(*refs):
        apply_body(sz, scale, refs)

    r, y, *faces = kernel_call(body, outs, arrays, flops=6 * 10**8, limit=32 << 20)
    return r, y, faces


def last_faces_body(sz, refs):
    take = iter(refs)
    r = next(take)
    halos = [next(take) for _ in range(4)]
    ra = next(take)
    outs = [next(take) for _ in range(sz.links)]
    ra[...] = r[...]
    add_xy(sz, ra, *halos)
    for j, out in enumerate(outs):
        out[...] = pack_z(sz, ra, None, [], j)


def last_faces(sz, r, halos):
    def body(*refs):
        last_faces_body(sz, refs)

    outs = [shape(sz.rows_all, sz.orb, F32)] + [shape(sz.zface, sz.orb, HALO)] * sz.links
    ra, *sent = kernel_call(body, outs, [r, *halos])
    return ra, sent


def add_local_body(weight, past, r, *refs):
    fields, out = refs[:past], refs[past]
    out[...] = r[...] + local_term(weight, fields, slice(0, out.shape[0]))


def add_local(sz, r, weight, fields):
    body = functools.partial(add_local_body, weight, len(fields))
    return kernel_call(body, [shape(sz.rows_all, sz.orb, F32)], [r, *fields])[0]


def finish_body(sz, r, *refs):
    zr = refs[: sz.links]
    out, ra, block, sent = refs[sz.links :]
    ra[...] = r[...]
    for j, face in enumerate(zr):
        add_z(sz, ra, j, face[...].astype(F32))
    nz = block.shape[2]
    pieces, copies = 3, []
    for k in range(pieces):
        first, last = k * sz.nx // pieces, (k + 1) * sz.nx // pieces
        value = ra[first * sz.line_x : last * sz.line_x, :]
        value = value.reshape(last - first, sz.ny, PAD, sz.orb)[:, :, :nz, :]
        block[first:last] = value
        copy = pltpu.make_async_copy(block.at[first:last], out.at[first:last], sent.at[k])
        copy.start()
        copies.append(copy)
    for copy in copies:
        copy.wait()


def finish(sz, r, zr, nz):
    outs = [jax.ShapeDtypeStruct((sz.nx, sz.ny, nz, sz.orb), F32)]
    scratch = [
        pltpu.VMEM((sz.rows_all, sz.orb), F32),
        pltpu.VMEM((sz.nx, sz.ny, nz, sz.orb), F32),
        pltpu.SemaphoreType.DMA((3,)),
    ]
    body = functools.partial(finish_body, sz)
    anywhere = [pl.BlockSpec(memory_space=pl.ANY)]
    return kernel_call(body, outs, [r, *zr], scratch=scratch, out_specs=anywhere)[0]


def swap_faces(axis, one, two):
    axes = ("gx", "gy")
    wide, deep = lax.axis_size("gx"), lax.axis_size("gy")
    count = wide if axis == "gx" else deep

    def partner(i, j, low):
        at = i if axis == "gx" else j
        to = at + 1 if at % 2 == low else at - 1
        if 0 <= to < count:
            return (to, j) if axis == "gx" else (i, to)
        if axis == "gy" and wide % 2 == 0:
            return (i ^ 1, j)
        ends = sorted({k for k in range(count) if not 0 <= k + (1 if k % 2 == low else -1) < count})
        to = ends[::-1][ends.index(at)]
        return (to, j) if axis == "gx" else (i, to)

    out = []
    for face, low in ((one, FIRST[axis]), (two, 1 - FIRST[axis])):
        pairs = []
        for i in range(wide):
            for j in range(deep):
                to = partner(i, j, low)
                pairs.append((i * deep + j, to[0] * deep + to[1]))
        out.append(lax.ppermute(face, axes, pairs))
    return out


def local(parts, cell_matrix, cell_potential, projectors, slot_atom, slot_cells, coupling):
    nx, ny, nz, orbitals = parts.shape
    nodes = cell_matrix.shape[0]
    devices = lax.axis_size("gz")
    sz = Sizes(nx, ny, nz, orbitals, devices - 1)
    ring = [[(i, (i + s) % devices) for i in range(devices)] for s in range(devices)]

    proj = projectors.reshape(nodes, POS * BLK * PA)
    proj = jnp.pad(proj, ((0, up(nodes, 16) - nodes), (0, 0)))
    cells = jnp.transpose(slot_cells.reshape(POS, BLK)).astype(F32)
    r, faces = start_faces(sz, parts, [cells, proj])

    def exchange_xy(sx_one, sx_two, sy_lo, sy_hi):
        xr = swap_faces("gx", sx_one, sx_two)
        cross = cross_faces(sz, *xr, sy_lo, sy_hi)
        yr = swap_faces("gy", *cross)
        return (*xr, *yr)

    halos = exchange_xy(*faces)
    qt, *face_rows = sum_matrices(sz, proj, cells)
    qfaces = []
    for j, shift in enumerate(link_shifts(sz)):
        back = [(target, source) for source, target in ring[shift]]
        qfaces.append(lax.ppermute(face_rows[j], "gz", back))
    pot = jnp.transpose(cell_potential, (1, 2, 3, 0)).reshape(len(sz.cells), nodes)
    q, kin, pot, maps, back, c_hi, c_lo = turn_matrices(
        sz,
        qt,
        cell_matrix,
        pot,
        slot_atom.reshape(devices, POS),
        jnp.transpose(coupling, (1, 2, 0)),
    )

    fields, scale = [], 1.0 / half_width
    weight = 0.0
    for step in range(STEPS):
        y, own, messages = project(sz, r, weight, fields, halos, q, qfaces, maps)
        received = [lax.ppermute(m, "gz", ring[s + 1]) for s, m in enumerate(messages)]
        own = couple_own(sz, own, back, c_hi, c_lo)
        r, y, faces = apply(sz, y, own, received, c_hi, c_lo, qt, kin, pot, scale)
        fields, weight = [y] + fields[:1], -center_value * scale
        scale = 2.0 / half_width
        halos = exchange_xy(*faces)
    r, sent = last_faces(sz, r, halos)
    zr = [lax.ppermute(f, "gz", ring[s]) for f, s in zip(sent, link_shifts(sz))]
    return finish(sz, add_local(sz, r, weight, fields), zr, nz)


def solution(mesh):
    in_specs = (
        P("gx", "gy", "gz", None),
        P(),
        P(None, "gx", "gy", "gz"),
        P("gx", "gy", "gz", None, None),
        P("gx", "gy", None, None),
        P("gx", "gy", "gz", None, None),
        P(("gx", "gy"), None, None),
    )
    out_specs = P("gx", "gy", "gz", None)
    return jax.shard_map(local, mesh=mesh, in_specs=in_specs, out_specs=out_specs, check_vma=False)
```

```python
import functools

import jax
import jax.numpy as jnp
import numpy as np
from jax import lax
from jax.experimental import pallas as pl
from jax.experimental.pallas import tpu as pltpu
from jax.sharding import PartitionSpec as P

ORDER = 6
STEPS = 3
PA = 12
POS = 32
BLK = 4

center_value = 2.0
half_width = 3.0

EDGE = ORDER + 1
PAD = 8
SLOTS = POS * PA
F32 = jnp.float32
BF16 = jnp.bfloat16
HALO = jnp.bfloat16


def up(value, multiple):
    return -(-value // multiple) * multiple


class Sizes:
    def __init__(self, nx, ny, nz, orbitals, shifts):
        assert nz == EDGE
        self.nx, self.ny, self.orb = nx, ny, orbitals
        self.cells = [(p, q) for p in range((nx - 1) // ORDER) for q in range((ny - 1) // ORDER)]
        self.rows = nx * ny * PAD
        self.line_x = ny * PAD
        self.xface = up(ny * PAD, 16)
        self.yface = up(nx * PAD, 16)
        self.face_b = up(ny, PAD)
        self.zface = up(nx * self.face_b, 16)
        self.cell_rows = EDGE * EDGE * PAD
        self.cell_pad = up(self.cell_rows, 16)
        self.all_pad = up(self.cell_pad * len(self.cells), 128)
        self.fcell = EDGE * PAD
        self.fall = up(self.fcell * len(self.cells), 256)
        self.shifts, self.links = shifts, min(2, shifts)
        self.rows_all = self.rows + (self.face_b - ny + 1) * PAD


VMEM = pl.BlockSpec(memory_space=pltpu.VMEM)


def kernel_call(body, outs, arrays, scratch=(), flops=0, limit=24 << 20, after=(), out_specs=None):
    used = len(arrays)

    def with_waits(*refs):
        body(*refs[:used], *refs[used + len(after) :])

    nbytes = sum(int(np.prod(a.shape)) * a.dtype.itemsize for a in list(arrays) + list(outs))
    return pl.pallas_call(
        with_waits,
        out_shape=outs,
        in_specs=[VMEM] * used + [pl.BlockSpec(memory_space=pl.ANY)] * len(after),
        out_specs=out_specs or [VMEM] * len(outs),
        scratch_shapes=list(scratch),
        compiler_params=pltpu.CompilerParams(vmem_limit_bytes=limit),
        cost_estimate=pl.CostEstimate(flops=flops, bytes_accessed=nbytes, transcendentals=0),
    )(*arrays, *after)


def shape(rows, cols, dtype):
    return jax.ShapeDtypeStruct((rows, cols), dtype)


def dot(a, b):
    return jnp.dot(a, b, preferred_element_type=F32)


FIRST = {"gx": 1, "gy": 0}


def if_first(axis, value, otherwise):
    return jnp.where(lax.rem(lax.axis_index(axis), 2) == FIRST[axis], value, otherwise)


def link_shifts(sz):
    return [1, sz.shifts][: sz.links]


def layer_sent(sz, j):
    if sz.links == 1:
        return jnp.where(lax.axis_index("gz") == 0, ORDER, 0)
    return [ORDER, 0][j]


def layer_received(sz, j):
    return layer_sent(sz, 0) if sz.links == 1 else [0, ORDER][j]


def link_valid(sz, j):
    if sz.links == 1:
        return None
    me = lax.axis_index("gz")
    return jnp.where(me < sz.shifts, 1, 0) if j == 0 else jnp.where(me > 0, 1, 0)


def iota(rows, cols, dim):
    return lax.broadcasted_iota(jnp.int32, (rows, cols), dim)


def twelfth(value):
    return (value * (2**19 // PA + 1)) >> 19


def node_key(i):
    low = i & (PAD - 1)
    return jnp.where((low < EDGE) & (i < EDGE * EDGE * PAD), (i >> 3) * EDGE + low, -1)


def dot_last(a, b, precision=None):
    dims = (((1,), (1,)), ((), ()))
    return lax.dot_general(a, b, dims, precision=precision, preferred_element_type=F32)


def sum_body(sz, proj, cells, qt, *qt_faces):
    nodes, cols = proj.shape
    i = iota(cols, POS, 0)
    first = iota(cols, POS, 1) * (BLK * PA)
    in_slot = ((i >= first) & (i < first + BLK * PA)).astype(BF16)
    of_block = dot_last(in_slot, cells[...].astype(BF16))
    i = iota(cols, BLK, 0)
    block = twelfth(i)
    cell = jnp.sum(
        jnp.where((block & (BLK - 1)) == iota(cols, BLK, 1), of_block, 0.0), axis=1, keepdims=True
    )
    i, block = i[:, :1], block[:, :1]
    row = (block >> (BLK.bit_length() - 1)) * PA + (i - block * PA)
    halves, group, width = [], cols // 2, SLOTS // 2
    targets = len(sz.cells) * width
    for h in range(2):
        mine = slice(h * group, (h + 1) * group)
        key = cell[mine].astype(jnp.int32) * width + (row[mine] - h * width)
        pick = (key == iota(group, targets, 1)).astype(BF16)
        halves.append(dot(proj[:, mine], pick))
    parts = []
    for g in range(len(sz.cells)):
        parts += [half[:, g * width : (g + 1) * width] for half in halves]
    summed = jnp.concatenate(parts, axis=1).astype(BF16)
    keys = [node_key(iota(sz.cell_pad, nodes, 0))]
    for j in range(sz.links):
        keys.append(
            jnp.where(
                iota(PAD * PAD, nodes, 0) < sz.fcell,
                node_key(iota(PAD * PAD, nodes, 0)) * EDGE + layer_received(sz, j),
                -1,
            )
        )
        low = iota(PAD * PAD, nodes, 0) & (PAD - 1)
        keys[-1] = jnp.where(low < EDGE, keys[-1], -1)
    expand = (jnp.concatenate(keys, axis=0) == iota(sz.cell_pad + sz.links * PAD * PAD, nodes, 1))
    full = dot(expand.astype(BF16), summed)
    for g in range(len(sz.cells)):
        value = full[:, g * SLOTS : (g + 1) * SLOTS]
        qt[g * sz.cell_pad : (g + 1) * sz.cell_pad, :] = value[: sz.cell_pad].astype(BF16)
    rest = sz.all_pad - sz.cell_pad * len(sz.cells)
    if rest:
        qt[sz.cell_pad * len(sz.cells) :, :] = jnp.zeros((rest, SLOTS), BF16)
    for j, qf in enumerate(qt_faces):
        at = sz.cell_pad + j * PAD * PAD
        rows = [full[at : at + PAD * PAD, g * SLOTS : (g + 1) * SLOTS] for g in range(len(sz.cells))]
        qf[...] = jnp.concatenate(rows, axis=0).T.astype(BF16)


def sum_matrices(sz, proj, cells):
    outs = [shape(sz.all_pad, SLOTS, BF16)]
    outs += [shape(SLOTS, len(sz.cells) * PAD * PAD, BF16)] * sz.links
    body = functools.partial(sum_body, sz)
    return kernel_call(body, outs, [proj, cells], flops=3 * 10**9, limit=32 << 20)


def slot_keys(sz, table, dim):
    exact = lax.Precision.HIGHEST
    shape2 = (SLOTS, POS) if dim == 0 else (POS, SLOTS)
    i, s = iota(*shape2, dim), iota(*shape2, 1 - dim)
    spread = ((i >= s * PA) & (i < s * PA + PA)).astype(F32)
    if dim == 0:
        atoms = dot_last(spread, table, exact)
    else:
        atoms = jnp.dot(table, spread, precision=exact, preferred_element_type=F32)
    devices = sz.shifts + 1
    at = iota(*atoms.shape, 1 - dim)
    me = lax.axis_index("gz")
    keys = []
    for shift in range(devices):
        chosen = jnp.where(at == lax.rem(me + shift, devices), atoms, 0.0)
        atom = jnp.sum(chosen, axis=1 - dim, keepdims=True).astype(jnp.int32)
        i = iota(*atom.shape, dim)
        keys.append((atom, jnp.where(atom >= 0, atom * PA + i - twelfth(i) * PA, -1)))
    return keys


def turn_body(sz, qt, kin, pot, atoms, coupling, *refs):
    q, kout, vout, maps = refs[:4]
    back = refs[4] if sz.links else None
    c_hi, c_lo, wide = refs[-3:]
    q[...] = qt[...].T
    nodes = kin.shape[0]
    expand = (node_key(iota(sz.cell_pad, nodes, 0)) == iota(sz.cell_pad, nodes, 1)).astype(BF16)
    gather = (node_key(iota(nodes, sz.cell_pad, 1)) == iota(nodes, sz.cell_pad, 0)).astype(BF16)
    tall = dot(expand, kin[...]).astype(BF16)
    kout[...] = dot(tall, gather).astype(BF16)
    value, values = pot[...], 0.0
    for _ in range(3):
        part = value.astype(BF16)
        values = values + dot_last(expand, part)
        value = value - part.astype(F32)
    for g in range(len(sz.cells)):
        vout[g * sz.cell_pad : (g + 1) * sz.cell_pad, :] = jnp.broadcast_to(
            values[:, g : g + 1], (sz.cell_pad, sz.orb)
        )
    table = atoms[...].astype(F32)
    rows, cols = slot_keys(sz, table, 0), slot_keys(sz, table, 1)
    known = [jnp.where(cols[0][1] >= 0, cols[0][1], -2)]
    for j, shift in enumerate(link_shifts(sz)):
        key = jnp.where(cols[shift][1] >= 0, cols[shift][1], -2)
        valid = link_valid(sz, j)
        known.append(key if valid is None else jnp.where(valid == 1, key, -2))
    for s in range(sz.shifts):
        for j, key in enumerate(known):
            maps[s * SLOTS : (s + 1) * SLOTS, j * SLOTS : (j + 1) * SLOTS] = (
                rows[s + 1][1] == key
            ).astype(BF16)
    for j, key in enumerate(known[1:]):
        back[:, j * SLOTS : (j + 1) * SLOTS] = (rows[0][1] == key).astype(BF16)
    pa, pb, atom_count = coupling.shape
    wide[...] = jnp.zeros(wide.shape, F32)
    wide[:, :pb, :] = coupling[...]
    table2 = wide[...].reshape(pa * 16, atom_count)
    hot = (rows[0][0] == iota(SLOTS, atom_count, 1)).astype(BF16)
    i, lane = iota(SLOTS, pa * 16, 0), iota(SLOTS, pa * 16, 1)
    own_row = (lane >> 4) == i - twelfth(i) * PA
    lane, j = iota(pa * 16, SLOTS, 0), iota(pa * 16, SLOTS, 1)
    fold = ((lane & 15) == j - twelfth(j) * PA).astype(BF16)
    same = twelfth(iota(SLOTS, SLOTS, 0)) == twelfth(iota(SLOTS, SLOTS, 1))
    for out in (c_hi, c_lo):
        part = table2.astype(BF16)
        table2 = table2 - part.astype(F32)
        picked = jnp.where(own_row, dot_last(hot, part), 0.0).astype(BF16)
        out[...] = jnp.where(same, dot(picked, fold), 0.0).astype(BF16)


def turn_matrices(sz, qt, kin, pot, atoms, coupling):
    known = (1 + sz.links) * SLOTS
    outs = [
        shape(SLOTS, sz.all_pad, BF16),
        shape(sz.cell_pad, sz.cell_pad, BF16),
        shape(len(sz.cells) * sz.cell_pad, sz.orb, F32),
        shape(sz.shifts * SLOTS, known, BF16),
        shape(SLOTS, sz.links * SLOTS, BF16),
        shape(SLOTS, SLOTS, BF16),
        shape(SLOTS, SLOTS, BF16),
    ]
    limit = (32 << 20) if sz.shifts < 8 else (56 << 20)
    return kernel_call(
        functools.partial(turn_body, sz),
        outs,
        [qt, kin, pot, atoms, coupling],
        scratch=[pltpu.VMEM((coupling.shape[0], 16, coupling.shape[2]), F32)],
        flops=10**9,
        limit=limit,
    )


def cell_block(sz, z, cell):
    p, q = cell
    layers = []
    for a in range(EDGE):
        start = (ORDER * p + a) * sz.line_x + ORDER * q * PAD
        layers.append(z[start : start + EDGE * PAD, :])
    layers.append(jnp.zeros((sz.cell_pad - sz.cell_rows, sz.orb), F32))
    return jnp.concatenate(layers, axis=0)


def write_pair(axis, low, high, first, second):
    first[...] = if_first(axis, high, low).astype(first.dtype)
    second[...] = if_first(axis, low, high).astype(second.dtype)


def read_pair(axis, first, second):
    one, two = first[...].astype(F32), second[...].astype(F32)
    low, high = if_first(axis, two, one), if_first(axis, one, two)
    at, last = lax.axis_index(axis), lax.axis_size(axis) - 1
    return jnp.where(at > 0, low, 0.0), jnp.where(at < last, high, 0.0)


def write_faces(sz, r, sx_one, sx_two, sy_lo, sy_hi):
    pad_x = jnp.zeros((sz.xface - sz.line_x, sz.orb), F32)
    pad_y = jnp.zeros((sz.yface - sz.nx * PAD, sz.orb), F32)
    last = (sz.nx - 1) * sz.line_x
    low = jnp.concatenate([r[0 : sz.line_x, :], pad_x], axis=0)
    high = jnp.concatenate([r[last : last + sz.line_x, :], pad_x], axis=0)
    write_pair("gx", low, high, sx_one, sx_two)
    for out, b in ((sy_lo, 0), (sy_hi, sz.ny - 1)):
        rows = [r[a * sz.line_x + b * PAD : a * sz.line_x + (b + 1) * PAD, :] for a in range(sz.nx)]
        out[...] = jnp.concatenate(rows + [pad_y], axis=0)


def face_outs(sz):
    return [shape(sz.xface, sz.orb, HALO)] * 2 + [shape(sz.yface, sz.orb, F32)] * 2


def start_body(sz, parts, cells, r, cells_out, *faces):
    cells_out[...] = cells[...].astype(F32)
    nz = parts.shape[2]
    r[...] = jnp.zeros(r.shape, F32)
    for a in range(sz.nx):
        for b in range(sz.ny):
            at = a * sz.line_x + b * PAD
            r[at : at + nz, :] = parts[a, b]
    write_faces(sz, r, *faces)


def start_faces(sz, parts, cells, after):
    outs = [shape(sz.rows_all, sz.orb, F32), shape(*cells.shape, F32)] + face_outs(sz)
    body = functools.partial(start_body, sz)
    r, cells, *faces = kernel_call(body, outs, [parts, cells], after=after)
    return r, cells, faces


def cross_body(sz, xr_one, xr_two, ry_lo, ry_hi, sy_one, sy_two):
    last = (sz.nx - 1) * PAD
    lo, hi = read_pair("gx", xr_one, xr_two)
    faces = []
    for raw, b in ((ry_lo, 0), (ry_hi, sz.ny - 1)):
        value = raw[...]
        parts = [
            value[:PAD] + lo[b * PAD : (b + 1) * PAD],
            value[PAD:last],
            value[last : last + PAD] + hi[b * PAD : (b + 1) * PAD],
            value[last + PAD :],
        ]
        faces.append(jnp.concatenate(parts, axis=0))
    write_pair("gy", *faces, sy_one, sy_two)


def cross_faces(sz, *faces):
    outs = [shape(sz.yface, sz.orb, HALO)] * 2
    return kernel_call(functools.partial(cross_body, sz), outs, list(faces))


def add_xy(sz, ra, xr_one, xr_two, yr_one, yr_two):
    last = (sz.nx - 1) * sz.line_x
    low, high = read_pair("gx", xr_one, xr_two)
    ra[0 : sz.line_x, :] += low[: sz.line_x]
    ra[last : last + sz.line_x, :] += high[: sz.line_x]
    for value, b in zip(read_pair("gy", yr_one, yr_two), (0, sz.ny - 1)):
        for a in range(sz.nx):
            at = a * sz.line_x + b * PAD
            ra[at : at + PAD, :] += value[a * PAD : (a + 1) * PAD]


def local_term(weight, fields, at):
    value = weight * fields[0][at, :]
    return value - fields[1][at, :] if len(fields) > 1 else value


def layer_rows(y, weight, fields, at):
    rows = pl.ds(at, PAD, stride=PAD)
    return y[rows, :] - local_term(weight, fields, rows) if fields else y[rows, :]


def pack_z(sz, y, weight, fields, j):
    rows, c = [], layer_sent(sz, j)
    for a in range(sz.nx):
        for b in range(0, sz.face_b, PAD):
            rows.append(layer_rows(y, weight, fields, a * sz.line_x + b * PAD + c))
    rest = sz.zface - sz.nx * sz.face_b
    if rest:
        rows.append(jnp.zeros((rest, sz.orb), F32))
    value, valid = jnp.concatenate(rows, axis=0), link_valid(sz, j)
    return (value if valid is None else value * valid.astype(F32)).astype(HALO)


def add_z(sz, y, j, face):
    c = layer_received(sz, j)
    for a in range(sz.nx):
        for b in range(0, sz.ny, PAD):
            n = min(PAD, sz.ny - b)
            at = pl.ds(a * sz.line_x + b * PAD + c, n, stride=PAD)
            y[at, :] = y[at, :] + face[a * sz.face_b + b : a * sz.face_b + b + n]


def face_cells(sz, y, weight, fields, j):
    rows, c = [], layer_sent(sz, j)
    for p, q in sz.cells:
        for a in range(EDGE):
            at = (ORDER * p + a) * sz.line_x + ORDER * q * PAD
            rows.append(layer_rows(y, weight, fields, at + c))
        rows.append(jnp.zeros((PAD, sz.orb), F32))
    return jnp.concatenate(rows, axis=0).astype(BF16)


def project_body(sz, weight, past, refs):
    take = iter(refs)
    r = next(take)
    fields = [next(take) for _ in range(past)]
    halos = [next(take) for _ in range(4)]
    q = next(take)
    qfaces = [next(take) for _ in range(sz.links)]
    maps = next(take)
    y, own = next(take), next(take)
    beside = [next(take) for _ in range(sz.links)]
    messages = [next(take) for _ in range(sz.shifts)]
    everything = slice(0, sz.rows_all)
    y[...] = r[...] + local_term(weight, fields, everything) if past else r[...]
    add_xy(sz, y, *halos)
    blocks = [cell_block(sz, y, cell).astype(BF16) for cell in sz.cells]
    rest = sz.all_pad - sz.cell_pad * len(sz.cells)
    if rest:
        blocks.append(jnp.zeros((rest, sz.orb), BF16))
    sums = dot(q[...], jnp.concatenate(blocks, axis=0))
    own[...] = sums
    known = [sums.astype(BF16)]
    for j, matrix in enumerate(qfaces):
        value, valid = dot(matrix[...], face_cells(sz, y, weight, fields, j)), link_valid(sz, j)
        beside[j][...] = (value if valid is None else value * valid.astype(F32)).astype(BF16)
        known.append(beside[j][...])
    shift_of = link_shifts(sz)
    for s, message in enumerate(messages):
        rows = slice(s * SLOTS, (s + 1) * SLOTS)
        mapped = [0] + [j + 1 for j, shift in enumerate(shift_of) if shift != s + 1]
        direct = [j for j, shift in enumerate(shift_of) if shift == s + 1]
        total = sum(dot(maps[rows, k * SLOTS : (k + 1) * SLOTS], known[k]) for k in mapped)
        for j in direct:
            total = total + known[j + 1].astype(F32)
            message[SLOTS : SLOTS + sz.zface, :] = pack_z(sz, y, weight, fields, j)
        message[0:SLOTS, :] = total.astype(HALO)


def project(sz, r, weight, fields, halos, q, qfaces, maps):
    outs = [shape(sz.rows_all, sz.orb, F32), shape(SLOTS, sz.orb, F32)]
    outs += [shape(SLOTS, sz.orb, BF16)] * sz.links
    for s in range(1, sz.shifts + 1):
        outs.append(shape(SLOTS + (sz.zface if s in link_shifts(sz) else 0), sz.orb, HALO))

    def body(*refs):
        project_body(sz, weight, len(fields), refs)

    y, own, *rest = kernel_call(
        body,
        outs,
        [r, *fields, *halos, q, *qfaces, maps],
        flops=4 * 10**8,
        limit=(32 << 20) if sz.shifts < 8 else (56 << 20),
    )
    return y, [own, *rest[: sz.links]], rest[sz.links :]


def couple(c_hi, c_lo, totals):
    high = totals.astype(BF16)
    low = (totals - high.astype(F32)).astype(BF16)
    return dot(c_hi[...], high) + (dot(c_hi[...], low) + dot(c_lo[...], high))


def couple_body(sz, own, *refs):
    beside = refs[: sz.links]
    back, c_hi, c_lo, coupled = refs[sz.links :]
    totals = own[...]
    for j, part in enumerate(beside):
        totals = totals + dot(back[:, j * SLOTS : (j + 1) * SLOTS], part[...])
    coupled[...] = couple(c_hi, c_lo, totals)


def couple_own(sz, own, back, c_hi, c_lo):
    outs = [shape(SLOTS, sz.orb, F32)]
    body = functools.partial(couple_body, sz)
    return kernel_call(body, outs, [*own, back, c_hi, c_lo], flops=2 * 10**8)[0]


def apply_body(sz, scale, refs):
    take = iter(refs)
    yin, own = next(take), next(take)
    messages = [next(take) for _ in range(sz.shifts)]
    c_hi, c_lo, qt, kin, pot = [next(take) for _ in range(5)]
    r, y = next(take), next(take)
    faces = [next(take) for _ in range(4)]
    if len(messages) == 1:
        high = messages[0][0:SLOTS, :].astype(BF16)
        coef = own[...] + (dot(c_hi[...], high) + dot(c_lo[...], high))
    else:
        totals = sum(message[0:SLOTS, :].astype(F32) for message in messages)
        coef = own[...] + couple(c_hi, c_lo, totals)
    coef = coef.astype(BF16)
    y[...] = yin[...]
    for j, shift in enumerate(link_shifts(sz)):
        add_z(sz, y, j, messages[shift - 1][SLOTS : SLOTS + sz.zface, :].astype(F32))
    blocks = [cell_block(sz, y, cell) for cell in sz.cells]
    stiff = dot(kin[...], jnp.concatenate([b.astype(BF16) for b in blocks], axis=1))
    spread = dot(qt[: sz.cell_pad * len(sz.cells), :], coef)
    for g, (p, q) in enumerate(sz.cells):
        rows = slice(g * sz.cell_pad, (g + 1) * sz.cell_pad)
        value = stiff[:, g * sz.orb : (g + 1) * sz.orb] + pot[rows, :] * blocks[g]
        value = (value + spread[rows]) * scale
        for a in range(EDGE):
            start = (ORDER * p + a) * sz.line_x + ORDER * q * PAD
            line = value[a * EDGE * PAD : (a + 1) * EDGE * PAD]
            shared = EDGE * PAD if p and a == 0 else PAD if q else 0
            if shared:
                r[start : start + shared, :] += line[:shared]
            if shared < EDGE * PAD:
                r[start + shared : start + EDGE * PAD, :] = line[shared:]
    r[sz.rows :, :] = jnp.zeros((sz.rows_all - sz.rows, sz.orb), F32)
    write_faces(sz, r, *faces)


def apply(sz, y, own, messages, c_hi, c_lo, qt, kin, pot, scale):
    outs = [shape(sz.rows_all, sz.orb, F32)] * 2 + face_outs(sz)
    arrays = [y, own, *messages, c_hi, c_lo, qt, kin, pot]

    def body(*refs):
        apply_body(sz, scale, refs)

    r, y, *faces = kernel_call(body, outs, arrays, flops=6 * 10**8, limit=32 << 20)
    return r, y, faces


def last_faces_body(sz, refs):
    take = iter(refs)
    r = next(take)
    halos = [next(take) for _ in range(4)]
    ra = next(take)
    outs = [next(take) for _ in range(sz.links)]
    ra[...] = r[...]
    add_xy(sz, ra, *halos)
    for j, out in enumerate(outs):
        out[...] = pack_z(sz, ra, None, [], j)


def last_faces(sz, r, halos):
    def body(*refs):
        last_faces_body(sz, refs)

    outs = [shape(sz.rows_all, sz.orb, F32)] + [shape(sz.zface, sz.orb, HALO)] * sz.links
    ra, *sent = kernel_call(body, outs, [r, *halos])
    return ra, sent


def add_local_body(weight, past, r, *refs):
    fields, out = refs[:past], refs[past]
    out[...] = r[...] + local_term(weight, fields, slice(0, out.shape[0]))


def add_local(sz, r, weight, fields):
    body = functools.partial(add_local_body, weight, len(fields))
    return kernel_call(body, [shape(sz.rows_all, sz.orb, F32)], [r, *fields])[0]


def finish_body(sz, r, *refs):
    zr = refs[: sz.links]
    out, ra, block, sent = refs[sz.links :]
    ra[...] = r[...]
    for j, face in enumerate(zr):
        add_z(sz, ra, j, face[...].astype(F32))
    nz = block.shape[2]
    pieces, copies = 3, []
    for k in range(pieces):
        first, last = k * sz.nx // pieces, (k + 1) * sz.nx // pieces
        value = ra[first * sz.line_x : last * sz.line_x, :]
        value = value.reshape(last - first, sz.ny, PAD, sz.orb)[:, :, :nz, :]
        block[first:last] = value
        copy = pltpu.make_async_copy(block.at[first:last], out.at[first:last], sent.at[k])
        copy.start()
        copies.append(copy)
    for copy in copies:
        copy.wait()


def finish(sz, r, zr, nz):
    outs = [jax.ShapeDtypeStruct((sz.nx, sz.ny, nz, sz.orb), F32)]
    scratch = [
        pltpu.VMEM((sz.rows_all, sz.orb), F32),
        pltpu.VMEM((sz.nx, sz.ny, nz, sz.orb), F32),
        pltpu.SemaphoreType.DMA((3,)),
    ]
    body = functools.partial(finish_body, sz)
    anywhere = [pl.BlockSpec(memory_space=pl.ANY)]
    return kernel_call(body, outs, [r, *zr], scratch=scratch, out_specs=anywhere)[0]


def swap_faces(axis, one, two):
    axes = ("gx", "gy")
    wide, deep = lax.axis_size("gx"), lax.axis_size("gy")
    count = wide if axis == "gx" else deep

    def partner(i, j, low):
        at = i if axis == "gx" else j
        to = at + 1 if at % 2 == low else at - 1
        if 0 <= to < count:
            return (to, j) if axis == "gx" else (i, to)
        if axis == "gy" and wide % 2 == 0:
            return (i ^ 1, j)
        ends = sorted({k for k in range(count) if not 0 <= k + (1 if k % 2 == low else -1) < count})
        to = ends[::-1][ends.index(at)]
        return (to, j) if axis == "gx" else (i, to)

    out = []
    for face, low in ((one, FIRST[axis]), (two, 1 - FIRST[axis])):
        pairs = []
        for i in range(wide):
            for j in range(deep):
                to = partner(i, j, low)
                pairs.append((i * deep + j, to[0] * deep + to[1]))
        out.append(lax.ppermute(face, axes, pairs))
    return out


def local(parts, cell_matrix, cell_potential, projectors, slot_atom, slot_cells, coupling):
    nx, ny, nz, orbitals = parts.shape
    nodes = cell_matrix.shape[0]
    devices = lax.axis_size("gz")
    sz = Sizes(nx, ny, nz, orbitals, devices - 1)
    ring = [[(i, (i + s) % devices) for i in range(devices)] for s in range(devices)]

    proj = projectors.reshape(nodes, POS * BLK * PA)
    proj = jnp.pad(proj, ((0, up(nodes, 16) - nodes), (0, 0)))
    cells = jnp.transpose(slot_cells.reshape(POS, BLK))
    r, cells, faces = start_faces(sz, parts, cells, [proj])

    def exchange_xy(sx_one, sx_two, sy_lo, sy_hi):
        xr = swap_faces("gx", sx_one, sx_two)
        cross = cross_faces(sz, *xr, sy_lo, sy_hi)
        yr = swap_faces("gy", *cross)
        return (*xr, *yr)

    halos = exchange_xy(*faces)
    qt, *face_rows = sum_matrices(sz, proj, cells)
    qfaces = []
    for j, shift in enumerate(link_shifts(sz)):
        back = [(target, source) for source, target in ring[shift]]
        qfaces.append(lax.ppermute(face_rows[j], "gz", back))
    pot = jnp.transpose(cell_potential, (1, 2, 3, 0)).reshape(len(sz.cells), nodes)
    q, kin, pot, maps, back, c_hi, c_lo = turn_matrices(
        sz,
        qt,
        cell_matrix,
        pot,
        slot_atom.reshape(devices, POS),
        jnp.transpose(coupling, (1, 2, 0)),
    )

    fields, scale = [], 1.0 / half_width
    weight = 0.0
    for step in range(STEPS):
        y, own, messages = project(sz, r, weight, fields, halos, q, qfaces, maps)
        received = [lax.ppermute(m, "gz", ring[s + 1]) for s, m in enumerate(messages)]
        own = couple_own(sz, own, back, c_hi, c_lo)
        r, y, faces = apply(sz, y, own, received, c_hi, c_lo, qt, kin, pot, scale)
        fields, weight = [y] + fields[:1], -center_value * scale
        scale = 2.0 / half_width
        halos = exchange_xy(*faces)
    r, sent = last_faces(sz, r, halos)
    zr = [lax.ppermute(f, "gz", ring[s]) for f, s in zip(sent, link_shifts(sz))]
    return finish(sz, add_local(sz, r, weight, fields), zr, nz)


def solution(mesh):
    in_specs = (
        P("gx", "gy", "gz", None),
        P(),
        P(None, "gx", "gy", "gz"),
        P("gx", "gy", "gz", None, None),
        P("gx", "gy", None, None),
        P("gx", "gy", "gz", None, None),
        P(("gx", "gy"), None, None),
    )
    out_specs = P("gx", "gy", "gz", None)
    return jax.shard_map(local, mesh=mesh, in_specs=in_specs, out_specs=out_specs, check_vma=False)
```

```python
import functools

import jax
import jax.numpy as jnp
import numpy as np
from jax import lax
from jax.experimental import pallas as pl
from jax.experimental.pallas import tpu as pltpu
from jax.sharding import PartitionSpec as P

ORDER = 6
STEPS = 3
PA = 12
POS = 32
BLK = 4

center_value = 2.0
half_width = 3.0

EDGE = ORDER + 1
PAD = 8
SLOTS = POS * PA
F32 = jnp.float32
BF16 = jnp.bfloat16
HALO = jnp.bfloat16


def up(value, multiple):
    return -(-value // multiple) * multiple


class Sizes:
    def __init__(self, nx, ny, nz, orbitals, shifts):
        assert nz == EDGE
        self.nx, self.ny, self.orb = nx, ny, orbitals
        self.cells = [(p, q) for p in range((nx - 1) // ORDER) for q in range((ny - 1) // ORDER)]
        self.rows = nx * ny * PAD
        self.line_x = ny * PAD
        self.xface = up(ny * PAD, 16)
        self.yface = up(nx * PAD, 16)
        self.face_b = up(ny, PAD)
        self.zface = up(nx * self.face_b, 16)
        self.cell_rows = EDGE * EDGE * PAD
        self.cell_pad = up(self.cell_rows, 16)
        self.all_pad = up(self.cell_pad * len(self.cells), 128)
        self.fcell = EDGE * PAD
        self.fall = up(self.fcell * len(self.cells), 256)
        self.shifts, self.links = shifts, min(2, shifts)
        self.pair = shifts == 1
        self.rows_all = self.rows + (self.face_b - ny + 1) * PAD


VMEM = pl.BlockSpec(memory_space=pltpu.VMEM)


def kernel_call(body, outs, arrays, scratch=(), flops=0, limit=24 << 20, after=(), out_specs=None):
    used = len(arrays)

    def with_waits(*refs):
        body(*refs[:used], *refs[used + len(after) :])

    nbytes = sum(int(np.prod(a.shape)) * a.dtype.itemsize for a in list(arrays) + list(outs))
    return pl.pallas_call(
        with_waits,
        out_shape=outs,
        in_specs=[VMEM] * used + [pl.BlockSpec(memory_space=pl.ANY)] * len(after),
        out_specs=out_specs or [VMEM] * len(outs),
        scratch_shapes=list(scratch),
        compiler_params=pltpu.CompilerParams(vmem_limit_bytes=limit),
        cost_estimate=pl.CostEstimate(flops=flops, bytes_accessed=nbytes, transcendentals=0),
    )(*arrays, *after)


def shape(rows, cols, dtype):
    return jax.ShapeDtypeStruct((rows, cols), dtype)


def dot(a, b):
    return jnp.dot(a, b, preferred_element_type=F32)


FIRST = {"gx": 1, "gy": 0}


def if_first(axis, value, otherwise):
    return jnp.where(lax.rem(lax.axis_index(axis), 2) == FIRST[axis], value, otherwise)


def link_shifts(sz):
    return [1, sz.shifts][: sz.links]


def layer_sent(sz, j):
    if sz.links == 1:
        return jnp.where(lax.axis_index("gz") == 0, ORDER, 0)
    return [ORDER, 0][j]


def layer_received(sz, j):
    return layer_sent(sz, 0) if sz.links == 1 else [0, ORDER][j]


def link_valid(sz, j):
    if sz.links == 1:
        return None
    me = lax.axis_index("gz")
    return jnp.where(me < sz.shifts, 1, 0) if j == 0 else jnp.where(me > 0, 1, 0)


def iota(rows, cols, dim):
    return lax.broadcasted_iota(jnp.int32, (rows, cols), dim)


def twelfth(value):
    return (value * (2**19 // PA + 1)) >> 19


def node_key(i):
    low = i & (PAD - 1)
    return jnp.where((low < EDGE) & (i < EDGE * EDGE * PAD), (i >> 3) * EDGE + low, -1)


def dot_last(a, b, precision=None):
    dims = (((1,), (1,)), ((), ()))
    return lax.dot_general(a, b, dims, precision=precision, preferred_element_type=F32)


def sum_body(sz, proj, cells, qt, *qt_faces):
    nodes, cols = proj.shape
    i = iota(cols, POS, 0)
    first = iota(cols, POS, 1) * (BLK * PA)
    in_slot = ((i >= first) & (i < first + BLK * PA)).astype(BF16)
    of_block = dot_last(in_slot, cells[...].astype(BF16))
    i = iota(cols, BLK, 0)
    block = twelfth(i)
    cell = jnp.sum(
        jnp.where((block & (BLK - 1)) == iota(cols, BLK, 1), of_block, 0.0), axis=1, keepdims=True
    )
    i, block = i[:, :1], block[:, :1]
    row = (block >> (BLK.bit_length() - 1)) * PA + (i - block * PA)
    halves, group, width = [], cols // 2, SLOTS // 2
    targets = len(sz.cells) * width
    for h in range(2):
        mine = slice(h * group, (h + 1) * group)
        key = cell[mine].astype(jnp.int32) * width + (row[mine] - h * width)
        pick = (key == iota(group, targets, 1)).astype(BF16)
        halves.append(dot(proj[:, mine], pick))
    parts = []
    for g in range(len(sz.cells)):
        parts += [half[:, g * width : (g + 1) * width] for half in halves]
    summed = jnp.concatenate(parts, axis=1).astype(BF16)
    keys = [node_key(iota(sz.cell_pad, nodes, 0))]
    for j in range(sz.links):
        keys.append(
            jnp.where(
                iota(PAD * PAD, nodes, 0) < sz.fcell,
                node_key(iota(PAD * PAD, nodes, 0)) * EDGE + layer_received(sz, j),
                -1,
            )
        )
        low = iota(PAD * PAD, nodes, 0) & (PAD - 1)
        keys[-1] = jnp.where(low < EDGE, keys[-1], -1)
    expand = (jnp.concatenate(keys, axis=0) == iota(sz.cell_pad + sz.links * PAD * PAD, nodes, 1))
    full = dot(expand.astype(BF16), summed)
    for g in range(len(sz.cells)):
        value = full[:, g * SLOTS : (g + 1) * SLOTS]
        qt[g * sz.cell_pad : (g + 1) * sz.cell_pad, :] = value[: sz.cell_pad].astype(BF16)
    rest = sz.all_pad - sz.cell_pad * len(sz.cells)
    if rest:
        qt[sz.cell_pad * len(sz.cells) :, :] = jnp.zeros((rest, SLOTS), BF16)
    for j, qf in enumerate(qt_faces):
        at = sz.cell_pad + j * PAD * PAD
        rows = [full[at : at + PAD * PAD, g * SLOTS : (g + 1) * SLOTS] for g in range(len(sz.cells))]
        qf[...] = jnp.concatenate(rows, axis=0).T.astype(BF16)


def sum_matrices(sz, proj, cells):
    outs = [shape(sz.all_pad, SLOTS, BF16)]
    outs += [shape(SLOTS, len(sz.cells) * PAD * PAD, BF16)] * sz.links
    body = functools.partial(sum_body, sz)
    return kernel_call(body, outs, [proj, cells], flops=3 * 10**9, limit=32 << 20)


def slot_keys(sz, table, dim):
    exact = lax.Precision.HIGHEST
    shape2 = (SLOTS, POS) if dim == 0 else (POS, SLOTS)
    i, s = iota(*shape2, dim), iota(*shape2, 1 - dim)
    spread = ((i >= s * PA) & (i < s * PA + PA)).astype(F32)
    if dim == 0:
        atoms = dot_last(spread, table, exact)
    else:
        atoms = jnp.dot(table, spread, precision=exact, preferred_element_type=F32)
    devices = sz.shifts + 1
    at = iota(*atoms.shape, 1 - dim)
    me = lax.axis_index("gz")
    keys = []
    for shift in range(devices):
        chosen = jnp.where(at == lax.rem(me + shift, devices), atoms, 0.0)
        atom = jnp.sum(chosen, axis=1 - dim, keepdims=True).astype(jnp.int32)
        i = iota(*atom.shape, dim)
        keys.append((atom, jnp.where(atom >= 0, atom * PA + i - twelfth(i) * PA, -1)))
    return keys


def turn_body(sz, qt, kin, pot, atoms, coupling, *refs):
    own_rows, refs = (refs[0], refs[1:]) if sz.pair else (None, refs)
    q, kout, vout, back, c_hi, c_lo = refs[:6]
    *others, wide = refs[6:]
    q[...] = qt[...].T
    nodes = kin.shape[0]
    expand = (node_key(iota(sz.cell_pad, nodes, 0)) == iota(sz.cell_pad, nodes, 1)).astype(BF16)
    gather = (node_key(iota(nodes, sz.cell_pad, 1)) == iota(nodes, sz.cell_pad, 0)).astype(BF16)
    tall = dot(expand, kin[...]).astype(BF16)
    kout[...] = dot(tall, gather).astype(BF16)
    value, values = pot[...], 0.0
    for _ in range(3):
        part = value.astype(BF16)
        values = values + dot_last(expand, part)
        value = value - part.astype(F32)
    for g in range(len(sz.cells)):
        vout[g * sz.cell_pad : (g + 1) * sz.cell_pad, :] = jnp.broadcast_to(
            values[:, g : g + 1], (sz.cell_pad, sz.orb)
        )
    table = atoms[...].astype(F32)
    rows, cols = slot_keys(sz, table, 0), slot_keys(sz, table, 1)
    known = [jnp.where(cols[0][1] >= 0, cols[0][1], -2)]
    for j, shift in enumerate(link_shifts(sz)):
        key = jnp.where(cols[shift][1] >= 0, cols[shift][1], -2)
        valid = link_valid(sz, j)
        known.append(key if valid is None else jnp.where(valid == 1, key, -2))
    for s in range(0 if sz.pair else sz.shifts):
        maps = others[0]
        for j, key in enumerate(known):
            maps[s * SLOTS : (s + 1) * SLOTS, j * SLOTS : (j + 1) * SLOTS] = (
                rows[s + 1][1] == key
            ).astype(BF16)
    for j, key in enumerate(known[1:]):
        back[:, j * SLOTS : (j + 1) * SLOTS] = (rows[0][1] == key).astype(BF16)
    pa, pb, atom_count = coupling.shape
    wide[...] = jnp.zeros(wide.shape, F32)
    wide[:, :pb, :] = coupling[...]
    table2 = wide[...].reshape(pa * 16, atom_count)
    hot = (rows[0][0] == iota(SLOTS, atom_count, 1)).astype(BF16)
    i, lane = iota(SLOTS, pa * 16, 0), iota(SLOTS, pa * 16, 1)
    own_row = (lane >> 4) == i - twelfth(i) * PA
    lane, j = iota(pa * 16, SLOTS, 0), iota(pa * 16, SLOTS, 1)
    fold = ((lane & 15) == j - twelfth(j) * PA).astype(BF16)
    same = twelfth(iota(SLOTS, SLOTS, 0)) == twelfth(iota(SLOTS, SLOTS, 1))
    for out in (c_hi, c_lo):
        part = table2.astype(BF16)
        table2 = table2 - part.astype(F32)
        picked = jnp.where(own_row, dot_last(hot, part), 0.0).astype(BF16)
        out[...] = jnp.where(same, dot(picked, fold), 0.0).astype(BF16)
    if sz.pair:
        m_hi, m_lo, c_rows = others
        m_hi[...] = dot(c_hi[...], back[...]).astype(BF16)
        m_lo[...] = dot(c_lo[...], back[...]).astype(BF16)
        c_rows[...] = (dot(c_hi[...], own_rows[...]) + dot(c_lo[...], own_rows[...])).astype(BF16)


def turn_matrices(sz, qt, kin, pot, atoms, coupling, face_rows):
    known = (1 + sz.links) * SLOTS
    outs = [
        shape(SLOTS, sz.all_pad, BF16),
        shape(sz.cell_pad, sz.cell_pad, BF16),
        shape(len(sz.cells) * sz.cell_pad, sz.orb, F32),
        shape(SLOTS, sz.links * SLOTS, BF16),
        shape(SLOTS, SLOTS, BF16),
        shape(SLOTS, SLOTS, BF16),
    ]
    if sz.pair:
        outs += [shape(SLOTS, SLOTS, BF16)] * 2 + [shape(*face_rows[0].shape, BF16)]
    else:
        outs += [shape(sz.shifts * SLOTS, known, BF16)]
    limit = (32 << 20) if sz.shifts < 8 else (56 << 20)
    return kernel_call(
        functools.partial(turn_body, sz),
        outs,
        [qt, kin, pot, atoms, coupling] + (face_rows if sz.pair else []),
        scratch=[pltpu.VMEM((coupling.shape[0], 16, coupling.shape[2]), F32)],
        flops=10**9,
        limit=limit,
    )


def cell_block(sz, z, cell):
    p, q = cell
    layers = []
    for a in range(EDGE):
        start = (ORDER * p + a) * sz.line_x + ORDER * q * PAD
        layers.append(z[start : start + EDGE * PAD, :])
    layers.append(jnp.zeros((sz.cell_pad - sz.cell_rows, sz.orb), F32))
    return jnp.concatenate(layers, axis=0)


def write_pair(axis, low, high, first, second):
    first[...] = if_first(axis, high, low).astype(first.dtype)
    second[...] = if_first(axis, low, high).astype(second.dtype)


def read_pair(axis, first, second):
    one, two = first[...].astype(F32), second[...].astype(F32)
    low, high = if_first(axis, two, one), if_first(axis, one, two)
    at, last = lax.axis_index(axis), lax.axis_size(axis) - 1
    return jnp.where(at > 0, low, 0.0), jnp.where(at < last, high, 0.0)


def write_faces(sz, r, sx_one, sx_two, sy_lo, sy_hi):
    pad_x = jnp.zeros((sz.xface - sz.line_x, sz.orb), F32)
    pad_y = jnp.zeros((sz.yface - sz.nx * PAD, sz.orb), F32)
    last = (sz.nx - 1) * sz.line_x
    low = jnp.concatenate([r[0 : sz.line_x, :], pad_x], axis=0)
    high = jnp.concatenate([r[last : last + sz.line_x, :], pad_x], axis=0)
    write_pair("gx", low, high, sx_one, sx_two)
    for out, b in ((sy_lo, 0), (sy_hi, sz.ny - 1)):
        rows = [r[a * sz.line_x + b * PAD : a * sz.line_x + (b + 1) * PAD, :] for a in range(sz.nx)]
        out[...] = jnp.concatenate(rows + [pad_y], axis=0)


def face_outs(sz):
    return [shape(sz.xface, sz.orb, HALO)] * 2 + [shape(sz.yface, sz.orb, F32)] * 2


def start_body(sz, parts, cells, r, cells_out, *faces):
    cells_out[...] = cells[...].astype(F32)
    nz = parts.shape[2]
    r[...] = jnp.zeros(r.shape, F32)
    for a in range(sz.nx):
        for b in range(sz.ny):
            at = a * sz.line_x + b * PAD
            r[at : at + nz, :] = parts[a, b]
    write_faces(sz, r, *faces)


def start_faces(sz, parts, cells, after):
    outs = [shape(sz.rows_all, sz.orb, F32), shape(*cells.shape, F32)] + face_outs(sz)
    body = functools.partial(start_body, sz)
    r, cells, *faces = kernel_call(body, outs, [parts, cells], after=after)
    return r, cells, faces


def cross_body(sz, xr_one, xr_two, ry_lo, ry_hi, sy_one, sy_two):
    last = (sz.nx - 1) * PAD
    lo, hi = read_pair("gx", xr_one, xr_two)
    faces = []
    for raw, b in ((ry_lo, 0), (ry_hi, sz.ny - 1)):
        value = raw[...]
        parts = [
            value[:PAD] + lo[b * PAD : (b + 1) * PAD],
            value[PAD:last],
            value[last : last + PAD] + hi[b * PAD : (b + 1) * PAD],
            value[last + PAD :],
        ]
        faces.append(jnp.concatenate(parts, axis=0))
    write_pair("gy", *faces, sy_one, sy_two)


def cross_faces(sz, *faces):
    outs = [shape(sz.yface, sz.orb, HALO)] * 2
    return kernel_call(functools.partial(cross_body, sz), outs, list(faces))


def add_xy(sz, ra, xr_one, xr_two, yr_one, yr_two):
    last = (sz.nx - 1) * sz.line_x
    low, high = read_pair("gx", xr_one, xr_two)
    ra[0 : sz.line_x, :] += low[: sz.line_x]
    ra[last : last + sz.line_x, :] += high[: sz.line_x]
    for value, b in zip(read_pair("gy", yr_one, yr_two), (0, sz.ny - 1)):
        for a in range(sz.nx):
            at = a * sz.line_x + b * PAD
            ra[at : at + PAD, :] += value[a * PAD : (a + 1) * PAD]


def local_term(weight, fields, at):
    value = weight * fields[0][at, :]
    return value - fields[1][at, :] if len(fields) > 1 else value


def layer_rows(y, weight, fields, at):
    rows = pl.ds(at, PAD, stride=PAD)
    return y[rows, :] - local_term(weight, fields, rows) if fields else y[rows, :]


def pack_z(sz, y, weight, fields, j):
    rows, c = [], layer_sent(sz, j)
    for a in range(sz.nx):
        for b in range(0, sz.face_b, PAD):
            rows.append(layer_rows(y, weight, fields, a * sz.line_x + b * PAD + c))
    rest = sz.zface - sz.nx * sz.face_b
    if rest:
        rows.append(jnp.zeros((rest, sz.orb), F32))
    value, valid = jnp.concatenate(rows, axis=0), link_valid(sz, j)
    return (value if valid is None else value * valid.astype(F32)).astype(HALO)


def add_z(sz, y, j, face):
    c = layer_received(sz, j)
    for a in range(sz.nx):
        for b in range(0, sz.ny, PAD):
            n = min(PAD, sz.ny - b)
            at = pl.ds(a * sz.line_x + b * PAD + c, n, stride=PAD)
            y[at, :] = y[at, :] + face[a * sz.face_b + b : a * sz.face_b + b + n]


def face_cells(sz, y, weight, fields, j):
    rows, c = [], layer_sent(sz, j)
    for p, q in sz.cells:
        for a in range(EDGE):
            at = (ORDER * p + a) * sz.line_x + ORDER * q * PAD
            rows.append(layer_rows(y, weight, fields, at + c))
        rows.append(jnp.zeros((PAD, sz.orb), F32))
    return jnp.concatenate(rows, axis=0).astype(BF16)


def message_cells(sz, face):
    rows = []
    for p, q in sz.cells:
        for a in range(EDGE):
            at = (ORDER * p + a) * sz.face_b + ORDER * q
            rows.append(face[at : at + PAD])
        rows.append(jnp.zeros((PAD, sz.orb), F32))
    return jnp.concatenate(rows, axis=0).astype(BF16)


def project_body(sz, weight, past, refs):
    take = iter(refs)
    r = next(take)
    fields = [next(take) for _ in range(past)]
    halos = [next(take) for _ in range(4)]
    q = next(take)
    if not sz.pair:
        qfaces = [next(take) for _ in range(sz.links)]
        maps = next(take)
    y, own = next(take), next(take)
    beside = [next(take) for _ in range(sz.links)]
    messages = [next(take) for _ in range(sz.shifts)]
    everything = slice(0, sz.rows_all)
    y[...] = r[...] + local_term(weight, fields, everything) if past else r[...]
    add_xy(sz, y, *halos)
    blocks = [cell_block(sz, y, cell).astype(BF16) for cell in sz.cells]
    rest = sz.all_pad - sz.cell_pad * len(sz.cells)
    if rest:
        blocks.append(jnp.zeros((rest, sz.orb), BF16))
    sums = dot(q[...], jnp.concatenate(blocks, axis=0))
    own[...] = sums
    if sz.pair:
        messages[0][0:SLOTS, :] = sums.astype(HALO)
        messages[0][SLOTS : SLOTS + sz.zface, :] = pack_z(sz, y, weight, fields, 0)
        beside[0][...] = face_cells(sz, y, weight, fields, 0)
        return
    known = [sums.astype(BF16)]
    for j, matrix in enumerate(qfaces):
        value, valid = dot(matrix[...], face_cells(sz, y, weight, fields, j)), link_valid(sz, j)
        beside[j][...] = (value if valid is None else value * valid.astype(F32)).astype(BF16)
        known.append(beside[j][...])
    shift_of = link_shifts(sz)
    for s, message in enumerate(messages):
        rows = slice(s * SLOTS, (s + 1) * SLOTS)
        mapped = [0] + [j + 1 for j, shift in enumerate(shift_of) if shift != s + 1]
        direct = [j for j, shift in enumerate(shift_of) if shift == s + 1]
        total = sum(dot(maps[rows, k * SLOTS : (k + 1) * SLOTS], known[k]) for k in mapped)
        for j in direct:
            total = total + known[j + 1].astype(F32)
            message[SLOTS : SLOTS + sz.zface, :] = pack_z(sz, y, weight, fields, j)
        message[0:SLOTS, :] = total.astype(HALO)


def project(sz, r, weight, fields, halos, q, mapping):
    outs = [shape(sz.rows_all, sz.orb, F32), shape(SLOTS, sz.orb, F32)]
    outs += [shape(sz.fall if sz.pair else SLOTS, sz.orb, BF16)] * sz.links
    for s in range(1, sz.shifts + 1):
        outs.append(shape(SLOTS + (sz.zface if s in link_shifts(sz) else 0), sz.orb, HALO))

    def body(*refs):
        project_body(sz, weight, len(fields), refs)

    y, own, *rest = kernel_call(
        body,
        outs,
        [r, *fields, *halos, q, *mapping],
        flops=4 * 10**8,
        limit=(32 << 20) if sz.shifts < 8 else (56 << 20),
    )
    return y, [own, *rest[: sz.links]], rest[sz.links :]


def couple(c_hi, c_lo, totals):
    high = totals.astype(BF16)
    low = (totals - high.astype(F32)).astype(BF16)
    return dot(c_hi[...], high) + (dot(c_hi[...], low) + dot(c_lo[...], high))


def couple_body(sz, own, *refs):
    beside = refs[: sz.links]
    *rows, back, c_hi, c_lo, coupled = refs[sz.links :]
    totals = own[...]
    for j, part in enumerate(beside):
        value = part[...]
        if sz.pair:
            value = dot(rows[0][...], value).astype(BF16)
        totals = totals + dot(back[:, j * SLOTS : (j + 1) * SLOTS], value)
    coupled[...] = couple(c_hi, c_lo, totals)


def couple_own(sz, own, qfaces, back, c_hi, c_lo):
    outs = [shape(SLOTS, sz.orb, F32)]
    body = functools.partial(couple_body, sz)
    arrays = [*own, *(qfaces if sz.pair else []), back, c_hi, c_lo]
    return kernel_call(body, outs, arrays, flops=2 * 10**8)[0]


def apply_body(sz, scale, refs):
    take = iter(refs)
    yin, own = next(take), next(take)
    messages = [next(take) for _ in range(sz.shifts)]
    factors = [next(take) for _ in range(3 if sz.pair else 2)]
    qt, kin, pot = [next(take) for _ in range(3)]
    r, y = next(take), next(take)
    faces = [next(take) for _ in range(4)]
    if sz.pair:
        m_hi, m_lo, c_rows = factors
        sums, message = messages[0][0:SLOTS, :].astype(BF16), messages[0]
        face = message[SLOTS : SLOTS + sz.zface, :].astype(F32)
        coef = dot(m_hi[...], sums) + dot(m_lo[...], sums)
        coef = own[...] + (coef + dot(c_rows[...], message_cells(sz, face)))
    else:
        totals = sum(message[0:SLOTS, :].astype(F32) for message in messages)
        coef = own[...] + couple(*factors, totals)
    coef = coef.astype(BF16)
    y[...] = yin[...]
    for j, shift in enumerate(link_shifts(sz)):
        add_z(sz, y, j, messages[shift - 1][SLOTS : SLOTS + sz.zface, :].astype(F32))
    blocks = [cell_block(sz, y, cell) for cell in sz.cells]
    stiff = dot(kin[...], jnp.concatenate([b.astype(BF16) for b in blocks], axis=1))
    spread = dot(qt[: sz.cell_pad * len(sz.cells), :], coef)
    for g, (p, q) in enumerate(sz.cells):
        rows = slice(g * sz.cell_pad, (g + 1) * sz.cell_pad)
        value = stiff[:, g * sz.orb : (g + 1) * sz.orb] + pot[rows, :] * blocks[g]
        value = (value + spread[rows]) * scale
        for a in range(EDGE):
            start = (ORDER * p + a) * sz.line_x + ORDER * q * PAD
            line = value[a * EDGE * PAD : (a + 1) * EDGE * PAD]
            shared = EDGE * PAD if p and a == 0 else PAD if q else 0
            if shared:
                r[start : start + shared, :] += line[:shared]
            if shared < EDGE * PAD:
                r[start + shared : start + EDGE * PAD, :] = line[shared:]
    r[sz.rows :, :] = jnp.zeros((sz.rows_all - sz.rows, sz.orb), F32)
    write_faces(sz, r, *faces)


def apply(sz, y, own, messages, factors, qt, kin, pot, scale):
    outs = [shape(sz.rows_all, sz.orb, F32)] * 2 + face_outs(sz)
    arrays = [y, own, *messages, *factors, qt, kin, pot]

    def body(*refs):
        apply_body(sz, scale, refs)

    r, y, *faces = kernel_call(body, outs, arrays, flops=6 * 10**8, limit=32 << 20)
    return r, y, faces


def last_faces_body(sz, refs):
    take = iter(refs)
    r = next(take)
    halos = [next(take) for _ in range(4)]
    ra = next(take)
    outs = [next(take) for _ in range(sz.links)]
    ra[...] = r[...]
    add_xy(sz, ra, *halos)
    for j, out in enumerate(outs):
        out[...] = pack_z(sz, ra, None, [], j)


def last_faces(sz, r, halos):
    def body(*refs):
        last_faces_body(sz, refs)

    outs = [shape(sz.rows_all, sz.orb, F32)] + [shape(sz.zface, sz.orb, HALO)] * sz.links
    ra, *sent = kernel_call(body, outs, [r, *halos])
    return ra, sent


def add_local_body(weight, past, r, *refs):
    fields, out = refs[:past], refs[past]
    out[...] = r[...] + local_term(weight, fields, slice(0, out.shape[0]))


def add_local(sz, r, weight, fields):
    body = functools.partial(add_local_body, weight, len(fields))
    return kernel_call(body, [shape(sz.rows_all, sz.orb, F32)], [r, *fields])[0]


def finish_body(sz, r, *refs):
    zr = refs[: sz.links]
    out, ra, block, sent = refs[sz.links :]
    ra[...] = r[...]
    for j, face in enumerate(zr):
        add_z(sz, ra, j, face[...].astype(F32))
    nz = block.shape[2]
    pieces, copies = 3, []
    for k in range(pieces):
        first, last = k * sz.nx // pieces, (k + 1) * sz.nx // pieces
        value = ra[first * sz.line_x : last * sz.line_x, :]
        value = value.reshape(last - first, sz.ny, PAD, sz.orb)[:, :, :nz, :]
        block[first:last] = value
        copy = pltpu.make_async_copy(block.at[first:last], out.at[first:last], sent.at[k])
        copy.start()
        copies.append(copy)
    for copy in copies:
        copy.wait()


def finish(sz, r, zr, nz):
    outs = [jax.ShapeDtypeStruct((sz.nx, sz.ny, nz, sz.orb), F32)]
    scratch = [
        pltpu.VMEM((sz.rows_all, sz.orb), F32),
        pltpu.VMEM((sz.nx, sz.ny, nz, sz.orb), F32),
        pltpu.SemaphoreType.DMA((3,)),
    ]
    body = functools.partial(finish_body, sz)
    anywhere = [pl.BlockSpec(memory_space=pl.ANY)]
    return kernel_call(body, outs, [r, *zr], scratch=scratch, out_specs=anywhere)[0]


def swap_faces(axis, one, two):
    axes = ("gx", "gy")
    wide, deep = lax.axis_size("gx"), lax.axis_size("gy")
    count = wide if axis == "gx" else deep

    def partner(i, j, low):
        at = i if axis == "gx" else j
        to = at + 1 if at % 2 == low else at - 1
        if 0 <= to < count:
            return (to, j) if axis == "gx" else (i, to)
        if axis == "gy" and wide % 2 == 0:
            return (i ^ 1, j)
        ends = sorted({k for k in range(count) if not 0 <= k + (1 if k % 2 == low else -1) < count})
        to = ends[::-1][ends.index(at)]
        return (to, j) if axis == "gx" else (i, to)

    out = []
    for face, low in ((one, FIRST[axis]), (two, 1 - FIRST[axis])):
        pairs = []
        for i in range(wide):
            for j in range(deep):
                to = partner(i, j, low)
                pairs.append((i * deep + j, to[0] * deep + to[1]))
        out.append(lax.ppermute(face, axes, pairs))
    return out


def local(parts, cell_matrix, cell_potential, projectors, slot_atom, slot_cells, coupling):
    nx, ny, nz, orbitals = parts.shape
    nodes = cell_matrix.shape[0]
    devices = lax.axis_size("gz")
    sz = Sizes(nx, ny, nz, orbitals, devices - 1)
    ring = [[(i, (i + s) % devices) for i in range(devices)] for s in range(devices)]

    proj = projectors.reshape(nodes, POS * BLK * PA)
    proj = jnp.pad(proj, ((0, up(nodes, 16) - nodes), (0, 0)))
    cells = jnp.transpose(slot_cells.reshape(POS, BLK))
    r, cells, faces = start_faces(sz, parts, cells, [proj])

    def exchange_xy(sx_one, sx_two, sy_lo, sy_hi):
        xr = swap_faces("gx", sx_one, sx_two)
        cross = cross_faces(sz, *xr, sy_lo, sy_hi)
        yr = swap_faces("gy", *cross)
        return (*xr, *yr)

    halos = exchange_xy(*faces)
    qt, *face_rows = sum_matrices(sz, proj, cells)
    qfaces = []
    for j, shift in enumerate(link_shifts(sz)):
        back = [(target, source) for source, target in ring[shift]]
        qfaces.append(lax.ppermute(face_rows[j], "gz", back))
    pot = jnp.transpose(cell_potential, (1, 2, 3, 0)).reshape(len(sz.cells), nodes)
    q, kin, pot, back, c_hi, c_lo, *others = turn_matrices(
        sz,
        qt,
        cell_matrix,
        pot,
        slot_atom.reshape(devices, POS),
        jnp.transpose(coupling, (1, 2, 0)),
        face_rows,
    )
    factors = others if sz.pair else [c_hi, c_lo]
    mapping = [] if sz.pair else [*qfaces, *others]

    fields, scale = [], 1.0 / half_width
    weight = 0.0
    for step in range(STEPS):
        y, own, messages = project(sz, r, weight, fields, halos, q, mapping)
        received = [lax.ppermute(m, "gz", ring[s + 1]) for s, m in enumerate(messages)]
        own = couple_own(sz, own, qfaces, back, c_hi, c_lo)
        r, y, faces = apply(sz, y, own, received, factors, qt, kin, pot, scale)
        fields, weight = [y] + fields[:1], -center_value * scale
        scale = 2.0 / half_width
        halos = exchange_xy(*faces)
    r, sent = last_faces(sz, r, halos)
    zr = [lax.ppermute(f, "gz", ring[s]) for f, s in zip(sent, link_shifts(sz))]
    return finish(sz, add_local(sz, r, weight, fields), zr, nz)


def solution(mesh):
    in_specs = (
        P("gx", "gy", "gz", None),
        P(),
        P(None, "gx", "gy", "gz"),
        P("gx", "gy", "gz", None, None),
        P("gx", "gy", None, None),
        P("gx", "gy", "gz", None, None),
        P(("gx", "gy"), None, None),
    )
    out_specs = P("gx", "gy", "gz", None)
    return jax.shard_map(local, mesh=mesh, in_specs=in_specs, out_specs=out_specs, check_vma=False)
```

```python
import functools

import jax
import jax.numpy as jnp
import numpy as np
from jax import lax
from jax.experimental import pallas as pl
from jax.experimental.pallas import tpu as pltpu
from jax.sharding import PartitionSpec as P

ORDER = 6
STEPS = 3
PA = 12
POS = 32
BLK = 4

center_value = 2.0
half_width = 3.0

EDGE = ORDER + 1
PAD = 8
SLOTS = POS * PA
F32 = jnp.float32
BF16 = jnp.bfloat16
HALO = jnp.bfloat16


def up(value, multiple):
    return -(-value // multiple) * multiple


class Sizes:
    def __init__(self, nx, ny, nz, orbitals, shifts):
        assert nz == EDGE
        self.nx, self.ny, self.orb = nx, ny, orbitals
        self.cells = [(p, q) for p in range((nx - 1) // ORDER) for q in range((ny - 1) // ORDER)]
        self.rows = nx * ny * PAD
        self.line_x = ny * PAD
        self.xface = up(ny * PAD, 16)
        self.yface = up(nx * PAD, 16)
        self.face_b = up(ny, PAD)
        self.zface = up(nx * self.face_b, 16)
        self.cell_rows = EDGE * EDGE * PAD
        self.cell_pad = up(self.cell_rows, 16)
        self.all_pad = up(self.cell_pad * len(self.cells), 128)
        self.fcell = EDGE * PAD
        self.fall = up(self.fcell * len(self.cells), 256)
        self.shifts, self.links = shifts, min(2, shifts)
        self.pair = shifts == 1
        self.rows_all = self.rows + (self.face_b - ny + 1) * PAD


VMEM = pl.BlockSpec(memory_space=pltpu.VMEM)


def kernel_call(body, outs, arrays, scratch=(), flops=0, limit=24 << 20, after=(), out_specs=None):
    used = len(arrays)

    def with_waits(*refs):
        body(*refs[:used], *refs[used + len(after) :])

    nbytes = sum(int(np.prod(a.shape)) * a.dtype.itemsize for a in list(arrays) + list(outs))
    return pl.pallas_call(
        with_waits,
        out_shape=outs,
        in_specs=[VMEM] * used + [pl.BlockSpec(memory_space=pl.ANY)] * len(after),
        out_specs=out_specs or [VMEM] * len(outs),
        scratch_shapes=list(scratch),
        compiler_params=pltpu.CompilerParams(vmem_limit_bytes=limit),
        cost_estimate=pl.CostEstimate(flops=flops, bytes_accessed=nbytes, transcendentals=0),
    )(*arrays, *after)


def shape(rows, cols, dtype):
    return jax.ShapeDtypeStruct((rows, cols), dtype)


def dot(a, b):
    return jnp.dot(a, b, preferred_element_type=F32)


FIRST = {"gx": 1, "gy": 0}


def if_first(axis, value, otherwise):
    return jnp.where(lax.rem(lax.axis_index(axis), 2) == FIRST[axis], value, otherwise)


def link_shifts(sz):
    return [1, sz.shifts][: sz.links]


def layer_sent(sz, j):
    if sz.links == 1:
        return jnp.where(lax.axis_index("gz") == 0, ORDER, 0)
    return [ORDER, 0][j]


def layer_received(sz, j):
    return layer_sent(sz, 0) if sz.links == 1 else [0, ORDER][j]


def link_valid(sz, j):
    if sz.links == 1:
        return None
    me = lax.axis_index("gz")
    return jnp.where(me < sz.shifts, 1, 0) if j == 0 else jnp.where(me > 0, 1, 0)


def iota(rows, cols, dim):
    return lax.broadcasted_iota(jnp.int32, (rows, cols), dim)


def twelfth(value):
    return (value * (2**19 // PA + 1)) >> 19


def node_key(i):
    low = i & (PAD - 1)
    return jnp.where((low < EDGE) & (i < EDGE * EDGE * PAD), (i >> 3) * EDGE + low, -1)


def dot_last(a, b, precision=None):
    dims = (((1,), (1,)), ((), ()))
    return lax.dot_general(a, b, dims, precision=precision, preferred_element_type=F32)


def sum_body(sz, proj, cells, qt, *qt_faces):
    nodes, cols = proj.shape
    i = iota(cols, POS, 0)
    first = iota(cols, POS, 1) * (BLK * PA)
    in_slot = ((i >= first) & (i < first + BLK * PA)).astype(BF16)
    of_block = dot_last(in_slot, cells[...].astype(BF16))
    i = iota(cols, BLK, 0)
    block = twelfth(i)
    cell = jnp.sum(
        jnp.where((block & (BLK - 1)) == iota(cols, BLK, 1), of_block, 0.0), axis=1, keepdims=True
    )
    i, block = i[:, :1], block[:, :1]
    row = (block >> (BLK.bit_length() - 1)) * PA + (i - block * PA)
    halves, group, width = [], cols // 2, SLOTS // 2
    targets = len(sz.cells) * width
    for h in range(2):
        mine = slice(h * group, (h + 1) * group)
        key = cell[mine].astype(jnp.int32) * width + (row[mine] - h * width)
        pick = (key == iota(group, targets, 1)).astype(BF16)
        halves.append(dot(proj[:, mine], pick))
    parts = []
    for g in range(len(sz.cells)):
        parts += [half[:, g * width : (g + 1) * width] for half in halves]
    summed = jnp.concatenate(parts, axis=1).astype(BF16)
    keys = [node_key(iota(sz.cell_pad, nodes, 0))]
    for j in range(sz.links):
        keys.append(
            jnp.where(
                iota(PAD * PAD, nodes, 0) < sz.fcell,
                node_key(iota(PAD * PAD, nodes, 0)) * EDGE + layer_received(sz, j),
                -1,
            )
        )
        low = iota(PAD * PAD, nodes, 0) & (PAD - 1)
        keys[-1] = jnp.where(low < EDGE, keys[-1], -1)
    expand = (jnp.concatenate(keys, axis=0) == iota(sz.cell_pad + sz.links * PAD * PAD, nodes, 1))
    full = dot(expand.astype(BF16), summed)
    for g in range(len(sz.cells)):
        value = full[:, g * SLOTS : (g + 1) * SLOTS]
        qt[g * sz.cell_pad : (g + 1) * sz.cell_pad, :] = value[: sz.cell_pad].astype(BF16)
    rest = sz.all_pad - sz.cell_pad * len(sz.cells)
    if rest:
        qt[sz.cell_pad * len(sz.cells) :, :] = jnp.zeros((rest, SLOTS), BF16)
    for j, qf in enumerate(qt_faces):
        at = sz.cell_pad + j * PAD * PAD
        rows = [full[at : at + PAD * PAD, g * SLOTS : (g + 1) * SLOTS] for g in range(len(sz.cells))]
        qf[...] = jnp.concatenate(rows, axis=0).T.astype(BF16)


def sum_matrices(sz, proj, cells):
    outs = [shape(sz.all_pad, SLOTS, BF16)]
    outs += [shape(SLOTS, len(sz.cells) * PAD * PAD, BF16)] * sz.links
    body = functools.partial(sum_body, sz)
    return kernel_call(body, outs, [proj, cells], flops=3 * 10**9, limit=32 << 20)


def slot_keys(sz, table, dim):
    exact = lax.Precision.HIGHEST
    shape2 = (SLOTS, POS) if dim == 0 else (POS, SLOTS)
    i, s = iota(*shape2, dim), iota(*shape2, 1 - dim)
    spread = ((i >= s * PA) & (i < s * PA + PA)).astype(F32)
    if dim == 0:
        atoms = dot_last(spread, table, exact)
    else:
        atoms = jnp.dot(table, spread, precision=exact, preferred_element_type=F32)
    devices = sz.shifts + 1
    at = iota(*atoms.shape, 1 - dim)
    me = lax.axis_index("gz")
    keys = []
    for shift in range(devices):
        chosen = jnp.where(at == lax.rem(me + shift, devices), atoms, 0.0)
        atom = jnp.sum(chosen, axis=1 - dim, keepdims=True).astype(jnp.int32)
        i = iota(*atom.shape, dim)
        keys.append((atom, jnp.where(atom >= 0, atom * PA + i - twelfth(i) * PA, -1)))
    return keys


def flip_body(sz, qt, *refs):
    rows, q, leaving = refs[: sz.links], refs[sz.links], refs[sz.links + 1 :]
    q[...] = qt[...].T
    for source, out in zip(rows, leaving):
        out[...] = source[...]


def flip_matrix(sz, qt, face_rows, after):
    outs = [shape(SLOTS, sz.all_pad, BF16)] + [shape(*f.shape, BF16) for f in face_rows]
    body = functools.partial(flip_body, sz)
    q, *leaving = kernel_call(body, outs, [qt, *face_rows], flops=10**8, after=after)
    return q, leaving


def turn_body(sz, kin, pot, atoms, coupling, *refs):
    own_rows, refs = (refs[0], refs[1:]) if sz.pair else (None, refs)
    kout, vout, back, c_hi, c_lo = refs[:5]
    *others, wide = refs[5:]
    nodes = kin.shape[0]
    expand = (node_key(iota(sz.cell_pad, nodes, 0)) == iota(sz.cell_pad, nodes, 1)).astype(BF16)
    gather = (node_key(iota(nodes, sz.cell_pad, 1)) == iota(nodes, sz.cell_pad, 0)).astype(BF16)
    tall = dot(expand, kin[...]).astype(BF16)
    kout[...] = dot(tall, gather).astype(BF16)
    value, values = pot[...], 0.0
    for _ in range(3):
        part = value.astype(BF16)
        values = values + dot_last(expand, part)
        value = value - part.astype(F32)
    for g in range(len(sz.cells)):
        vout[g * sz.cell_pad : (g + 1) * sz.cell_pad, :] = jnp.broadcast_to(
            values[:, g : g + 1], (sz.cell_pad, sz.orb)
        )
    table = atoms[...].astype(F32)
    rows, cols = slot_keys(sz, table, 0), slot_keys(sz, table, 1)
    known = [jnp.where(cols[0][1] >= 0, cols[0][1], -2)]
    for j, shift in enumerate(link_shifts(sz)):
        key = jnp.where(cols[shift][1] >= 0, cols[shift][1], -2)
        valid = link_valid(sz, j)
        known.append(key if valid is None else jnp.where(valid == 1, key, -2))
    for s in range(0 if sz.pair else sz.shifts):
        maps = others[0]
        for j, key in enumerate(known):
            maps[s * SLOTS : (s + 1) * SLOTS, j * SLOTS : (j + 1) * SLOTS] = (
                rows[s + 1][1] == key
            ).astype(BF16)
    for j, key in enumerate(known[1:]):
        back[:, j * SLOTS : (j + 1) * SLOTS] = (rows[0][1] == key).astype(BF16)
    pa, pb, atom_count = coupling.shape
    wide[...] = jnp.zeros(wide.shape, F32)
    wide[:, :pb, :] = coupling[...]
    table2 = wide[...].reshape(pa * 16, atom_count)
    hot = (rows[0][0] == iota(SLOTS, atom_count, 1)).astype(BF16)
    i, lane = iota(SLOTS, pa * 16, 0), iota(SLOTS, pa * 16, 1)
    own_row = (lane >> 4) == i - twelfth(i) * PA
    lane, j = iota(pa * 16, SLOTS, 0), iota(pa * 16, SLOTS, 1)
    fold = ((lane & 15) == j - twelfth(j) * PA).astype(BF16)
    same = twelfth(iota(SLOTS, SLOTS, 0)) == twelfth(iota(SLOTS, SLOTS, 1))
    for out in (c_hi, c_lo):
        part = table2.astype(BF16)
        table2 = table2 - part.astype(F32)
        picked = jnp.where(own_row, dot_last(hot, part), 0.0).astype(BF16)
        out[...] = jnp.where(same, dot(picked, fold), 0.0).astype(BF16)
    if sz.pair:
        m_hi, m_lo, c_rows = others
        m_hi[...] = dot(c_hi[...], back[...]).astype(BF16)
        m_lo[...] = dot(c_lo[...], back[...]).astype(BF16)
        c_rows[...] = (dot(c_hi[...], own_rows[...]) + dot(c_lo[...], own_rows[...])).astype(BF16)


def turn_matrices(sz, kin, pot, atoms, coupling, face_rows, after):
    known = (1 + sz.links) * SLOTS
    outs = [
        shape(sz.cell_pad, sz.cell_pad, BF16),
        shape(len(sz.cells) * sz.cell_pad, sz.orb, F32),
        shape(SLOTS, sz.links * SLOTS, BF16),
        shape(SLOTS, SLOTS, BF16),
        shape(SLOTS, SLOTS, BF16),
    ]
    if sz.pair:
        outs += [shape(SLOTS, SLOTS, BF16)] * 2 + [shape(*face_rows[0].shape, BF16)]
    else:
        outs += [shape(sz.shifts * SLOTS, known, BF16)]
    limit = (32 << 20) if sz.shifts < 8 else (56 << 20)
    return kernel_call(
        functools.partial(turn_body, sz),
        outs,
        [kin, pot, atoms, coupling] + (face_rows if sz.pair else []),
        scratch=[pltpu.VMEM((coupling.shape[0], 16, coupling.shape[2]), F32)],
        flops=10**9,
        limit=limit,
        after=after,
    )


def cell_block(sz, z, cell):
    p, q = cell
    layers = []
    for a in range(EDGE):
        start = (ORDER * p + a) * sz.line_x + ORDER * q * PAD
        layers.append(z[start : start + EDGE * PAD, :])
    layers.append(jnp.zeros((sz.cell_pad - sz.cell_rows, sz.orb), F32))
    return jnp.concatenate(layers, axis=0)


def write_pair(axis, low, high, first, second):
    first[...] = if_first(axis, high, low).astype(first.dtype)
    second[...] = if_first(axis, low, high).astype(second.dtype)


def read_pair(axis, first, second):
    one, two = first[...].astype(F32), second[...].astype(F32)
    low, high = if_first(axis, two, one), if_first(axis, one, two)
    at, last = lax.axis_index(axis), lax.axis_size(axis) - 1
    return jnp.where(at > 0, low, 0.0), jnp.where(at < last, high, 0.0)


def write_faces(sz, r, sx_one, sx_two, sy_lo, sy_hi):
    pad_x = jnp.zeros((sz.xface - sz.line_x, sz.orb), F32)
    pad_y = jnp.zeros((sz.yface - sz.nx * PAD, sz.orb), F32)
    last = (sz.nx - 1) * sz.line_x
    low = jnp.concatenate([r[0 : sz.line_x, :], pad_x], axis=0)
    high = jnp.concatenate([r[last : last + sz.line_x, :], pad_x], axis=0)
    write_pair("gx", low, high, sx_one, sx_two)
    for out, b in ((sy_lo, 0), (sy_hi, sz.ny - 1)):
        rows = [r[a * sz.line_x + b * PAD : a * sz.line_x + (b + 1) * PAD, :] for a in range(sz.nx)]
        out[...] = jnp.concatenate(rows + [pad_y], axis=0)


def face_outs(sz):
    return [shape(sz.xface, sz.orb, HALO)] * 2 + [shape(sz.yface, sz.orb, F32)] * 2


def start_body(sz, parts, cells, r, cells_out, *faces):
    cells_out[...] = cells[...].astype(F32)
    nz = parts.shape[2]
    r[...] = jnp.zeros(r.shape, F32)
    for a in range(sz.nx):
        for b in range(sz.ny):
            at = a * sz.line_x + b * PAD
            r[at : at + nz, :] = parts[a, b]
    write_faces(sz, r, *faces)


def start_faces(sz, parts, cells, after):
    outs = [shape(sz.rows_all, sz.orb, F32), shape(*cells.shape, F32)] + face_outs(sz)
    body = functools.partial(start_body, sz)
    r, cells, *faces = kernel_call(body, outs, [parts, cells], after=after)
    return r, cells, faces


def cross_body(sz, xr_one, xr_two, ry_lo, ry_hi, sy_one, sy_two):
    last = (sz.nx - 1) * PAD
    lo, hi = read_pair("gx", xr_one, xr_two)
    faces = []
    for raw, b in ((ry_lo, 0), (ry_hi, sz.ny - 1)):
        value = raw[...]
        parts = [
            value[:PAD] + lo[b * PAD : (b + 1) * PAD],
            value[PAD:last],
            value[last : last + PAD] + hi[b * PAD : (b + 1) * PAD],
            value[last + PAD :],
        ]
        faces.append(jnp.concatenate(parts, axis=0))
    write_pair("gy", *faces, sy_one, sy_two)


def cross_faces(sz, *faces, after=()):
    outs = [shape(sz.yface, sz.orb, HALO)] * 2
    return kernel_call(functools.partial(cross_body, sz), outs, list(faces), after=after)


def add_xy(sz, ra, xr_one, xr_two, yr_one, yr_two):
    last = (sz.nx - 1) * sz.line_x
    low, high = read_pair("gx", xr_one, xr_two)
    ra[0 : sz.line_x, :] += low[: sz.line_x]
    ra[last : last + sz.line_x, :] += high[: sz.line_x]
    for value, b in zip(read_pair("gy", yr_one, yr_two), (0, sz.ny - 1)):
        for a in range(sz.nx):
            at = a * sz.line_x + b * PAD
            ra[at : at + PAD, :] += value[a * PAD : (a + 1) * PAD]


def local_term(weight, fields, at):
    value = weight * fields[0][at, :]
    return value - fields[1][at, :] if len(fields) > 1 else value


def layer_rows(y, weight, fields, at):
    rows = pl.ds(at, PAD, stride=PAD)
    return y[rows, :] - local_term(weight, fields, rows) if fields else y[rows, :]


def pack_z(sz, y, weight, fields, j):
    rows, c = [], layer_sent(sz, j)
    for a in range(sz.nx):
        for b in range(0, sz.face_b, PAD):
            rows.append(layer_rows(y, weight, fields, a * sz.line_x + b * PAD + c))
    rest = sz.zface - sz.nx * sz.face_b
    if rest:
        rows.append(jnp.zeros((rest, sz.orb), F32))
    value, valid = jnp.concatenate(rows, axis=0), link_valid(sz, j)
    return (value if valid is None else value * valid.astype(F32)).astype(HALO)


def add_z(sz, y, j, face):
    c = layer_received(sz, j)
    for a in range(sz.nx):
        for b in range(0, sz.ny, PAD):
            n = min(PAD, sz.ny - b)
            at = pl.ds(a * sz.line_x + b * PAD + c, n, stride=PAD)
            y[at, :] = y[at, :] + face[a * sz.face_b + b : a * sz.face_b + b + n]


def face_cells(sz, y, weight, fields, j):
    rows, c = [], layer_sent(sz, j)
    for p, q in sz.cells:
        for a in range(EDGE):
            at = (ORDER * p + a) * sz.line_x + ORDER * q * PAD
            rows.append(layer_rows(y, weight, fields, at + c))
        rows.append(jnp.zeros((PAD, sz.orb), F32))
    return jnp.concatenate(rows, axis=0).astype(BF16)


def message_cells(sz, face):
    rows = []
    for p, q in sz.cells:
        for a in range(EDGE):
            at = (ORDER * p + a) * sz.face_b + ORDER * q
            rows.append(face[at : at + PAD])
        rows.append(jnp.zeros((PAD, sz.orb), F32))
    return jnp.concatenate(rows, axis=0).astype(BF16)


def project_body(sz, weight, past, refs):
    take = iter(refs)
    r = next(take)
    fields = [next(take) for _ in range(past)]
    halos = [next(take) for _ in range(4)]
    q = next(take)
    if not sz.pair:
        qfaces = [next(take) for _ in range(sz.links)]
        maps = next(take)
    y, own = next(take), next(take)
    beside = [next(take) for _ in range(sz.links)]
    messages = [next(take) for _ in range(sz.shifts)]
    everything = slice(0, sz.rows_all)
    y[...] = r[...] + local_term(weight, fields, everything) if past else r[...]
    add_xy(sz, y, *halos)
    blocks = [cell_block(sz, y, cell).astype(BF16) for cell in sz.cells]
    rest = sz.all_pad - sz.cell_pad * len(sz.cells)
    if rest:
        blocks.append(jnp.zeros((rest, sz.orb), BF16))
    sums = dot(q[...], jnp.concatenate(blocks, axis=0))
    own[...] = sums
    if sz.pair:
        messages[0][0:SLOTS, :] = sums.astype(HALO)
        messages[0][SLOTS : SLOTS + sz.zface, :] = pack_z(sz, y, weight, fields, 0)
        beside[0][...] = face_cells(sz, y, weight, fields, 0)
        return
    known = [sums.astype(BF16)]
    for j, matrix in enumerate(qfaces):
        value, valid = dot(matrix[...], face_cells(sz, y, weight, fields, j)), link_valid(sz, j)
        beside[j][...] = (value if valid is None else value * valid.astype(F32)).astype(BF16)
        known.append(beside[j][...])
    shift_of = link_shifts(sz)
    for s, message in enumerate(messages):
        rows = slice(s * SLOTS, (s + 1) * SLOTS)
        mapped = [0] + [j + 1 for j, shift in enumerate(shift_of) if shift != s + 1]
        direct = [j for j, shift in enumerate(shift_of) if shift == s + 1]
        total = sum(dot(maps[rows, k * SLOTS : (k + 1) * SLOTS], known[k]) for k in mapped)
        for j in direct:
            total = total + known[j + 1].astype(F32)
            message[SLOTS : SLOTS + sz.zface, :] = pack_z(sz, y, weight, fields, j)
        message[0:SLOTS, :] = total.astype(HALO)


def project(sz, r, weight, fields, halos, q, mapping):
    outs = [shape(sz.rows_all, sz.orb, F32), shape(SLOTS, sz.orb, F32)]
    outs += [shape(sz.fall if sz.pair else SLOTS, sz.orb, BF16)] * sz.links
    for s in range(1, sz.shifts + 1):
        outs.append(shape(SLOTS + (sz.zface if s in link_shifts(sz) else 0), sz.orb, HALO))

    def body(*refs):
        project_body(sz, weight, len(fields), refs)

    y, own, *rest = kernel_call(
        body,
        outs,
        [r, *fields, *halos, q, *mapping],
        flops=4 * 10**8,
        limit=(32 << 20) if sz.shifts < 8 else (56 << 20),
    )
    return y, [own, *rest[: sz.links]], rest[sz.links :]


def couple(c_hi, c_lo, totals):
    high = totals.astype(BF16)
    low = (totals - high.astype(F32)).astype(BF16)
    return dot(c_hi[...], high) + (dot(c_hi[...], low) + dot(c_lo[...], high))


def couple_body(sz, own, *refs):
    beside = refs[: sz.links]
    *rows, back, c_hi, c_lo, coupled = refs[sz.links :]
    totals = own[...]
    for j, part in enumerate(beside):
        value = part[...]
        if sz.pair:
            value = dot(rows[0][...], value).astype(BF16)
        totals = totals + dot(back[:, j * SLOTS : (j + 1) * SLOTS], value)
    coupled[...] = couple(c_hi, c_lo, totals)


def couple_own(sz, own, qfaces, back, c_hi, c_lo):
    outs = [shape(SLOTS, sz.orb, F32)]
    body = functools.partial(couple_body, sz)
    arrays = [*own, *(qfaces if sz.pair else []), back, c_hi, c_lo]
    return kernel_call(body, outs, arrays, flops=2 * 10**8)[0]


def apply_body(sz, scale, refs):
    take = iter(refs)
    yin, own = next(take), next(take)
    messages = [next(take) for _ in range(sz.shifts)]
    factors = [next(take) for _ in range(3 if sz.pair else 2)]
    qt, kin, pot = [next(take) for _ in range(3)]
    r, y = next(take), next(take)
    faces = [next(take) for _ in range(4)]
    if sz.pair:
        m_hi, m_lo, c_rows = factors
        sums, message = messages[0][0:SLOTS, :].astype(BF16), messages[0]
        face = message[SLOTS : SLOTS + sz.zface, :].astype(F32)
        coef = dot(m_hi[...], sums) + dot(m_lo[...], sums)
        coef = own[...] + (coef + dot(c_rows[...], message_cells(sz, face)))
    else:
        totals = sum(message[0:SLOTS, :].astype(F32) for message in messages)
        coef = own[...] + couple(*factors, totals)
    coef = coef.astype(BF16)
    y[...] = yin[...]
    for j, shift in enumerate(link_shifts(sz)):
        add_z(sz, y, j, messages[shift - 1][SLOTS : SLOTS + sz.zface, :].astype(F32))
    blocks = [cell_block(sz, y, cell) for cell in sz.cells]
    stiff = dot(kin[...], jnp.concatenate([b.astype(BF16) for b in blocks], axis=1))
    spread = dot(qt[: sz.cell_pad * len(sz.cells), :], coef)
    for g, (p, q) in enumerate(sz.cells):
        rows = slice(g * sz.cell_pad, (g + 1) * sz.cell_pad)
        value = stiff[:, g * sz.orb : (g + 1) * sz.orb] + pot[rows, :] * blocks[g]
        value = (value + spread[rows]) * scale
        for a in range(EDGE):
            start = (ORDER * p + a) * sz.line_x + ORDER * q * PAD
            line = value[a * EDGE * PAD : (a + 1) * EDGE * PAD]
            shared = EDGE * PAD if p and a == 0 else PAD if q else 0
            if shared:
                r[start : start + shared, :] += line[:shared]
            if shared < EDGE * PAD:
                r[start + shared : start + EDGE * PAD, :] = line[shared:]
    r[sz.rows :, :] = jnp.zeros((sz.rows_all - sz.rows, sz.orb), F32)
    write_faces(sz, r, *faces)


def apply(sz, y, own, messages, factors, qt, kin, pot, scale):
    outs = [shape(sz.rows_all, sz.orb, F32)] * 2 + face_outs(sz)
    arrays = [y, own, *messages, *factors, qt, kin, pot]

    def body(*refs):
        apply_body(sz, scale, refs)

    r, y, *faces = kernel_call(body, outs, arrays, flops=6 * 10**8, limit=32 << 20)
    return r, y, faces


def last_faces_body(sz, refs):
    take = iter(refs)
    r = next(take)
    halos = [next(take) for _ in range(4)]
    ra = next(take)
    outs = [next(take) for _ in range(sz.links)]
    ra[...] = r[...]
    add_xy(sz, ra, *halos)
    for j, out in enumerate(outs):
        out[...] = pack_z(sz, ra, None, [], j)


def last_faces(sz, r, halos):
    def body(*refs):
        last_faces_body(sz, refs)

    outs = [shape(sz.rows_all, sz.orb, F32)] + [shape(sz.zface, sz.orb, HALO)] * sz.links
    ra, *sent = kernel_call(body, outs, [r, *halos])
    return ra, sent


def add_local_body(weight, past, r, *refs):
    fields, out = refs[:past], refs[past]
    out[...] = r[...] + local_term(weight, fields, slice(0, out.shape[0]))


def add_local(sz, r, weight, fields):
    body = functools.partial(add_local_body, weight, len(fields))
    return kernel_call(body, [shape(sz.rows_all, sz.orb, F32)], [r, *fields])[0]


def finish_body(sz, r, *refs):
    zr = refs[: sz.links]
    out, ra, block, sent = refs[sz.links :]
    ra[...] = r[...]
    for j, face in enumerate(zr):
        add_z(sz, ra, j, face[...].astype(F32))
    nz = block.shape[2]
    pieces, copies = 3, []
    for k in range(pieces):
        first, last = k * sz.nx // pieces, (k + 1) * sz.nx // pieces
        value = ra[first * sz.line_x : last * sz.line_x, :]
        value = value.reshape(last - first, sz.ny, PAD, sz.orb)[:, :, :nz, :]
        block[first:last] = value
        copy = pltpu.make_async_copy(block.at[first:last], out.at[first:last], sent.at[k])
        copy.start()
        copies.append(copy)
    for copy in copies:
        copy.wait()


def finish(sz, r, zr, nz):
    outs = [jax.ShapeDtypeStruct((sz.nx, sz.ny, nz, sz.orb), F32)]
    scratch = [
        pltpu.VMEM((sz.rows_all, sz.orb), F32),
        pltpu.VMEM((sz.nx, sz.ny, nz, sz.orb), F32),
        pltpu.SemaphoreType.DMA((3,)),
    ]
    body = functools.partial(finish_body, sz)
    anywhere = [pl.BlockSpec(memory_space=pl.ANY)]
    return kernel_call(body, outs, [r, *zr], scratch=scratch, out_specs=anywhere)[0]


def swap_faces(axis, one, two):
    axes = ("gx", "gy")
    wide, deep = lax.axis_size("gx"), lax.axis_size("gy")
    count = wide if axis == "gx" else deep

    def partner(i, j, low):
        at = i if axis == "gx" else j
        to = at + 1 if at % 2 == low else at - 1
        if 0 <= to < count:
            return (to, j) if axis == "gx" else (i, to)
        if axis == "gy" and wide % 2 == 0:
            return (i ^ 1, j)
        ends = sorted({k for k in range(count) if not 0 <= k + (1 if k % 2 == low else -1) < count})
        to = ends[::-1][ends.index(at)]
        return (to, j) if axis == "gx" else (i, to)

    out = []
    for face, low in ((one, FIRST[axis]), (two, 1 - FIRST[axis])):
        pairs = []
        for i in range(wide):
            for j in range(deep):
                to = partner(i, j, low)
                pairs.append((i * deep + j, to[0] * deep + to[1]))
        out.append(lax.ppermute(face, axes, pairs))
    return out


def local(parts, cell_matrix, cell_potential, projectors, slot_atom, slot_cells, coupling):
    nx, ny, nz, orbitals = parts.shape
    nodes = cell_matrix.shape[0]
    devices = lax.axis_size("gz")
    sz = Sizes(nx, ny, nz, orbitals, devices - 1)
    ring = [[(i, (i + s) % devices) for i in range(devices)] for s in range(devices)]

    proj = projectors.reshape(nodes, POS * BLK * PA)
    proj = jnp.pad(proj, ((0, up(nodes, 16) - nodes), (0, 0)))
    cells = jnp.transpose(slot_cells.reshape(POS, BLK))
    r, cells, faces = start_faces(sz, parts, cells, [proj])

    def exchange_xy(sx_one, sx_two, sy_lo, sy_hi, after=()):
        xr = swap_faces("gx", sx_one, sx_two)
        cross = cross_faces(sz, *xr, sy_lo, sy_hi, after=after)
        yr = swap_faces("gy", *cross)
        return [*xr, *yr], cross

    qt, *face_rows = sum_matrices(sz, proj, cells)
    halos, cross = exchange_xy(*faces, after=[qt])
    q, leaving = flip_matrix(sz, qt, face_rows, [cross[0]])
    qfaces = []
    for j, shift in enumerate(link_shifts(sz)):
        home = [(target, source) for source, target in ring[shift]]
        qfaces.append(lax.ppermute(leaving[j], "gz", home))

    def make_matrices(after):
        return turn_matrices(
            sz,
            cell_matrix,
            jnp.transpose(cell_potential, (1, 2, 3, 0)).reshape(len(sz.cells), nodes),
            slot_atom.reshape(devices, POS),
            jnp.transpose(coupling, (1, 2, 0)),
            face_rows,
            after,
        )

    mapping = []
    if not sz.pair:
        kin, pot, back, c_hi, c_lo, *others = make_matrices([])
        factors, mapping = [c_hi, c_lo], [*qfaces, *others]

    fields, scale = [], 1.0 / half_width
    weight = 0.0
    for step in range(STEPS):
        y, own, messages = project(sz, r, weight, fields, halos, q, mapping)
        received = [lax.ppermute(m, "gz", ring[s + 1]) for s, m in enumerate(messages)]
        if sz.pair and step == 0:
            kin, pot, back, c_hi, c_lo, *factors = make_matrices([own[0]])
        own = couple_own(sz, own, qfaces, back, c_hi, c_lo)
        r, y, faces = apply(sz, y, own, received, factors, qt, kin, pot, scale)
        fields, weight = [y] + fields[:1], -center_value * scale
        scale = 2.0 / half_width
        halos, _ = exchange_xy(*faces)
    r, sent = last_faces(sz, r, halos)
    zr = [lax.ppermute(f, "gz", ring[s]) for f, s in zip(sent, link_shifts(sz))]
    return finish(sz, add_local(sz, r, weight, fields), zr, nz)


def solution(mesh):
    in_specs = (
        P("gx", "gy", "gz", None),
        P(),
        P(None, "gx", "gy", "gz"),
        P("gx", "gy", "gz", None, None),
        P("gx", "gy", None, None),
        P("gx", "gy", "gz", None, None),
        P(("gx", "gy"), None, None),
    )
    out_specs = P("gx", "gy", "gz", None)
    return jax.shard_map(local, mesh=mesh, in_specs=in_specs, out_specs=out_specs, check_vma=False)
```

```python
import functools

import jax
import jax.numpy as jnp
import numpy as np
from jax import lax
from jax.experimental import pallas as pl
from jax.experimental.pallas import tpu as pltpu
from jax.sharding import PartitionSpec as P

ORDER = 6
STEPS = 3
PA = 12
POS = 32
BLK = 4

center_value = 2.0
half_width = 3.0

EDGE = ORDER + 1
PAD = 8
SLOTS = POS * PA
F32 = jnp.float32
BF16 = jnp.bfloat16
HALO = jnp.bfloat16


def up(value, multiple):
    return -(-value // multiple) * multiple


class Sizes:
    def __init__(self, nx, ny, nz, orbitals, shifts):
        assert nz == EDGE
        self.nx, self.ny, self.orb = nx, ny, orbitals
        self.cells = [(p, q) for p in range((nx - 1) // ORDER) for q in range((ny - 1) // ORDER)]
        self.rows = nx * ny * PAD
        self.line_x = ny * PAD
        self.xface = up(ny * PAD, 16)
        self.yface = up(nx * PAD, 16)
        self.face_b = up(ny, PAD)
        self.zface = up(nx * self.face_b, 16)
        self.cell_rows = EDGE * EDGE * PAD
        self.cell_pad = up(self.cell_rows, 16)
        self.all_pad = up(self.cell_pad * len(self.cells), 128)
        self.fcell = EDGE * PAD
        self.fall = up(self.fcell * len(self.cells), 16)
        self.shifts, self.links = shifts, min(2, shifts)
        self.pair = shifts == 1
        self.rows_all = self.rows + (self.face_b - ny + 1) * PAD


VMEM = pl.BlockSpec(memory_space=pltpu.VMEM)


def kernel_call(body, outs, arrays, scratch=(), flops=0, limit=24 << 20, after=(), out_specs=None):
    used = len(arrays)

    def with_waits(*refs):
        body(*refs[:used], *refs[used + len(after) :])

    nbytes = sum(int(np.prod(a.shape)) * a.dtype.itemsize for a in list(arrays) + list(outs))
    return pl.pallas_call(
        with_waits,
        out_shape=outs,
        in_specs=[VMEM] * used + [pl.BlockSpec(memory_space=pl.ANY)] * len(after),
        out_specs=out_specs or [VMEM] * len(outs),
        scratch_shapes=list(scratch),
        compiler_params=pltpu.CompilerParams(vmem_limit_bytes=limit),
        cost_estimate=pl.CostEstimate(flops=flops, bytes_accessed=nbytes, transcendentals=0),
    )(*arrays, *after)


def shape(rows, cols, dtype):
    return jax.ShapeDtypeStruct((rows, cols), dtype)


def dot(a, b):
    return jnp.dot(a, b, preferred_element_type=F32)


FIRST = {"gx": 1, "gy": 0}


def if_first(axis, value, otherwise):
    return jnp.where(lax.rem(lax.axis_index(axis), 2) == FIRST[axis], value, otherwise)


def link_shifts(sz):
    return [1, sz.shifts][: sz.links]


def layer_sent(sz, j):
    if sz.links == 1:
        return jnp.where(lax.axis_index("gz") == 0, ORDER, 0)
    return [ORDER, 0][j]


def layer_received(sz, j):
    return layer_sent(sz, 0) if sz.links == 1 else [0, ORDER][j]


def link_valid(sz, j):
    if sz.links == 1:
        return None
    me = lax.axis_index("gz")
    return jnp.where(me < sz.shifts, 1, 0) if j == 0 else jnp.where(me > 0, 1, 0)


def iota(rows, cols, dim):
    return lax.broadcasted_iota(jnp.int32, (rows, cols), dim)


def twelfth(value):
    return (value * (2**19 // PA + 1)) >> 19


def node_key(i):
    low = i & (PAD - 1)
    return jnp.where((low < EDGE) & (i < EDGE * EDGE * PAD), (i >> 3) * EDGE + low, -1)


def dot_last(a, b, precision=None):
    dims = (((1,), (1,)), ((), ()))
    return lax.dot_general(a, b, dims, precision=precision, preferred_element_type=F32)


def dot_first(a, b):
    dims = (((0,), (0,)), ((), ()))
    return lax.dot_general(a, b, dims, preferred_element_type=F32)


def sum_body(sz, proj, cells, qt, *qt_faces):
    nodes, cols = proj.shape
    i = iota(cols, POS, 0)
    first = iota(cols, POS, 1) * (BLK * PA)
    in_slot = ((i >= first) & (i < first + BLK * PA)).astype(BF16)
    of_block = dot_last(in_slot, cells[...].astype(BF16))
    i = iota(cols, BLK, 0)
    block = twelfth(i)
    cell = jnp.sum(
        jnp.where((block & (BLK - 1)) == iota(cols, BLK, 1), of_block, 0.0), axis=1, keepdims=True
    )
    i, block = i[:, :1], block[:, :1]
    row = (block >> (BLK.bit_length() - 1)) * PA + (i - block * PA)
    halves, group, width = [], cols // 2, SLOTS // 2
    targets = len(sz.cells) * width
    for h in range(2):
        mine = slice(h * group, (h + 1) * group)
        key = cell[mine].astype(jnp.int32) * width + (row[mine] - h * width)
        pick = (key == iota(group, targets, 1)).astype(BF16)
        halves.append(dot(proj[:, mine], pick))
    parts = []
    for g in range(len(sz.cells)):
        parts += [half[:, g * width : (g + 1) * width] for half in halves]
    summed = jnp.concatenate(parts, axis=1).astype(BF16)
    keys = [node_key(iota(sz.cell_pad, nodes, 0))]
    for j in range(sz.links):
        keys.append(
            jnp.where(
                iota(PAD * PAD, nodes, 0) < sz.fcell,
                node_key(iota(PAD * PAD, nodes, 0)) * EDGE + layer_received(sz, j),
                -1,
            )
        )
        low = iota(PAD * PAD, nodes, 0) & (PAD - 1)
        keys[-1] = jnp.where(low < EDGE, keys[-1], -1)
    expand = (jnp.concatenate(keys, axis=0) == iota(sz.cell_pad + sz.links * PAD * PAD, nodes, 1))
    full = dot(expand.astype(BF16), summed)
    for g in range(len(sz.cells)):
        value = full[:, g * SLOTS : (g + 1) * SLOTS]
        qt[g * sz.cell_pad : (g + 1) * sz.cell_pad, :] = value[: sz.cell_pad].astype(BF16)
    rest = sz.all_pad - sz.cell_pad * len(sz.cells)
    if rest:
        qt[sz.cell_pad * len(sz.cells) :, :] = jnp.zeros((rest, SLOTS), BF16)
    for j, qf in enumerate(qt_faces):
        at = sz.cell_pad + j * PAD * PAD
        rows = [full[at : at + sz.fcell, g * SLOTS : (g + 1) * SLOTS] for g in range(len(sz.cells))]
        rest = sz.fall - sz.fcell * len(sz.cells)
        if rest:
            rows.append(jnp.zeros((rest, SLOTS), F32))
        qf[...] = jnp.concatenate(rows, axis=0).astype(BF16)


def sum_matrices(sz, proj, cells):
    outs = [shape(sz.all_pad, SLOTS, BF16)]
    outs += [shape(sz.fall, SLOTS, BF16)] * sz.links
    body = functools.partial(sum_body, sz)
    return kernel_call(body, outs, [proj, cells], flops=3 * 10**9, limit=32 << 20)


def slot_keys(sz, table, dim):
    exact = lax.Precision.HIGHEST
    shape2 = (SLOTS, POS) if dim == 0 else (POS, SLOTS)
    i, s = iota(*shape2, dim), iota(*shape2, 1 - dim)
    spread = ((i >= s * PA) & (i < s * PA + PA)).astype(F32)
    if dim == 0:
        atoms = dot_last(spread, table, exact)
    else:
        atoms = jnp.dot(table, spread, precision=exact, preferred_element_type=F32)
    devices = sz.shifts + 1
    at = iota(*atoms.shape, 1 - dim)
    me = lax.axis_index("gz")
    keys = []
    for shift in range(devices):
        chosen = jnp.where(at == lax.rem(me + shift, devices), atoms, 0.0)
        atom = jnp.sum(chosen, axis=1 - dim, keepdims=True).astype(jnp.int32)
        i = iota(*atom.shape, dim)
        keys.append((atom, jnp.where(atom >= 0, atom * PA + i - twelfth(i) * PA, -1)))
    return keys


def turn_body(sz, qt, kin, pot, atoms, coupling, *refs):
    own_rows, refs = (refs[0], refs[1:]) if sz.pair else (None, refs)
    q, kout, vout, back, c_hi, c_lo = refs[:6]
    *others, wide = refs[6:]
    q[...] = qt[...].T
    nodes = kin.shape[0]
    expand = (node_key(iota(sz.cell_pad, nodes, 0)) == iota(sz.cell_pad, nodes, 1)).astype(BF16)
    gather = (node_key(iota(nodes, sz.cell_pad, 1)) == iota(nodes, sz.cell_pad, 0)).astype(BF16)
    tall = dot(expand, kin[...]).astype(BF16)
    kout[...] = dot(tall, gather).astype(BF16)
    value, values = pot[...], 0.0
    for _ in range(3):
        part = value.astype(BF16)
        values = values + dot_last(expand, part)
        value = value - part.astype(F32)
    for g in range(len(sz.cells)):
        vout[g * sz.cell_pad : (g + 1) * sz.cell_pad, :] = jnp.broadcast_to(
            values[:, g : g + 1], (sz.cell_pad, sz.orb)
        )
    table = atoms[...].astype(F32)
    rows, cols = slot_keys(sz, table, 0), slot_keys(sz, table, 1)
    known = [jnp.where(cols[0][1] >= 0, cols[0][1], -2)]
    for j, shift in enumerate(link_shifts(sz)):
        key = jnp.where(cols[shift][1] >= 0, cols[shift][1], -2)
        valid = link_valid(sz, j)
        known.append(key if valid is None else jnp.where(valid == 1, key, -2))
    for s in range(0 if sz.pair else sz.shifts):
        maps = others[0]
        for j, key in enumerate(known):
            maps[s * SLOTS : (s + 1) * SLOTS, j * SLOTS : (j + 1) * SLOTS] = (
                rows[s + 1][1] == key
            ).astype(BF16)
    for j, key in enumerate(known[1:]):
        back[:, j * SLOTS : (j + 1) * SLOTS] = (rows[0][1] == key).astype(BF16)
    pa, pb, atom_count = coupling.shape
    wide[...] = jnp.zeros(wide.shape, F32)
    wide[:, :pb, :] = coupling[...]
    table2 = wide[...].reshape(pa * 16, atom_count)
    hot = (rows[0][0] == iota(SLOTS, atom_count, 1)).astype(BF16)
    i, lane = iota(SLOTS, pa * 16, 0), iota(SLOTS, pa * 16, 1)
    own_row = (lane >> 4) == i - twelfth(i) * PA
    lane, j = iota(pa * 16, SLOTS, 0), iota(pa * 16, SLOTS, 1)
    fold = ((lane & 15) == j - twelfth(j) * PA).astype(BF16)
    same = twelfth(iota(SLOTS, SLOTS, 0)) == twelfth(iota(SLOTS, SLOTS, 1))
    for out in (c_hi, c_lo):
        part = table2.astype(BF16)
        table2 = table2 - part.astype(F32)
        picked = jnp.where(own_row, dot_last(hot, part), 0.0).astype(BF16)
        out[...] = jnp.where(same, dot(picked, fold), 0.0).astype(BF16)
    if sz.pair:
        m_hi, m_lo, c_rows = others
        m_hi[...] = dot(c_hi[...], back[...]).astype(BF16)
        m_lo[...] = dot(c_lo[...], back[...]).astype(BF16)
        c_rows[...] = (dot_last(c_hi[...], own_rows[...]) + dot_last(c_lo[...], own_rows[...])).astype(BF16)


def turn_matrices(sz, qt, kin, pot, atoms, coupling, face_rows):
    known = (1 + sz.links) * SLOTS
    outs = [
        shape(SLOTS, sz.all_pad, BF16),
        shape(sz.cell_pad, sz.cell_pad, BF16),
        shape(len(sz.cells) * sz.cell_pad, sz.orb, F32),
        shape(SLOTS, sz.links * SLOTS, BF16),
        shape(SLOTS, SLOTS, BF16),
        shape(SLOTS, SLOTS, BF16),
    ]
    if sz.pair:
        outs += [shape(SLOTS, SLOTS, BF16)] * 2 + [shape(SLOTS, sz.fall, BF16)]
    else:
        outs += [shape(sz.shifts * SLOTS, known, BF16)]
    limit = (32 << 20) if sz.shifts < 8 else (56 << 20)
    return kernel_call(
        functools.partial(turn_body, sz),
        outs,
        [qt, kin, pot, atoms, coupling] + (face_rows if sz.pair else []),
        scratch=[pltpu.VMEM((coupling.shape[0], 16, coupling.shape[2]), F32)],
        flops=10**9,
        limit=limit,
    )


def cell_block(sz, z, cell):
    p, q = cell
    layers = []
    for a in range(EDGE):
        start = (ORDER * p + a) * sz.line_x + ORDER * q * PAD
        layers.append(z[start : start + EDGE * PAD, :])
    layers.append(jnp.zeros((sz.cell_pad - sz.cell_rows, sz.orb), F32))
    return jnp.concatenate(layers, axis=0)


def write_pair(axis, low, high, first, second):
    first[...] = if_first(axis, high, low).astype(first.dtype)
    second[...] = if_first(axis, low, high).astype(second.dtype)


def read_pair(axis, first, second):
    one, two = first[...].astype(F32), second[...].astype(F32)
    low, high = if_first(axis, two, one), if_first(axis, one, two)
    at, last = lax.axis_index(axis), lax.axis_size(axis) - 1
    return jnp.where(at > 0, low, 0.0), jnp.where(at < last, high, 0.0)


def write_faces(sz, r, sx_one, sx_two, sy_lo, sy_hi):
    pad_x = jnp.zeros((sz.xface - sz.line_x, sz.orb), F32)
    pad_y = jnp.zeros((sz.yface - sz.nx * PAD, sz.orb), F32)
    last = (sz.nx - 1) * sz.line_x
    low = jnp.concatenate([r[0 : sz.line_x, :], pad_x], axis=0)
    high = jnp.concatenate([r[last : last + sz.line_x, :], pad_x], axis=0)
    write_pair("gx", low, high, sx_one, sx_two)
    for out, b in ((sy_lo, 0), (sy_hi, sz.ny - 1)):
        rows = [r[a * sz.line_x + b * PAD : a * sz.line_x + (b + 1) * PAD, :] for a in range(sz.nx)]
        out[...] = jnp.concatenate(rows + [pad_y], axis=0)


def face_outs(sz):
    return [shape(sz.xface, sz.orb, HALO)] * 2 + [shape(sz.yface, sz.orb, F32)] * 2


def start_body(sz, parts, cells, r, cells_out, *faces):
    cells_out[...] = cells[...].astype(F32)
    nz = parts.shape[2]
    r[...] = jnp.zeros(r.shape, F32)
    for a in range(sz.nx):
        for b in range(sz.ny):
            at = a * sz.line_x + b * PAD
            r[at : at + nz, :] = parts[a, b]
    write_faces(sz, r, *faces)


def start_faces(sz, parts, cells, after):
    outs = [shape(sz.rows_all, sz.orb, F32), shape(*cells.shape, F32)] + face_outs(sz)
    body = functools.partial(start_body, sz)
    r, cells, *faces = kernel_call(body, outs, [parts, cells], after=after)
    return r, cells, faces


def cross_body(sz, xr_one, xr_two, ry_lo, ry_hi, sy_one, sy_two):
    last = (sz.nx - 1) * PAD
    lo, hi = read_pair("gx", xr_one, xr_two)
    faces = []
    for raw, b in ((ry_lo, 0), (ry_hi, sz.ny - 1)):
        value = raw[...]
        parts = [
            value[:PAD] + lo[b * PAD : (b + 1) * PAD],
            value[PAD:last],
            value[last : last + PAD] + hi[b * PAD : (b + 1) * PAD],
            value[last + PAD :],
        ]
        faces.append(jnp.concatenate(parts, axis=0))
    write_pair("gy", *faces, sy_one, sy_two)


def cross_faces(sz, *faces):
    outs = [shape(sz.yface, sz.orb, HALO)] * 2
    return kernel_call(functools.partial(cross_body, sz), outs, list(faces))


def add_xy(sz, ra, xr_one, xr_two, yr_one, yr_two):
    last = (sz.nx - 1) * sz.line_x
    low, high = read_pair("gx", xr_one, xr_two)
    ra[0 : sz.line_x, :] += low[: sz.line_x]
    ra[last : last + sz.line_x, :] += high[: sz.line_x]
    for value, b in zip(read_pair("gy", yr_one, yr_two), (0, sz.ny - 1)):
        for a in range(sz.nx):
            at = a * sz.line_x + b * PAD
            ra[at : at + PAD, :] += value[a * PAD : (a + 1) * PAD]


def local_term(weight, fields, at):
    value = weight * fields[0][at, :]
    return value - fields[1][at, :] if len(fields) > 1 else value


def layer_rows(y, weight, fields, at):
    rows = pl.ds(at, PAD, stride=PAD)
    return y[rows, :] - local_term(weight, fields, rows) if fields else y[rows, :]


def pack_z(sz, y, weight, fields, j):
    rows, c = [], layer_sent(sz, j)
    for a in range(sz.nx):
        for b in range(0, sz.face_b, PAD):
            rows.append(layer_rows(y, weight, fields, a * sz.line_x + b * PAD + c))
    rest = sz.zface - sz.nx * sz.face_b
    if rest:
        rows.append(jnp.zeros((rest, sz.orb), F32))
    value, valid = jnp.concatenate(rows, axis=0), link_valid(sz, j)
    return (value if valid is None else value * valid.astype(F32)).astype(HALO)


def add_z(sz, y, j, face):
    c = layer_received(sz, j)
    for a in range(sz.nx):
        for b in range(0, sz.ny, PAD):
            n = min(PAD, sz.ny - b)
            at = pl.ds(a * sz.line_x + b * PAD + c, n, stride=PAD)
            y[at, :] = y[at, :] + face[a * sz.face_b + b : a * sz.face_b + b + n]


def face_cells(sz, y, weight, fields, j):
    rows, c = [], layer_sent(sz, j)
    for p, q in sz.cells:
        for a in range(EDGE):
            at = (ORDER * p + a) * sz.line_x + ORDER * q * PAD
            rows.append(layer_rows(y, weight, fields, at + c))
    rest = sz.fall - sz.fcell * len(sz.cells)
    if rest:
        rows.append(jnp.zeros((rest, sz.orb), F32))
    return jnp.concatenate(rows, axis=0).astype(BF16)


def message_cells(sz, face):
    rows = []
    for p, q in sz.cells:
        for a in range(EDGE):
            at = (ORDER * p + a) * sz.face_b + ORDER * q
            rows.append(face[at : at + PAD])
    rest = sz.fall - sz.fcell * len(sz.cells)
    if rest:
        rows.append(jnp.zeros((rest, sz.orb), F32))
    return jnp.concatenate(rows, axis=0).astype(BF16)


def project_body(sz, weight, past, refs):
    take = iter(refs)
    r = next(take)
    fields = [next(take) for _ in range(past)]
    halos = [next(take) for _ in range(4)]
    q = next(take)
    if not sz.pair:
        qfaces = [next(take) for _ in range(sz.links)]
        maps = next(take)
    y, own = next(take), next(take)
    beside = [next(take) for _ in range(sz.links)]
    messages = [next(take) for _ in range(sz.shifts)]
    everything = slice(0, sz.rows_all)
    y[...] = r[...] + local_term(weight, fields, everything) if past else r[...]
    add_xy(sz, y, *halos)
    blocks = [cell_block(sz, y, cell).astype(BF16) for cell in sz.cells]
    rest = sz.all_pad - sz.cell_pad * len(sz.cells)
    if rest:
        blocks.append(jnp.zeros((rest, sz.orb), BF16))
    sums = dot(q[...], jnp.concatenate(blocks, axis=0))
    own[...] = sums
    if sz.pair:
        messages[0][0:SLOTS, :] = sums.astype(HALO)
        messages[0][SLOTS : SLOTS + sz.zface, :] = pack_z(sz, y, weight, fields, 0)
        beside[0][...] = face_cells(sz, y, weight, fields, 0)
        return
    known = [sums.astype(BF16)]
    for j, matrix in enumerate(qfaces):
        value, valid = dot_first(matrix[...], face_cells(sz, y, weight, fields, j)), link_valid(sz, j)
        beside[j][...] = (value if valid is None else value * valid.astype(F32)).astype(BF16)
        known.append(beside[j][...])
    shift_of = link_shifts(sz)
    for s, message in enumerate(messages):
        rows = slice(s * SLOTS, (s + 1) * SLOTS)
        mapped = [0] + [j + 1 for j, shift in enumerate(shift_of) if shift != s + 1]
        direct = [j for j, shift in enumerate(shift_of) if shift == s + 1]
        total = sum(dot(maps[rows, k * SLOTS : (k + 1) * SLOTS], known[k]) for k in mapped)
        for j in direct:
            total = total + known[j + 1].astype(F32)
            message[SLOTS : SLOTS + sz.zface, :] = pack_z(sz, y, weight, fields, j)
        message[0:SLOTS, :] = total.astype(HALO)


def project(sz, r, weight, fields, halos, q, mapping):
    outs = [shape(sz.rows_all, sz.orb, F32), shape(SLOTS, sz.orb, F32)]
    outs += [shape(sz.fall if sz.pair else SLOTS, sz.orb, BF16)] * sz.links
    for s in range(1, sz.shifts + 1):
        outs.append(shape(SLOTS + (sz.zface if s in link_shifts(sz) else 0), sz.orb, HALO))

    def body(*refs):
        project_body(sz, weight, len(fields), refs)

    y, own, *rest = kernel_call(
        body,
        outs,
        [r, *fields, *halos, q, *mapping],
        flops=4 * 10**8,
        limit=(32 << 20) if sz.shifts < 8 else (56 << 20),
    )
    return y, [own, *rest[: sz.links]], rest[sz.links :]


def couple(c_hi, c_lo, totals):
    high = totals.astype(BF16)
    low = (totals - high.astype(F32)).astype(BF16)
    return dot(c_hi[...], high) + (dot(c_hi[...], low) + dot(c_lo[...], high))


def couple_body(sz, own, *refs):
    beside = refs[: sz.links]
    *rows, back, c_hi, c_lo, coupled = refs[sz.links :]
    totals = own[...]
    for j, part in enumerate(beside):
        value = part[...]
        if sz.pair:
            value = dot_first(rows[0][...], value).astype(BF16)
        totals = totals + dot(back[:, j * SLOTS : (j + 1) * SLOTS], value)
    coupled[...] = couple(c_hi, c_lo, totals)


def couple_own(sz, own, qfaces, back, c_hi, c_lo):
    outs = [shape(SLOTS, sz.orb, F32)]
    body = functools.partial(couple_body, sz)
    arrays = [*own, *(qfaces if sz.pair else []), back, c_hi, c_lo]
    return kernel_call(body, outs, arrays, flops=2 * 10**8)[0]


def apply_body(sz, scale, refs):
    take = iter(refs)
    yin, own = next(take), next(take)
    messages = [next(take) for _ in range(sz.shifts)]
    factors = [next(take) for _ in range(3 if sz.pair else 2)]
    qt, kin, pot = [next(take) for _ in range(3)]
    r, y = next(take), next(take)
    faces = [next(take) for _ in range(4)]
    if sz.pair:
        m_hi, m_lo, c_rows = factors
        sums, message = messages[0][0:SLOTS, :].astype(BF16), messages[0]
        face = message[SLOTS : SLOTS + sz.zface, :].astype(F32)
        coef = dot(m_hi[...], sums) + dot(m_lo[...], sums)
        coef = own[...] + (coef + dot(c_rows[...], message_cells(sz, face)))
    else:
        totals = sum(message[0:SLOTS, :].astype(F32) for message in messages)
        coef = own[...] + couple(*factors, totals)
    coef = coef.astype(BF16)
    y[...] = yin[...]
    for j, shift in enumerate(link_shifts(sz)):
        add_z(sz, y, j, messages[shift - 1][SLOTS : SLOTS + sz.zface, :].astype(F32))
    blocks = [cell_block(sz, y, cell) for cell in sz.cells]
    stiff = dot(kin[...], jnp.concatenate([b.astype(BF16) for b in blocks], axis=1))
    spread = dot(qt[: sz.cell_pad * len(sz.cells), :], coef)
    for g, (p, q) in enumerate(sz.cells):
        rows = slice(g * sz.cell_pad, (g + 1) * sz.cell_pad)
        value = stiff[:, g * sz.orb : (g + 1) * sz.orb] + pot[rows, :] * blocks[g]
        value = (value + spread[rows]) * scale
        for a in range(EDGE):
            start = (ORDER * p + a) * sz.line_x + ORDER * q * PAD
            line = value[a * EDGE * PAD : (a + 1) * EDGE * PAD]
            shared = EDGE * PAD if p and a == 0 else PAD if q else 0
            if shared:
                r[start : start + shared, :] += line[:shared]
            if shared < EDGE * PAD:
                r[start + shared : start + EDGE * PAD, :] = line[shared:]
    r[sz.rows :, :] = jnp.zeros((sz.rows_all - sz.rows, sz.orb), F32)
    write_faces(sz, r, *faces)


def apply(sz, y, own, messages, factors, qt, kin, pot, scale):
    outs = [shape(sz.rows_all, sz.orb, F32)] * 2 + face_outs(sz)
    arrays = [y, own, *messages, *factors, qt, kin, pot]

    def body(*refs):
        apply_body(sz, scale, refs)

    r, y, *faces = kernel_call(body, outs, arrays, flops=6 * 10**8, limit=32 << 20)
    return r, y, faces


def last_faces_body(sz, refs):
    take = iter(refs)
    r = next(take)
    halos = [next(take) for _ in range(4)]
    ra = next(take)
    outs = [next(take) for _ in range(sz.links)]
    ra[...] = r[...]
    add_xy(sz, ra, *halos)
    for j, out in enumerate(outs):
        out[...] = pack_z(sz, ra, None, [], j)


def last_faces(sz, r, halos):
    def body(*refs):
        last_faces_body(sz, refs)

    outs = [shape(sz.rows_all, sz.orb, F32)] + [shape(sz.zface, sz.orb, HALO)] * sz.links
    ra, *sent = kernel_call(body, outs, [r, *halos])
    return ra, sent


def add_local_body(weight, past, r, *refs):
    fields, out = refs[:past], refs[past]
    out[...] = r[...] + local_term(weight, fields, slice(0, out.shape[0]))


def add_local(sz, r, weight, fields):
    body = functools.partial(add_local_body, weight, len(fields))
    return kernel_call(body, [shape(sz.rows_all, sz.orb, F32)], [r, *fields])[0]


def finish_body(sz, r, *refs):
    zr = refs[: sz.links]
    out, ra, block, sent = refs[sz.links :]
    ra[...] = r[...]
    for j, face in enumerate(zr):
        add_z(sz, ra, j, face[...].astype(F32))
    nz = block.shape[2]
    pieces, copies = 3, []
    for k in range(pieces):
        first, last = k * sz.nx // pieces, (k + 1) * sz.nx // pieces
        value = ra[first * sz.line_x : last * sz.line_x, :]
        value = value.reshape(last - first, sz.ny, PAD, sz.orb)[:, :, :nz, :]
        block[first:last] = value
        copy = pltpu.make_async_copy(block.at[first:last], out.at[first:last], sent.at[k])
        copy.start()
        copies.append(copy)
    for copy in copies:
        copy.wait()


def finish(sz, r, zr, nz):
    outs = [jax.ShapeDtypeStruct((sz.nx, sz.ny, nz, sz.orb), F32)]
    scratch = [
        pltpu.VMEM((sz.rows_all, sz.orb), F32),
        pltpu.VMEM((sz.nx, sz.ny, nz, sz.orb), F32),
        pltpu.SemaphoreType.DMA((3,)),
    ]
    body = functools.partial(finish_body, sz)
    anywhere = [pl.BlockSpec(memory_space=pl.ANY)]
    return kernel_call(body, outs, [r, *zr], scratch=scratch, out_specs=anywhere)[0]


def swap_faces(axis, one, two):
    axes = ("gx", "gy")
    wide, deep = lax.axis_size("gx"), lax.axis_size("gy")
    count = wide if axis == "gx" else deep

    def partner(i, j, low):
        at = i if axis == "gx" else j
        to = at + 1 if at % 2 == low else at - 1
        if 0 <= to < count:
            return (to, j) if axis == "gx" else (i, to)
        if axis == "gy" and wide % 2 == 0:
            return (i ^ 1, j)
        ends = sorted({k for k in range(count) if not 0 <= k + (1 if k % 2 == low else -1) < count})
        to = ends[::-1][ends.index(at)]
        return (to, j) if axis == "gx" else (i, to)

    out = []
    for face, low in ((one, FIRST[axis]), (two, 1 - FIRST[axis])):
        pairs = []
        for i in range(wide):
            for j in range(deep):
                to = partner(i, j, low)
                pairs.append((i * deep + j, to[0] * deep + to[1]))
        out.append(lax.ppermute(face, axes, pairs))
    return out


def local(parts, cell_matrix, cell_potential, projectors, slot_atom, slot_cells, coupling):
    nx, ny, nz, orbitals = parts.shape
    nodes = cell_matrix.shape[0]
    devices = lax.axis_size("gz")
    sz = Sizes(nx, ny, nz, orbitals, devices - 1)
    ring = [[(i, (i + s) % devices) for i in range(devices)] for s in range(devices)]

    proj = projectors.reshape(nodes, POS * BLK * PA)
    proj = jnp.pad(proj, ((0, up(nodes, 16) - nodes), (0, 0)))
    cells = jnp.transpose(slot_cells.reshape(POS, BLK))
    r, cells, faces = start_faces(sz, parts, cells, [proj])

    def exchange_xy(sx_one, sx_two, sy_lo, sy_hi):
        xr = swap_faces("gx", sx_one, sx_two)
        cross = cross_faces(sz, *xr, sy_lo, sy_hi)
        yr = swap_faces("gy", *cross)
        return (*xr, *yr)

    halos = exchange_xy(*faces)
    qt, *face_rows = sum_matrices(sz, proj, cells)
    qfaces = []
    for j, shift in enumerate(link_shifts(sz)):
        back = [(target, source) for source, target in ring[shift]]
        qfaces.append(lax.ppermute(face_rows[j], "gz", back))
    pot = jnp.transpose(cell_potential, (1, 2, 3, 0)).reshape(len(sz.cells), nodes)
    q, kin, pot, back, c_hi, c_lo, *others = turn_matrices(
        sz,
        qt,
        cell_matrix,
        pot,
        slot_atom.reshape(devices, POS),
        jnp.transpose(coupling, (1, 2, 0)),
        face_rows,
    )
    factors = others if sz.pair else [c_hi, c_lo]
    mapping = [] if sz.pair else [*qfaces, *others]

    fields, scale = [], 1.0 / half_width
    weight = 0.0
    for step in range(STEPS):
        y, own, messages = project(sz, r, weight, fields, halos, q, mapping)
        received = [lax.ppermute(m, "gz", ring[s + 1]) for s, m in enumerate(messages)]
        own = couple_own(sz, own, qfaces, back, c_hi, c_lo)
        r, y, faces = apply(sz, y, own, received, factors, qt, kin, pot, scale)
        fields, weight = [y] + fields[:1], -center_value * scale
        scale = 2.0 / half_width
        halos = exchange_xy(*faces)
    r, sent = last_faces(sz, r, halos)
    zr = [lax.ppermute(f, "gz", ring[s]) for f, s in zip(sent, link_shifts(sz))]
    return finish(sz, add_local(sz, r, weight, fields), zr, nz)


def solution(mesh):
    in_specs = (
        P("gx", "gy", "gz", None),
        P(),
        P(None, "gx", "gy", "gz"),
        P("gx", "gy", "gz", None, None),
        P("gx", "gy", None, None),
        P("gx", "gy", "gz", None, None),
        P(("gx", "gy"), None, None),
    )
    out_specs = P("gx", "gy", "gz", None)
    return jax.shard_map(local, mesh=mesh, in_specs=in_specs, out_specs=out_specs, check_vma=False)
```

```python
import functools

import jax
import jax.numpy as jnp
import numpy as np
from jax import lax
from jax.experimental import pallas as pl
from jax.experimental.pallas import tpu as pltpu
from jax.sharding import PartitionSpec as P

ORDER = 6
STEPS = 3
PA = 12
POS = 32
BLK = 4

center_value = 2.0
half_width = 3.0

EDGE = ORDER + 1
PAD = 8
SLOTS = POS * PA
F32 = jnp.float32
BF16 = jnp.bfloat16
HALO = jnp.bfloat16


def up(value, multiple):
    return -(-value // multiple) * multiple


class Sizes:
    def __init__(self, nx, ny, nz, orbitals, shifts):
        assert nz == EDGE
        self.nx, self.ny, self.orb = nx, ny, orbitals
        self.cells = [(p, q) for p in range((nx - 1) // ORDER) for q in range((ny - 1) // ORDER)]
        self.rows = nx * ny * PAD
        self.line_x = ny * PAD
        self.xface = up(ny * PAD, 16)
        self.yface = up(nx * PAD, 16)
        self.face_b = up(ny, PAD)
        self.zface = up(nx * self.face_b, 16)
        self.cell_rows = EDGE * EDGE * PAD
        self.cell_pad = up(self.cell_rows, 16)
        self.all_pad = up(self.cell_pad * len(self.cells), 128)
        self.fcell = EDGE * PAD
        self.fall = up(self.fcell * len(self.cells), 16)
        self.shifts, self.links = shifts, min(2, shifts)
        self.pair = shifts == 1
        self.rows_all = self.rows + (self.face_b - ny + 1) * PAD


VMEM = pl.BlockSpec(memory_space=pltpu.VMEM)


def kernel_call(body, outs, arrays, scratch=(), flops=0, limit=24 << 20, after=(), out_specs=None):
    used = len(arrays)

    def with_waits(*refs):
        body(*refs[:used], *refs[used + len(after) :])

    nbytes = sum(int(np.prod(a.shape)) * a.dtype.itemsize for a in list(arrays) + list(outs))
    return pl.pallas_call(
        with_waits,
        out_shape=outs,
        in_specs=[VMEM] * used + [pl.BlockSpec(memory_space=pl.ANY)] * len(after),
        out_specs=out_specs or [VMEM] * len(outs),
        scratch_shapes=list(scratch),
        compiler_params=pltpu.CompilerParams(vmem_limit_bytes=limit),
        cost_estimate=pl.CostEstimate(flops=flops, bytes_accessed=nbytes, transcendentals=0),
    )(*arrays, *after)


def shape(rows, cols, dtype):
    return jax.ShapeDtypeStruct((rows, cols), dtype)


def dot(a, b):
    return jnp.dot(a, b, preferred_element_type=F32)


FIRST = {"gx": 1, "gy": 0}


def if_first(axis, value, otherwise):
    return jnp.where(lax.rem(lax.axis_index(axis), 2) == FIRST[axis], value, otherwise)


def link_shifts(sz):
    return [1, sz.shifts][: sz.links]


def layer_sent(sz, j):
    if sz.links == 1:
        return jnp.where(lax.axis_index("gz") == 0, ORDER, 0)
    return [ORDER, 0][j]


def layer_received(sz, j):
    return layer_sent(sz, 0) if sz.links == 1 else [0, ORDER][j]


def link_valid(sz, j):
    if sz.links == 1:
        return None
    me = lax.axis_index("gz")
    return jnp.where(me < sz.shifts, 1, 0) if j == 0 else jnp.where(me > 0, 1, 0)


def iota(rows, cols, dim):
    return lax.broadcasted_iota(jnp.int32, (rows, cols), dim)


def twelfth(value):
    return (value * (2**19 // PA + 1)) >> 19


def node_key(i):
    low = i & (PAD - 1)
    return jnp.where((low < EDGE) & (i < EDGE * EDGE * PAD), (i >> 3) * EDGE + low, -1)


def dot_last(a, b, precision=None):
    dims = (((1,), (1,)), ((), ()))
    return lax.dot_general(a, b, dims, precision=precision, preferred_element_type=F32)


def dot_first(a, b):
    dims = (((0,), (0,)), ((), ()))
    return lax.dot_general(a, b, dims, preferred_element_type=F32)


def sum_body(sz, proj, cells, qt, *qt_faces):
    nodes, cols = proj.shape
    i = iota(cols, POS, 0)
    first = iota(cols, POS, 1) * (BLK * PA)
    in_slot = ((i >= first) & (i < first + BLK * PA)).astype(BF16)
    of_block = dot_last(in_slot, cells[...].astype(BF16))
    i = iota(cols, BLK, 0)
    block = twelfth(i)
    cell = jnp.sum(
        jnp.where((block & (BLK - 1)) == iota(cols, BLK, 1), of_block, 0.0), axis=1, keepdims=True
    )
    i, block = i[:, :1], block[:, :1]
    row = (block >> (BLK.bit_length() - 1)) * PA + (i - block * PA)
    halves, group, width = [], cols // 2, SLOTS // 2
    targets = len(sz.cells) * width
    for h in range(2):
        mine = slice(h * group, (h + 1) * group)
        key = cell[mine].astype(jnp.int32) * width + (row[mine] - h * width)
        pick = (key == iota(group, targets, 1)).astype(BF16)
        halves.append(dot(proj[:, mine], pick))
    parts = []
    for g in range(len(sz.cells)):
        parts += [half[:, g * width : (g + 1) * width] for half in halves]
    summed = jnp.concatenate(parts, axis=1).astype(BF16)
    keys = [node_key(iota(sz.cell_pad, nodes, 0))]
    for j in range(sz.links):
        keys.append(
            jnp.where(
                iota(PAD * PAD, nodes, 0) < sz.fcell,
                node_key(iota(PAD * PAD, nodes, 0)) * EDGE + layer_received(sz, j),
                -1,
            )
        )
        low = iota(PAD * PAD, nodes, 0) & (PAD - 1)
        keys[-1] = jnp.where(low < EDGE, keys[-1], -1)
    expand = (jnp.concatenate(keys, axis=0) == iota(sz.cell_pad + sz.links * PAD * PAD, nodes, 1))
    full = dot(expand.astype(BF16), summed)
    for g in range(len(sz.cells)):
        value = full[:, g * SLOTS : (g + 1) * SLOTS]
        qt[g * sz.cell_pad : (g + 1) * sz.cell_pad, :] = value[: sz.cell_pad].astype(BF16)
    rest = sz.all_pad - sz.cell_pad * len(sz.cells)
    if rest:
        qt[sz.cell_pad * len(sz.cells) :, :] = jnp.zeros((rest, SLOTS), BF16)
    for j, qf in enumerate(qt_faces):
        at = sz.cell_pad + j * PAD * PAD
        rows = [full[at : at + sz.fcell, g * SLOTS : (g + 1) * SLOTS] for g in range(len(sz.cells))]
        rest = sz.fall - sz.fcell * len(sz.cells)
        if rest:
            rows.append(jnp.zeros((rest, SLOTS), F32))
        qf[...] = jnp.concatenate(rows, axis=0).astype(BF16)


def sum_matrices(sz, proj, cells):
    outs = [shape(sz.all_pad, SLOTS, BF16)]
    outs += [shape(sz.fall, SLOTS, BF16)] * sz.links
    body = functools.partial(sum_body, sz)
    return kernel_call(body, outs, [proj, cells], flops=3 * 10**9, limit=32 << 20)


def slot_keys(sz, table, dim):
    exact = lax.Precision.HIGHEST
    shape2 = (SLOTS, POS) if dim == 0 else (POS, SLOTS)
    i, s = iota(*shape2, dim), iota(*shape2, 1 - dim)
    spread = ((i >= s * PA) & (i < s * PA + PA)).astype(F32)
    if dim == 0:
        atoms = dot_last(spread, table, exact)
    else:
        atoms = jnp.dot(table, spread, precision=exact, preferred_element_type=F32)
    devices = sz.shifts + 1
    at = iota(*atoms.shape, 1 - dim)
    me = lax.axis_index("gz")
    keys = []
    for shift in range(devices):
        chosen = jnp.where(at == lax.rem(me + shift, devices), atoms, 0.0)
        atom = jnp.sum(chosen, axis=1 - dim, keepdims=True).astype(jnp.int32)
        i = iota(*atom.shape, dim)
        keys.append((atom, jnp.where(atom >= 0, atom * PA + i - twelfth(i) * PA, -1)))
    return keys


def turn_body(sz, qt, kin, pot, atoms, coupling, *refs):
    own_rows, refs = (refs[0], refs[1:]) if sz.pair else (None, refs)
    q, kout, vout, back, c_hi, c_lo = refs[:6]
    *others, wide = refs[6:]
    q[...] = qt[...].T
    nodes = kin.shape[0]
    expand = (node_key(iota(sz.cell_pad, nodes, 0)) == iota(sz.cell_pad, nodes, 1)).astype(BF16)
    gather = (node_key(iota(nodes, sz.cell_pad, 1)) == iota(nodes, sz.cell_pad, 0)).astype(BF16)
    tall = dot(expand, kin[...]).astype(BF16)
    kout[...] = dot(tall, gather).astype(BF16)
    value, values = pot[...], 0.0
    for _ in range(3):
        part = value.astype(BF16)
        values = values + dot_last(expand, part)
        value = value - part.astype(F32)
    for g in range(len(sz.cells)):
        vout[g * sz.cell_pad : (g + 1) * sz.cell_pad, :] = jnp.broadcast_to(
            values[:, g : g + 1], (sz.cell_pad, sz.orb)
        )
    table = atoms[...].astype(F32)
    rows, cols = slot_keys(sz, table, 0), slot_keys(sz, table, 1)
    known = [jnp.where(cols[0][1] >= 0, cols[0][1], -2)]
    for j, shift in enumerate(link_shifts(sz)):
        key = jnp.where(cols[shift][1] >= 0, cols[shift][1], -2)
        valid = link_valid(sz, j)
        known.append(key if valid is None else jnp.where(valid == 1, key, -2))
    for s in range(0 if sz.pair else sz.shifts):
        maps = others[0]
        for j, key in enumerate(known):
            maps[s * SLOTS : (s + 1) * SLOTS, j * SLOTS : (j + 1) * SLOTS] = (
                rows[s + 1][1] == key
            ).astype(BF16)
    for j, key in enumerate(known[1:]):
        back[:, j * SLOTS : (j + 1) * SLOTS] = (rows[0][1] == key).astype(BF16)
    pa, pb, atom_count = coupling.shape
    wide[...] = jnp.zeros(wide.shape, F32)
    wide[:, :pb, :] = coupling[...]
    table2 = wide[...].reshape(pa * 16, atom_count)
    hot = (rows[0][0] == iota(SLOTS, atom_count, 1)).astype(BF16)
    i, lane = iota(SLOTS, pa * 16, 0), iota(SLOTS, pa * 16, 1)
    own_row = (lane >> 4) == i - twelfth(i) * PA
    lane, j = iota(pa * 16, SLOTS, 0), iota(pa * 16, SLOTS, 1)
    fold = ((lane & 15) == j - twelfth(j) * PA).astype(BF16)
    same = twelfth(iota(SLOTS, SLOTS, 0)) == twelfth(iota(SLOTS, SLOTS, 1))
    for out in (c_hi, c_lo):
        part = table2.astype(BF16)
        table2 = table2 - part.astype(F32)
        picked = jnp.where(own_row, dot_last(hot, part), 0.0).astype(BF16)
        out[...] = jnp.where(same, dot(picked, fold), 0.0).astype(BF16)
    if sz.pair:
        m_hi, m_lo, c_rows = others
        m_hi[...] = dot(c_hi[...], back[...]).astype(BF16)
        m_lo[...] = dot(c_lo[...], back[...]).astype(BF16)
        c_rows[...] = (dot_last(c_hi[...], own_rows[...]) + dot_last(c_lo[...], own_rows[...])).astype(BF16)


def turn_matrices(sz, qt, kin, pot, atoms, coupling, face_rows):
    known = (1 + sz.links) * SLOTS
    outs = [
        shape(SLOTS, sz.all_pad, BF16),
        shape(sz.cell_pad, sz.cell_pad, BF16),
        shape(len(sz.cells) * sz.cell_pad, sz.orb, F32),
        shape(SLOTS, sz.links * SLOTS, BF16),
        shape(SLOTS, SLOTS, BF16),
        shape(SLOTS, SLOTS, BF16),
    ]
    if sz.pair:
        outs += [shape(SLOTS, SLOTS, BF16)] * 2 + [shape(SLOTS, sz.fall, BF16)]
    else:
        outs += [shape(sz.shifts * SLOTS, known, BF16)]
    limit = (32 << 20) if sz.shifts < 8 else (56 << 20)
    return kernel_call(
        functools.partial(turn_body, sz),
        outs,
        [qt, kin, pot, atoms, coupling] + (face_rows if sz.pair else []),
        scratch=[pltpu.VMEM((coupling.shape[0], 16, coupling.shape[2]), F32)],
        flops=10**9,
        limit=limit,
    )


def cell_block(sz, z, cell):
    p, q = cell
    layers = []
    for a in range(EDGE):
        start = (ORDER * p + a) * sz.line_x + ORDER * q * PAD
        layers.append(z[start : start + EDGE * PAD, :])
    layers.append(jnp.zeros((sz.cell_pad - sz.cell_rows, sz.orb), F32))
    return jnp.concatenate(layers, axis=0)


def write_pair(axis, low, high, first, second):
    first[...] = if_first(axis, high, low).astype(first.dtype)
    second[...] = if_first(axis, low, high).astype(second.dtype)


def read_pair(axis, first, second):
    one, two = first[...].astype(F32), second[...].astype(F32)
    low, high = if_first(axis, two, one), if_first(axis, one, two)
    at, last = lax.axis_index(axis), lax.axis_size(axis) - 1
    return jnp.where(at > 0, low, 0.0), jnp.where(at < last, high, 0.0)


def write_faces(sz, r, sx_one, sx_two, sy_lo, sy_hi):
    pad_x = jnp.zeros((sz.xface - sz.line_x, sz.orb), F32)
    pad_y = jnp.zeros((sz.yface - sz.nx * PAD, sz.orb), F32)
    last = (sz.nx - 1) * sz.line_x
    low = jnp.concatenate([r[0 : sz.line_x, :], pad_x], axis=0)
    high = jnp.concatenate([r[last : last + sz.line_x, :], pad_x], axis=0)
    write_pair("gx", low, high, sx_one, sx_two)
    for out, b in ((sy_lo, 0), (sy_hi, sz.ny - 1)):
        rows = [r[a * sz.line_x + b * PAD : a * sz.line_x + (b + 1) * PAD, :] for a in range(sz.nx)]
        out[...] = jnp.concatenate(rows + [pad_y], axis=0)


def face_outs(sz):
    return [shape(sz.xface, sz.orb, HALO)] * 2 + [shape(sz.yface, sz.orb, F32)] * 2


def start_body(sz, parts, cells, r, cells_out, *faces):
    cells_out[...] = cells[...].astype(F32)
    nz = parts.shape[2]
    r[...] = jnp.zeros(r.shape, F32)
    for a in range(sz.nx):
        for b in range(sz.ny):
            at = a * sz.line_x + b * PAD
            r[at : at + nz, :] = parts[a, b]
    write_faces(sz, r, *faces)


def start_faces(sz, parts, cells, after):
    outs = [shape(sz.rows_all, sz.orb, F32), shape(*cells.shape, F32)] + face_outs(sz)
    body = functools.partial(start_body, sz)
    r, cells, *faces = kernel_call(body, outs, [parts, cells], after=after)
    return r, cells, faces


def cross_body(sz, xr_one, xr_two, ry_lo, ry_hi, sy_one, sy_two):
    last = (sz.nx - 1) * PAD
    lo, hi = read_pair("gx", xr_one, xr_two)
    faces = []
    for raw, b in ((ry_lo, 0), (ry_hi, sz.ny - 1)):
        value = raw[...]
        parts = [
            value[:PAD] + lo[b * PAD : (b + 1) * PAD],
            value[PAD:last],
            value[last : last + PAD] + hi[b * PAD : (b + 1) * PAD],
            value[last + PAD :],
        ]
        faces.append(jnp.concatenate(parts, axis=0))
    write_pair("gy", *faces, sy_one, sy_two)


def cross_faces(sz, *faces):
    outs = [shape(sz.yface, sz.orb, HALO)] * 2
    return kernel_call(functools.partial(cross_body, sz), outs, list(faces))


def add_xy(sz, ra, xr_one, xr_two, yr_one, yr_two):
    last = (sz.nx - 1) * sz.line_x
    low, high = read_pair("gx", xr_one, xr_two)
    ra[0 : sz.line_x, :] += low[: sz.line_x]
    ra[last : last + sz.line_x, :] += high[: sz.line_x]
    for value, b in zip(read_pair("gy", yr_one, yr_two), (0, sz.ny - 1)):
        for a in range(sz.nx):
            at = a * sz.line_x + b * PAD
            ra[at : at + PAD, :] += value[a * PAD : (a + 1) * PAD]


def local_term(weight, fields, at):
    value = weight * fields[0][at, :]
    return value - fields[1][at, :] if len(fields) > 1 else value


def layer_rows(y, weight, fields, at):
    rows = pl.ds(at, PAD, stride=PAD)
    return y[rows, :] - local_term(weight, fields, rows) if fields else y[rows, :]


def pack_z(sz, y, weight, fields, j):
    rows, c = [], layer_sent(sz, j)
    for a in range(sz.nx):
        for b in range(0, sz.face_b, PAD):
            rows.append(layer_rows(y, weight, fields, a * sz.line_x + b * PAD + c))
    rest = sz.zface - sz.nx * sz.face_b
    if rest:
        rows.append(jnp.zeros((rest, sz.orb), F32))
    value, valid = jnp.concatenate(rows, axis=0), link_valid(sz, j)
    return (value if valid is None else value * valid.astype(F32)).astype(HALO)


def add_z(sz, y, j, face, layers=None):
    c = layer_received(sz, j)
    for a in layers or range(sz.nx):
        for b in range(0, sz.ny, PAD):
            n = min(PAD, sz.ny - b)
            at = pl.ds(a * sz.line_x + b * PAD + c, n, stride=PAD)
            y[at, :] = y[at, :] + face[a * sz.face_b + b : a * sz.face_b + b + n]


def face_cells(sz, y, weight, fields, j):
    rows, c = [], layer_sent(sz, j)
    for p, q in sz.cells:
        for a in range(EDGE):
            at = (ORDER * p + a) * sz.line_x + ORDER * q * PAD
            rows.append(layer_rows(y, weight, fields, at + c))
    rest = sz.fall - sz.fcell * len(sz.cells)
    if rest:
        rows.append(jnp.zeros((rest, sz.orb), F32))
    return jnp.concatenate(rows, axis=0).astype(BF16)


def message_cells(sz, face):
    rows = []
    for p, q in sz.cells:
        for a in range(EDGE):
            at = (ORDER * p + a) * sz.face_b + ORDER * q
            rows.append(face[at : at + PAD])
    rest = sz.fall - sz.fcell * len(sz.cells)
    if rest:
        rows.append(jnp.zeros((rest, sz.orb), F32))
    return jnp.concatenate(rows, axis=0).astype(BF16)


def project_body(sz, weight, past, refs):
    take = iter(refs)
    r = next(take)
    fields = [next(take) for _ in range(past)]
    halos = [next(take) for _ in range(4)]
    q = next(take)
    if not sz.pair:
        qfaces = [next(take) for _ in range(sz.links)]
        maps = next(take)
    y, own = next(take), next(take)
    beside = [next(take) for _ in range(sz.links)]
    messages = [next(take) for _ in range(sz.shifts)]
    everything = slice(0, sz.rows_all)
    y[...] = r[...] + local_term(weight, fields, everything) if past else r[...]
    add_xy(sz, y, *halos)
    blocks = [cell_block(sz, y, cell).astype(BF16) for cell in sz.cells]
    rest = sz.all_pad - sz.cell_pad * len(sz.cells)
    if rest:
        blocks.append(jnp.zeros((rest, sz.orb), BF16))
    sums = dot(q[...], jnp.concatenate(blocks, axis=0))
    own[...] = sums
    if sz.pair:
        messages[0][0:SLOTS, :] = sums.astype(HALO)
        messages[0][SLOTS : SLOTS + sz.zface, :] = pack_z(sz, y, weight, fields, 0)
        beside[0][...] = face_cells(sz, y, weight, fields, 0)
        return
    known = [sums.astype(BF16)]
    for j, matrix in enumerate(qfaces):
        value, valid = dot_first(matrix[...], face_cells(sz, y, weight, fields, j)), link_valid(sz, j)
        beside[j][...] = (value if valid is None else value * valid.astype(F32)).astype(BF16)
        known.append(beside[j][...])
    shift_of = link_shifts(sz)
    for s, message in enumerate(messages):
        rows = slice(s * SLOTS, (s + 1) * SLOTS)
        mapped = [0] + [j + 1 for j, shift in enumerate(shift_of) if shift != s + 1]
        direct = [j for j, shift in enumerate(shift_of) if shift == s + 1]
        total = sum(dot(maps[rows, k * SLOTS : (k + 1) * SLOTS], known[k]) for k in mapped)
        for j in direct:
            total = total + known[j + 1].astype(F32)
            message[SLOTS : SLOTS + sz.zface, :] = pack_z(sz, y, weight, fields, j)
        message[0:SLOTS, :] = total.astype(HALO)


def project(sz, r, weight, fields, halos, q, mapping):
    outs = [shape(sz.rows_all, sz.orb, F32), shape(SLOTS, sz.orb, F32)]
    outs += [shape(sz.fall if sz.pair else SLOTS, sz.orb, BF16)] * sz.links
    for s in range(1, sz.shifts + 1):
        outs.append(shape(SLOTS + (sz.zface if s in link_shifts(sz) else 0), sz.orb, HALO))

    def body(*refs):
        project_body(sz, weight, len(fields), refs)

    y, own, *rest = kernel_call(
        body,
        outs,
        [r, *fields, *halos, q, *mapping],
        flops=4 * 10**8,
        limit=(32 << 20) if sz.shifts < 8 else (56 << 20),
    )
    return y, [own, *rest[: sz.links]], rest[sz.links :]


def couple(c_hi, c_lo, totals):
    high = totals.astype(BF16)
    low = (totals - high.astype(F32)).astype(BF16)
    return dot(c_hi[...], high) + (dot(c_hi[...], low) + dot(c_lo[...], high))


def couple_body(sz, own, *refs):
    beside = refs[: sz.links]
    *rows, back, c_hi, c_lo, coupled = refs[sz.links :]
    totals = own[...]
    for j, part in enumerate(beside):
        value = part[...]
        if sz.pair:
            value = dot_first(rows[0][...], value).astype(BF16)
        totals = totals + dot(back[:, j * SLOTS : (j + 1) * SLOTS], value)
    coupled[...] = couple(c_hi, c_lo, totals)


def couple_own(sz, own, qfaces, back, c_hi, c_lo):
    outs = [shape(SLOTS, sz.orb, F32)]
    body = functools.partial(couple_body, sz)
    arrays = [*own, *(qfaces if sz.pair else []), back, c_hi, c_lo]
    return kernel_call(body, outs, arrays, flops=2 * 10**8)[0]


def apply_body(sz, scale, refs):
    take = iter(refs)
    yin, own = next(take), next(take)
    messages = [next(take) for _ in range(sz.shifts)]
    factors = [next(take) for _ in range(3 if sz.pair else 2)]
    qt, kin, pot = [next(take) for _ in range(3)]
    r, y = next(take), next(take)
    faces = [next(take) for _ in range(4)]
    if sz.pair:
        m_hi, m_lo, c_rows = factors
        sums, message = messages[0][0:SLOTS, :].astype(BF16), messages[0]
        face = message[SLOTS : SLOTS + sz.zface, :].astype(F32)
        coef = dot(m_hi[...], sums) + dot(m_lo[...], sums)
        coef = own[...] + (coef + dot(c_rows[...], message_cells(sz, face)))
    else:
        totals = sum(message[0:SLOTS, :].astype(F32) for message in messages)
        coef = own[...] + couple(*factors, totals)
    coef = coef.astype(BF16)
    y[...] = yin[...]
    for j, shift in enumerate(link_shifts(sz)):
        add_z(sz, y, j, messages[shift - 1][SLOTS : SLOTS + sz.zface, :].astype(F32))
    blocks = [cell_block(sz, y, cell) for cell in sz.cells]
    stiff = dot(kin[...], jnp.concatenate([b.astype(BF16) for b in blocks], axis=1))
    spread = dot(qt[: sz.cell_pad * len(sz.cells), :], coef)
    for g, (p, q) in enumerate(sz.cells):
        rows = slice(g * sz.cell_pad, (g + 1) * sz.cell_pad)
        value = stiff[:, g * sz.orb : (g + 1) * sz.orb] + pot[rows, :] * blocks[g]
        value = (value + spread[rows]) * scale
        for a in range(EDGE):
            start = (ORDER * p + a) * sz.line_x + ORDER * q * PAD
            line = value[a * EDGE * PAD : (a + 1) * EDGE * PAD]
            shared = EDGE * PAD if p and a == 0 else PAD if q else 0
            if shared:
                r[start : start + shared, :] += line[:shared]
            if shared < EDGE * PAD:
                r[start + shared : start + EDGE * PAD, :] = line[shared:]
    r[sz.rows :, :] = jnp.zeros((sz.rows_all - sz.rows, sz.orb), F32)
    write_faces(sz, r, *faces)


def apply(sz, y, own, messages, factors, qt, kin, pot, scale):
    outs = [shape(sz.rows_all, sz.orb, F32)] * 2 + face_outs(sz)
    arrays = [y, own, *messages, *factors, qt, kin, pot]

    def body(*refs):
        apply_body(sz, scale, refs)

    r, y, *faces = kernel_call(body, outs, arrays, flops=6 * 10**8, limit=32 << 20)
    return r, y, faces


def last_faces_body(sz, refs):
    take = iter(refs)
    r = next(take)
    halos = [next(take) for _ in range(4)]
    ra = next(take)
    outs = [next(take) for _ in range(sz.links)]
    ra[...] = r[...]
    add_xy(sz, ra, *halos)
    for j, out in enumerate(outs):
        out[...] = pack_z(sz, ra, None, [], j)


def last_faces(sz, r, halos):
    def body(*refs):
        last_faces_body(sz, refs)

    outs = [shape(sz.rows_all, sz.orb, F32)] + [shape(sz.zface, sz.orb, HALO)] * sz.links
    ra, *sent = kernel_call(body, outs, [r, *halos])
    return ra, sent


def add_local_body(weight, past, r, *refs):
    fields, out = refs[:past], refs[past]
    out[...] = r[...] + local_term(weight, fields, slice(0, out.shape[0]))


def add_local(sz, r, weight, fields):
    body = functools.partial(add_local_body, weight, len(fields))
    return kernel_call(body, [shape(sz.rows_all, sz.orb, F32)], [r, *fields])[0]


def finish_body(sz, r, *refs):
    zr = refs[: sz.links]
    out, ra, block, sent = refs[sz.links :]
    received = [face[...].astype(F32) for face in zr]
    nz = block.shape[2]
    pieces, copies = 3, []
    for k in range(pieces):
        first, last = k * sz.nx // pieces, (k + 1) * sz.nx // pieces
        rows = slice(first * sz.line_x, last * sz.line_x)
        ra[rows, :] = r[rows, :]
        for j, face in enumerate(received):
            add_z(sz, ra, j, face, range(first, last))
        value = ra[rows, :]
        value = value.reshape(last - first, sz.ny, PAD, sz.orb)[:, :, :nz, :]
        block[first:last] = value
        copy = pltpu.make_async_copy(block.at[first:last], out.at[first:last], sent.at[k])
        copy.start()
        copies.append(copy)
    for copy in copies:
        copy.wait()


def finish(sz, r, zr, nz):
    outs = [jax.ShapeDtypeStruct((sz.nx, sz.ny, nz, sz.orb), F32)]
    scratch = [
        pltpu.VMEM((sz.rows_all, sz.orb), F32),
        pltpu.VMEM((sz.nx, sz.ny, nz, sz.orb), F32),
        pltpu.SemaphoreType.DMA((3,)),
    ]
    body = functools.partial(finish_body, sz)
    anywhere = [pl.BlockSpec(memory_space=pl.ANY)]
    return kernel_call(body, outs, [r, *zr], scratch=scratch, out_specs=anywhere)[0]


def swap_faces(axis, one, two):
    axes = ("gx", "gy")
    wide, deep = lax.axis_size("gx"), lax.axis_size("gy")
    count = wide if axis == "gx" else deep

    def partner(i, j, low):
        at = i if axis == "gx" else j
        to = at + 1 if at % 2 == low else at - 1
        if 0 <= to < count:
            return (to, j) if axis == "gx" else (i, to)
        if axis == "gy" and wide % 2 == 0:
            return (i ^ 1, j)
        ends = sorted({k for k in range(count) if not 0 <= k + (1 if k % 2 == low else -1) < count})
        to = ends[::-1][ends.index(at)]
        return (to, j) if axis == "gx" else (i, to)

    out = []
    for face, low in ((one, FIRST[axis]), (two, 1 - FIRST[axis])):
        pairs = []
        for i in range(wide):
            for j in range(deep):
                to = partner(i, j, low)
                pairs.append((i * deep + j, to[0] * deep + to[1]))
        out.append(lax.ppermute(face, axes, pairs))
    return out


def local(parts, cell_matrix, cell_potential, projectors, slot_atom, slot_cells, coupling):
    nx, ny, nz, orbitals = parts.shape
    nodes = cell_matrix.shape[0]
    devices = lax.axis_size("gz")
    sz = Sizes(nx, ny, nz, orbitals, devices - 1)
    ring = [[(i, (i + s) % devices) for i in range(devices)] for s in range(devices)]

    proj = projectors.reshape(nodes, POS * BLK * PA)
    proj = jnp.pad(proj, ((0, up(nodes, 16) - nodes), (0, 0)))
    cells = jnp.transpose(slot_cells.reshape(POS, BLK))
    r, cells, faces = start_faces(sz, parts, cells, [proj])

    def exchange_xy(sx_one, sx_two, sy_lo, sy_hi):
        xr = swap_faces("gx", sx_one, sx_two)
        cross = cross_faces(sz, *xr, sy_lo, sy_hi)
        yr = swap_faces("gy", *cross)
        return (*xr, *yr)

    halos = exchange_xy(*faces)
    qt, *face_rows = sum_matrices(sz, proj, cells)
    qfaces = []
    for j, shift in enumerate(link_shifts(sz)):
        back = [(target, source) for source, target in ring[shift]]
        qfaces.append(lax.ppermute(face_rows[j], "gz", back))
    pot = jnp.transpose(cell_potential, (1, 2, 3, 0)).reshape(len(sz.cells), nodes)
    q, kin, pot, back, c_hi, c_lo, *others = turn_matrices(
        sz,
        qt,
        cell_matrix,
        pot,
        slot_atom.reshape(devices, POS),
        jnp.transpose(coupling, (1, 2, 0)),
        face_rows,
    )
    factors = others if sz.pair else [c_hi, c_lo]
    mapping = [] if sz.pair else [*qfaces, *others]

    fields, scale = [], 1.0 / half_width
    weight = 0.0
    for step in range(STEPS):
        y, own, messages = project(sz, r, weight, fields, halos, q, mapping)
        received = [lax.ppermute(m, "gz", ring[s + 1]) for s, m in enumerate(messages)]
        own = couple_own(sz, own, qfaces, back, c_hi, c_lo)
        r, y, faces = apply(sz, y, own, received, factors, qt, kin, pot, scale)
        fields, weight = [y] + fields[:1], -center_value * scale
        scale = 2.0 / half_width
        halos = exchange_xy(*faces)
    r, sent = last_faces(sz, r, halos)
    zr = [lax.ppermute(f, "gz", ring[s]) for f, s in zip(sent, link_shifts(sz))]
    return finish(sz, add_local(sz, r, weight, fields), zr, nz)


def solution(mesh):
    in_specs = (
        P("gx", "gy", "gz", None),
        P(),
        P(None, "gx", "gy", "gz"),
        P("gx", "gy", "gz", None, None),
        P("gx", "gy", None, None),
        P("gx", "gy", "gz", None, None),
        P(("gx", "gy"), None, None),
    )
    out_specs = P("gx", "gy", "gz", None)
    return jax.shard_map(local, mesh=mesh, in_specs=in_specs, out_specs=out_specs, check_vma=False)
```
